32 devices in a mesh: circ: 8 (over z, core), span: 4 (over y, x).
Axes of the slice: x: 2, y: 2, z: 4, core: 2. Of those that a mesh axis runs over, the one named last changes fastest.
Arguments:
- adjoint_rotor: float32 [6, 8, 4, 2048], P(None, 'span', None, 'circ'), may hold values from -6 to 6
- adjoint_stator: float32 [6, 8, 4, 2048], P(None, 'span', None, 'circ'), may hold values from -6 to 6
- jac_diag_rotor: float32 [6, 8, 4, 2048], P(None, 'span', None, 'circ'), may hold values from 2 to 4
- jac_diag_stator: float32 [6, 8, 4, 2048], P(None, 'span', None, 'circ'), may hold values from 2 to 4
- jac_off_rotor: bfloat16 [6, 6, 8, 4, 2048], P(None, None, 'span', None, 'circ'), may hold values from -1 to 1
- jac_off_stator: bfloat16 [6, 6, 8, 4, 2048], P(None, None, 'span', None, 'circ'), may hold values from -1 to 1
- source_rotor: float32 [6, 8, 4, 2048], P(None, 'span', None, 'circ'), may hold values from -6 to 6
- source_stator: float32 [6, 8, 4, 2048], P(None, 'span', None, 'circ'), may hold values from -6 to 6
- rotor_state: bfloat16 [6, 8, 2048], P(None, 'span', 'circ'), may hold values from -6 to 6
- margin_block: int32 [8, 16, 4], P('span'), may hold values from 0 to 15, as said below
- face_count: int32 [8, 16], P('span'), may hold values from 1 to 4
- margin_weight: float32 [8, 16, 4, 128], P('span'), may hold values from 0.2 to 1
Outputs:
- rotor_adjoint: float32 [6, 8, 4, 2048], P(None, 'span', None, 'circ')
- stator_adjoint: float32 [6, 8, 4, 2048], P(None, 'span', None, 'circ')
The draws below stay inside these ranges and needn't reach their ends.
Inputs may be any that keep to these rules, and one draw needn't show every extreme that they name: `margin_block`: entry k of the list of stator block b in spanwise row s is rotor block (b + o + 2 * 2 * s + 1 + j + k) mod 16, with one o for the whole array and j from 0 to 2 for each block of each row.
All inputs are finite; a program needn't handle non-finite values.
Results may differ from the reference program's by a relative error of at most 0.00055.
Values may be sent and summed in bfloat16 or wider, within the bound.
No kernel may reach another device: no remote copies, remote signals or barrier semaphores. Data moves between devices by JAX's collectives and lax.ppermute only.
A program may use at most 64 MiB of HBM per device.

```python
import jax
import jax.numpy as jnp
from jax import lax

VARS = 6
LAYERS = 4
BLOCKS_DEV = 2
BLOCK = 128
MARGINS = 4
STEPS = 2
SPANS = 8
BLOCKS = 16
CELLS = 2048


def draw_margin_block(key, part):
    rotation = jax.random.randint(jax.random.fold_in(key, 11), (), 0, BLOCKS, dtype=jnp.int32)
    jitter = jax.random.randint(jax.random.fold_in(key, 12), (SPANS, BLOCKS, 1), 0, 3, dtype=jnp.int32)
    lean = (2 * BLOCKS_DEV * jnp.arange(SPANS, dtype=jnp.int32) + BLOCKS_DEV - 1)[:, None, None]
    stator_blocks = jnp.arange(BLOCKS, dtype=jnp.int32)[None, :, None]
    entries = jnp.arange(MARGINS, dtype=jnp.int32)[None, None, :]
    return ((stator_blocks + rotation + lean + jitter + entries) % BLOCKS).astype(jnp.int32)


def with_ends(values, stream_key, low, top_value):
    longest = values.shape.index(max(values.shape))
    spots = []
    for shift in (0, 1):
        where = [jax.random.randint(jax.random.fold_in(stream_key, axis), (), 0, length) for axis, length in enumerate(values.shape)]
        where[longest] = (where[longest] + shift) % values.shape[longest]
        spots.append(tuple(where))
    return values.at[spots[0]].set(low).at[spots[1]].set(top_value)


def block_scale(own_key, dims, shards, smallest, largest):
    def one(dim, blocks):
        heights = jax.random.uniform(jax.random.fold_in(jax.random.fold_in(own_key, 6), dim), (blocks,), jnp.float32, smallest / len(shards), largest / len(shards))
        return jnp.repeat(jnp.exp(heights), dims[dim] // blocks).reshape((-1,) + (1,) * (len(dims) - dim - 1))

    factor_of = one(*shards[0])
    for cut in shards[1:]:
        factor_of = factor_of * one(*cut)
    return factor_of


def gaussian(stream_key, dims, scale, limit, cuts=(), kind=jnp.bfloat16):
    result = scale * jax.random.normal(stream_key, dims, jnp.float32)
    if cuts:
        result = result * block_scale(stream_key, dims, cuts, -0.22, 0.18)
    return jnp.clip(result, -limit, limit).astype(kind)


def setup_inputs(seed: int = 0) -> dict:
    key_list = jax.random.split(jax.random.key(seed), 13)
    adjoint_rotor = gaussian(key_list[0], (VARS, SPANS, LAYERS, CELLS), 1.0, 6.0, ((1, 4), (3, 8)), jnp.float32)
    adjoint_stator = gaussian(key_list[1], (VARS, SPANS, LAYERS, CELLS), 1.0, 6.0, ((1, 4), (3, 8)), jnp.float32)
    jac_diag_rotor = jnp.clip(2.0 + 2.0 * jax.random.uniform(key_list[2], (VARS, SPANS, LAYERS, CELLS), jnp.float32) ** block_scale(key_list[2], (VARS, SPANS, LAYERS, CELLS), ((1, 4), (3, 8)), -0.2, 0.2), 2.0, 4.0)
    jac_diag_stator = jnp.clip(2.0 + 2.0 * jax.random.uniform(key_list[3], (VARS, SPANS, LAYERS, CELLS), jnp.float32) ** block_scale(key_list[3], (VARS, SPANS, LAYERS, CELLS), ((1, 4), (3, 8)), -0.2, 0.2), 2.0, 4.0)
    jac_off_rotor = gaussian(key_list[4], (VARS, VARS, SPANS, LAYERS, CELLS), 0.3, 1.0, ((2, 4), (4, 8)))
    jac_off_stator = gaussian(key_list[5], (VARS, VARS, SPANS, LAYERS, CELLS), 0.3, 1.0, ((2, 4), (4, 8)))
    source_rotor = gaussian(key_list[6], (VARS, SPANS, LAYERS, CELLS), 1.0, 6.0, ((1, 4), (3, 8)), jnp.float32)
    source_stator = gaussian(key_list[7], (VARS, SPANS, LAYERS, CELLS), 1.0, 6.0, ((1, 4), (3, 8)), jnp.float32)
    rotor_state = gaussian(key_list[8], (VARS, SPANS, CELLS), 1.0, 6.0, ((1, 4), (2, 8)))
    margin_block = draw_margin_block(jax.random.fold_in(key_list[12], 71), 0)
    face_count = with_ends(jax.random.randint(key_list[10], (SPANS, BLOCKS), 1, MARGINS + 1), jax.random.fold_in(key_list[10], 1), 1, MARGINS).astype(jnp.int32)
    margin_weight = jnp.clip(0.2 + 0.8 * jax.random.uniform(key_list[11], (SPANS, BLOCKS, MARGINS, BLOCK), jnp.float32) ** block_scale(key_list[11], (SPANS, BLOCKS, MARGINS, BLOCK), ((0, 4),), -0.2, 0.2), 0.2, 1.0)
    return dict(adjoint_rotor=adjoint_rotor, adjoint_stator=adjoint_stator, jac_diag_rotor=jac_diag_rotor, jac_diag_stator=jac_diag_stator, jac_off_rotor=jac_off_rotor, jac_off_stator=jac_off_stator, source_rotor=source_rotor, source_stator=source_stator, rotor_state=rotor_state, margin_block=margin_block, face_count=face_count, margin_weight=margin_weight)


step_size = 0.1
coupling = 0.2

def interface_flux(primal, adjoint):
    speeds = jnp.sqrt(1.0 + primal * primal)
    projection = lax.optimization_barrier(jnp.sum(primal * adjoint, axis=0)) / (6.0 + lax.optimization_barrier(jnp.sum(primal * primal, axis=0)))
    return speeds * adjoint + 0.5 * primal * projection[None]

def jacobian_apply(jac_diag, jac_off, adjoint):
    applied = jac_diag * adjoint
    for source_var in range(adjoint.shape[0]):
        applied = applied + jac_off[source_var].astype(jnp.float32) * adjoint[source_var][None]
    return applied

def neighbours(adjoint):
    beside_all = jnp.roll(adjoint, 1, axis=3) + jnp.roll(adjoint, -1, axis=3)
    layer_pad = jnp.pad(adjoint, ((0, 0), (0, 0), (1, 1), (0, 0)))
    beside_all = beside_all + layer_pad[:, :, 2:] + layer_pad[:, :, :-2]
    span_pad = jnp.pad(adjoint, ((0, 0), (1, 1), (0, 0), (0, 0)))
    return beside_all + span_pad[:, 2:] + span_pad[:, :-2]

def reference(adjoint_rotor, adjoint_stator, jac_diag_rotor, jac_diag_stator, jac_off_rotor, jac_off_stator, source_rotor, source_stator, rotor_state, margin_block, face_count, margin_weight):
    live_mask = (jnp.arange(MARGINS, dtype=jnp.int32)[None, None, :] < face_count[:, :, None]).astype(jnp.float32)
    weights_live = margin_weight * live_mask[:, :, :, None]
    rotor_blocks = rotor_state.astype(jnp.float32).reshape(VARS, SPANS, BLOCKS, BLOCK)
    span_index = jnp.arange(SPANS, dtype=jnp.int32)[:, None]
    stator_primal = jnp.zeros((VARS, SPANS, BLOCKS, BLOCK), jnp.float32)
    for column in range(MARGINS):
        picked = rotor_blocks[:, span_index, margin_block[:, :, column], :]
        stator_primal = stator_primal + weights_live[None, :, :, column, :] * picked
    stator_primal = stator_primal.reshape(VARS, SPANS, CELLS)
    rotor_adj, stator_adj = (adjoint_rotor, adjoint_stator)
    for sweep in range(STEPS):
        face_flux = interface_flux(stator_primal, stator_adj[:, :, 0, :])
        flux_wire = lax.optimization_barrier(face_flux.astype(jnp.bfloat16)).astype(jnp.float32)
        flux_blocks = flux_wire.reshape(VARS, SPANS, BLOCKS, BLOCK)
        pulled = jnp.zeros((VARS, SPANS, BLOCKS, BLOCK), jnp.float32)
        for column in range(MARGINS):
            pulled = pulled.at[:, span_index, margin_block[:, :, column], :].add(weights_live[None, :, :, column, :] * flux_blocks)
        pulled = pulled.reshape(VARS, SPANS, CELLS)
        rotor_res = jacobian_apply(jac_diag_rotor, jac_off_rotor, rotor_adj) - coupling * neighbours(rotor_adj) - source_rotor
        rotor_res = rotor_res.at[:, :, LAYERS - 1, :].add(-pulled)
        stator_res = jacobian_apply(jac_diag_stator, jac_off_stator, stator_adj) - coupling * neighbours(stator_adj) - source_stator
        stator_res = stator_res.at[:, :, 0, :].add(face_flux)
        rotor_adj = rotor_adj - step_size * rotor_res
        stator_adj = stator_adj - step_size * stator_res
    return (rotor_adj, stator_adj)
```

```python
import jax
import jax.numpy as jnp
from jax import lax
from jax.sharding import PartitionSpec as P

STEPS = 2


step_size = 0.1
coupling = 0.2
highest = lax.Precision.HIGHEST


def extended(x, sides, width):
    for axis, dim in sides:
        size, length = (lax.axis_size(axis), x.shape[dim])
        up = [(i, (i + 1) % size) for i in range(size)]
        down = [(j, i) for i, j in up]
        last = lax.slice_in_dim(x, length - width, length, axis=dim)
        first = lax.slice_in_dim(x, 0, width, axis=dim)
        before = lax.ppermute(last, axis, up)
        after = lax.ppermute(first, axis, down)
        x = jnp.concatenate([before, x, after], axis=dim)
    return x


def interface_flux(primal, adjoint):
    speeds = jnp.sqrt(1.0 + primal * primal)
    projection = jnp.sum(primal * adjoint, axis=0) / (6.0 + jnp.sum(primal * primal, axis=0))
    return speeds * adjoint + 0.5 * primal * projection[None]


def jacobian_apply(jac_diag, jac_off, adjoint):
    applied = jac_diag * adjoint
    for source_var in range(adjoint.shape[0]):
        applied = applied + jac_off[source_var].astype(jnp.float32) * adjoint[source_var][None]
    return applied


def per_device(
    adjoint_rotor,
    adjoint_stator,
    jac_diag_rotor,
    jac_diag_stator,
    jac_off_rotor,
    jac_off_stator,
    source_rotor,
    source_stator,
    rotor_state,
    margin_block,
    face_count,
    margin_weight,
):
    var_count = adjoint_rotor.shape[0]
    span_rows = adjoint_rotor.shape[1]
    layer_count = adjoint_rotor.shape[2]
    cell_count = adjoint_rotor.shape[3]
    entry_total = margin_weight.shape[2]
    block_width = margin_weight.shape[3]
    own_blocks = cell_count // block_width
    circ_at = lax.axis_index("circ")
    first_block = circ_at * own_blocks
    span_at = lax.axis_index("span")
    span_total = lax.axis_size("span")
    live_mask = (
        jnp.arange(entry_total, dtype=jnp.int32)[None, None, :] < face_count[:, :, None]
    ).astype(jnp.float32)
    weights_live = margin_weight * live_mask[:, :, :, None]
    own_ids = lax.dynamic_slice_in_dim(margin_block, first_block, own_blocks, 1)
    own_weights = lax.dynamic_slice_in_dim(weights_live, first_block, own_blocks, 1)
    portion = lax.all_gather(rotor_state, "circ", axis=2, tiled=True)
    row_count = portion.shape[2] // block_width
    blocks = portion.reshape(var_count, span_rows, row_count, block_width).astype(jnp.float32)
    pick_one_hot = (
        own_ids[:, :, :, None] == jnp.arange(row_count, dtype=jnp.int32)[None, None, None, :]
    ).astype(jnp.float32)
    pick_mixing = jnp.einsum("sbkj,sbkc->sbjc", pick_one_hot, own_weights, precision=highest)
    stator_primal = jnp.einsum("sbjc,vsjc->vsbc", pick_mixing, blocks, precision=highest).reshape(
        var_count, span_rows, cell_count
    )
    low_keep = jnp.where(span_at == 0, 0.0, 1.0).astype(jnp.float32)
    high_keep = jnp.where(span_at == span_total - 1, 0.0, 1.0).astype(jnp.float32)
    below_mask = jnp.ones((span_rows,), jnp.float32).at[0].set(low_keep)[None, None, :, None, None]
    above_mask = (
        jnp.ones((span_rows,), jnp.float32)
        .at[span_rows - 1]
        .set(high_keep)[None, None, :, None, None]
    )
    reached = first_block + jnp.arange(own_blocks, dtype=jnp.int32)
    pull_one_hot = (
        margin_block[:, None, :, :] == reached[None, :, None, None]
    ).astype(jnp.float32)
    pull_mixing = jnp.einsum("sjbk,sbkc->sjbc", pull_one_hot, weights_live, precision=highest)
    rotor_adj, stator_adj = (adjoint_rotor, adjoint_stator)
    for sweep in range(STEPS):
        stacked = jnp.stack((rotor_adj, stator_adj))
        padded = extended(stacked.astype(jnp.bfloat16), (("circ", 4), ("span", 2)), 1).astype(
            stacked.dtype
        )
        inner = padded[:, :, 1:-1, :, :]
        beside_all = inner[:, :, :, :, 2:] + inner[:, :, :, :, :-2]
        layer_pad = jnp.pad(stacked, ((0, 0), (0, 0), (0, 0), (1, 1), (0, 0)))
        beside_all = beside_all + layer_pad[:, :, :, 2:] + layer_pad[:, :, :, :-2]
        beside_all = (
            beside_all
            + padded[:, :, :-2, :, 1:-1] * below_mask
            + padded[:, :, 2:, :, 1:-1] * above_mask
        )
        face_flux = interface_flux(stator_primal, stator_adj[:, :, 0, :])
        flux_wire = face_flux.astype(jnp.bfloat16)
        flux_blocks = flux_wire.astype(jnp.float32).reshape(
            var_count, span_rows, own_blocks, block_width
        )
        gathered = lax.all_gather(flux_wire, "circ", axis=2, tiled=True)
        gathered_blocks = gathered.astype(jnp.float32).reshape(
            var_count, span_rows, row_count, block_width
        )
        pulled = jnp.einsum(
            "sjbc,vsbc->vsjc", pull_mixing, gathered_blocks, precision=highest
        ).reshape(var_count, span_rows, cell_count)
        rotor_res = (
            jacobian_apply(jac_diag_rotor, jac_off_rotor, rotor_adj)
            - coupling * beside_all[0]
            - source_rotor
        )
        rotor_res = rotor_res.at[:, :, layer_count - 1, :].add(-pulled)
        stator_res = (
            jacobian_apply(jac_diag_stator, jac_off_stator, stator_adj)
            - coupling * beside_all[1]
            - source_stator
        )
        stator_res = stator_res.at[:, :, 0, :].add(face_flux)
        rotor_adj = rotor_adj - step_size * rotor_res
        stator_adj = stator_adj - step_size * stator_res
    return (rotor_adj, stator_adj)


def solution(mesh):
    placed = (
        P(None, "span", None, "circ"),
        P(None, "span", None, "circ"),
        P(None, "span", None, "circ"),
        P(None, "span", None, "circ"),
        P(None, None, "span", None, "circ"),
        P(None, None, "span", None, "circ"),
        P(None, "span", None, "circ"),
        P(None, "span", None, "circ"),
        P(None, "span", "circ"),
        P("span", None, None),
        P("span", None),
        P("span", None, None, None),
    )
    return jax.shard_map(
        per_device,
        mesh=mesh,
        in_specs=placed,
        out_specs=(P(None, "span", None, "circ"), P(None, "span", None, "circ")),
        check_vma=False,
    )
```

```python
import jax
import jax.numpy as jnp
from jax import lax
from jax.experimental import pallas as pl
from jax.experimental.pallas import tpu as pltpu
from jax.sharding import PartitionSpec as P

step_size = 0.1
coupling = 0.2
carry = step_size * coupling
REACH = 8
TILE = 128
f32 = jnp.float32
params = pltpu.CompilerParams(vmem_limit_bytes=24 * 1024 * 1024)


def iota(shape, dim):
    return lax.broadcasted_iota(jnp.int32, shape, dim)


def wrapped(x, count):
    if count & (count - 1) == 0:
        return jnp.bitwise_and(x, count - 1)
    return lax.rem(x + 4 * count, count)


def lanes_apart(x):
    cells = x.shape[1]
    lane = iota(x.shape, 1)
    before = jnp.where(lane == 0, 0.0, pltpu.roll(x, 1, 1))
    after = jnp.where(lane == cells - 1, 0.0, pltpu.roll(x, cells - 1, 1))
    return before + after


def layers_apart(x):
    return pltpu.roll(x, 1, 0) + pltpu.roll(x, 7, 0)


def edge_pick(row, cells):
    at = iota((8, cells), 0)
    lane = iota((8, cells), 1)
    first = jnp.logical_and(at == row, lane == 0)
    last = jnp.logical_and(at == 4 + row, lane == cells - 1)
    return jnp.where(jnp.logical_or(first, last), 1.0, 0.0).astype(f32)


def flux_of(primal, adjoint):
    speeds = jnp.sqrt(1.0 + primal * primal)
    over = jnp.sum(primal * adjoint, axis=0, keepdims=True)
    under = 6.0 + jnp.sum(primal * primal, axis=0, keepdims=True)
    return speeds * adjoint + 0.5 * primal * (over / under)


def jacobian_row(diag, off, state, v, s, var_count):
    total = diag[v, s] * state[v]
    for w in range(var_count):
        total = total + off[w, v, s].astype(f32) * state[w]
    return total


def pull_row(flux, weights, margin, count, s, slot, first_block, base, total):
    target = wrapped(first_block + slot + total, total)
    acc = jnp.zeros((8, TILE), f32)
    for e in range(REACH):
        b = wrapped(base + slot + e, total)
        k = wrapped(target - margin[s, b, 0] + total, total)
        live = jnp.where(k < count[s, b], 1.0, 0.0).astype(f32)
        kept = jnp.minimum(k, weights.shape[2] - 1)
        acc = acc + (weights[s, b, pl.ds(kept, 1), :] * live) * flux(slot + e)
    return acc


def first_kernel(a_r, a_s, jd_r, jd_s, jo_r, jo_s, src_r, src_s, state, v_r, v_s, out, *xs):
    var_count, rows, layers, cells = a_r.shape
    own_blocks = cells // TILE
    out[...] = jnp.zeros(out.shape, f32)
    for x in xs:
        x[...] = jnp.zeros(x.shape, f32)
    fields = ((a_r, jd_r, jo_r, src_r, v_r, xs[0], xs[2]), (a_s, jd_s, jo_s, src_s, v_s, xs[1], xs[3]))
    for a, jd, jo, src, partial, x_a, x_p in fields:
        for v in range(var_count):
            for s in range(rows):
                x_a[v * rows + s, 0:layers, :] = a[v, s]
        for s in range(rows):
            state_row = [a[v, s] for v in range(var_count)]
            for v in range(var_count):
                wide = x_a[v * rows + s]
                beside = (lanes_apart(wide) + layers_apart(wide))[0:layers]
                if s > 0:
                    beside = beside + a[v, s - 1]
                if s < rows - 1:
                    beside = beside + a[v, s + 1]
                res = jacobian_row(jd, jo, state_row, v, s, var_count) - coupling * beside - src[v, s]
                new = state_row[v] - step_size * res
                partial[v, s] = new
                x_p[v * rows + s, 0:layers, :] = new
    edges = jnp.zeros((8, TILE), f32)
    for q in range(4):
        flat = xs[q][...].reshape(TILE, cells)
        edges = edges + lax.dot_general(
            edge_pick(q, cells), flat, (((1,), (1,)), ((), ())), preferred_element_type=f32
        )
    for v in range(var_count):
        rotor = state[v].astype(f32)
        for s in range(rows):
            for i in range(own_blocks):
                cut = slice(i * TILE, (i + 1) * TILE)
                at = s * 8 + v
                out[i, at : at + 1, :] = rotor[s : s + 1, cut]
                out[i, rows * 8 + at : rows * 8 + at + 1, :] = a_s[v, s, 0:1, cut]
                out[i, rows * 16 + at : rows * 16 + at + 1, :] = v_s[v, s, 0:1, cut]
    for side, i in ((0, 0), (1, own_blocks - 1)):
        out[i, 6:8, :] = edges[4 * side : 4 * side + 2]
        out[i, 14:16, :] = edges[4 * side + 2 : 4 * side + 4]


def second_kernel(
    g, v_r, v_s, a_r, a_s, weights, margin, count,
    o_r, o_s, h_r, h_s, q_out, p_out, up, down, flux, held, spot,
):
    var_count, rows, layers, cells = a_r.shape
    total = g.shape[0]
    own_blocks = cells // TILE
    entries = weights.shape[2]
    spread = REACH + own_blocks + 1
    first_block = lax.axis_index("circ") * own_blocks
    row8 = iota((8, TILE), 0)
    lane = iota((8, TILE), 1)
    lane_all = iota((layers, cells), 1)
    layer_all = iota((layers, cells), 0)
    edge = jnp.logical_or(lane_all == 0, lane_all == cells - 1)
    left = wrapped(first_block - 1 + total, total)
    right = wrapped(first_block + own_blocks, total)

    spot[0:2, :] = g[left, 6:8, :]
    spot[2:4, :] = g[left, 14:16, :]
    spot[4:6, :] = g[right, 6:8, :]
    spot[6:8, :] = g[right, 14:16, :]
    spots = spot[...]
    columns = [
        lax.dot_general(spots, edge_pick(q, cells), (((0,), (0,)), ((), ())), preferred_element_type=f32)
        for q in range(4)
    ]

    def block(s, b):
        primal = jnp.zeros((8, TILE), f32)
        for k in range(entries):
            live = jnp.where(k < count[s, b], 1.0, 0.0).astype(f32)
            primal = primal + (weights[s, b, k : k + 1, :] * live) * g[margin[s, b, k], s * 8 : s * 8 + 8, :]
        primal = jnp.where(row8 < var_count, primal, 0.0)
        adjoint = g[b, rows * 8 + s * 8 : rows * 8 + s * 8 + 8, :]
        return primal, flux_of(primal, adjoint)

    def advanced(s, b, moved):
        at = slice(rows * 8 + s * 8, rows * 8 + s * 8 + 8)
        place = lax.rem(b, own_blocks)
        before = jnp.where(place == 0, carry, 0.0).astype(f32)
        after = jnp.where(place == own_blocks - 1, carry, 0.0).astype(f32)
        low = pltpu.roll(g[wrapped(b - 1 + total, total), at, :], 1, 1)
        high = pltpu.roll(g[wrapped(b + 1, total), at, :], TILE - 1, 1)
        base = g[b, rows * 16 + s * 8 : rows * 16 + s * 8 + 8, :]
        base = base + jnp.where(lane == 0, low * before, 0.0) + jnp.where(lane == TILE - 1, high * after, 0.0)
        return base - step_size * moved

    for s in range(rows):
        base = first_block - margin[s, 0, 0] - 5 + 4 * total
        for t in range(spread):
            b = wrapped(base - 1 + t, total)
            primal, moved = block(s, b)
            flux[s, t] = moved.astype(jnp.bfloat16).astype(f32)
            if 0 < t < spread - 1:
                q_out[s, t - 1] = primal
                p_out[s, t - 1] = advanced(s, b, moved)
        own = []
        for i in range(own_blocks):
            primal, moved = block(s, first_block + i)
            own.append(moved)
            q_out[s, spread - 2 + i] = primal
            p_out[s, spread - 2 + i] = advanced(s, first_block + i, moved)
        blank = [jnp.zeros((8, TILE), f32)] * (own_blocks - 2)
        side_flux = [block(s, left)[1], block(s, right)[1]]
        pulls = [
            pull_row(lambda t: flux[s, t + 1], weights, margin, count, s, slot, first_block, base, total)
            for slot in range(-1, own_blocks + 1)
        ]

        def at_sides(low, high):
            return jnp.concatenate([pltpu.roll(low, 1, 1), *blank, pltpu.roll(high, TILE - 1, 1)], axis=1)

        pulled = step_size * jnp.concatenate(pulls[1:-1], axis=1)
        pulled_side = step_size * at_sides(pulls[0], pulls[-1])
        pushed = step_size * jnp.concatenate(own, axis=1)
        pushed_side = step_size * at_sides(*side_flux)
        for v in range(var_count):
            at = (v * rows + s) * 8
            cut = slice(at, at + layers)
            o_r[v, s] = (
                v_r[v, s] + carry * columns[0][cut] + jnp.where(layer_all == layers - 1, pulled[v : v + 1], 0.0)
            )
            o_s[v, s] = v_s[v, s] + carry * columns[1][cut] - jnp.where(layer_all == 0, pushed[v : v + 1], 0.0)
            h_r[v, s] = columns[2][cut] + jnp.where(
                edge, carry * a_r[v, s] + jnp.where(layer_all == layers - 1, pulled_side[v : v + 1], 0.0), 0.0
            )
            h_s[v, s] = columns[3][cut] + jnp.where(
                edge, carry * a_s[v, s] - jnp.where(layer_all == 0, pushed_side[v : v + 1], 0.0), 0.0
            )

    last = jnp.concatenate([spots, jnp.ones((8, TILE), f32)], axis=0).astype(jnp.bfloat16)
    for to, s in ((up, rows - 1), (down, 0)):
        at = slice(rows * 8 + s * 8, rows * 8 + s * 8 + 8)
        for j in range(total // 2):
            to[j] = jnp.concatenate([g[2 * j, at, :], g[2 * j + 1, at, :]], axis=0).astype(jnp.bfloat16)
        for v in range(var_count):
            for n, ref in enumerate((a_r, a_s, o_r, o_s)):
                held[v, n * layers : (n + 1) * layers, :] = ref[v, s]
            for i in range(own_blocks):
                to[total // 2 + v * own_blocks + i] = held[v, :, i * TILE : (i + 1) * TILE].astype(jnp.bfloat16)
        to[total // 2 + var_count * own_blocks] = last


def third_kernel(
    low, high, o_r, o_s, h_r, h_s, q, p, a_r, a_s, jd_r, jd_s, jo_r, jo_s, src_r, src_s, weights, margin, count,
    out_r, out_s, flux, x_r, x_s, rows_low, rows_high,
):
    var_count, rows, layers, cells = a_r.shape
    total = weights.shape[1]
    own_blocks = cells // TILE
    spread = REACH + own_blocks + 1
    first_block = lax.axis_index("circ") * own_blocks
    lane = iota((8, TILE), 1)
    layer_all = iota((layers, cells), 0)
    end = total // 2 + var_count * own_blocks
    for x in (x_r, x_s):
        x[...] = jnp.zeros(x.shape, f32)
    for ref, to in ((low, rows_low), (high, rows_high)):
        for v in range(var_count):
            for i in range(own_blocks):
                to[v, :, i * TILE : (i + 1) * TILE] = ref[total // 2 + v * own_blocks + i].astype(f32)
    ends = [ref[end].astype(f32) for ref in (low, high)]
    inside = [jnp.concatenate([x[8:9]] * own_blocks, axis=1) for x in ends]
    group = lax.rem(lax.shift_right_logical(lane, 3), rows)
    corner = jnp.where(group == 0, pltpu.roll(ends[0][0:8], (TILE - 8 * (rows - 1)) % TILE, 1), 0.0)
    corner = corner + jnp.where(group == rows - 1, pltpu.roll(ends[1][0:8], 8 * (rows - 1), 1), 0.0)
    columns = [
        lax.dot_general(corner, edge_pick(n, cells), (((0,), (0,)), ((), ())), preferred_element_type=f32)
        for n in range(2)
    ]

    def halo(ref, b):
        both = ref[lax.shift_right_logical(b, 1)].astype(f32)
        return jnp.where(jnp.bitwise_and(b, 1) == 1, both[8:16], both[0:8])

    extra = []
    for s in range(rows):
        base = first_block - margin[s, 0, 0] - 5 + 4 * total
        own = []
        for t in range(spread - 2 + own_blocks):
            b = wrapped(base + t, total) if t < spread - 2 else first_block + t - (spread - 2)
            adjoint = p[s, t]
            if s == 0:
                adjoint = adjoint + carry * halo(low, b)
            if s == rows - 1:
                adjoint = adjoint + carry * halo(high, b)
            moved = flux_of(q[s, t], adjoint)
            if t < spread - 2:
                flux[s, t] = moved.astype(jnp.bfloat16).astype(f32)
            else:
                own.append(moved)
        pulls = [
            pull_row(lambda t: flux[s, t], weights, margin, count, s, slot, first_block, base, total)
            for slot in range(own_blocks)
        ]
        extra.append((step_size * jnp.concatenate(pulls, axis=1), -step_size * jnp.concatenate(own, axis=1)))

    fields = (
        (o_r, h_r, a_r, jd_r, jo_r, src_r, x_r, out_r, layers - 1),
        (o_s, h_s, a_s, jd_s, jo_s, src_s, x_s, out_s, 0),
    )
    for n, (o, h, a, jd, jo, src, x, out, layer) in enumerate(fields):
        old = slice(n * layers, (n + 1) * layers)
        new = slice((2 + n) * layers, (3 + n) * layers)
        for v in range(var_count):
            for s in range(rows):
                value = o[v, s]
                if s == 0:
                    value = value + carry * rows_low[v, old, :]
                if s == rows - 1:
                    value = value + carry * rows_high[v, old, :]
                x[v * rows + s, 0:layers, :] = value
        for s in range(rows):
            state_row = [x[v * rows + s, 0:layers, :] for v in range(var_count)]
            for v in range(var_count):
                wide = x[v * rows + s]
                beside = (lanes_apart(wide) + layers_apart(wide))[0:layers]
                at = (v * rows + s) * 8
                beside = beside + h[v, s] + carry * columns[n][at : at + layers]
                if s > 0:
                    beside = beside + x[v * rows + s - 1, 0:layers, :]
                else:
                    beside = beside + inside[0] * (rows_low[v, new, :] + carry * a[v, 0])
                if s < rows - 1:
                    beside = beside + x[v * rows + s + 1, 0:layers, :]
                else:
                    beside = beside + inside[1] * (rows_high[v, new, :] + carry * a[v, rows - 1])
                res = jacobian_row(jd, jo, state_row, v, s, var_count) - coupling * beside - src[v, s]
                out[v, s] = (
                    state_row[v] - step_size * res + jnp.where(layer_all == layer, extra[s][n][v : v + 1], 0.0)
                )


def per_device(
    adjoint_rotor,
    adjoint_stator,
    jac_diag_rotor,
    jac_diag_stator,
    jac_off_rotor,
    jac_off_stator,
    source_rotor,
    source_stator,
    rotor_state,
    margin_block,
    face_count,
    margin_weight,
):
    var_count, rows, layers, cells = adjoint_rotor.shape
    own_blocks = cells // TILE
    total = margin_block.shape[1]
    spread = REACH + own_blocks + 1
    field = jax.ShapeDtypeStruct(adjoint_rotor.shape, f32)
    vmem = pl.BlockSpec(memory_space=pltpu.VMEM)
    smem = pl.BlockSpec(memory_space=pltpu.SMEM)
    padded = pltpu.VMEM((TILE // 8, 8, cells), f32)

    v_r, v_s, share = pl.pallas_call(
        first_kernel,
        out_shape=(field, field, jax.ShapeDtypeStruct((own_blocks, rows * 24, TILE), f32)),
        in_specs=[vmem] * 9,
        out_specs=(vmem,) * 3,
        scratch_shapes=[padded] * 4,
        compiler_params=params,
        name="local_part",
    )(
        adjoint_rotor, adjoint_stator, jac_diag_rotor, jac_diag_stator, jac_off_rotor, jac_off_stator,
        source_rotor, source_stator, rotor_state,
    )
    whole = lax.all_gather(share, "circ", axis=0, tiled=True)
    tiles = jax.ShapeDtypeStruct((total // 2 + var_count * own_blocks + 1, 16, TILE), jnp.bfloat16)
    listed = jax.ShapeDtypeStruct((rows, spread - 2 + own_blocks, 8, TILE), f32)
    o_r, o_s, h_r, h_s, q, p, up, down = pl.pallas_call(
        second_kernel,
        out_shape=(field, field, field, field, listed, listed, tiles, tiles),
        in_specs=[vmem] * 6 + [smem] * 2,
        out_specs=(vmem,) * 8,
        scratch_shapes=[
            pltpu.VMEM((rows, spread, 8, TILE), f32),
            pltpu.VMEM((var_count, 4 * layers, cells), f32),
            pltpu.VMEM((8, TILE), f32),
        ],
        compiler_params=params,
        name="interface_part",
    )(whole, v_r, v_s, adjoint_rotor, adjoint_stator, margin_weight, margin_block, face_count)
    bands = lax.axis_size("span")
    low = lax.ppermute(up, "span", [(i, i + 1) for i in range(bands - 1)])
    high = lax.ppermute(down, "span", [(i + 1, i) for i in range(bands - 1)])
    out_r, out_s = pl.pallas_call(
        third_kernel,
        out_shape=(field, field),
        in_specs=[vmem] * 17 + [smem] * 2,
        out_specs=(vmem,) * 2,
        scratch_shapes=[
            pltpu.VMEM((rows, spread - 2, 8, TILE), f32),
            padded,
            padded,
            pltpu.VMEM((var_count, 4 * layers, cells), f32),
            pltpu.VMEM((var_count, 4 * layers, cells), f32),
        ],
        compiler_params=params,
        name="final_part",
    )(
        low, high, o_r, o_s, h_r, h_s, q, p, adjoint_rotor, adjoint_stator, jac_diag_rotor, jac_diag_stator,
        jac_off_rotor, jac_off_stator, source_rotor, source_stator, margin_weight, margin_block, face_count,
    )
    return (out_r, out_s)


def solution(mesh):
    field = P(None, "span", None, "circ")
    placed = (
        (field,) * 4
        + (P(None, None, "span", None, "circ"),) * 2
        + (field,) * 2
        + (P(None, "span", "circ"), P("span", None, None), P("span", None), P("span", None, None, None))
    )
    return jax.shard_map(
        per_device, mesh=mesh, in_specs=placed, out_specs=(field, field), check_vma=False
    )
```

```python
import jax
import jax.numpy as jnp
from jax import lax
from jax.experimental import pallas as pl
from jax.experimental.pallas import tpu as pltpu
from jax.sharding import PartitionSpec as P

step_size = 0.1
coupling = 0.2
carry = step_size * coupling
REACH = 8
TILE = 128
f32 = jnp.float32
params = pltpu.CompilerParams(vmem_limit_bytes=24 * 1024 * 1024)


def iota(shape, dim):
    return lax.broadcasted_iota(jnp.int32, shape, dim)


def wrapped(x, count):
    if count & (count - 1) == 0:
        return jnp.bitwise_and(x, count - 1)
    return lax.rem(x + 4 * count, count)


def lanes_apart(x):
    cells = x.shape[1]
    lane = iota(x.shape, 1)
    before = jnp.where(lane == 0, 0.0, pltpu.roll(x, 1, 1))
    after = jnp.where(lane == cells - 1, 0.0, pltpu.roll(x, cells - 1, 1))
    return before + after


def layers_apart(x):
    return pltpu.roll(x, 1, 0) + pltpu.roll(x, 7, 0)


def edge_pick(row, cells):
    at = iota((8, cells), 0)
    lane = iota((8, cells), 1)
    first = jnp.logical_and(at == row, lane == 0)
    last = jnp.logical_and(at == 4 + row, lane == cells - 1)
    return jnp.where(jnp.logical_or(first, last), 1.0, 0.0).astype(f32)


def flux_of(primal, adjoint):
    speeds = jnp.sqrt(1.0 + primal * primal)
    over = jnp.sum(primal * adjoint, axis=0, keepdims=True)
    under = 6.0 + jnp.sum(primal * primal, axis=0, keepdims=True)
    return speeds * adjoint + 0.5 * primal * (over / under)


def jacobian_row(diag, off, state, v, s, var_count):
    total = diag[v, s] * state[v]
    for w in range(var_count):
        total = total + off[w, v, s].astype(f32) * state[w]
    return total


def pull_row(flux, weights, margin, count, s, slot, first_block, base, total):
    target = wrapped(first_block + slot + total, total)
    acc = jnp.zeros((8, TILE), f32)
    for e in range(REACH):
        b = wrapped(base + slot + e, total)
        k = wrapped(target - margin[s, 0, b] + total, total)
        live = jnp.where(k < count[s, b], 1.0, 0.0).astype(f32)
        kept = jnp.minimum(k, weights.shape[2] - 1)
        acc = acc + (weights[s, b, pl.ds(kept, 1), :] * live) * flux(slot + e)
    return acc


def first_kernel(*refs):
    outer, refs = refs[:12], refs[12:]
    v_r, v_s, out, a_r, a_s, weights, margin, count = refs[:8]
    jd_r, jd_s, jo_r, jo_s, src_r, src_s, state = refs[8:15]
    xs, sems = refs[15:19], refs[19]
    var_count, rows, layers, cells = a_r.shape
    own_blocks = cells // TILE
    inner = (a_r, a_s, jd_r, jd_s, jo_r, jo_s, src_r, src_s, state, margin, count, weights)
    copies = [pltpu.make_async_copy(x, y, sems.at[n]) for n, (x, y) in enumerate(zip(outer, inner))]
    for copy in copies:
        copy.start()
    out[...] = jnp.zeros(out.shape, f32)
    for x in xs:
        x[...] = jnp.zeros(x.shape, f32)
    for copy in copies:
        copy.wait()
    fields = ((a_r, jd_r, jo_r, src_r, v_r, xs[0], xs[2]), (a_s, jd_s, jo_s, src_s, v_s, xs[1], xs[3]))
    for a, jd, jo, src, partial, x_a, x_p in fields:
        for v in range(var_count):
            for s in range(rows):
                x_a[v * rows + s, 0:layers, :] = a[v, s]
        for s in range(rows):
            state_row = [a[v, s] for v in range(var_count)]
            for v in range(var_count):
                wide = x_a[v * rows + s]
                beside = (lanes_apart(wide) + layers_apart(wide))[0:layers]
                if s > 0:
                    beside = beside + a[v, s - 1]
                if s < rows - 1:
                    beside = beside + a[v, s + 1]
                res = jacobian_row(jd, jo, state_row, v, s, var_count) - coupling * beside - src[v, s]
                new = state_row[v] - step_size * res
                partial[v, s] = new
                x_p[v * rows + s, 0:layers, :] = new
    edges = jnp.zeros((8, TILE), f32)
    for q in range(4):
        flat = xs[q][...].reshape(TILE, cells)
        edges = edges + lax.dot_general(
            edge_pick(q, cells), flat, (((1,), (1,)), ((), ())), preferred_element_type=f32
        )
    for v in range(var_count):
        rotor = state[v].astype(f32)
        for s in range(rows):
            for i in range(own_blocks):
                cut = slice(i * TILE, (i + 1) * TILE)
                at = s * 8 + v
                out[i, at : at + 1, :] = rotor[s : s + 1, cut]
                out[i, rows * 8 + at : rows * 8 + at + 1, :] = a_s[v, s, 0:1, cut]
                out[i, rows * 16 + at : rows * 16 + at + 1, :] = v_s[v, s, 0:1, cut]
    for side, i in ((0, 0), (1, own_blocks - 1)):
        out[i, 6:8, :] = edges[4 * side : 4 * side + 2]
        out[i, 14:16, :] = edges[4 * side + 2 : 4 * side + 4]


def second_kernel(
    g, v_r, v_s, a_r, a_s, weights, margin, count,
    o_r, o_s, h_r, h_s, q_out, p_out, up, down, flux, held, spot,
):
    var_count, rows, layers, cells = a_r.shape
    total = g.shape[0]
    own_blocks = cells // TILE
    entries = weights.shape[2]
    spread = REACH + own_blocks + 1
    first_block = lax.axis_index("circ") * own_blocks
    row8 = iota((8, TILE), 0)
    lane = iota((8, TILE), 1)
    lane_all = iota((layers, cells), 1)
    layer_all = iota((layers, cells), 0)
    edge = jnp.logical_or(lane_all == 0, lane_all == cells - 1)
    left = wrapped(first_block - 1 + total, total)
    right = wrapped(first_block + own_blocks, total)

    spot[0:2, :] = g[left, 6:8, :]
    spot[2:4, :] = g[left, 14:16, :]
    spot[4:6, :] = g[right, 6:8, :]
    spot[6:8, :] = g[right, 14:16, :]
    spots = spot[...]
    columns = [
        lax.dot_general(spots, edge_pick(q, cells), (((0,), (0,)), ((), ())), preferred_element_type=f32)
        for q in range(4)
    ]

    def block(s, b):
        primal = jnp.zeros((8, TILE), f32)
        for k in range(entries):
            live = jnp.where(k < count[s, b], 1.0, 0.0).astype(f32)
            primal = primal + (weights[s, b, k : k + 1, :] * live) * g[margin[s, k, b], s * 8 : s * 8 + 8, :]
        primal = jnp.where(row8 < var_count, primal, 0.0)
        adjoint = g[b, rows * 8 + s * 8 : rows * 8 + s * 8 + 8, :]
        return primal, flux_of(primal, adjoint)

    def advanced(s, b, moved):
        at = slice(rows * 8 + s * 8, rows * 8 + s * 8 + 8)
        place = lax.rem(b, own_blocks)
        before = jnp.where(place == 0, carry, 0.0).astype(f32)
        after = jnp.where(place == own_blocks - 1, carry, 0.0).astype(f32)
        low = pltpu.roll(g[wrapped(b - 1 + total, total), at, :], 1, 1)
        high = pltpu.roll(g[wrapped(b + 1, total), at, :], TILE - 1, 1)
        base = g[b, rows * 16 + s * 8 : rows * 16 + s * 8 + 8, :]
        base = base + jnp.where(lane == 0, low * before, 0.0) + jnp.where(lane == TILE - 1, high * after, 0.0)
        return base - step_size * moved

    for s in range(rows):
        base = first_block - margin[s, 0, 0] - 5 + 4 * total
        for t in range(spread):
            b = wrapped(base - 1 + t, total)
            primal, moved = block(s, b)
            flux[s, t] = moved.astype(jnp.bfloat16).astype(f32)
            if 0 < t < spread - 1:
                q_out[s, t - 1] = primal
                p_out[s, t - 1] = advanced(s, b, moved)
        own = []
        for i in range(own_blocks):
            primal, moved = block(s, first_block + i)
            own.append(moved)
            q_out[s, spread - 2 + i] = primal
            p_out[s, spread - 2 + i] = advanced(s, first_block + i, moved)
        blank = [jnp.zeros((8, TILE), f32)] * (own_blocks - 2)
        side_flux = [block(s, left)[1], block(s, right)[1]]
        pulls = [
            pull_row(lambda t: flux[s, t + 1], weights, margin, count, s, slot, first_block, base, total)
            for slot in range(-1, own_blocks + 1)
        ]

        def at_sides(low, high):
            return jnp.concatenate([pltpu.roll(low, 1, 1), *blank, pltpu.roll(high, TILE - 1, 1)], axis=1)

        pulled = step_size * jnp.concatenate(pulls[1:-1], axis=1)
        pulled_side = step_size * at_sides(pulls[0], pulls[-1])
        pushed = step_size * jnp.concatenate(own, axis=1)
        pushed_side = step_size * at_sides(*side_flux)
        for v in range(var_count):
            at = (v * rows + s) * 8
            cut = slice(at, at + layers)
            o_r[v, s] = (
                v_r[v, s] + carry * columns[0][cut] + jnp.where(layer_all == layers - 1, pulled[v : v + 1], 0.0)
            )
            o_s[v, s] = v_s[v, s] + carry * columns[1][cut] - jnp.where(layer_all == 0, pushed[v : v + 1], 0.0)
            h_r[v, s] = columns[2][cut] + jnp.where(
                edge, carry * a_r[v, s] + jnp.where(layer_all == layers - 1, pulled_side[v : v + 1], 0.0), 0.0
            )
            h_s[v, s] = columns[3][cut] + jnp.where(
                edge, carry * a_s[v, s] - jnp.where(layer_all == 0, pushed_side[v : v + 1], 0.0), 0.0
            )

    last = jnp.concatenate([spots, jnp.ones((8, TILE), f32)], axis=0).astype(jnp.bfloat16)
    for to, s in ((up, rows - 1), (down, 0)):
        at = slice(rows * 8 + s * 8, rows * 8 + s * 8 + 8)
        for j in range(total // 2):
            to[j] = jnp.concatenate([g[2 * j, at, :], g[2 * j + 1, at, :]], axis=0).astype(jnp.bfloat16)
        for v in range(var_count):
            for n, ref in enumerate((a_r, a_s, o_r, o_s)):
                held[v, n * layers : (n + 1) * layers, :] = ref[v, s]
            for i in range(own_blocks):
                to[total // 2 + v * own_blocks + i] = held[v, :, i * TILE : (i + 1) * TILE].astype(jnp.bfloat16)
        to[total // 2 + var_count * own_blocks] = last


def third_kernel(
    low, high, o_r, o_s, h_r, h_s, q, p, a_r, a_s, jd_r, jd_s, jo_r, jo_s, src_r, src_s, weights, margin, count,
    out_r, out_s, flux, x_r, x_s, rows_low, rows_high,
):
    var_count, rows, layers, cells = a_r.shape
    total = weights.shape[1]
    own_blocks = cells // TILE
    spread = REACH + own_blocks + 1
    first_block = lax.axis_index("circ") * own_blocks
    lane = iota((8, TILE), 1)
    layer_all = iota((layers, cells), 0)
    end = total // 2 + var_count * own_blocks
    for x in (x_r, x_s):
        x[...] = jnp.zeros(x.shape, f32)
    for ref, to in ((low, rows_low), (high, rows_high)):
        for v in range(var_count):
            for i in range(own_blocks):
                to[v, :, i * TILE : (i + 1) * TILE] = ref[total // 2 + v * own_blocks + i].astype(f32)
    ends = [ref[end].astype(f32) for ref in (low, high)]
    inside = [jnp.concatenate([x[8:9]] * own_blocks, axis=1) for x in ends]
    group = lax.rem(lax.shift_right_logical(lane, 3), rows)
    corner = jnp.where(group == 0, pltpu.roll(ends[0][0:8], (TILE - 8 * (rows - 1)) % TILE, 1), 0.0)
    corner = corner + jnp.where(group == rows - 1, pltpu.roll(ends[1][0:8], 8 * (rows - 1), 1), 0.0)
    columns = [
        lax.dot_general(corner, edge_pick(n, cells), (((0,), (0,)), ((), ())), preferred_element_type=f32)
        for n in range(2)
    ]

    def halo(ref, b):
        both = ref[lax.shift_right_logical(b, 1)].astype(f32)
        return jnp.where(jnp.bitwise_and(b, 1) == 1, both[8:16], both[0:8])

    extra = []
    for s in range(rows):
        base = first_block - margin[s, 0, 0] - 5 + 4 * total
        own = []
        for t in range(spread - 2 + own_blocks):
            b = wrapped(base + t, total) if t < spread - 2 else first_block + t - (spread - 2)
            adjoint = p[s, t]
            if s == 0:
                adjoint = adjoint + carry * halo(low, b)
            if s == rows - 1:
                adjoint = adjoint + carry * halo(high, b)
            moved = flux_of(q[s, t], adjoint)
            if t < spread - 2:
                flux[s, t] = moved.astype(jnp.bfloat16).astype(f32)
            else:
                own.append(moved)
        pulls = [
            pull_row(lambda t: flux[s, t], weights, margin, count, s, slot, first_block, base, total)
            for slot in range(own_blocks)
        ]
        extra.append((step_size * jnp.concatenate(pulls, axis=1), -step_size * jnp.concatenate(own, axis=1)))

    fields = (
        (o_r, h_r, a_r, jd_r, jo_r, src_r, x_r, out_r, layers - 1),
        (o_s, h_s, a_s, jd_s, jo_s, src_s, x_s, out_s, 0),
    )
    for n, (o, h, a, jd, jo, src, x, out, layer) in enumerate(fields):
        old = slice(n * layers, (n + 1) * layers)
        new = slice((2 + n) * layers, (3 + n) * layers)
        for v in range(var_count):
            for s in range(rows):
                value = o[v, s]
                if s == 0:
                    value = value + carry * rows_low[v, old, :]
                if s == rows - 1:
                    value = value + carry * rows_high[v, old, :]
                x[v * rows + s, 0:layers, :] = value
        for s in range(rows):
            state_row = [x[v * rows + s, 0:layers, :] for v in range(var_count)]
            for v in range(var_count):
                wide = x[v * rows + s]
                beside = (lanes_apart(wide) + layers_apart(wide))[0:layers]
                at = (v * rows + s) * 8
                beside = beside + h[v, s] + carry * columns[n][at : at + layers]
                if s > 0:
                    beside = beside + x[v * rows + s - 1, 0:layers, :]
                else:
                    beside = beside + inside[0] * (rows_low[v, new, :] + carry * a[v, 0])
                if s < rows - 1:
                    beside = beside + x[v * rows + s + 1, 0:layers, :]
                else:
                    beside = beside + inside[1] * (rows_high[v, new, :] + carry * a[v, rows - 1])
                res = jacobian_row(jd, jo, state_row, v, s, var_count) - coupling * beside - src[v, s]
                out[v, s] = (
                    state_row[v] - step_size * res + jnp.where(layer_all == layer, extra[s][n][v : v + 1], 0.0)
                )


def per_device(
    adjoint_rotor,
    adjoint_stator,
    jac_diag_rotor,
    jac_diag_stator,
    jac_off_rotor,
    jac_off_stator,
    source_rotor,
    source_stator,
    rotor_state,
    margin_block,
    face_count,
    margin_weight,
):
    var_count, rows, layers, cells = adjoint_rotor.shape
    own_blocks = cells // TILE
    total = margin_block.shape[1]
    spread = REACH + own_blocks + 1
    field = jax.ShapeDtypeStruct(adjoint_rotor.shape, f32)
    vmem = pl.BlockSpec(memory_space=pltpu.VMEM)
    smem = pl.BlockSpec(memory_space=pltpu.SMEM)
    padded = pltpu.VMEM((TILE // 8, 8, cells), f32)

    margin = jnp.swapaxes(margin_block, 1, 2)
    arguments = (
        adjoint_rotor, adjoint_stator, jac_diag_rotor, jac_diag_stator, jac_off_rotor, jac_off_stator,
        source_rotor, source_stator, rotor_state, margin, face_count, margin_weight,
    )
    shapes = [jax.ShapeDtypeStruct(x.shape, x.dtype) for x in arguments]
    v_r, v_s, share, a_r, a_s, weights, margin, count = pl.pallas_call(
        first_kernel,
        out_shape=(
            field, field, jax.ShapeDtypeStruct((own_blocks, rows * 24, TILE), f32),
            shapes[0], shapes[1], shapes[11], shapes[9], shapes[10],
        ),
        in_specs=[pl.BlockSpec(memory_space=pl.ANY)] * 12,
        out_specs=(vmem,) * 8,
        scratch_shapes=[pltpu.VMEM(x.shape, x.dtype) for x in shapes[2:9]]
        + [padded] * 4
        + [pltpu.SemaphoreType.DMA((12,))],
        compiler_params=params,
        name="local_part",
    )(*arguments)
    whole = lax.all_gather(share, "circ", axis=0, tiled=True)
    tiles = jax.ShapeDtypeStruct((total // 2 + var_count * own_blocks + 1, 16, TILE), jnp.bfloat16)
    listed = jax.ShapeDtypeStruct((rows, spread - 2 + own_blocks, 8, TILE), f32)
    o_r, o_s, h_r, h_s, q, p, up, down = pl.pallas_call(
        second_kernel,
        out_shape=(field, field, field, field, listed, listed, tiles, tiles),
        in_specs=[vmem] * 6 + [smem] * 2,
        out_specs=(vmem,) * 8,
        scratch_shapes=[
            pltpu.VMEM((rows, spread, 8, TILE), f32),
            pltpu.VMEM((var_count, 4 * layers, cells), f32),
            pltpu.VMEM((8, TILE), f32),
        ],
        compiler_params=params,
        name="interface_part",
    )(whole, v_r, v_s, a_r, a_s, weights, margin, count)
    bands = lax.axis_size("span")
    low = lax.ppermute(up, "span", [(i, i + 1) for i in range(bands - 1)])
    high = lax.ppermute(down, "span", [(i + 1, i) for i in range(bands - 1)])
    out_r, out_s = pl.pallas_call(
        third_kernel,
        out_shape=(field, field),
        in_specs=[vmem] * 17 + [smem] * 2,
        out_specs=(vmem,) * 2,
        scratch_shapes=[
            pltpu.VMEM((rows, spread - 2, 8, TILE), f32),
            padded,
            padded,
            pltpu.VMEM((var_count, 4 * layers, cells), f32),
            pltpu.VMEM((var_count, 4 * layers, cells), f32),
        ],
        compiler_params=params,
        name="final_part",
    )(
        low, high, o_r, o_s, h_r, h_s, q, p, a_r, a_s, jac_diag_rotor, jac_diag_stator,
        jac_off_rotor, jac_off_stator, source_rotor, source_stator, weights, margin, count,
    )
    return (out_r, out_s)


def solution(mesh):
    field = P(None, "span", None, "circ")
    placed = (
        (field,) * 4
        + (P(None, None, "span", None, "circ"),) * 2
        + (field,) * 2
        + (P(None, "span", "circ"), P("span", None, None), P("span", None), P("span", None, None, None))
    )
    return jax.shard_map(
        per_device, mesh=mesh, in_specs=placed, out_specs=(field, field), check_vma=False
    )
```

```python
import jax
import jax.numpy as jnp
from jax import lax
from jax.experimental import pallas as pl
from jax.experimental.pallas import tpu as pltpu
from jax.sharding import PartitionSpec as P

step_size = 0.1
coupling = 0.2
carry = step_size * coupling
REACH = 8
TILE = 128
f32 = jnp.float32
params = pltpu.CompilerParams(vmem_limit_bytes=24 * 1024 * 1024)


def iota(shape, dim):
    return lax.broadcasted_iota(jnp.int32, shape, dim)


def wrapped(x, count):
    if count & (count - 1) == 0:
        return jnp.bitwise_and(x, count - 1)
    return lax.rem(x + 4 * count, count)


def lanes_apart(x):
    cells = x.shape[1]
    lane = iota(x.shape, 1)
    before = jnp.where(lane == 0, 0.0, pltpu.roll(x, 1, 1))
    after = jnp.where(lane == cells - 1, 0.0, pltpu.roll(x, cells - 1, 1))
    return before + after


def layers_apart(x):
    return pltpu.roll(x, 1, 0) + pltpu.roll(x, 7, 0)


def edge_pick(row, cells):
    at = iota((8, cells), 0)
    lane = iota((8, cells), 1)
    first = jnp.logical_and(at == row, lane == 0)
    last = jnp.logical_and(at == 4 + row, lane == cells - 1)
    return jnp.where(jnp.logical_or(first, last), 1.0, 0.0).astype(f32)


def flux_of(primal, adjoint):
    speeds = jnp.sqrt(1.0 + primal * primal)
    over = jnp.sum(primal * adjoint, axis=0, keepdims=True)
    under = 6.0 + jnp.sum(primal * primal, axis=0, keepdims=True)
    return speeds * adjoint + 0.5 * primal * (over / under)


def jacobian_row(diag, off, state, v, s, var_count):
    total = diag[v, s] * state[v]
    for w in range(var_count):
        total = total + off[w, v, s].astype(f32) * state[w]
    return total


def pull_row(flux, weights, margin, count, s, slot, first_block, base, total):
    target = wrapped(first_block + slot + total, total)
    acc = jnp.zeros((8, TILE), f32)
    for e in range(REACH):
        b = wrapped(base + slot + e, total)
        k = wrapped(target - margin[s, 0, b] + total, total)
        live = jnp.where(k < count[s, b], 1.0, 0.0).astype(f32)
        kept = jnp.minimum(k, weights.shape[2] - 1)
        acc = acc + (weights[s, b, pl.ds(kept, 1), :] * live) * flux(slot + e)
    return acc


def first_kernel(*refs):
    outer, refs = refs[:12], refs[12:]
    v_r, v_s, out, a_r, a_s, weights, margin, count = refs[:8]
    jd_r, jd_s, jo_r, jo_s, src_r, src_s, state = refs[8:15]
    xs, sems = refs[15:19], refs[19]
    var_count, rows, layers, cells = a_r.shape
    own_blocks = cells // TILE
    inner = (a_r, a_s, jd_r, jd_s, jo_r, jo_s, src_r, src_s, state, margin, count, weights)
    copies = [pltpu.make_async_copy(x, y, sems.at[n]) for n, (x, y) in enumerate(zip(outer, inner))]
    for copy in copies:
        copy.start()
    out[...] = jnp.zeros(out.shape, f32)
    for x in xs:
        x[...] = jnp.zeros(x.shape, f32)
    for copy in copies:
        copy.wait()
    fields = ((a_r, jd_r, jo_r, src_r, v_r, xs[0], xs[2]), (a_s, jd_s, jo_s, src_s, v_s, xs[1], xs[3]))
    for a, jd, jo, src, partial, x_a, x_p in fields:
        for v in range(var_count):
            for s in range(rows):
                x_a[v * rows + s, 0:layers, :] = a[v, s]
        for s in range(rows):
            state_row = [a[v, s] for v in range(var_count)]
            for v in range(var_count):
                wide = x_a[v * rows + s]
                beside = (lanes_apart(wide) + layers_apart(wide))[0:layers]
                if s > 0:
                    beside = beside + a[v, s - 1]
                if s < rows - 1:
                    beside = beside + a[v, s + 1]
                res = jacobian_row(jd, jo, state_row, v, s, var_count) - coupling * beside - src[v, s]
                new = state_row[v] - step_size * res
                partial[v, s] = new
                x_p[v * rows + s, 0:layers, :] = new
    edges = jnp.zeros((8, TILE), f32)
    for q in range(4):
        flat = xs[q][...].reshape(TILE, cells)
        edges = edges + lax.dot_general(
            edge_pick(q, cells), flat, (((1,), (1,)), ((), ())), preferred_element_type=f32
        )
    for v in range(var_count):
        rotor = state[v].astype(f32)
        for s in range(rows):
            for i in range(own_blocks):
                cut = slice(i * TILE, (i + 1) * TILE)
                at = s * 8 + v
                out[i, at : at + 1, :] = rotor[s : s + 1, cut]
                out[i, rows * 8 + at : rows * 8 + at + 1, :] = a_s[v, s, 0:1, cut]
                out[i, rows * 16 + at : rows * 16 + at + 1, :] = v_s[v, s, 0:1, cut]
    for side, i in ((0, 0), (1, own_blocks - 1)):
        out[i, 6:8, :] = edges[4 * side : 4 * side + 2]
        out[i, 14:16, :] = edges[4 * side + 2 : 4 * side + 4]


def second_kernel(
    g, v_r, v_s, a_r, a_s, weights, margin, count,
    o_r, o_s, h_r, h_s, q_out, p_out, up, down, flux, held, spot,
):
    var_count, rows, layers, cells = a_r.shape
    total = g.shape[0]
    own_blocks = cells // TILE
    entries = weights.shape[2]
    spread = REACH + own_blocks + 1
    first_block = lax.axis_index("circ") * own_blocks
    row8 = iota((8, TILE), 0)
    lane = iota((8, TILE), 1)
    lane_all = iota((layers, cells), 1)
    layer_all = iota((layers, cells), 0)
    edge = jnp.logical_or(lane_all == 0, lane_all == cells - 1)
    left = wrapped(first_block - 1 + total, total)
    right = wrapped(first_block + own_blocks, total)

    spot[0:2, :] = g[left, 6:8, :]
    spot[2:4, :] = g[left, 14:16, :]
    spot[4:6, :] = g[right, 6:8, :]
    spot[6:8, :] = g[right, 14:16, :]
    spots = spot[...]
    columns = [
        lax.dot_general(spots, edge_pick(q, cells), (((0,), (0,)), ((), ())), preferred_element_type=f32)
        for q in range(4)
    ]

    def block(s, b):
        primal = jnp.zeros((8, TILE), f32)
        for k in range(entries):
            live = jnp.where(k < count[s, b], 1.0, 0.0).astype(f32)
            primal = primal + (weights[s, b, k : k + 1, :] * live) * g[margin[s, k, b], s * 8 : s * 8 + 8, :]
        primal = jnp.where(row8 < var_count, primal, 0.0)
        adjoint = g[b, rows * 8 + s * 8 : rows * 8 + s * 8 + 8, :]
        return primal, flux_of(primal, adjoint)

    def advanced(s, b, moved):
        at = slice(rows * 8 + s * 8, rows * 8 + s * 8 + 8)
        place = lax.rem(b, own_blocks)
        before = jnp.where(place == 0, carry, 0.0).astype(f32)
        after = jnp.where(place == own_blocks - 1, carry, 0.0).astype(f32)
        low = pltpu.roll(g[wrapped(b - 1 + total, total), at, :], 1, 1)
        high = pltpu.roll(g[wrapped(b + 1, total), at, :], TILE - 1, 1)
        base = g[b, rows * 16 + s * 8 : rows * 16 + s * 8 + 8, :]
        base = base + jnp.where(lane == 0, low * before, 0.0) + jnp.where(lane == TILE - 1, high * after, 0.0)
        return base - step_size * moved

    for s in range(rows):
        base = first_block - margin[s, 0, 0] - 5 + 4 * total
        for t in range(spread):
            b = wrapped(base - 1 + t, total)
            primal, moved = block(s, b)
            flux[s, t] = moved.astype(jnp.bfloat16).astype(f32)
            if 0 < t < spread - 1:
                q_out[s, t - 1] = primal
                p_out[s, t - 1] = advanced(s, b, moved)
        own = []
        for i in range(own_blocks):
            primal, moved = block(s, first_block + i)
            own.append(moved)
            q_out[s, spread - 2 + i] = primal
            p_out[s, spread - 2 + i] = advanced(s, first_block + i, moved)
        blank = [jnp.zeros((8, TILE), f32)] * (own_blocks - 2)
        side_flux = [block(s, left)[1], block(s, right)[1]]
        pulls = [
            pull_row(lambda t: flux[s, t + 1], weights, margin, count, s, slot, first_block, base, total)
            for slot in range(-1, own_blocks + 1)
        ]

        def at_sides(low, high):
            return jnp.concatenate([pltpu.roll(low, 1, 1), *blank, pltpu.roll(high, TILE - 1, 1)], axis=1)

        pulled = step_size * jnp.concatenate(pulls[1:-1], axis=1)
        pulled_side = step_size * at_sides(pulls[0], pulls[-1])
        pushed = step_size * jnp.concatenate(own, axis=1)
        pushed_side = step_size * at_sides(*side_flux)
        for v in range(var_count):
            at = (v * rows + s) * 8
            cut = slice(at, at + layers)
            o_r[v, s] = (
                v_r[v, s] + carry * columns[0][cut] + jnp.where(layer_all == layers - 1, pulled[v : v + 1], 0.0)
            )
            o_s[v, s] = v_s[v, s] + carry * columns[1][cut] - jnp.where(layer_all == 0, pushed[v : v + 1], 0.0)
            h_r[v, s] = columns[2][cut] + jnp.where(
                edge, carry * a_r[v, s] + jnp.where(layer_all == layers - 1, pulled_side[v : v + 1], 0.0), 0.0
            )
            h_s[v, s] = columns[3][cut] + jnp.where(
                edge, carry * a_s[v, s] - jnp.where(layer_all == 0, pushed_side[v : v + 1], 0.0), 0.0
            )

    last = jnp.concatenate([spots, jnp.ones((8, TILE), f32)], axis=0).astype(jnp.bfloat16)
    for to, s in ((up, rows - 1), (down, 0)):
        at = slice(rows * 8 + s * 8, rows * 8 + s * 8 + 8)
        for j in range(total // 2):
            to[j] = jnp.concatenate([g[2 * j, at, :], g[2 * j + 1, at, :]], axis=0).astype(jnp.bfloat16)
        for v in range(var_count):
            for n, ref in enumerate((a_r, a_s, o_r, o_s)):
                held[v, n * layers : (n + 1) * layers, :] = ref[v, s]
            for i in range(own_blocks):
                to[total // 2 + v * own_blocks + i] = held[v, :, i * TILE : (i + 1) * TILE].astype(jnp.bfloat16)
        to[total // 2 + var_count * own_blocks] = last


def third_kernel(
    low, high, o_r, o_s, h_r, h_s, q, p, a_r, a_s, jd_r, jd_s, jo_r, jo_s, src_r, src_s, weights, margin, count,
    out_r, out_s, flux, x_r, x_s, rows_low, rows_high,
):
    var_count, rows, layers, cells = a_r.shape
    total = weights.shape[1]
    own_blocks = cells // TILE
    spread = REACH + own_blocks + 1
    first_block = lax.axis_index("circ") * own_blocks
    lane = iota((8, TILE), 1)
    layer_all = iota((layers, cells), 0)
    end = total // 2 + var_count * own_blocks
    for x in (x_r, x_s):
        x[...] = jnp.zeros(x.shape, f32)
    for ref, to in ((low, rows_low), (high, rows_high)):
        for v in range(var_count):
            for i in range(own_blocks):
                to[v, :, i * TILE : (i + 1) * TILE] = ref[total // 2 + v * own_blocks + i].astype(f32)
    ends = [ref[end].astype(f32) for ref in (low, high)]
    inside = [jnp.concatenate([x[8:9]] * own_blocks, axis=1) for x in ends]
    group = lax.rem(lax.shift_right_logical(lane, 3), rows)
    corner = jnp.where(group == 0, pltpu.roll(ends[0][0:8], (TILE - 8 * (rows - 1)) % TILE, 1), 0.0)
    corner = corner + jnp.where(group == rows - 1, pltpu.roll(ends[1][0:8], 8 * (rows - 1), 1), 0.0)
    columns = [
        lax.dot_general(corner, edge_pick(n, cells), (((0,), (0,)), ((), ())), preferred_element_type=f32)
        for n in range(2)
    ]

    def halo(ref, b):
        both = ref[lax.shift_right_logical(b, 1)].astype(f32)
        return jnp.where(jnp.bitwise_and(b, 1) == 1, both[8:16], both[0:8])

    extra = []
    for s in range(rows):
        base = first_block - margin[s, 0, 0] - 5 + 4 * total
        own = []
        for t in range(spread - 2 + own_blocks):
            b = wrapped(base + t, total) if t < spread - 2 else first_block + t - (spread - 2)
            adjoint = p[s, t]
            if s == 0:
                adjoint = adjoint + carry * halo(low, b)
            if s == rows - 1:
                adjoint = adjoint + carry * halo(high, b)
            moved = flux_of(q[s, t], adjoint)
            if t < spread - 2:
                flux[s, t] = moved.astype(jnp.bfloat16).astype(f32)
            else:
                own.append(moved)
        pulls = [
            pull_row(lambda t: flux[s, t], weights, margin, count, s, slot, first_block, base, total)
            for slot in range(own_blocks)
        ]
        extra.append((step_size * jnp.concatenate(pulls, axis=1), -step_size * jnp.concatenate(own, axis=1)))

    fields = (
        (o_r, h_r, a_r, jd_r, jo_r, src_r, x_r, out_r, layers - 1),
        (o_s, h_s, a_s, jd_s, jo_s, src_s, x_s, out_s, 0),
    )
    for n, (o, h, a, jd, jo, src, x, out, layer) in enumerate(fields):
        old = slice(n * layers, (n + 1) * layers)
        new = slice((2 + n) * layers, (3 + n) * layers)
        for v in range(var_count):
            for s in range(rows):
                value = o[v, s]
                if s == 0:
                    value = value + carry * rows_low[v, old, :]
                if s == rows - 1:
                    value = value + carry * rows_high[v, old, :]
                x[v * rows + s, 0:layers, :] = value
        for s in range(rows):
            state_row = [x[v * rows + s, 0:layers, :] for v in range(var_count)]
            for v in range(var_count):
                wide = x[v * rows + s]
                beside = (lanes_apart(wide) + layers_apart(wide))[0:layers]
                at = (v * rows + s) * 8
                beside = beside + h[v, s] + carry * columns[n][at : at + layers]
                if s > 0:
                    beside = beside + x[v * rows + s - 1, 0:layers, :]
                else:
                    beside = beside + inside[0] * (rows_low[v, new, :] + carry * a[v, 0])
                if s < rows - 1:
                    beside = beside + x[v * rows + s + 1, 0:layers, :]
                else:
                    beside = beside + inside[1] * (rows_high[v, new, :] + carry * a[v, rows - 1])
                res = jacobian_row(jd, jo, state_row, v, s, var_count) - coupling * beside - src[v, s]
                out[v, s] = (
                    state_row[v] - step_size * res + jnp.where(layer_all == layer, extra[s][n][v : v + 1], 0.0)
                )


def per_device(
    adjoint_rotor,
    adjoint_stator,
    jac_diag_rotor,
    jac_diag_stator,
    jac_off_rotor,
    jac_off_stator,
    source_rotor,
    source_stator,
    rotor_state,
    margin_block,
    face_count,
    margin_weight,
):
    var_count, rows, layers, cells = adjoint_rotor.shape
    own_blocks = cells // TILE
    total = margin_block.shape[1]
    spread = REACH + own_blocks + 1
    field = jax.ShapeDtypeStruct(adjoint_rotor.shape, f32)
    vmem = pl.BlockSpec(memory_space=pltpu.VMEM)
    smem = pl.BlockSpec(memory_space=pltpu.SMEM)
    padded = pltpu.VMEM((TILE // 8, 8, cells), f32)

    margin = jnp.swapaxes(margin_block, 1, 2)
    arguments = (
        adjoint_rotor, adjoint_stator, jac_diag_rotor, jac_diag_stator, jac_off_rotor, jac_off_stator,
        source_rotor, source_stator, rotor_state, margin, face_count, margin_weight,
    )
    shapes = [jax.ShapeDtypeStruct(x.shape, x.dtype) for x in arguments]
    v_r, v_s, share, a_r, a_s, weights, margin, count = pl.pallas_call(
        first_kernel,
        out_shape=(
            field, field, jax.ShapeDtypeStruct((own_blocks, rows * 24, TILE), f32),
            shapes[0], shapes[1], shapes[11], shapes[9], shapes[10],
        ),
        in_specs=[pl.BlockSpec(memory_space=pltpu.HBM)] * 12,
        out_specs=(vmem,) * 8,
        scratch_shapes=[pltpu.VMEM(x.shape, x.dtype) for x in shapes[2:9]]
        + [padded] * 4
        + [pltpu.SemaphoreType.DMA((12,))],
        compiler_params=params,
        name="local_part",
    )(*[pltpu.with_memory_space_constraint(x, pltpu.HBM) for x in arguments])
    whole = lax.all_gather(share, "circ", axis=0, tiled=True)
    tiles = jax.ShapeDtypeStruct((total // 2 + var_count * own_blocks + 1, 16, TILE), jnp.bfloat16)
    listed = jax.ShapeDtypeStruct((rows, spread - 2 + own_blocks, 8, TILE), f32)
    o_r, o_s, h_r, h_s, q, p, up, down = pl.pallas_call(
        second_kernel,
        out_shape=(field, field, field, field, listed, listed, tiles, tiles),
        in_specs=[vmem] * 6 + [smem] * 2,
        out_specs=(vmem,) * 8,
        scratch_shapes=[
            pltpu.VMEM((rows, spread, 8, TILE), f32),
            pltpu.VMEM((var_count, 4 * layers, cells), f32),
            pltpu.VMEM((8, TILE), f32),
        ],
        compiler_params=params,
        name="interface_part",
    )(whole, v_r, v_s, a_r, a_s, weights, margin, count)
    bands = lax.axis_size("span")
    low = lax.ppermute(up, "span", [(i, i + 1) for i in range(bands - 1)])
    high = lax.ppermute(down, "span", [(i + 1, i) for i in range(bands - 1)])
    out_r, out_s = pl.pallas_call(
        third_kernel,
        out_shape=(field, field),
        in_specs=[vmem] * 17 + [smem] * 2,
        out_specs=(vmem,) * 2,
        scratch_shapes=[
            pltpu.VMEM((rows, spread - 2, 8, TILE), f32),
            padded,
            padded,
            pltpu.VMEM((var_count, 4 * layers, cells), f32),
            pltpu.VMEM((var_count, 4 * layers, cells), f32),
        ],
        compiler_params=params,
        name="final_part",
    )(
        low, high, o_r, o_s, h_r, h_s, q, p, a_r, a_s, jac_diag_rotor, jac_diag_stator,
        jac_off_rotor, jac_off_stator, source_rotor, source_stator, weights, margin, count,
    )
    return (out_r, out_s)


def solution(mesh):
    field = P(None, "span", None, "circ")
    placed = (
        (field,) * 4
        + (P(None, None, "span", None, "circ"),) * 2
        + (field,) * 2
        + (P(None, "span", "circ"), P("span", None, None), P("span", None), P("span", None, None, None))
    )
    return jax.shard_map(
        per_device, mesh=mesh, in_specs=placed, out_specs=(field, field), check_vma=False
    )
```

```python
import jax
import jax.numpy as jnp
from jax import lax
from jax.experimental import pallas as pl
from jax.experimental.pallas import tpu as pltpu
from jax.sharding import PartitionSpec as P

step_size = 0.1
coupling = 0.2
carry = step_size * coupling
REACH = 8
TILE = 128
f32 = jnp.float32
params = pltpu.CompilerParams(vmem_limit_bytes=24 * 1024 * 1024)


def iota(shape, dim):
    return lax.broadcasted_iota(jnp.int32, shape, dim)


def wrapped(x, count):
    if count & (count - 1) == 0:
        return jnp.bitwise_and(x, count - 1)
    return lax.rem(x + 4 * count, count)


def lanes_apart(x):
    cells = x.shape[1]
    lane = iota(x.shape, 1)
    before = jnp.where(lane == 0, 0.0, pltpu.roll(x, 1, 1))
    after = jnp.where(lane == cells - 1, 0.0, pltpu.roll(x, cells - 1, 1))
    return before + after


def layers_apart(x):
    return pltpu.roll(x, 1, 0) + pltpu.roll(x, 7, 0)


def edge_pick(row, cells):
    at = iota((8, cells), 0)
    lane = iota((8, cells), 1)
    first = jnp.logical_and(at == row, lane == 0)
    last = jnp.logical_and(at == 4 + row, lane == cells - 1)
    return jnp.where(jnp.logical_or(first, last), 1.0, 0.0).astype(f32)


def flux_of(primal, adjoint):
    speeds = jnp.sqrt(1.0 + primal * primal)
    over = jnp.sum(primal * adjoint, axis=0, keepdims=True)
    under = 6.0 + jnp.sum(primal * primal, axis=0, keepdims=True)
    return speeds * adjoint + 0.5 * primal * (over / under)


def jacobian_row(diag, off, state, v, s, var_count):
    total = diag[v, s] * state[v]
    for w in range(var_count):
        total = total + off[w, v, s].astype(f32) * state[w]
    return total


def pull_row(flux, weights, margin, count, s, slot, first_block, base, total):
    target = wrapped(first_block + slot + total, total)
    acc = jnp.zeros((8, TILE), f32)
    for e in range(REACH):
        b = wrapped(base + slot + e, total)
        k = wrapped(target - margin[s, 0, b] + total, total)
        live = jnp.where(k < count[s, b], 1.0, 0.0).astype(f32)
        kept = jnp.minimum(k, weights.shape[2] - 1)
        acc = acc + (weights[s, b, pl.ds(kept, 1), :] * live) * flux(slot + e)
    return acc


def first_kernel(*refs):
    outer, refs = refs[:12], refs[12:]
    v_r, v_s, out, a_r, a_s, weights, margin, count = refs[:8]
    jd_r, jd_s, jo_r, jo_s, src_r, src_s, state = refs[8:15]
    xs, sems = refs[15:19], refs[19]
    var_count, rows, layers, cells = a_r.shape
    own_blocks = cells // TILE
    inner = (a_r, a_s, jd_r, jd_s, jo_r, jo_s, src_r, src_s, state, margin, count, weights)
    copies = [pltpu.make_async_copy(x, y, sems.at[n]) for n, (x, y) in enumerate(zip(outer, inner))]
    for copy in copies:
        copy.start()
    out[...] = jnp.zeros(out.shape, f32)
    for x in xs:
        x[...] = jnp.zeros(x.shape, f32)
    for copy in copies:
        copy.wait()
    fields = ((a_r, jd_r, jo_r, src_r, v_r, xs[0], xs[2]), (a_s, jd_s, jo_s, src_s, v_s, xs[1], xs[3]))
    for a, jd, jo, src, partial, x_a, x_p in fields:
        for v in range(var_count):
            for s in range(rows):
                x_a[v * rows + s, 0:layers, :] = a[v, s]
        for s in range(rows):
            state_row = [a[v, s] for v in range(var_count)]
            for v in range(var_count):
                wide = x_a[v * rows + s]
                beside = (lanes_apart(wide) + layers_apart(wide))[0:layers]
                if s > 0:
                    beside = beside + a[v, s - 1]
                if s < rows - 1:
                    beside = beside + a[v, s + 1]
                res = jacobian_row(jd, jo, state_row, v, s, var_count) - coupling * beside - src[v, s]
                new = state_row[v] - step_size * res
                partial[v, s] = new
                x_p[v * rows + s, 0:layers, :] = new
    edges = jnp.zeros((8, TILE), f32)
    for q in range(4):
        flat = xs[q][...].reshape(TILE, cells)
        edges = edges + lax.dot_general(
            edge_pick(q, cells), flat, (((1,), (1,)), ((), ())), preferred_element_type=f32
        )
    for v in range(var_count):
        rotor = state[v].astype(f32)
        for s in range(rows):
            for i in range(own_blocks):
                cut = slice(i * TILE, (i + 1) * TILE)
                at = s * 8 + v
                out[i, at : at + 1, :] = rotor[s : s + 1, cut]
                out[i, rows * 8 + at : rows * 8 + at + 1, :] = a_s[v, s, 0:1, cut]
                out[i, rows * 16 + at : rows * 16 + at + 1, :] = v_s[v, s, 0:1, cut]
    for side, i in ((0, 0), (1, own_blocks - 1)):
        out[i, 6:8, :] = edges[4 * side : 4 * side + 2]
        out[i, 14:16, :] = edges[4 * side + 2 : 4 * side + 4]


def second_kernel(
    mine, other, v_r, v_s, a_r, a_s, weights, margin, count,
    o_r, o_s, h_r, h_s, q_out, p_out, up, down, flux, held, spot, g,
):
    var_count, rows, layers, cells = a_r.shape
    total = g.shape[0]
    own_blocks = cells // TILE
    entries = weights.shape[2]
    spread = REACH + own_blocks + 1
    first_block = lax.axis_index("circ") * own_blocks
    row8 = iota((8, TILE), 0)
    lane = iota((8, TILE), 1)
    lane_all = iota((layers, cells), 1)
    layer_all = iota((layers, cells), 0)
    edge = jnp.logical_or(lane_all == 0, lane_all == cells - 1)
    left = wrapped(first_block - 1 + total, total)
    right = wrapped(first_block + own_blocks, total)

    core = jnp.bitwise_and(lax.axis_index("circ"), 1)
    for chip in range(total // own_blocks // 2):
        for i in range(own_blocks):
            g[(2 * chip + core) * own_blocks + i] = mine[chip * own_blocks + i]
            g[(2 * chip + 1 - core) * own_blocks + i] = other[chip * own_blocks + i]
    spot[0:2, :] = g[left, 6:8, :]
    spot[2:4, :] = g[left, 14:16, :]
    spot[4:6, :] = g[right, 6:8, :]
    spot[6:8, :] = g[right, 14:16, :]
    spots = spot[...]
    columns = [
        lax.dot_general(spots, edge_pick(q, cells), (((0,), (0,)), ((), ())), preferred_element_type=f32)
        for q in range(4)
    ]

    def block(s, b):
        primal = jnp.zeros((8, TILE), f32)
        for k in range(entries):
            live = jnp.where(k < count[s, b], 1.0, 0.0).astype(f32)
            primal = primal + (weights[s, b, k : k + 1, :] * live) * g[margin[s, k, b], s * 8 : s * 8 + 8, :]
        primal = jnp.where(row8 < var_count, primal, 0.0)
        adjoint = g[b, rows * 8 + s * 8 : rows * 8 + s * 8 + 8, :]
        return primal, flux_of(primal, adjoint)

    def advanced(s, b, moved):
        at = slice(rows * 8 + s * 8, rows * 8 + s * 8 + 8)
        place = lax.rem(b, own_blocks)
        before = jnp.where(place == 0, carry, 0.0).astype(f32)
        after = jnp.where(place == own_blocks - 1, carry, 0.0).astype(f32)
        low = pltpu.roll(g[wrapped(b - 1 + total, total), at, :], 1, 1)
        high = pltpu.roll(g[wrapped(b + 1, total), at, :], TILE - 1, 1)
        base = g[b, rows * 16 + s * 8 : rows * 16 + s * 8 + 8, :]
        base = base + jnp.where(lane == 0, low * before, 0.0) + jnp.where(lane == TILE - 1, high * after, 0.0)
        return base - step_size * moved

    for s in range(rows):
        base = first_block - margin[s, 0, 0] - 5 + 4 * total
        for t in range(spread):
            b = wrapped(base - 1 + t, total)
            primal, moved = block(s, b)
            flux[s, t] = moved.astype(jnp.bfloat16).astype(f32)
            if 0 < t < spread - 1:
                q_out[s, t - 1] = primal
                p_out[s, t - 1] = advanced(s, b, moved)
        own = []
        for i in range(own_blocks):
            primal, moved = block(s, first_block + i)
            own.append(moved)
            q_out[s, spread - 2 + i] = primal
            p_out[s, spread - 2 + i] = advanced(s, first_block + i, moved)
        blank = [jnp.zeros((8, TILE), f32)] * (own_blocks - 2)
        side_flux = [block(s, left)[1], block(s, right)[1]]
        pulls = [
            pull_row(lambda t: flux[s, t + 1], weights, margin, count, s, slot, first_block, base, total)
            for slot in range(-1, own_blocks + 1)
        ]

        def at_sides(low, high):
            return jnp.concatenate([pltpu.roll(low, 1, 1), *blank, pltpu.roll(high, TILE - 1, 1)], axis=1)

        pulled = step_size * jnp.concatenate(pulls[1:-1], axis=1)
        pulled_side = step_size * at_sides(pulls[0], pulls[-1])
        pushed = step_size * jnp.concatenate(own, axis=1)
        pushed_side = step_size * at_sides(*side_flux)
        for v in range(var_count):
            at = (v * rows + s) * 8
            cut = slice(at, at + layers)
            o_r[v, s] = (
                v_r[v, s] + carry * columns[0][cut] + jnp.where(layer_all == layers - 1, pulled[v : v + 1], 0.0)
            )
            o_s[v, s] = v_s[v, s] + carry * columns[1][cut] - jnp.where(layer_all == 0, pushed[v : v + 1], 0.0)
            h_r[v, s] = columns[2][cut] + jnp.where(
                edge, carry * a_r[v, s] + jnp.where(layer_all == layers - 1, pulled_side[v : v + 1], 0.0), 0.0
            )
            h_s[v, s] = columns[3][cut] + jnp.where(
                edge, carry * a_s[v, s] - jnp.where(layer_all == 0, pushed_side[v : v + 1], 0.0), 0.0
            )

    last = jnp.concatenate([spots, jnp.ones((8, TILE), f32)], axis=0).astype(jnp.bfloat16)
    for to, s in ((up, rows - 1), (down, 0)):
        at = slice(rows * 8 + s * 8, rows * 8 + s * 8 + 8)
        for j in range(total // 2):
            to[j] = jnp.concatenate([g[2 * j, at, :], g[2 * j + 1, at, :]], axis=0).astype(jnp.bfloat16)
        for v in range(var_count):
            for n, ref in enumerate((a_r, a_s, o_r, o_s)):
                held[v, n * layers : (n + 1) * layers, :] = ref[v, s]
            for i in range(own_blocks):
                to[total // 2 + v * own_blocks + i] = held[v, :, i * TILE : (i + 1) * TILE].astype(jnp.bfloat16)
        to[total // 2 + var_count * own_blocks] = last


def third_kernel(
    low, high, o_r, o_s, h_r, h_s, q, p, a_r, a_s, jd_r, jd_s, jo_r, jo_s, src_r, src_s, weights, margin, count,
    out_r, out_s, flux, x_r, x_s, rows_low, rows_high,
):
    var_count, rows, layers, cells = a_r.shape
    total = weights.shape[1]
    own_blocks = cells // TILE
    spread = REACH + own_blocks + 1
    first_block = lax.axis_index("circ") * own_blocks
    lane = iota((8, TILE), 1)
    layer_all = iota((layers, cells), 0)
    end = total // 2 + var_count * own_blocks
    for x in (x_r, x_s):
        x[...] = jnp.zeros(x.shape, f32)
    for ref, to in ((low, rows_low), (high, rows_high)):
        for v in range(var_count):
            for i in range(own_blocks):
                to[v, :, i * TILE : (i + 1) * TILE] = ref[total // 2 + v * own_blocks + i].astype(f32)
    ends = [ref[end].astype(f32) for ref in (low, high)]
    inside = [jnp.concatenate([x[8:9]] * own_blocks, axis=1) for x in ends]
    group = lax.rem(lax.shift_right_logical(lane, 3), rows)
    corner = jnp.where(group == 0, pltpu.roll(ends[0][0:8], (TILE - 8 * (rows - 1)) % TILE, 1), 0.0)
    corner = corner + jnp.where(group == rows - 1, pltpu.roll(ends[1][0:8], 8 * (rows - 1), 1), 0.0)
    columns = [
        lax.dot_general(corner, edge_pick(n, cells), (((0,), (0,)), ((), ())), preferred_element_type=f32)
        for n in range(2)
    ]

    def halo(ref, b):
        both = ref[lax.shift_right_logical(b, 1)].astype(f32)
        return jnp.where(jnp.bitwise_and(b, 1) == 1, both[8:16], both[0:8])

    extra = []
    for s in range(rows):
        base = first_block - margin[s, 0, 0] - 5 + 4 * total
        own = []
        for t in range(spread - 2 + own_blocks):
            b = wrapped(base + t, total) if t < spread - 2 else first_block + t - (spread - 2)
            adjoint = p[s, t]
            if s == 0:
                adjoint = adjoint + carry * halo(low, b)
            if s == rows - 1:
                adjoint = adjoint + carry * halo(high, b)
            moved = flux_of(q[s, t], adjoint)
            if t < spread - 2:
                flux[s, t] = moved.astype(jnp.bfloat16).astype(f32)
            else:
                own.append(moved)
        pulls = [
            pull_row(lambda t: flux[s, t], weights, margin, count, s, slot, first_block, base, total)
            for slot in range(own_blocks)
        ]
        extra.append((step_size * jnp.concatenate(pulls, axis=1), -step_size * jnp.concatenate(own, axis=1)))

    fields = (
        (o_r, h_r, a_r, jd_r, jo_r, src_r, x_r, out_r, layers - 1),
        (o_s, h_s, a_s, jd_s, jo_s, src_s, x_s, out_s, 0),
    )
    for n, (o, h, a, jd, jo, src, x, out, layer) in enumerate(fields):
        old = slice(n * layers, (n + 1) * layers)
        new = slice((2 + n) * layers, (3 + n) * layers)
        for v in range(var_count):
            for s in range(rows):
                value = o[v, s]
                if s == 0:
                    value = value + carry * rows_low[v, old, :]
                if s == rows - 1:
                    value = value + carry * rows_high[v, old, :]
                x[v * rows + s, 0:layers, :] = value
        for s in range(rows):
            state_row = [x[v * rows + s, 0:layers, :] for v in range(var_count)]
            for v in range(var_count):
                wide = x[v * rows + s]
                beside = (lanes_apart(wide) + layers_apart(wide))[0:layers]
                at = (v * rows + s) * 8
                beside = beside + h[v, s] + carry * columns[n][at : at + layers]
                if s > 0:
                    beside = beside + x[v * rows + s - 1, 0:layers, :]
                else:
                    beside = beside + inside[0] * (rows_low[v, new, :] + carry * a[v, 0])
                if s < rows - 1:
                    beside = beside + x[v * rows + s + 1, 0:layers, :]
                else:
                    beside = beside + inside[1] * (rows_high[v, new, :] + carry * a[v, rows - 1])
                res = jacobian_row(jd, jo, state_row, v, s, var_count) - coupling * beside - src[v, s]
                out[v, s] = (
                    state_row[v] - step_size * res + jnp.where(layer_all == layer, extra[s][n][v : v + 1], 0.0)
                )


def per_device(
    adjoint_rotor,
    adjoint_stator,
    jac_diag_rotor,
    jac_diag_stator,
    jac_off_rotor,
    jac_off_stator,
    source_rotor,
    source_stator,
    rotor_state,
    margin_block,
    face_count,
    margin_weight,
):
    var_count, rows, layers, cells = adjoint_rotor.shape
    own_blocks = cells // TILE
    total = margin_block.shape[1]
    spread = REACH + own_blocks + 1
    field = jax.ShapeDtypeStruct(adjoint_rotor.shape, f32)
    vmem = pl.BlockSpec(memory_space=pltpu.VMEM)
    smem = pl.BlockSpec(memory_space=pltpu.SMEM)
    padded = pltpu.VMEM((TILE // 8, 8, cells), f32)

    margin = jnp.swapaxes(margin_block, 1, 2)
    arguments = (
        adjoint_rotor, adjoint_stator, jac_diag_rotor, jac_diag_stator, jac_off_rotor, jac_off_stator,
        source_rotor, source_stator, rotor_state, margin, face_count, margin_weight,
    )
    shapes = [jax.ShapeDtypeStruct(x.shape, x.dtype) for x in arguments]
    v_r, v_s, share, a_r, a_s, weights, margin, count = pl.pallas_call(
        first_kernel,
        out_shape=(
            field, field, jax.ShapeDtypeStruct((own_blocks, rows * 24, TILE), f32),
            shapes[0], shapes[1], shapes[11], shapes[9], shapes[10],
        ),
        in_specs=[pl.BlockSpec(memory_space=pltpu.HBM)] * 12,
        out_specs=(vmem,) * 8,
        scratch_shapes=[pltpu.VMEM(x.shape, x.dtype) for x in shapes[2:9]]
        + [padded] * 4
        + [pltpu.SemaphoreType.DMA((12,))],
        compiler_params=params,
        name="local_part",
    )(*[pltpu.with_memory_space_constraint(x, pltpu.HBM) for x in arguments])
    members = lax.axis_size("circ")
    cores = 2
    alike = [list(range(core, members, cores)) for core in range(cores)]
    mine = lax.all_gather(share, "circ", axis=0, tiled=True, axis_index_groups=alike)
    other = lax.ppermute(mine, "circ", [(i, i ^ 1) for i in range(members)])
    tiles = jax.ShapeDtypeStruct((total // 2 + var_count * own_blocks + 1, 16, TILE), jnp.bfloat16)
    listed = jax.ShapeDtypeStruct((rows, spread - 2 + own_blocks, 8, TILE), f32)
    o_r, o_s, h_r, h_s, q, p, up, down = pl.pallas_call(
        second_kernel,
        out_shape=(field, field, field, field, listed, listed, tiles, tiles),
        in_specs=[vmem] * 7 + [smem] * 2,
        out_specs=(vmem,) * 8,
        scratch_shapes=[
            pltpu.VMEM((rows, spread, 8, TILE), f32),
            pltpu.VMEM((var_count, 4 * layers, cells), f32),
            pltpu.VMEM((8, TILE), f32),
            pltpu.VMEM((total, rows * 24, TILE), f32),
        ],
        compiler_params=params,
        name="interface_part",
    )(mine, other, v_r, v_s, a_r, a_s, weights, margin, count)
    bands = lax.axis_size("span")
    low = lax.ppermute(up, "span", [(i, i + 1) for i in range(bands - 1)])
    high = lax.ppermute(down, "span", [(i + 1, i) for i in range(bands - 1)])
    out_r, out_s = pl.pallas_call(
        third_kernel,
        out_shape=(field, field),
        in_specs=[vmem] * 17 + [smem] * 2,
        out_specs=(vmem,) * 2,
        scratch_shapes=[
            pltpu.VMEM((rows, spread - 2, 8, TILE), f32),
            padded,
            padded,
            pltpu.VMEM((var_count, 4 * layers, cells), f32),
            pltpu.VMEM((var_count, 4 * layers, cells), f32),
        ],
        compiler_params=params,
        name="final_part",
    )(
        low, high, o_r, o_s, h_r, h_s, q, p, a_r, a_s, jac_diag_rotor, jac_diag_stator,
        jac_off_rotor, jac_off_stator, source_rotor, source_stator, weights, margin, count,
    )
    return (out_r, out_s)


def solution(mesh):
    field = P(None, "span", None, "circ")
    placed = (
        (field,) * 4
        + (P(None, None, "span", None, "circ"),) * 2
        + (field,) * 2
        + (P(None, "span", "circ"), P("span", None, None), P("span", None), P("span", None, None, None))
    )
    return jax.shard_map(
        per_device, mesh=mesh, in_specs=placed, out_specs=(field, field), check_vma=False
    )
```

```python
import jax
import jax.numpy as jnp
from jax import lax
from jax.experimental import pallas as pl
from jax.experimental.pallas import tpu as pltpu
from jax.sharding import PartitionSpec as P

step_size = 0.1
coupling = 0.2
carry = step_size * coupling
REACH = 8
TILE = 128
f32 = jnp.float32
params = pltpu.CompilerParams(vmem_limit_bytes=24 * 1024 * 1024)


def iota(shape, dim):
    return lax.broadcasted_iota(jnp.int32, shape, dim)


def wrapped(x, count):
    if count & (count - 1) == 0:
        return jnp.bitwise_and(x, count - 1)
    return lax.rem(x + 4 * count, count)


def lanes_apart(x):
    cells = x.shape[1]
    lane = iota(x.shape, 1)
    before = jnp.where(lane == 0, 0.0, pltpu.roll(x, 1, 1))
    after = jnp.where(lane == cells - 1, 0.0, pltpu.roll(x, cells - 1, 1))
    return before + after


def layers_apart(x):
    return pltpu.roll(x, 1, 0) + pltpu.roll(x, 7, 0)


def edge_pick(row, cells):
    at = iota((8, cells), 0)
    lane = iota((8, cells), 1)
    first = jnp.logical_and(at == row, lane == 0)
    last = jnp.logical_and(at == 4 + row, lane == cells - 1)
    return jnp.where(jnp.logical_or(first, last), 1.0, 0.0).astype(f32)


def split(x):
    high = x.astype(jnp.bfloat16).astype(f32)
    return high, x - high


def flux_of(primal, adjoint):
    speeds = jnp.sqrt(1.0 + primal * primal)
    over = jnp.sum(primal * adjoint, axis=0, keepdims=True)
    under = 6.0 + jnp.sum(primal * primal, axis=0, keepdims=True)
    return speeds * adjoint + 0.5 * primal * (over / under)


def jacobian_row(diag, off, state, v, s, var_count):
    total = diag[v, s] * state[v]
    for w in range(var_count):
        total = total + off[w, v, s].astype(f32) * state[w]
    return total


def pull_row(flux, weights, margin, count, s, slot, first_block, base, total):
    target = wrapped(first_block + slot + total, total)
    acc = jnp.zeros((8, TILE), f32)
    for e in range(REACH):
        b = wrapped(base + slot + e, total)
        k = wrapped(target - margin[s, 0, b] + total, total)
        live = jnp.where(k < count[s, b], 1.0, 0.0).astype(f32)
        kept = jnp.minimum(k, weights.shape[2] - 1)
        acc = acc + (weights[s, b, pl.ds(kept, 1), :] * live) * flux(slot + e)
    return acc


def first_kernel(*refs):
    outer, refs = refs[:12], refs[12:]
    v_r, v_s, out, a_r, a_s, weights, margin, count = refs[:8]
    jd_r, jd_s, jo_r, jo_s, src_r, src_s, state = refs[8:15]
    xs, sems, wide_out = refs[15:19], refs[19], refs[20]
    var_count, rows, layers, cells = a_r.shape
    own_blocks = cells // TILE
    inner = (a_r, a_s, jd_r, jd_s, jo_r, jo_s, src_r, src_s, state, margin, count, weights)
    copies = [pltpu.make_async_copy(x, y, sems.at[n]) for n, (x, y) in enumerate(zip(outer, inner))]
    for copy in copies:
        copy.start()
    wide_out[...] = jnp.zeros(wide_out.shape, f32)
    for x in xs:
        x[...] = jnp.zeros(x.shape, f32)
    for copy in copies:
        copy.wait()
    fields = ((a_r, jd_r, jo_r, src_r, v_r, xs[0], xs[2]), (a_s, jd_s, jo_s, src_s, v_s, xs[1], xs[3]))
    for a, jd, jo, src, partial, x_a, x_p in fields:
        for v in range(var_count):
            for s in range(rows):
                x_a[v * rows + s, 0:layers, :] = a[v, s]
        for s in range(rows):
            state_row = [a[v, s] for v in range(var_count)]
            for v in range(var_count):
                wide = x_a[v * rows + s]
                beside = (lanes_apart(wide) + layers_apart(wide))[0:layers]
                if s > 0:
                    beside = beside + a[v, s - 1]
                if s < rows - 1:
                    beside = beside + a[v, s + 1]
                res = jacobian_row(jd, jo, state_row, v, s, var_count) - coupling * beside - src[v, s]
                new = state_row[v] - step_size * res
                partial[v, s] = new
                x_p[v * rows + s, 0:layers, :] = new
    edges = jnp.zeros((8, TILE), f32)
    for q in range(4):
        flat = xs[q][...].reshape(TILE, cells)
        edges = edges + lax.dot_general(
            edge_pick(q, cells), flat, (((1,), (1,)), ((), ())), preferred_element_type=f32
        )
    for v in range(var_count):
        rotor = state[v].astype(f32)
        for s in range(rows):
            for i in range(own_blocks):
                cut = slice(i * TILE, (i + 1) * TILE)
                wide_out[i, s, v : v + 1, :] = rotor[s : s + 1, cut]
                wide_out[i, rows + s, v : v + 1, :] = a_s[v, s, 0:1, cut]
                wide_out[i, 2 * rows + s, v : v + 1, :] = v_s[v, s, 0:1, cut]
    row8 = iota((8, TILE), 0)
    filled = row8 < var_count
    for i in range(own_blocks):
        if i in (0, own_blocks - 1):
            side = 4 if i else 0
            for s in range(rows):
                wide_out[i, 2 * rows + s, 6:8, :] = edges[side + 2 * s : side + 2 * s + 2]
        groups = []
        for s in range(rows):
            p_high, p_rest = split(wide_out[i, rows + s])
            u_high, u_rest = split(wide_out[i, 2 * rows + s])
            groups.append((
                jnp.where(filled, wide_out[i, s], pltpu.roll(u_rest, 6, 0)),
                jnp.where(filled, p_high, pltpu.roll(u_rest, 4, 0)),
                jnp.where(filled, p_rest, pltpu.roll(u_rest, 2, 0)),
                u_high,
            ))
        for n in range(4):
            out[i, n * 16 : n * 16 + 16, :] = jnp.concatenate([x[n] for x in groups], axis=0).astype(jnp.bfloat16)


def second_kernel(
    whole, v_r, v_s, a_r, a_s, weights, margin, count,
    o_r, o_s, h_r, h_s, q_out, p_out, inner, outer, flux, held, spot, g,
):
    var_count, rows, layers, cells = a_r.shape
    total = whole.shape[0]
    own_blocks = cells // TILE
    entries = weights.shape[2]
    spread = REACH + own_blocks + 1
    first_block = lax.axis_index("circ") * own_blocks
    row8 = iota((8, TILE), 0)
    lane = iota((8, TILE), 1)
    lane_all = iota((layers, cells), 1)
    layer_all = iota((layers, cells), 0)
    edge = jnp.logical_or(lane_all == 0, lane_all == cells - 1)
    left = wrapped(first_block - 1 + total, total)
    right = wrapped(first_block + own_blocks, total)

    filled = row8 < var_count
    for b in range(total):
        tiles = [whole[b, n * 16 : n * 16 + 16, :].astype(f32) for n in range(4)]
        for s in range(rows):
            rotor, p_high, p_rest, u_high = [x[s * 8 : s * 8 + 8] for x in tiles]
            u_rest = jnp.where(
                row8 < 2, pltpu.roll(rotor, 2, 0), jnp.where(row8 < 4, pltpu.roll(p_high, 4, 0), pltpu.roll(p_rest, 6, 0))
            )
            g[b, s] = rotor
            g[b, rows + s] = p_high + p_rest
            g[b, 2 * rows + s] = u_high + jnp.where(filled, u_rest, 0.0)
    spot[0:2, :] = g[left, 2 * rows, 6:8, :]
    spot[2:4, :] = g[left, 2 * rows + 1, 6:8, :]
    spot[4:6, :] = g[right, 2 * rows, 6:8, :]
    spot[6:8, :] = g[right, 2 * rows + 1, 6:8, :]
    spots = spot[...]
    columns = [
        lax.dot_general(spots, edge_pick(q, cells), (((0,), (0,)), ((), ())), preferred_element_type=f32)
        for q in range(4)
    ]

    def block(s, b):
        primal = jnp.zeros((8, TILE), f32)
        for k in range(entries):
            live = jnp.where(k < count[s, b], 1.0, 0.0).astype(f32)
            primal = primal + (weights[s, b, k : k + 1, :] * live) * g[margin[s, k, b], s]
        primal = jnp.where(filled, primal, 0.0)
        adjoint = g[b, rows + s]
        return primal, flux_of(primal, adjoint)

    def advanced(s, b, moved):
        place = lax.rem(b, own_blocks)
        before = jnp.where(place == 0, carry, 0.0).astype(f32)
        after = jnp.where(place == own_blocks - 1, carry, 0.0).astype(f32)
        low = pltpu.roll(g[wrapped(b - 1 + total, total), rows + s], 1, 1)
        high = pltpu.roll(g[wrapped(b + 1, total), rows + s], TILE - 1, 1)
        base = g[b, 2 * rows + s]
        base = base + jnp.where(lane == 0, low * before, 0.0) + jnp.where(lane == TILE - 1, high * after, 0.0)
        return base - step_size * moved

    for s in range(rows):
        base = first_block - margin[s, 0, 0] - 5 + 4 * total
        for t in range(spread):
            b = wrapped(base - 1 + t, total)
            primal, moved = block(s, b)
            flux[s, t] = moved.astype(jnp.bfloat16).astype(f32)
            if 0 < t < spread - 1:
                q_out[s, t - 1] = primal
                p_out[s, t - 1] = advanced(s, b, moved)
        own = []
        for i in range(own_blocks):
            primal, moved = block(s, first_block + i)
            own.append(moved)
            q_out[s, spread - 2 + i] = primal
            p_out[s, spread - 2 + i] = advanced(s, first_block + i, moved)
        blank = [jnp.zeros((8, TILE), f32)] * (own_blocks - 2)
        side_flux = [block(s, left)[1], block(s, right)[1]]
        pulls = [
            pull_row(lambda t: flux[s, t + 1], weights, margin, count, s, slot, first_block, base, total)
            for slot in range(-1, own_blocks + 1)
        ]

        def at_sides(low, high):
            return jnp.concatenate([pltpu.roll(low, 1, 1), *blank, pltpu.roll(high, TILE - 1, 1)], axis=1)

        pulled = step_size * jnp.concatenate(pulls[1:-1], axis=1)
        pulled_side = step_size * at_sides(pulls[0], pulls[-1])
        pushed = step_size * jnp.concatenate(own, axis=1)
        pushed_side = step_size * at_sides(*side_flux)
        for v in range(var_count):
            at = (v * rows + s) * 8
            cut = slice(at, at + layers)
            o_r[v, s] = (
                v_r[v, s] + carry * columns[0][cut] + jnp.where(layer_all == layers - 1, pulled[v : v + 1], 0.0)
            )
            o_s[v, s] = v_s[v, s] + carry * columns[1][cut] - jnp.where(layer_all == 0, pushed[v : v + 1], 0.0)
            h_r[v, s] = columns[2][cut] + jnp.where(
                edge, carry * a_r[v, s] + jnp.where(layer_all == layers - 1, pulled_side[v : v + 1], 0.0), 0.0
            )
            h_s[v, s] = columns[3][cut] + jnp.where(
                edge, carry * a_s[v, s] - jnp.where(layer_all == 0, pushed_side[v : v + 1], 0.0), 0.0
            )

    last = jnp.concatenate([spots, jnp.ones((8, TILE), f32)], axis=0).astype(jnp.bfloat16)
    odd = jnp.bitwise_and(lax.axis_index("span"), 1)
    for to, s in ((inner, (1 - odd) * (rows - 1)), (outer, odd * (rows - 1))):
        for j in range(total // 2):
            to[j] = jnp.concatenate([g[2 * j, rows + s], g[2 * j + 1, rows + s]], axis=0).astype(jnp.bfloat16)
        for v in range(var_count):
            for n, ref in enumerate((a_r, a_s, o_r, o_s)):
                held[v, n * layers : (n + 1) * layers, :] = ref[v, s]
            for i in range(own_blocks):
                to[total // 2 + v * own_blocks + i] = held[v, :, i * TILE : (i + 1) * TILE].astype(jnp.bfloat16)
        to[total // 2 + var_count * own_blocks] = last


def third_kernel(
    inner, outer, o_r, o_s, h_r, h_s, q, p, a_r, a_s, jd_r, jd_s, jo_r, jo_s, src_r, src_s, weights, margin, count,
    out_r, out_s, flux, x_r, x_s, rows_low, rows_high,
):
    var_count, rows, layers, cells = a_r.shape
    total = weights.shape[1]
    own_blocks = cells // TILE
    spread = REACH + own_blocks + 1
    first_block = lax.axis_index("circ") * own_blocks
    lane = iota((8, TILE), 1)
    layer_all = iota((layers, cells), 0)
    end = total // 2 + var_count * own_blocks
    for x in (x_r, x_s):
        x[...] = jnp.zeros(x.shape, f32)
    odd = jnp.bitwise_and(lax.axis_index("span"), 1) == 1

    def low(n):
        return jnp.where(odd, inner[n].astype(f32), outer[n].astype(f32))

    def high(n):
        return jnp.where(odd, outer[n].astype(f32), inner[n].astype(f32))

    for side, to in ((low, rows_low), (high, rows_high)):
        for v in range(var_count):
            for i in range(own_blocks):
                to[v, :, i * TILE : (i + 1) * TILE] = side(total // 2 + v * own_blocks + i)
    ends = [low(end), high(end)]
    inside = [jnp.concatenate([x[8:9]] * own_blocks, axis=1) for x in ends]
    group = lax.rem(lax.shift_right_logical(lane, 3), rows)
    corner = jnp.where(group == 0, pltpu.roll(ends[0][0:8], (TILE - 8 * (rows - 1)) % TILE, 1), 0.0)
    corner = corner + jnp.where(group == rows - 1, pltpu.roll(ends[1][0:8], 8 * (rows - 1), 1), 0.0)
    columns = [
        lax.dot_general(corner, edge_pick(n, cells), (((0,), (0,)), ((), ())), preferred_element_type=f32)
        for n in range(2)
    ]

    def halo(side, b):
        both = side(lax.shift_right_logical(b, 1))
        return jnp.where(jnp.bitwise_and(b, 1) == 1, both[8:16], both[0:8])

    extra = []
    for s in range(rows):
        base = first_block - margin[s, 0, 0] - 5 + 4 * total
        own = []
        for t in range(spread - 2 + own_blocks):
            b = wrapped(base + t, total) if t < spread - 2 else first_block + t - (spread - 2)
            adjoint = p[s, t]
            if s == 0:
                adjoint = adjoint + carry * halo(low, b)
            if s == rows - 1:
                adjoint = adjoint + carry * halo(high, b)
            moved = flux_of(q[s, t], adjoint)
            if t < spread - 2:
                flux[s, t] = moved.astype(jnp.bfloat16).astype(f32)
            else:
                own.append(moved)
        pulls = [
            pull_row(lambda t: flux[s, t], weights, margin, count, s, slot, first_block, base, total)
            for slot in range(own_blocks)
        ]
        extra.append((step_size * jnp.concatenate(pulls, axis=1), -step_size * jnp.concatenate(own, axis=1)))

    fields = (
        (o_r, h_r, a_r, jd_r, jo_r, src_r, x_r, out_r, layers - 1),
        (o_s, h_s, a_s, jd_s, jo_s, src_s, x_s, out_s, 0),
    )
    for n, (o, h, a, jd, jo, src, x, out, layer) in enumerate(fields):
        old = slice(n * layers, (n + 1) * layers)
        new = slice((2 + n) * layers, (3 + n) * layers)
        for v in range(var_count):
            for s in range(rows):
                value = o[v, s]
                if s == 0:
                    value = value + carry * rows_low[v, old, :]
                if s == rows - 1:
                    value = value + carry * rows_high[v, old, :]
                x[v * rows + s, 0:layers, :] = value
        for s in range(rows):
            state_row = [x[v * rows + s, 0:layers, :] for v in range(var_count)]
            for v in range(var_count):
                wide = x[v * rows + s]
                beside = (lanes_apart(wide) + layers_apart(wide))[0:layers]
                at = (v * rows + s) * 8
                beside = beside + h[v, s] + carry * columns[n][at : at + layers]
                if s > 0:
                    beside = beside + x[v * rows + s - 1, 0:layers, :]
                else:
                    beside = beside + inside[0] * (rows_low[v, new, :] + carry * a[v, 0])
                if s < rows - 1:
                    beside = beside + x[v * rows + s + 1, 0:layers, :]
                else:
                    beside = beside + inside[1] * (rows_high[v, new, :] + carry * a[v, rows - 1])
                res = jacobian_row(jd, jo, state_row, v, s, var_count) - coupling * beside - src[v, s]
                out[v, s] = (
                    state_row[v] - step_size * res + jnp.where(layer_all == layer, extra[s][n][v : v + 1], 0.0)
                )


def per_device(
    adjoint_rotor,
    adjoint_stator,
    jac_diag_rotor,
    jac_diag_stator,
    jac_off_rotor,
    jac_off_stator,
    source_rotor,
    source_stator,
    rotor_state,
    margin_block,
    face_count,
    margin_weight,
):
    var_count, rows, layers, cells = adjoint_rotor.shape
    own_blocks = cells // TILE
    total = margin_block.shape[1]
    spread = REACH + own_blocks + 1
    field = jax.ShapeDtypeStruct(adjoint_rotor.shape, f32)
    vmem = pl.BlockSpec(memory_space=pltpu.VMEM)
    smem = pl.BlockSpec(memory_space=pltpu.SMEM)
    padded = pltpu.VMEM((TILE // 8, 8, cells), f32)

    margin = jnp.swapaxes(margin_block, 1, 2)
    arguments = (
        adjoint_rotor, adjoint_stator, jac_diag_rotor, jac_diag_stator, jac_off_rotor, jac_off_stator,
        source_rotor, source_stator, rotor_state, margin, face_count, margin_weight,
    )
    shapes = [jax.ShapeDtypeStruct(x.shape, x.dtype) for x in arguments]
    v_r, v_s, share, a_r, a_s, weights, margin, count = pl.pallas_call(
        first_kernel,
        out_shape=(
            field, field, jax.ShapeDtypeStruct((own_blocks, 64, TILE), jnp.bfloat16),
            shapes[0], shapes[1], shapes[11], shapes[9], shapes[10],
        ),
        in_specs=[pl.BlockSpec(memory_space=pltpu.HBM)] * 12,
        out_specs=(vmem,) * 8,
        scratch_shapes=[pltpu.VMEM(x.shape, x.dtype) for x in shapes[2:9]]
        + [padded] * 4
        + [pltpu.SemaphoreType.DMA((12,)), pltpu.VMEM((own_blocks, 3 * rows, 8, TILE), f32)],
        compiler_params=params,
        name="local_part",
    )(*[pltpu.with_memory_space_constraint(x, pltpu.HBM) for x in arguments])
    whole = lax.all_gather(share, "circ", axis=0, tiled=True)
    tiles = jax.ShapeDtypeStruct((total // 2 + var_count * own_blocks + 1, 16, TILE), jnp.bfloat16)
    listed = jax.ShapeDtypeStruct((rows, spread - 2 + own_blocks, 8, TILE), f32)
    o_r, o_s, h_r, h_s, q, p, inner, outer = pl.pallas_call(
        second_kernel,
        out_shape=(field, field, field, field, listed, listed, tiles, tiles),
        in_specs=[vmem] * 6 + [smem] * 2,
        out_specs=(vmem,) * 8,
        scratch_shapes=[
            pltpu.VMEM((rows, spread, 8, TILE), f32),
            pltpu.VMEM((var_count, 4 * layers, cells), f32),
            pltpu.VMEM((8, TILE), f32),
            pltpu.VMEM((total, 3 * rows, 8, TILE), f32),
        ],
        compiler_params=params,
        name="interface_part",
    )(whole, v_r, v_s, a_r, a_s, weights, margin, count)
    bands = lax.axis_size("span")
    near = [(i, i ^ 1) for i in range(bands)]
    far = [pair for i in range(1, bands - 1, 2) for pair in ((i, i + 1), (i + 1, i))]
    inner = lax.ppermute(inner, "span", near)
    outer = lax.ppermute(outer, "span", far)
    out_r, out_s = pl.pallas_call(
        third_kernel,
        out_shape=(field, field),
        in_specs=[vmem] * 17 + [smem] * 2,
        out_specs=(vmem,) * 2,
        scratch_shapes=[
            pltpu.VMEM((rows, spread - 2, 8, TILE), f32),
            padded,
            padded,
            pltpu.VMEM((var_count, 4 * layers, cells), f32),
            pltpu.VMEM((var_count, 4 * layers, cells), f32),
        ],
        compiler_params=params,
        name="final_part",
    )(
        inner, outer, o_r, o_s, h_r, h_s, q, p, a_r, a_s, jac_diag_rotor, jac_diag_stator,
        jac_off_rotor, jac_off_stator, source_rotor, source_stator, weights, margin, count,
    )
    return (out_r, out_s)


def solution(mesh):
    field = P(None, "span", None, "circ")
    placed = (
        (field,) * 4
        + (P(None, None, "span", None, "circ"),) * 2
        + (field,) * 2
        + (P(None, "span", "circ"), P("span", None, None), P("span", None), P("span", None, None, None))
    )
    return jax.shard_map(
        per_device, mesh=mesh, in_specs=placed, out_specs=(field, field), check_vma=False
    )
```

```python
import jax
import jax.numpy as jnp
from jax import lax
from jax.experimental import pallas as pl
from jax.experimental.pallas import tpu as pltpu
from jax.sharding import PartitionSpec as P

step_size = 0.1
coupling = 0.2
carry = step_size * coupling
REACH = 8
TILE = 128
f32 = jnp.float32
params = pltpu.CompilerParams(vmem_limit_bytes=24 * 1024 * 1024)


def iota(shape, dim):
    return lax.broadcasted_iota(jnp.int32, shape, dim)


def wrapped(x, count):
    if count & (count - 1) == 0:
        return jnp.bitwise_and(x, count - 1)
    return lax.rem(x + 4 * count, count)


def lanes_apart(x):
    cells = x.shape[1]
    lane = iota(x.shape, 1)
    before = jnp.where(lane == 0, 0.0, pltpu.roll(x, 1, 1))
    after = jnp.where(lane == cells - 1, 0.0, pltpu.roll(x, cells - 1, 1))
    return before + after


def layers_apart(x):
    return pltpu.roll(x, 1, 0) + pltpu.roll(x, 7, 0)


def edge_pick(row, cells):
    at = iota((8, cells), 0)
    lane = iota((8, cells), 1)
    first = jnp.logical_and(at == row, lane == 0)
    last = jnp.logical_and(at == 4 + row, lane == cells - 1)
    return jnp.where(jnp.logical_or(first, last), 1.0, 0.0).astype(f32)


def split(x):
    high = x.astype(jnp.bfloat16).astype(f32)
    return high, x - high


def flux_of(primal, adjoint):
    speeds = jnp.sqrt(1.0 + primal * primal)
    over = jnp.sum(primal * adjoint, axis=0, keepdims=True)
    under = 6.0 + jnp.sum(primal * primal, axis=0, keepdims=True)
    return speeds * adjoint + 0.5 * primal * (over / under)


def jacobian_row(diag, off, state, v, s, var_count):
    total = diag[v, s] * state[v]
    for w in range(var_count):
        total = total + off[w, v, s].astype(f32) * state[w]
    return total


def pull_row(flux, weights, margin, count, s, slot, first_block, base, total):
    target = wrapped(first_block + slot + total, total)
    acc = jnp.zeros((8, TILE), f32)
    for e in range(REACH):
        b = wrapped(base + slot + e, total)
        k = wrapped(target - margin[s, 0, b] + total, total)
        live = jnp.where(k < count[s, b], 1.0, 0.0).astype(f32)
        kept = jnp.minimum(k, weights.shape[2] - 1)
        acc = acc + (weights[s, b, pl.ds(kept, 1), :] * live) * flux(slot + e)
    return acc


def first_kernel(*refs):
    outer, refs = refs[:12], refs[12:]
    v_r, v_s, out, a_r, a_s, weights, margin, count = refs[:8]
    jd_r, jd_s, jo_r, jo_s, src_r, src_s, state = refs[8:15]
    xs, sems, wide_out = refs[15:19], refs[19], refs[20]
    var_count, rows, layers, cells = a_r.shape
    own_blocks = cells // TILE
    inner = (a_r, a_s, jd_r, jd_s, jo_r, jo_s, src_r, src_s, state, margin, count, weights)
    copies = [pltpu.make_async_copy(x, y, sems.at[n]) for n, (x, y) in enumerate(zip(outer, inner))]
    for copy in copies:
        copy.start()
    wide_out[...] = jnp.zeros(wide_out.shape, f32)
    for x in xs:
        x[...] = jnp.zeros(x.shape, f32)
    for copy in copies:
        copy.wait()
    fields = ((a_r, jd_r, jo_r, src_r, v_r, xs[0], xs[2]), (a_s, jd_s, jo_s, src_s, v_s, xs[1], xs[3]))
    for a, jd, jo, src, partial, x_a, x_p in fields:
        for v in range(var_count):
            for s in range(rows):
                x_a[v * rows + s, 0:layers, :] = a[v, s]
        for s in range(rows):
            state_row = [a[v, s] for v in range(var_count)]
            for v in range(var_count):
                wide = x_a[v * rows + s]
                beside = (lanes_apart(wide) + layers_apart(wide))[0:layers]
                if s > 0:
                    beside = beside + a[v, s - 1]
                if s < rows - 1:
                    beside = beside + a[v, s + 1]
                res = jacobian_row(jd, jo, state_row, v, s, var_count) - coupling * beside - src[v, s]
                new = state_row[v] - step_size * res
                partial[v, s] = new
                x_p[v * rows + s, 0:layers, :] = new
    edges = jnp.zeros((8, TILE), f32)
    for q in range(4):
        flat = xs[q][...].reshape(TILE, cells)
        edges = edges + lax.dot_general(
            edge_pick(q, cells), flat, (((1,), (1,)), ((), ())), preferred_element_type=f32
        )
    for v in range(var_count):
        rotor = state[v].astype(f32)
        for s in range(rows):
            for i in range(own_blocks):
                cut = slice(i * TILE, (i + 1) * TILE)
                wide_out[i, s, v : v + 1, :] = rotor[s : s + 1, cut]
                wide_out[i, rows + s, v : v + 1, :] = a_s[v, s, 0:1, cut]
                wide_out[i, 2 * rows + s, v : v + 1, :] = v_s[v, s, 0:1, cut]
    row8 = iota((8, TILE), 0)
    filled = row8 < var_count
    for i in range(own_blocks):
        if i in (0, own_blocks - 1):
            side = 4 if i else 0
            for s in range(rows):
                wide_out[i, 2 * rows + s, 6:8, :] = edges[side + 2 * s : side + 2 * s + 2]
        groups = []
        for s in range(rows):
            p_high, p_rest = split(wide_out[i, rows + s])
            u_high, u_rest = split(wide_out[i, 2 * rows + s])
            groups.append((
                jnp.where(filled, wide_out[i, s], pltpu.roll(u_rest, 6, 0)),
                jnp.where(filled, p_high, pltpu.roll(u_rest, 4, 0)),
                jnp.where(filled, p_rest, pltpu.roll(u_rest, 2, 0)),
                u_high,
            ))
        for n in range(4):
            tile = jnp.concatenate([x[n] for x in groups], axis=0).astype(jnp.bfloat16)
            for member in range(out.shape[0] // own_blocks):
                out[member * own_blocks + i, n * 16 : n * 16 + 16, :] = tile


def second_kernel(
    whole, v_r, v_s, a_r, a_s, weights, margin, count,
    o_r, o_s, h_r, h_s, q_out, p_out, inner, outer, flux, held, spot, g,
):
    var_count, rows, layers, cells = a_r.shape
    total = whole.shape[0]
    own_blocks = cells // TILE
    entries = weights.shape[2]
    spread = REACH + own_blocks + 1
    first_block = lax.axis_index("circ") * own_blocks
    row8 = iota((8, TILE), 0)
    lane = iota((8, TILE), 1)
    lane_all = iota((layers, cells), 1)
    layer_all = iota((layers, cells), 0)
    edge = jnp.logical_or(lane_all == 0, lane_all == cells - 1)
    left = wrapped(first_block - 1 + total, total)
    right = wrapped(first_block + own_blocks, total)

    filled = row8 < var_count
    for b in range(total):
        tiles = [whole[b, n * 16 : n * 16 + 16, :].astype(f32) for n in range(4)]
        for s in range(rows):
            rotor, p_high, p_rest, u_high = [x[s * 8 : s * 8 + 8] for x in tiles]
            u_rest = jnp.where(
                row8 < 2, pltpu.roll(rotor, 2, 0), jnp.where(row8 < 4, pltpu.roll(p_high, 4, 0), pltpu.roll(p_rest, 6, 0))
            )
            g[b, s] = rotor
            g[b, rows + s] = p_high + p_rest
            g[b, 2 * rows + s] = u_high + jnp.where(filled, u_rest, 0.0)
    spot[0:2, :] = g[left, 2 * rows, 6:8, :]
    spot[2:4, :] = g[left, 2 * rows + 1, 6:8, :]
    spot[4:6, :] = g[right, 2 * rows, 6:8, :]
    spot[6:8, :] = g[right, 2 * rows + 1, 6:8, :]
    spots = spot[...]
    columns = [
        lax.dot_general(spots, edge_pick(q, cells), (((0,), (0,)), ((), ())), preferred_element_type=f32)
        for q in range(4)
    ]

    def block(s, b):
        primal = jnp.zeros((8, TILE), f32)
        for k in range(entries):
            live = jnp.where(k < count[s, b], 1.0, 0.0).astype(f32)
            primal = primal + (weights[s, b, k : k + 1, :] * live) * g[margin[s, k, b], s]
        primal = jnp.where(filled, primal, 0.0)
        adjoint = g[b, rows + s]
        return primal, flux_of(primal, adjoint)

    def advanced(s, b, moved):
        place = lax.rem(b, own_blocks)
        before = jnp.where(place == 0, carry, 0.0).astype(f32)
        after = jnp.where(place == own_blocks - 1, carry, 0.0).astype(f32)
        low = pltpu.roll(g[wrapped(b - 1 + total, total), rows + s], 1, 1)
        high = pltpu.roll(g[wrapped(b + 1, total), rows + s], TILE - 1, 1)
        base = g[b, 2 * rows + s]
        base = base + jnp.where(lane == 0, low * before, 0.0) + jnp.where(lane == TILE - 1, high * after, 0.0)
        return base - step_size * moved

    for s in range(rows):
        base = first_block - margin[s, 0, 0] - 5 + 4 * total
        for t in range(spread):
            b = wrapped(base - 1 + t, total)
            primal, moved = block(s, b)
            flux[s, t] = moved.astype(jnp.bfloat16).astype(f32)
            if 0 < t < spread - 1:
                q_out[s, t - 1] = primal
                p_out[s, t - 1] = advanced(s, b, moved)
        own = []
        for i in range(own_blocks):
            primal, moved = block(s, first_block + i)
            own.append(moved)
            q_out[s, spread - 2 + i] = primal
            p_out[s, spread - 2 + i] = advanced(s, first_block + i, moved)
        blank = [jnp.zeros((8, TILE), f32)] * (own_blocks - 2)
        side_flux = [block(s, left)[1], block(s, right)[1]]
        pulls = [
            pull_row(lambda t: flux[s, t + 1], weights, margin, count, s, slot, first_block, base, total)
            for slot in range(-1, own_blocks + 1)
        ]

        def at_sides(low, high):
            return jnp.concatenate([pltpu.roll(low, 1, 1), *blank, pltpu.roll(high, TILE - 1, 1)], axis=1)

        pulled = step_size * jnp.concatenate(pulls[1:-1], axis=1)
        pulled_side = step_size * at_sides(pulls[0], pulls[-1])
        pushed = step_size * jnp.concatenate(own, axis=1)
        pushed_side = step_size * at_sides(*side_flux)
        for v in range(var_count):
            at = (v * rows + s) * 8
            cut = slice(at, at + layers)
            o_r[v, s] = (
                v_r[v, s] + carry * columns[0][cut] + jnp.where(layer_all == layers - 1, pulled[v : v + 1], 0.0)
            )
            o_s[v, s] = v_s[v, s] + carry * columns[1][cut] - jnp.where(layer_all == 0, pushed[v : v + 1], 0.0)
            h_r[v, s] = columns[2][cut] + jnp.where(
                edge, carry * a_r[v, s] + jnp.where(layer_all == layers - 1, pulled_side[v : v + 1], 0.0), 0.0
            )
            h_s[v, s] = columns[3][cut] + jnp.where(
                edge, carry * a_s[v, s] - jnp.where(layer_all == 0, pushed_side[v : v + 1], 0.0), 0.0
            )

    last = jnp.concatenate([spots, jnp.ones((8, TILE), f32)], axis=0).astype(jnp.bfloat16)
    odd = jnp.bitwise_and(lax.axis_index("span"), 1)
    for to, s in ((inner, (1 - odd) * (rows - 1)), (outer, odd * (rows - 1))):
        for j in range(total // 2):
            to[j] = jnp.concatenate([g[2 * j, rows + s], g[2 * j + 1, rows + s]], axis=0).astype(jnp.bfloat16)
        for v in range(var_count):
            for n, ref in enumerate((a_r, a_s, o_r, o_s)):
                held[v, n * layers : (n + 1) * layers, :] = ref[v, s]
            for i in range(own_blocks):
                to[total // 2 + v * own_blocks + i] = held[v, :, i * TILE : (i + 1) * TILE].astype(jnp.bfloat16)
        to[total // 2 + var_count * own_blocks] = last


def third_kernel(
    inner, outer, o_r, o_s, h_r, h_s, q, p, a_r, a_s, jd_r, jd_s, jo_r, jo_s, src_r, src_s, weights, margin, count,
    out_r, out_s, flux, x_r, x_s, rows_low, rows_high,
):
    var_count, rows, layers, cells = a_r.shape
    total = weights.shape[1]
    own_blocks = cells // TILE
    spread = REACH + own_blocks + 1
    first_block = lax.axis_index("circ") * own_blocks
    lane = iota((8, TILE), 1)
    layer_all = iota((layers, cells), 0)
    end = total // 2 + var_count * own_blocks
    for x in (x_r, x_s):
        x[...] = jnp.zeros(x.shape, f32)
    odd = jnp.bitwise_and(lax.axis_index("span"), 1) == 1

    def low(n):
        return jnp.where(odd, inner[n].astype(f32), outer[n].astype(f32))

    def high(n):
        return jnp.where(odd, outer[n].astype(f32), inner[n].astype(f32))

    for side, to in ((low, rows_low), (high, rows_high)):
        for v in range(var_count):
            for i in range(own_blocks):
                to[v, :, i * TILE : (i + 1) * TILE] = side(total // 2 + v * own_blocks + i)
    ends = [low(end), high(end)]
    inside = [jnp.concatenate([x[8:9]] * own_blocks, axis=1) for x in ends]
    group = lax.rem(lax.shift_right_logical(lane, 3), rows)
    corner = jnp.where(group == 0, pltpu.roll(ends[0][0:8], (TILE - 8 * (rows - 1)) % TILE, 1), 0.0)
    corner = corner + jnp.where(group == rows - 1, pltpu.roll(ends[1][0:8], 8 * (rows - 1), 1), 0.0)
    columns = [
        lax.dot_general(corner, edge_pick(n, cells), (((0,), (0,)), ((), ())), preferred_element_type=f32)
        for n in range(2)
    ]

    def halo(side, b):
        both = side(lax.shift_right_logical(b, 1))
        return jnp.where(jnp.bitwise_and(b, 1) == 1, both[8:16], both[0:8])

    extra = []
    for s in range(rows):
        base = first_block - margin[s, 0, 0] - 5 + 4 * total
        own = []
        for t in range(spread - 2 + own_blocks):
            b = wrapped(base + t, total) if t < spread - 2 else first_block + t - (spread - 2)
            adjoint = p[s, t]
            if s == 0:
                adjoint = adjoint + carry * halo(low, b)
            if s == rows - 1:
                adjoint = adjoint + carry * halo(high, b)
            moved = flux_of(q[s, t], adjoint)
            if t < spread - 2:
                flux[s, t] = moved.astype(jnp.bfloat16).astype(f32)
            else:
                own.append(moved)
        pulls = [
            pull_row(lambda t: flux[s, t], weights, margin, count, s, slot, first_block, base, total)
            for slot in range(own_blocks)
        ]
        extra.append((step_size * jnp.concatenate(pulls, axis=1), -step_size * jnp.concatenate(own, axis=1)))

    fields = (
        (o_r, h_r, a_r, jd_r, jo_r, src_r, x_r, out_r, layers - 1),
        (o_s, h_s, a_s, jd_s, jo_s, src_s, x_s, out_s, 0),
    )
    for n, (o, h, a, jd, jo, src, x, out, layer) in enumerate(fields):
        old = slice(n * layers, (n + 1) * layers)
        new = slice((2 + n) * layers, (3 + n) * layers)
        for v in range(var_count):
            for s in range(rows):
                value = o[v, s]
                if s == 0:
                    value = value + carry * rows_low[v, old, :]
                if s == rows - 1:
                    value = value + carry * rows_high[v, old, :]
                x[v * rows + s, 0:layers, :] = value
        for s in range(rows):
            state_row = [x[v * rows + s, 0:layers, :] for v in range(var_count)]
            for v in range(var_count):
                wide = x[v * rows + s]
                beside = (lanes_apart(wide) + layers_apart(wide))[0:layers]
                at = (v * rows + s) * 8
                beside = beside + h[v, s] + carry * columns[n][at : at + layers]
                if s > 0:
                    beside = beside + x[v * rows + s - 1, 0:layers, :]
                else:
                    beside = beside + inside[0] * (rows_low[v, new, :] + carry * a[v, 0])
                if s < rows - 1:
                    beside = beside + x[v * rows + s + 1, 0:layers, :]
                else:
                    beside = beside + inside[1] * (rows_high[v, new, :] + carry * a[v, rows - 1])
                res = jacobian_row(jd, jo, state_row, v, s, var_count) - coupling * beside - src[v, s]
                out[v, s] = (
                    state_row[v] - step_size * res + jnp.where(layer_all == layer, extra[s][n][v : v + 1], 0.0)
                )


def per_device(
    adjoint_rotor,
    adjoint_stator,
    jac_diag_rotor,
    jac_diag_stator,
    jac_off_rotor,
    jac_off_stator,
    source_rotor,
    source_stator,
    rotor_state,
    margin_block,
    face_count,
    margin_weight,
):
    var_count, rows, layers, cells = adjoint_rotor.shape
    own_blocks = cells // TILE
    total = margin_block.shape[1]
    spread = REACH + own_blocks + 1
    field = jax.ShapeDtypeStruct(adjoint_rotor.shape, f32)
    vmem = pl.BlockSpec(memory_space=pltpu.VMEM)
    smem = pl.BlockSpec(memory_space=pltpu.SMEM)
    padded = pltpu.VMEM((TILE // 8, 8, cells), f32)

    margin = jnp.swapaxes(margin_block, 1, 2)
    arguments = (
        adjoint_rotor, adjoint_stator, jac_diag_rotor, jac_diag_stator, jac_off_rotor, jac_off_stator,
        source_rotor, source_stator, rotor_state, margin, face_count, margin_weight,
    )
    shapes = [jax.ShapeDtypeStruct(x.shape, x.dtype) for x in arguments]
    v_r, v_s, share, a_r, a_s, weights, margin, count = pl.pallas_call(
        first_kernel,
        out_shape=(
            field, field, jax.ShapeDtypeStruct((total, 64, TILE), jnp.bfloat16),
            shapes[0], shapes[1], shapes[11], shapes[9], shapes[10],
        ),
        in_specs=[pl.BlockSpec(memory_space=pltpu.HBM)] * 12,
        out_specs=(vmem,) * 8,
        scratch_shapes=[pltpu.VMEM(x.shape, x.dtype) for x in shapes[2:9]]
        + [padded] * 4
        + [pltpu.SemaphoreType.DMA((12,)), pltpu.VMEM((own_blocks, 3 * rows, 8, TILE), f32)],
        compiler_params=params,
        name="local_part",
    )(*[pltpu.with_memory_space_constraint(x, pltpu.HBM) for x in arguments])
    whole = lax.all_to_all(share, "circ", 0, 0, tiled=True)
    tiles = jax.ShapeDtypeStruct((total // 2 + var_count * own_blocks + 1, 16, TILE), jnp.bfloat16)
    listed = jax.ShapeDtypeStruct((rows, spread - 2 + own_blocks, 8, TILE), f32)
    o_r, o_s, h_r, h_s, q, p, inner, outer = pl.pallas_call(
        second_kernel,
        out_shape=(field, field, field, field, listed, listed, tiles, tiles),
        in_specs=[vmem] * 6 + [smem] * 2,
        out_specs=(vmem,) * 8,
        scratch_shapes=[
            pltpu.VMEM((rows, spread, 8, TILE), f32),
            pltpu.VMEM((var_count, 4 * layers, cells), f32),
            pltpu.VMEM((8, TILE), f32),
            pltpu.VMEM((total, 3 * rows, 8, TILE), f32),
        ],
        compiler_params=params,
        name="interface_part",
    )(whole, v_r, v_s, a_r, a_s, weights, margin, count)
    bands = lax.axis_size("span")
    near = [(i, i ^ 1) for i in range(bands)]
    far = [pair for i in range(1, bands - 1, 2) for pair in ((i, i + 1), (i + 1, i))]
    inner = lax.ppermute(inner, "span", near)
    outer = lax.ppermute(outer, "span", far)
    out_r, out_s = pl.pallas_call(
        third_kernel,
        out_shape=(field, field),
        in_specs=[vmem] * 17 + [smem] * 2,
        out_specs=(vmem,) * 2,
        scratch_shapes=[
            pltpu.VMEM((rows, spread - 2, 8, TILE), f32),
            padded,
            padded,
            pltpu.VMEM((var_count, 4 * layers, cells), f32),
            pltpu.VMEM((var_count, 4 * layers, cells), f32),
        ],
        compiler_params=params,
        name="final_part",
    )(
        inner, outer, o_r, o_s, h_r, h_s, q, p, a_r, a_s, jac_diag_rotor, jac_diag_stator,
        jac_off_rotor, jac_off_stator, source_rotor, source_stator, weights, margin, count,
    )
    return (out_r, out_s)


def solution(mesh):
    field = P(None, "span", None, "circ")
    placed = (
        (field,) * 4
        + (P(None, None, "span", None, "circ"),) * 2
        + (field,) * 2
        + (P(None, "span", "circ"), P("span", None, None), P("span", None), P("span", None, None, None))
    )
    return jax.shard_map(
        per_device, mesh=mesh, in_specs=placed, out_specs=(field, field), check_vma=False
    )
```

```python
import functools

import jax
import jax.numpy as jnp
from jax import lax
from jax.experimental import pallas as pl
from jax.experimental.pallas import tpu as pltpu
from jax.sharding import PartitionSpec as P

step_size = 0.1
coupling = 0.2
carry = step_size * coupling
REACH = 8
TILE = 128
f32 = jnp.float32
params = pltpu.CompilerParams(vmem_limit_bytes=24 * 1024 * 1024)


def iota(shape, dim):
    return lax.broadcasted_iota(jnp.int32, shape, dim)


def wrapped(x, count):
    if count & (count - 1) == 0:
        return jnp.bitwise_and(x, count - 1)
    return lax.rem(x + 4 * count, count)


def lanes_apart(x):
    cells = x.shape[1]
    lane = iota(x.shape, 1)
    before = jnp.where(lane == 0, 0.0, pltpu.roll(x, 1, 1))
    after = jnp.where(lane == cells - 1, 0.0, pltpu.roll(x, cells - 1, 1))
    return before + after


def layers_apart(x):
    return pltpu.roll(x, 1, 0) + pltpu.roll(x, 7, 0)


def edge_pick(row, cells):
    at = iota((8, cells), 0)
    lane = iota((8, cells), 1)
    first = jnp.logical_and(at == row, lane == 0)
    last = jnp.logical_and(at == 4 + row, lane == cells - 1)
    return jnp.where(jnp.logical_or(first, last), 1.0, 0.0).astype(f32)


def split(x):
    high = x.astype(jnp.bfloat16).astype(f32)
    return high, x - high


def flux_of(primal, adjoint):
    speeds = jnp.sqrt(1.0 + primal * primal)
    over = jnp.sum(primal * adjoint, axis=0, keepdims=True)
    under = 6.0 + jnp.sum(primal * primal, axis=0, keepdims=True)
    return speeds * adjoint + 0.5 * primal * (over / under)


def jacobian_row(diag, off, state, v, s, var_count):
    total = diag[v, s] * state[v]
    for w in range(var_count):
        total = total + off[w, v, s].astype(f32) * state[w]
    return total


def pull_row(flux, weights, margin, count, s, slot, first_block, base, total):
    target = wrapped(first_block + slot + total, total)
    acc = jnp.zeros((8, TILE), f32)
    for e in range(REACH):
        b = wrapped(base + slot + e, total)
        k = wrapped(target - margin[s, 0, b] + total, total)
        live = jnp.where(k < count[s, b], 1.0, 0.0).astype(f32)
        kept = jnp.minimum(k, weights.shape[2] - 1)
        acc = acc + (weights[s, b, pl.ds(kept, 1), :] * live) * flux(slot + e)
    return acc


def first_kernel(*refs):
    outer, refs = refs[:12], refs[12:]
    v_r, v_s, out, a_r, a_s, weights, margin, count = refs[:8]
    jd_r, jd_s, jo_r, jo_s, src_r, src_s, state = refs[8:15]
    xs, sems, wide_out = refs[15:19], refs[19], refs[20]
    var_count, rows, layers, cells = a_r.shape
    own_blocks = cells // TILE
    inner = (a_r, a_s, jd_r, jd_s, jo_r, jo_s, src_r, src_s, state, margin, count, weights)
    copies = [pltpu.make_async_copy(x, y, sems.at[n]) for n, (x, y) in enumerate(zip(outer, inner))]
    for copy in copies:
        copy.start()
    wide_out[...] = jnp.zeros(wide_out.shape, f32)
    for x in xs:
        x[...] = jnp.zeros(x.shape, f32)
    for copy in copies:
        copy.wait()
    fields = ((a_r, jd_r, jo_r, src_r, v_r, xs[0], xs[2]), (a_s, jd_s, jo_s, src_s, v_s, xs[1], xs[3]))
    for a, jd, jo, src, partial, x_a, x_p in fields:
        for v in range(var_count):
            for s in range(rows):
                x_a[v * rows + s, 0:layers, :] = a[v, s]
        for s in range(rows):
            state_row = [a[v, s] for v in range(var_count)]
            for v in range(var_count):
                wide = x_a[v * rows + s]
                beside = (lanes_apart(wide) + layers_apart(wide))[0:layers]
                if s > 0:
                    beside = beside + a[v, s - 1]
                if s < rows - 1:
                    beside = beside + a[v, s + 1]
                res = jacobian_row(jd, jo, state_row, v, s, var_count) - coupling * beside - src[v, s]
                new = state_row[v] - step_size * res
                partial[v, s] = new
                x_p[v * rows + s, 0:layers, :] = new
    edges = jnp.zeros((8, TILE), f32)
    for q in range(4):
        flat = xs[q][...].reshape(TILE, cells)
        edges = edges + lax.dot_general(
            edge_pick(q, cells), flat, (((1,), (1,)), ((), ())), preferred_element_type=f32
        )
    for v in range(var_count):
        rotor = state[v].astype(f32)
        for s in range(rows):
            for i in range(own_blocks):
                cut = slice(i * TILE, (i + 1) * TILE)
                wide_out[i, s, v : v + 1, :] = rotor[s : s + 1, cut]
                wide_out[i, rows + s, v : v + 1, :] = a_s[v, s, 0:1, cut]
                wide_out[i, 2 * rows + s, v : v + 1, :] = v_s[v, s, 0:1, cut]
    row8 = iota((8, TILE), 0)
    filled = row8 < var_count
    for i in range(own_blocks):
        if i in (0, own_blocks - 1):
            side = 4 if i else 0
            for s in range(rows):
                wide_out[i, 2 * rows + s, 6:8, :] = edges[side + 2 * s : side + 2 * s + 2]
        groups = []
        for s in range(rows):
            p_high, p_rest = split(wide_out[i, rows + s])
            u_high, u_rest = split(wide_out[i, 2 * rows + s])
            groups.append((
                jnp.where(filled, wide_out[i, s], pltpu.roll(u_rest, 6, 0)),
                jnp.where(filled, p_high, pltpu.roll(u_rest, 4, 0)),
                jnp.where(filled, p_rest, pltpu.roll(u_rest, 2, 0)),
                u_high,
            ))
        for n in range(4):
            out[i, n * 16 : n * 16 + 16, :] = jnp.concatenate([x[n] for x in groups], axis=0).astype(jnp.bfloat16)


def second_kernel(
    masks, mine, other, v_r, v_s, a_r, a_s, weights, margin, count,
    o_r, o_s, h_r, h_s, q_out, p_out, outer, inner, flux, held, spot, g,
):
    var_count, rows, layers, cells = a_r.shape
    total = 2 * mine.shape[0]
    own_blocks = cells // TILE
    entries = weights.shape[2]
    spread = REACH + own_blocks + 1
    first_block = lax.axis_index("circ") * own_blocks
    row8 = iota((8, TILE), 0)
    lane = iota((8, TILE), 1)
    lane_all = iota((layers, cells), 1)
    layer_all = iota((layers, cells), 0)
    edge = jnp.logical_or(lane_all == 0, lane_all == cells - 1)
    left = wrapped(first_block - 1 + total, total)
    right = wrapped(first_block + own_blocks, total)

    filled = row8 < var_count
    here = lax.axis_index("circ")
    for at in range(total):
        half, part = divmod(at, total // 2)
        place, i = divmod(part, own_blocks)
        mask = half + sum(m for n, m in enumerate(masks) if place >> n & 1)
        b = jnp.bitwise_xor(here, mask) * own_blocks + i
        whole = other if half else mine
        tiles = [whole[part, n * 16 : n * 16 + 16, :].astype(f32) for n in range(4)]
        for s in range(rows):
            rotor, p_high, p_rest, u_high = [x[s * 8 : s * 8 + 8] for x in tiles]
            u_rest = jnp.where(
                row8 < 2, pltpu.roll(rotor, 2, 0), jnp.where(row8 < 4, pltpu.roll(p_high, 4, 0), pltpu.roll(p_rest, 6, 0))
            )
            g[b, s] = rotor
            g[b, rows + s] = p_high + p_rest
            g[b, 2 * rows + s] = u_high + jnp.where(filled, u_rest, 0.0)
    spot[0:2, :] = g[left, 2 * rows, 6:8, :]
    spot[2:4, :] = g[left, 2 * rows + 1, 6:8, :]
    spot[4:6, :] = g[right, 2 * rows, 6:8, :]
    spot[6:8, :] = g[right, 2 * rows + 1, 6:8, :]
    spots = spot[...]
    columns = [
        lax.dot_general(spots, edge_pick(q, cells), (((0,), (0,)), ((), ())), preferred_element_type=f32)
        for q in range(4)
    ]

    def block(s, b):
        primal = jnp.zeros((8, TILE), f32)
        for k in range(entries):
            live = jnp.where(k < count[s, b], 1.0, 0.0).astype(f32)
            primal = primal + (weights[s, b, k : k + 1, :] * live) * g[margin[s, k, b], s]
        primal = jnp.where(filled, primal, 0.0)
        adjoint = g[b, rows + s]
        return primal, flux_of(primal, adjoint)

    def advanced(s, b, moved):
        place = lax.rem(b, own_blocks)
        before = jnp.where(place == 0, carry, 0.0).astype(f32)
        after = jnp.where(place == own_blocks - 1, carry, 0.0).astype(f32)
        low = pltpu.roll(g[wrapped(b - 1 + total, total), rows + s], 1, 1)
        high = pltpu.roll(g[wrapped(b + 1, total), rows + s], TILE - 1, 1)
        base = g[b, 2 * rows + s]
        base = base + jnp.where(lane == 0, low * before, 0.0) + jnp.where(lane == TILE - 1, high * after, 0.0)
        return base - step_size * moved

    for s in range(rows):
        base = first_block - margin[s, 0, 0] - 5 + 4 * total
        for t in range(spread):
            b = wrapped(base - 1 + t, total)
            primal, moved = block(s, b)
            flux[s, t] = moved.astype(jnp.bfloat16).astype(f32)
            if 0 < t < spread - 1:
                q_out[s, t - 1] = primal
                p_out[s, t - 1] = advanced(s, b, moved)
        own = []
        for i in range(own_blocks):
            primal, moved = block(s, first_block + i)
            own.append(moved)
            q_out[s, spread - 2 + i] = primal
            p_out[s, spread - 2 + i] = advanced(s, first_block + i, moved)
        blank = [jnp.zeros((8, TILE), f32)] * (own_blocks - 2)
        side_flux = [block(s, left)[1], block(s, right)[1]]
        pulls = [
            pull_row(lambda t: flux[s, t + 1], weights, margin, count, s, slot, first_block, base, total)
            for slot in range(-1, own_blocks + 1)
        ]

        def at_sides(low, high):
            return jnp.concatenate([pltpu.roll(low, 1, 1), *blank, pltpu.roll(high, TILE - 1, 1)], axis=1)

        pulled = step_size * jnp.concatenate(pulls[1:-1], axis=1)
        pulled_side = step_size * at_sides(pulls[0], pulls[-1])
        pushed = step_size * jnp.concatenate(own, axis=1)
        pushed_side = step_size * at_sides(*side_flux)
        for v in range(var_count):
            at = (v * rows + s) * 8
            cut = slice(at, at + layers)
            o_r[v, s] = (
                v_r[v, s] + carry * columns[0][cut] + jnp.where(layer_all == layers - 1, pulled[v : v + 1], 0.0)
            )
            o_s[v, s] = v_s[v, s] + carry * columns[1][cut] - jnp.where(layer_all == 0, pushed[v : v + 1], 0.0)
            h_r[v, s] = columns[2][cut] + jnp.where(
                edge, carry * a_r[v, s] + jnp.where(layer_all == layers - 1, pulled_side[v : v + 1], 0.0), 0.0
            )
            h_s[v, s] = columns[3][cut] + jnp.where(
                edge, carry * a_s[v, s] - jnp.where(layer_all == 0, pushed_side[v : v + 1], 0.0), 0.0
            )

    last = jnp.concatenate([spots, jnp.ones((8, TILE), f32)], axis=0).astype(jnp.bfloat16)
    odd = jnp.bitwise_and(lax.axis_index("span"), 1)
    for to, s in ((inner, (1 - odd) * (rows - 1)), (outer, odd * (rows - 1))):
        for j in range(total // 2):
            to[j] = jnp.concatenate([g[2 * j, rows + s], g[2 * j + 1, rows + s]], axis=0).astype(jnp.bfloat16)
        for v in range(var_count):
            for n, ref in enumerate((a_r, a_s, o_r, o_s)):
                held[v, n * layers : (n + 1) * layers, :] = ref[v, s]
            for i in range(own_blocks):
                to[total // 2 + v * own_blocks + i] = held[v, :, i * TILE : (i + 1) * TILE].astype(jnp.bfloat16)
        to[total // 2 + var_count * own_blocks] = last


def third_kernel(
    outer, inner, o_r, o_s, h_r, h_s, q, p, a_r, a_s, jd_r, jd_s, jo_r, jo_s, src_r, src_s, weights, margin, count,
    out_r, out_s, flux, x_r, x_s, rows_low, rows_high,
):
    var_count, rows, layers, cells = a_r.shape
    total = weights.shape[1]
    own_blocks = cells // TILE
    spread = REACH + own_blocks + 1
    first_block = lax.axis_index("circ") * own_blocks
    lane = iota((8, TILE), 1)
    layer_all = iota((layers, cells), 0)
    end = total // 2 + var_count * own_blocks
    for x in (x_r, x_s):
        x[...] = jnp.zeros(x.shape, f32)
    odd = jnp.bitwise_and(lax.axis_index("span"), 1) == 1

    def low(n):
        return jnp.where(odd, inner[n].astype(f32), outer[n].astype(f32))

    def high(n):
        return jnp.where(odd, outer[n].astype(f32), inner[n].astype(f32))

    for side, to in ((low, rows_low), (high, rows_high)):
        for v in range(var_count):
            for i in range(own_blocks):
                to[v, :, i * TILE : (i + 1) * TILE] = side(total // 2 + v * own_blocks + i)
    ends = [low(end), high(end)]
    inside = [jnp.concatenate([x[8:9]] * own_blocks, axis=1) for x in ends]
    group = lax.rem(lax.shift_right_logical(lane, 3), rows)
    corner = jnp.where(group == 0, pltpu.roll(ends[0][0:8], (TILE - 8 * (rows - 1)) % TILE, 1), 0.0)
    corner = corner + jnp.where(group == rows - 1, pltpu.roll(ends[1][0:8], 8 * (rows - 1), 1), 0.0)
    columns = [
        lax.dot_general(corner, edge_pick(n, cells), (((0,), (0,)), ((), ())), preferred_element_type=f32)
        for n in range(2)
    ]

    def halo(side, b):
        both = side(lax.shift_right_logical(b, 1))
        return jnp.where(jnp.bitwise_and(b, 1) == 1, both[8:16], both[0:8])

    extra = []
    for s in range(rows):
        base = first_block - margin[s, 0, 0] - 5 + 4 * total
        own = []
        for t in range(spread - 2 + own_blocks):
            b = wrapped(base + t, total) if t < spread - 2 else first_block + t - (spread - 2)
            adjoint = p[s, t]
            if s == 0:
                adjoint = adjoint + carry * halo(low, b)
            if s == rows - 1:
                adjoint = adjoint + carry * halo(high, b)
            moved = flux_of(q[s, t], adjoint)
            if t < spread - 2:
                flux[s, t] = moved.astype(jnp.bfloat16).astype(f32)
            else:
                own.append(moved)
        pulls = [
            pull_row(lambda t: flux[s, t], weights, margin, count, s, slot, first_block, base, total)
            for slot in range(own_blocks)
        ]
        extra.append((step_size * jnp.concatenate(pulls, axis=1), -step_size * jnp.concatenate(own, axis=1)))

    fields = (
        (o_r, h_r, a_r, jd_r, jo_r, src_r, x_r, out_r, layers - 1),
        (o_s, h_s, a_s, jd_s, jo_s, src_s, x_s, out_s, 0),
    )
    for n, (o, h, a, jd, jo, src, x, out, layer) in enumerate(fields):
        old = slice(n * layers, (n + 1) * layers)
        new = slice((2 + n) * layers, (3 + n) * layers)
        for v in range(var_count):
            for s in range(rows):
                value = o[v, s]
                if s == 0:
                    value = value + carry * rows_low[v, old, :]
                if s == rows - 1:
                    value = value + carry * rows_high[v, old, :]
                x[v * rows + s, 0:layers, :] = value
        for s in range(rows):
            state_row = [x[v * rows + s, 0:layers, :] for v in range(var_count)]
            for v in range(var_count):
                wide = x[v * rows + s]
                beside = (lanes_apart(wide) + layers_apart(wide))[0:layers]
                at = (v * rows + s) * 8
                beside = beside + h[v, s] + carry * columns[n][at : at + layers]
                if s > 0:
                    beside = beside + x[v * rows + s - 1, 0:layers, :]
                else:
                    beside = beside + inside[0] * (rows_low[v, new, :] + carry * a[v, 0])
                if s < rows - 1:
                    beside = beside + x[v * rows + s + 1, 0:layers, :]
                else:
                    beside = beside + inside[1] * (rows_high[v, new, :] + carry * a[v, rows - 1])
                res = jacobian_row(jd, jo, state_row, v, s, var_count) - coupling * beside - src[v, s]
                out[v, s] = (
                    state_row[v] - step_size * res + jnp.where(layer_all == layer, extra[s][n][v : v + 1], 0.0)
                )


def per_device(
    adjoint_rotor,
    adjoint_stator,
    jac_diag_rotor,
    jac_diag_stator,
    jac_off_rotor,
    jac_off_stator,
    source_rotor,
    source_stator,
    rotor_state,
    margin_block,
    face_count,
    margin_weight,
):
    var_count, rows, layers, cells = adjoint_rotor.shape
    own_blocks = cells // TILE
    total = margin_block.shape[1]
    spread = REACH + own_blocks + 1
    field = jax.ShapeDtypeStruct(adjoint_rotor.shape, f32)
    vmem = pl.BlockSpec(memory_space=pltpu.VMEM)
    smem = pl.BlockSpec(memory_space=pltpu.SMEM)
    padded = pltpu.VMEM((TILE // 8, 8, cells), f32)

    margin = jnp.swapaxes(margin_block, 1, 2)
    arguments = (
        adjoint_rotor, adjoint_stator, jac_diag_rotor, jac_diag_stator, jac_off_rotor, jac_off_stator,
        source_rotor, source_stator, rotor_state, margin, face_count, margin_weight,
    )
    shapes = [jax.ShapeDtypeStruct(x.shape, x.dtype) for x in arguments]
    v_r, v_s, share, a_r, a_s, weights, margin, count = pl.pallas_call(
        first_kernel,
        out_shape=(
            field, field, jax.ShapeDtypeStruct((own_blocks, 64, TILE), jnp.bfloat16),
            shapes[0], shapes[1], shapes[11], shapes[9], shapes[10],
        ),
        in_specs=[pl.BlockSpec(memory_space=pltpu.HBM)] * 12,
        out_specs=(vmem,) * 8,
        scratch_shapes=[pltpu.VMEM(x.shape, x.dtype) for x in shapes[2:9]]
        + [padded] * 4
        + [pltpu.SemaphoreType.DMA((12,)), pltpu.VMEM((own_blocks, 3 * rows, 8, TILE), f32)],
        compiler_params=params,
        name="local_part",
    )(*[pltpu.with_memory_space_constraint(x, pltpu.HBM) for x in arguments])
    members = lax.axis_size("circ")
    mine, masks = share, []
    mask = members // 2
    while mask > 0:
        other = lax.ppermute(mine, "circ", [(i, i ^ mask) for i in range(members)])
        if mask > 1:
            mine = jnp.concatenate([mine, other], axis=0)
            masks.append(mask)
        mask //= 2
    tiles = jax.ShapeDtypeStruct((total // 2 + var_count * own_blocks + 1, 16, TILE), jnp.bfloat16)
    listed = jax.ShapeDtypeStruct((rows, spread - 2 + own_blocks, 8, TILE), f32)
    o_r, o_s, h_r, h_s, q, p, outer, inner = pl.pallas_call(
        functools.partial(second_kernel, masks),
        out_shape=(field, field, field, field, listed, listed, tiles, tiles),
        in_specs=[vmem] * 7 + [smem] * 2,
        out_specs=(vmem,) * 8,
        scratch_shapes=[
            pltpu.VMEM((rows, spread, 8, TILE), f32),
            pltpu.VMEM((var_count, 4 * layers, cells), f32),
            pltpu.VMEM((8, TILE), f32),
            pltpu.VMEM((total, 3 * rows, 8, TILE), f32),
        ],
        compiler_params=params,
        name="interface_part",
    )(mine, other, v_r, v_s, a_r, a_s, weights, margin, count)
    bands = lax.axis_size("span")
    near = [(i, i ^ 1) for i in range(bands)]
    far = [pair for i in range(1, bands - 1, 2) for pair in ((i, i + 1), (i + 1, i))]
    outer = lax.ppermute(outer, "span", far)
    inner = lax.ppermute(inner, "span", near)
    out_r, out_s = pl.pallas_call(
        third_kernel,
        out_shape=(field, field),
        in_specs=[vmem] * 17 + [smem] * 2,
        out_specs=(vmem,) * 2,
        scratch_shapes=[
            pltpu.VMEM((rows, spread - 2, 8, TILE), f32),
            padded,
            padded,
            pltpu.VMEM((var_count, 4 * layers, cells), f32),
            pltpu.VMEM((var_count, 4 * layers, cells), f32),
        ],
        compiler_params=params,
        name="final_part",
    )(
        outer, inner, o_r, o_s, h_r, h_s, q, p, a_r, a_s, jac_diag_rotor, jac_diag_stator,
        jac_off_rotor, jac_off_stator, source_rotor, source_stator, weights, margin, count,
    )
    return (out_r, out_s)


def solution(mesh):
    field = P(None, "span", None, "circ")
    placed = (
        (field,) * 4
        + (P(None, None, "span", None, "circ"),) * 2
        + (field,) * 2
        + (P(None, "span", "circ"), P("span", None, None), P("span", None), P("span", None, None, None))
    )
    return jax.shard_map(
        per_device, mesh=mesh, in_specs=placed, out_specs=(field, field), check_vma=False
    )
```

```python
import functools

import jax
import jax.numpy as jnp
from jax import lax
from jax.experimental import pallas as pl
from jax.experimental.pallas import tpu as pltpu
from jax.sharding import PartitionSpec as P

step_size = 0.1
coupling = 0.2
carry = step_size * coupling
REACH = 8
TILE = 128
f32 = jnp.float32
params = pltpu.CompilerParams(vmem_limit_bytes=24 * 1024 * 1024)


def iota(shape, dim):
    return lax.broadcasted_iota(jnp.int32, shape, dim)


def wrapped(x, count):
    if count & (count - 1) == 0:
        return jnp.bitwise_and(x, count - 1)
    return lax.rem(x + 4 * count, count)


def lanes_apart(x):
    cells = x.shape[1]
    lane = iota(x.shape, 1)
    before = jnp.where(lane == 0, 0.0, pltpu.roll(x, 1, 1))
    after = jnp.where(lane == cells - 1, 0.0, pltpu.roll(x, cells - 1, 1))
    return before + after


def layers_apart(x):
    return pltpu.roll(x, 1, 0) + pltpu.roll(x, 7, 0)


def edge_pick(row, cells):
    at = iota((8, cells), 0)
    lane = iota((8, cells), 1)
    first = jnp.logical_and(at == row, lane == 0)
    last = jnp.logical_and(at == 4 + row, lane == cells - 1)
    return jnp.where(jnp.logical_or(first, last), 1.0, 0.0).astype(f32)


def split(x):
    high = x.astype(jnp.bfloat16).astype(f32)
    return high, x - high


def flux_of(primal, adjoint):
    speeds = jnp.sqrt(1.0 + primal * primal)
    over = jnp.sum(primal * adjoint, axis=0, keepdims=True)
    under = 6.0 + jnp.sum(primal * primal, axis=0, keepdims=True)
    return speeds * adjoint + 0.5 * primal * (over / under)


def jacobian_row(diag, off, state, v, s, var_count):
    total = diag[v, s] * state[v]
    for w in range(var_count):
        total = total + off[w, v, s].astype(f32) * state[w]
    return total


def pull_row(flux, weights, margin, count, s, slot, first_block, base, total):
    target = wrapped(first_block + slot + total, total)
    acc = jnp.zeros((8, TILE), f32)
    for e in range(REACH):
        b = wrapped(base + slot + e, total)
        k = wrapped(target - margin[s, 0, b] + total, total)
        live = jnp.where(k < count[s, b], 1.0, 0.0).astype(f32)
        kept = jnp.minimum(k, weights.shape[2] - 1)
        acc = acc + (weights[s, b, pl.ds(kept, 1), :] * live) * flux(slot + e)
    return acc


def first_kernel(*refs):
    outer, refs = refs[:12], refs[12:]
    v_r, v_s, out, a_r, a_s, weights, margin, count = refs[:8]
    jd_r, jd_s, jo_r, jo_s, src_r, src_s, state = refs[8:15]
    xs, sems, wide_out = refs[15:19], refs[19], refs[20]
    var_count, rows, layers, cells = a_r.shape
    own_blocks = cells // TILE
    inner = (a_r, a_s, jd_r, jd_s, jo_r, jo_s, src_r, src_s, state, margin, count, weights)
    copies = [pltpu.make_async_copy(x, y, sems.at[n]) for n, (x, y) in enumerate(zip(outer, inner))]
    for copy in copies:
        copy.start()
    wide_out[...] = jnp.zeros(wide_out.shape, f32)
    for x in xs:
        x[...] = jnp.zeros(x.shape, f32)
    for copy in copies:
        copy.wait()
    fields = ((a_r, jd_r, jo_r, src_r, v_r, xs[0], xs[2]), (a_s, jd_s, jo_s, src_s, v_s, xs[1], xs[3]))
    for a, jd, jo, src, partial, x_a, x_p in fields:
        for v in range(var_count):
            for s in range(rows):
                x_a[v * rows + s, 0:layers, :] = a[v, s]
        for s in range(rows):
            state_row = [a[v, s] for v in range(var_count)]
            for v in range(var_count):
                wide = x_a[v * rows + s]
                beside = (lanes_apart(wide) + layers_apart(wide))[0:layers]
                if s > 0:
                    beside = beside + a[v, s - 1]
                if s < rows - 1:
                    beside = beside + a[v, s + 1]
                res = jacobian_row(jd, jo, state_row, v, s, var_count) - coupling * beside - src[v, s]
                new = state_row[v] - step_size * res
                partial[v, s] = new
                x_p[v * rows + s, 0:layers, :] = new
    edges = jnp.zeros((8, TILE), f32)
    for q in range(4):
        flat = xs[q][...].reshape(TILE, cells)
        edges = edges + lax.dot_general(
            edge_pick(q, cells), flat, (((1,), (1,)), ((), ())), preferred_element_type=f32
        )
    for v in range(var_count):
        rotor = state[v].astype(f32)
        for s in range(rows):
            for i in range(own_blocks):
                cut = slice(i * TILE, (i + 1) * TILE)
                wide_out[i, s, v : v + 1, :] = rotor[s : s + 1, cut]
                wide_out[i, rows + s, v : v + 1, :] = a_s[v, s, 0:1, cut]
                wide_out[i, 2 * rows + s, v : v + 1, :] = v_s[v, s, 0:1, cut]
    row8 = iota((8, TILE), 0)
    filled = row8 < var_count
    for i in range(own_blocks):
        if i in (0, own_blocks - 1):
            side = 4 if i else 0
            for s in range(rows):
                wide_out[i, 2 * rows + s, 6:8, :] = edges[side + 2 * s : side + 2 * s + 2]
        groups = []
        for s in range(rows):
            p_high, p_rest = split(wide_out[i, rows + s])
            u_high, u_rest = split(wide_out[i, 2 * rows + s])
            groups.append((
                jnp.where(filled, wide_out[i, s], pltpu.roll(u_rest, 6, 0)),
                jnp.where(filled, p_high, pltpu.roll(u_rest, 4, 0)),
                jnp.where(filled, p_rest, pltpu.roll(u_rest, 2, 0)),
                u_high,
            ))
        for n in range(4):
            out[i, n * 16 : n * 16 + 16, :] = jnp.concatenate([x[n] for x in groups], axis=0).astype(jnp.bfloat16)


def early_kernel(a_r, a_s, v_r, v_s, outer, inner, held):
    var_count, rows, layers, cells = a_r.shape
    own_blocks = cells // TILE
    odd = jnp.bitwise_and(lax.axis_index("span"), 1)
    for to, s in ((outer, odd * (rows - 1)), (inner, (1 - odd) * (rows - 1))):
        for v in range(var_count):
            for n, ref in enumerate((a_r, a_s, v_r, v_s)):
                held[v, n * layers : (n + 1) * layers, :] = ref[v, s]
            for i in range(own_blocks):
                to[v * own_blocks + i] = held[v, :, i * TILE : (i + 1) * TILE].astype(jnp.bfloat16)


def second_kernel(
    var_count, masks, mine, other, weights, margin, count,
    q_out, p_out, pulls_out, moved_out, spot, outer, inner, flux, g,
):
    rows, total, entries, _ = weights.shape
    own_blocks = pulls_out.shape[1] - 2
    spread = REACH + own_blocks + 1
    here = lax.axis_index("circ")
    first_block = here * own_blocks
    row8 = iota((8, TILE), 0)
    lane = iota((8, TILE), 1)
    left = wrapped(first_block - 1 + total, total)
    right = wrapped(first_block + own_blocks, total)

    filled = row8 < var_count
    for at in range(total):
        half, part = divmod(at, total // 2)
        place, i = divmod(part, own_blocks)
        mask = half + sum(m for n, m in enumerate(masks) if place >> n & 1)
        b = jnp.bitwise_xor(here, mask) * own_blocks + i
        whole = other if half else mine
        tiles = [whole[part, n * 16 : n * 16 + 16, :].astype(f32) for n in range(4)]
        for s in range(rows):
            rotor, p_high, p_rest, u_high = [x[s * 8 : s * 8 + 8] for x in tiles]
            u_rest = jnp.where(
                row8 < 2, pltpu.roll(rotor, 2, 0), jnp.where(row8 < 4, pltpu.roll(p_high, 4, 0), pltpu.roll(p_rest, 6, 0))
            )
            g[b, s] = rotor
            g[b, rows + s] = p_high + p_rest
            g[b, 2 * rows + s] = u_high + jnp.where(filled, u_rest, 0.0)
    spot[0:2, :] = g[left, 2 * rows, 6:8, :]
    spot[2:4, :] = g[left, 2 * rows + 1, 6:8, :]
    spot[4:6, :] = g[right, 2 * rows, 6:8, :]
    spot[6:8, :] = g[right, 2 * rows + 1, 6:8, :]

    def block(s, b):
        primal = jnp.zeros((8, TILE), f32)
        for k in range(entries):
            live = jnp.where(k < count[s, b], 1.0, 0.0).astype(f32)
            primal = primal + (weights[s, b, k : k + 1, :] * live) * g[margin[s, k, b], s]
        primal = jnp.where(filled, primal, 0.0)
        adjoint = g[b, rows + s]
        return primal, flux_of(primal, adjoint)

    def advanced(s, b, moved):
        place = lax.rem(b, own_blocks)
        before = jnp.where(place == 0, carry, 0.0).astype(f32)
        after = jnp.where(place == own_blocks - 1, carry, 0.0).astype(f32)
        low = pltpu.roll(g[wrapped(b - 1 + total, total), rows + s], 1, 1)
        high = pltpu.roll(g[wrapped(b + 1, total), rows + s], TILE - 1, 1)
        base = g[b, 2 * rows + s]
        base = base + jnp.where(lane == 0, low * before, 0.0) + jnp.where(lane == TILE - 1, high * after, 0.0)
        return base - step_size * moved

    for s in range(rows):
        base = first_block - margin[s, 0, 0] - 5 + 4 * total
        for t in range(spread):
            b = wrapped(base - 1 + t, total)
            primal, moved = block(s, b)
            flux[s, t] = moved.astype(jnp.bfloat16).astype(f32)
            if 0 < t < spread - 1:
                q_out[s, t - 1] = primal
                p_out[s, t - 1] = advanced(s, b, moved)
        for i in range(own_blocks):
            primal, moved = block(s, first_block + i)
            moved_out[s, 1 + i] = moved
            q_out[s, spread - 2 + i] = primal
            p_out[s, spread - 2 + i] = advanced(s, first_block + i, moved)
        moved_out[s, 0] = block(s, left)[1]
        moved_out[s, own_blocks + 1] = block(s, right)[1]
        for slot in range(-1, own_blocks + 1):
            pulls_out[s, slot + 1] = pull_row(
                lambda t: flux[s, t + 1], weights, margin, count, s, slot, first_block, base, total
            )

    odd = jnp.bitwise_and(lax.axis_index("span"), 1)
    last = jnp.concatenate([spot[...], jnp.zeros((8, TILE), f32)], axis=0).astype(jnp.bfloat16)
    for to, s in ((outer, odd * (rows - 1)), (inner, (1 - odd) * (rows - 1))):
        for j in range(total // 2):
            to[j] = jnp.concatenate([g[2 * j, rows + s], g[2 * j + 1, rows + s]], axis=0).astype(jnp.bfloat16)
        for i in range(own_blocks):
            pair = jnp.concatenate([pulls_out[s, 1 + i], moved_out[s, 1 + i]], axis=0)
            to[total // 2 + i] = pair.astype(jnp.bfloat16)
        to[total // 2 + own_blocks] = last


def third_kernel(
    bands, outer, inner, v_r, v_s, a_r, a_s, pulls, moved, spot, jd_r, jd_s, jo_r, jo_s, src_r, src_s,
    part_r, part_s, x_r, x_s, rows_low, rows_high,
):
    var_count, rows, layers, cells = a_r.shape
    own_blocks = cells // TILE
    band = lax.axis_index("span")
    odd = jnp.bitwise_and(band, 1) == 1
    lane_all = iota((layers, cells), 1)
    layer_all = iota((layers, cells), 0)
    edge = jnp.logical_or(lane_all == 0, lane_all == cells - 1)
    for x in (x_r, x_s):
        x[...] = jnp.zeros(x.shape, f32)
    for v in range(var_count):
        for i in range(own_blocks):
            one = outer[v * own_blocks + i].astype(f32)
            two = inner[v * own_blocks + i].astype(f32)
            rows_low[v, :, i * TILE : (i + 1) * TILE] = jnp.where(odd, two, one)
            rows_high[v, :, i * TILE : (i + 1) * TILE] = jnp.where(odd, one, two)
    inside = (jnp.where(band > 0, 1.0, 0.0).astype(f32), jnp.where(band < bands - 1, 1.0, 0.0).astype(f32))
    spots = spot[...]
    columns = [
        lax.dot_general(spots, edge_pick(q, cells), (((0,), (0,)), ((), ())), preferred_element_type=f32)
        for q in range(4)
    ]
    blank = [jnp.zeros((8, TILE), f32)] * (own_blocks - 2)

    def middle(ref, s):
        return jnp.concatenate([ref[s, 1 + i] for i in range(own_blocks)], axis=1)

    def sides(ref, s):
        low = pltpu.roll(ref[s, 0], 1, 1)
        high = pltpu.roll(ref[s, own_blocks + 1], TILE - 1, 1)
        return jnp.concatenate([low, *blank, high], axis=1)

    fields = (
        (0, v_r, a_r, jd_r, jo_r, src_r, x_r, part_r, layers - 1, pulls, step_size),
        (1, v_s, a_s, jd_s, jo_s, src_s, x_s, part_s, 0, moved, -step_size),
    )
    for n, local, a, jd, jo, src, x, part, layer, source, factor in fields:
        old = slice(n * layers, (n + 1) * layers)
        new = slice((2 + n) * layers, (3 + n) * layers)
        centre = [factor * middle(source, s) for s in range(rows)]
        beyond = [factor * sides(source, s) for s in range(rows)]
        for v in range(var_count):
            for s in range(rows):
                at = (v * rows + s) * 8
                value = local[v, s] + carry * columns[n][at : at + layers]
                value = value + jnp.where(layer_all == layer, centre[s][v : v + 1], 0.0)
                if s == 0:
                    value = value + carry * rows_low[v, old, :]
                if s == rows - 1:
                    value = value + carry * rows_high[v, old, :]
                x[v * rows + s, 0:layers, :] = value
        for s in range(rows):
            state_row = [x[v * rows + s, 0:layers, :] for v in range(var_count)]
            for v in range(var_count):
                wide = x[v * rows + s]
                at = (v * rows + s) * 8
                beside = (lanes_apart(wide) + layers_apart(wide))[0:layers]
                beside = beside + columns[2 + n][at : at + layers] + jnp.where(
                    edge, carry * a[v, s] + jnp.where(layer_all == layer, beyond[s][v : v + 1], 0.0), 0.0
                )
                if s > 0:
                    beside = beside + x[v * rows + s - 1, 0:layers, :]
                else:
                    beside = beside + inside[0] * (rows_low[v, new, :] + carry * a[v, 0])
                if s < rows - 1:
                    beside = beside + x[v * rows + s + 1, 0:layers, :]
                else:
                    beside = beside + inside[1] * (rows_high[v, new, :] + carry * a[v, rows - 1])
                res = jacobian_row(jd, jo, state_row, v, s, var_count) - coupling * beside - src[v, s]
                part[v, s] = state_row[v] - step_size * res


def fourth_kernel(outer, inner, q, p, part_r, part_s, weights, margin, count, out_r, out_s, flux):
    var_count, rows, layers, cells = part_r.shape
    total = weights.shape[1]
    own_blocks = cells // TILE
    spread = REACH + own_blocks + 1
    first_block = lax.axis_index("circ") * own_blocks
    lane = iota((8, TILE), 1)
    layer_all = iota((layers, cells), 0)
    end = total // 2 + own_blocks
    odd = jnp.bitwise_and(lax.axis_index("span"), 1) == 1

    def low(n):
        return jnp.where(odd, inner[n].astype(f32), outer[n].astype(f32))

    def high(n):
        return jnp.where(odd, outer[n].astype(f32), inner[n].astype(f32))

    group = lax.rem(lax.shift_right_logical(lane, 3), rows)
    corner = jnp.where(group == 0, pltpu.roll(low(end)[0:8], (TILE - 8 * (rows - 1)) % TILE, 1), 0.0)
    corner = corner + jnp.where(group == rows - 1, pltpu.roll(high(end)[0:8], 8 * (rows - 1), 1), 0.0)
    columns = [
        lax.dot_general(corner, edge_pick(n, cells), (((0,), (0,)), ((), ())), preferred_element_type=f32)
        for n in range(2)
    ]
    beside = []
    for side in (low, high):
        pairs = [side(total // 2 + i) for i in range(own_blocks)]
        beside.append([
            (carry * step_size) * jnp.concatenate([x[0:8] for x in pairs], axis=1),
            -(carry * step_size) * jnp.concatenate([x[8:16] for x in pairs], axis=1),
        ])

    def halo(side, b):
        both = side(lax.shift_right_logical(b, 1))
        return jnp.where(jnp.bitwise_and(b, 1) == 1, both[8:16], both[0:8])

    for s in range(rows):
        base = first_block - margin[s, 0, 0] - 5 + 4 * total
        own = []
        for t in range(spread - 2 + own_blocks):
            b = wrapped(base + t, total) if t < spread - 2 else first_block + t - (spread - 2)
            adjoint = p[s, t]
            if s == 0:
                adjoint = adjoint + carry * halo(low, b)
            if s == rows - 1:
                adjoint = adjoint + carry * halo(high, b)
            moved = flux_of(q[s, t], adjoint)
            if t < spread - 2:
                flux[s, t] = moved.astype(jnp.bfloat16).astype(f32)
            else:
                own.append(moved)
        pulls = [
            pull_row(lambda t: flux[s, t], weights, margin, count, s, slot, first_block, base, total)
            for slot in range(own_blocks)
        ]
        extra = [step_size * jnp.concatenate(pulls, axis=1), -step_size * jnp.concatenate(own, axis=1)]
        for n, (part, out, layer) in enumerate(((part_r, out_r, layers - 1), (part_s, out_s, 0))):
            more = extra[n]
            edges = 0
            if s == 0:
                more = more + beside[0][n]
                edges = edges + 1
            if s == rows - 1:
                more = more + beside[1][n]
                edges = edges + 1
            for v in range(var_count):
                at = (v * rows + s) * 8
                value = part[v, s] + jnp.where(layer_all == layer, more[v : v + 1], 0.0)
                if edges:
                    value = value + (2.0 * carry * carry) * columns[n][at : at + layers]
                out[v, s] = value


def per_device(
    adjoint_rotor,
    adjoint_stator,
    jac_diag_rotor,
    jac_diag_stator,
    jac_off_rotor,
    jac_off_stator,
    source_rotor,
    source_stator,
    rotor_state,
    margin_block,
    face_count,
    margin_weight,
):
    var_count, rows, layers, cells = adjoint_rotor.shape
    own_blocks = cells // TILE
    total = margin_block.shape[1]
    spread = REACH + own_blocks + 1
    field = jax.ShapeDtypeStruct(adjoint_rotor.shape, f32)
    vmem = pl.BlockSpec(memory_space=pltpu.VMEM)
    smem = pl.BlockSpec(memory_space=pltpu.SMEM)
    padded = pltpu.VMEM((TILE // 8, 8, cells), f32)

    margin = jnp.swapaxes(margin_block, 1, 2)
    arguments = (
        adjoint_rotor, adjoint_stator, jac_diag_rotor, jac_diag_stator, jac_off_rotor, jac_off_stator,
        source_rotor, source_stator, rotor_state, margin, face_count, margin_weight,
    )
    shapes = [jax.ShapeDtypeStruct(x.shape, x.dtype) for x in arguments]
    v_r, v_s, share, a_r, a_s, weights, margin, count = pl.pallas_call(
        first_kernel,
        out_shape=(
            field, field, jax.ShapeDtypeStruct((own_blocks, 64, TILE), jnp.bfloat16),
            shapes[0], shapes[1], shapes[11], shapes[9], shapes[10],
        ),
        in_specs=[pl.BlockSpec(memory_space=pltpu.HBM)] * 12,
        out_specs=(vmem,) * 8,
        scratch_shapes=[pltpu.VMEM(x.shape, x.dtype) for x in shapes[2:9]]
        + [padded] * 4
        + [pltpu.SemaphoreType.DMA((12,)), pltpu.VMEM((own_blocks, 3 * rows, 8, TILE), f32)],
        compiler_params=params,
        name="local_part",
    )(*[pltpu.with_memory_space_constraint(x, pltpu.HBM) for x in arguments])
    held = pltpu.VMEM((var_count, 4 * layers, cells), f32)
    bands = lax.axis_size("span")
    near = [(i, i ^ 1) for i in range(bands)]
    far = [pair for i in range(1, bands - 1, 2) for pair in ((i, i + 1), (i + 1, i))]
    members = lax.axis_size("circ")
    mine, masks = share, []
    mask = members // 2
    while mask > 0:
        other = lax.ppermute(mine, "circ", [(i, i ^ mask) for i in range(members)])
        if mask == members // 2:
            early = jax.ShapeDtypeStruct((var_count * own_blocks, 16, TILE), jnp.bfloat16)
            early_outer, early_inner = pl.pallas_call(
                early_kernel,
                out_shape=(early, early),
                in_specs=[vmem] * 4,
                out_specs=(vmem,) * 2,
                scratch_shapes=[held],
                compiler_params=params,
                name="early_rows",
            )(a_r, a_s, v_r, v_s)
            early_outer = lax.ppermute(early_outer, "span", far)
            early_inner = lax.ppermute(early_inner, "span", near)
        if mask > 1:
            mine = jnp.concatenate([mine, other], axis=0)
            masks.append(mask)
        mask //= 2
    tiles = jax.ShapeDtypeStruct((total // 2 + own_blocks + 1, 16, TILE), jnp.bfloat16)
    listed = jax.ShapeDtypeStruct((rows, spread - 2 + own_blocks, 8, TILE), f32)
    around = jax.ShapeDtypeStruct((rows, own_blocks + 2, 8, TILE), f32)
    q, p, pulls, moved, spot, outer, inner = pl.pallas_call(
        functools.partial(second_kernel, var_count, masks),
        out_shape=(listed, listed, around, around, jax.ShapeDtypeStruct((8, TILE), f32), tiles, tiles),
        in_specs=[vmem] * 3 + [smem] * 2,
        out_specs=(vmem,) * 7,
        scratch_shapes=[
            pltpu.VMEM((rows, spread, 8, TILE), f32),
            pltpu.VMEM((total, 3 * rows, 8, TILE), f32),
        ],
        compiler_params=params,
        name="interface_part",
    )(mine, other, weights, margin, count)
    outer = lax.ppermute(outer, "span", far)
    inner = lax.ppermute(inner, "span", near)
    part_r, part_s = pl.pallas_call(
        functools.partial(third_kernel, bands),
        out_shape=(field, field),
        in_specs=[vmem] * 15,
        out_specs=(vmem,) * 2,
        scratch_shapes=[padded, padded, held, held],
        compiler_params=params,
        name="own_part",
    )(
        early_outer, early_inner, v_r, v_s, a_r, a_s, pulls, moved, spot, jac_diag_rotor, jac_diag_stator,
        jac_off_rotor, jac_off_stator, source_rotor, source_stator,
    )
    out_r, out_s = pl.pallas_call(
        fourth_kernel,
        out_shape=(field, field),
        in_specs=[vmem] * 7 + [smem] * 2,
        out_specs=(vmem,) * 2,
        scratch_shapes=[pltpu.VMEM((rows, spread - 2, 8, TILE), f32)],
        compiler_params=params,
        name="final_part",
    )(outer, inner, q, p, part_r, part_s, weights, margin, count)
    return (out_r, out_s)


def solution(mesh):
    field = P(None, "span", None, "circ")
    placed = (
        (field,) * 4
        + (P(None, None, "span", None, "circ"),) * 2
        + (field,) * 2
        + (P(None, "span", "circ"), P("span", None, None), P("span", None), P("span", None, None, None))
    )
    return jax.shard_map(
        per_device, mesh=mesh, in_specs=placed, out_specs=(field, field), check_vma=False
    )
```

```python
import functools

import jax
import jax.numpy as jnp
from jax import lax
from jax.experimental import pallas as pl
from jax.experimental.pallas import tpu as pltpu
from jax.sharding import PartitionSpec as P

step_size = 0.1
coupling = 0.2
carry = step_size * coupling
REACH = 8
TILE = 128
f32 = jnp.float32
params = pltpu.CompilerParams(vmem_limit_bytes=24 * 1024 * 1024)


def iota(shape, dim):
    return lax.broadcasted_iota(jnp.int32, shape, dim)


def wrapped(x, count):
    if count & (count - 1) == 0:
        return jnp.bitwise_and(x, count - 1)
    return lax.rem(x + 4 * count, count)


def lanes_apart(x):
    cells = x.shape[1]
    lane = iota(x.shape, 1)
    before = jnp.where(lane == 0, 0.0, pltpu.roll(x, 1, 1))
    after = jnp.where(lane == cells - 1, 0.0, pltpu.roll(x, cells - 1, 1))
    return before + after


def layers_apart(x):
    return pltpu.roll(x, 1, 0) + pltpu.roll(x, 7, 0)


def edge_pick(row, cells):
    at = iota((8, cells), 0)
    lane = iota((8, cells), 1)
    first = jnp.logical_and(at == row, lane == 0)
    last = jnp.logical_and(at == 4 + row, lane == cells - 1)
    return jnp.where(jnp.logical_or(first, last), 1.0, 0.0).astype(f32)


def split(x):
    high = x.astype(jnp.bfloat16).astype(f32)
    return high, x - high


def flux_of(primal, adjoint):
    speeds = jnp.sqrt(1.0 + primal * primal)
    over = jnp.sum(primal * adjoint, axis=0, keepdims=True)
    under = 6.0 + jnp.sum(primal * primal, axis=0, keepdims=True)
    return speeds * adjoint + 0.5 * primal * (over / under)


def jacobian_row(diag, off, state, v, s, var_count):
    total = diag[v, s] * state[v]
    for w in range(var_count):
        total = total + off[w, v, s].astype(f32) * state[w]
    return total


def pull_row(flux, weights, margin, count, s, slot, first_block, base, total):
    target = wrapped(first_block + slot + total, total)
    acc = jnp.zeros((8, TILE), f32)
    for e in range(REACH):
        b = wrapped(base + slot + e, total)
        k = wrapped(target - margin[s, 0, b] + total, total)
        live = jnp.where(k < count[s, b], 1.0, 0.0).astype(f32)
        kept = jnp.minimum(k, weights.shape[2] - 1)
        acc = acc + (weights[s, b, pl.ds(kept, 1), :] * live) * flux(slot + e)
    return acc


def first_kernel(*refs):
    outer, refs = refs[:12], refs[12:]
    v_r, v_s, out, a_r, a_s, weights, margin, count = refs[:8]
    jd_r, jd_s, jo_r, jo_s, src_r, src_s, state = refs[8:15]
    xs, sems, wide_out = refs[15:19], refs[19], refs[20]
    var_count, rows, layers, cells = a_r.shape
    own_blocks = cells // TILE
    inner = (a_r, a_s, jd_r, jd_s, jo_r, jo_s, src_r, src_s, state, margin, count, weights)
    copies = [pltpu.make_async_copy(x, y, sems.at[n]) for n, (x, y) in enumerate(zip(outer, inner))]
    for copy in copies:
        copy.start()
    wide_out[...] = jnp.zeros(wide_out.shape, f32)
    for x in xs:
        x[...] = jnp.zeros(x.shape, f32)
    for copy in copies:
        copy.wait()
    fields = ((a_r, jd_r, jo_r, src_r, v_r, xs[0], xs[2]), (a_s, jd_s, jo_s, src_s, v_s, xs[1], xs[3]))
    for a, jd, jo, src, partial, x_a, x_p in fields:
        for v in range(var_count):
            for s in range(rows):
                x_a[v * rows + s, 0:layers, :] = a[v, s]
        for s in range(rows):
            state_row = [a[v, s] for v in range(var_count)]
            for v in range(var_count):
                wide = x_a[v * rows + s]
                beside = (lanes_apart(wide) + layers_apart(wide))[0:layers]
                if s > 0:
                    beside = beside + a[v, s - 1]
                if s < rows - 1:
                    beside = beside + a[v, s + 1]
                res = jacobian_row(jd, jo, state_row, v, s, var_count) - coupling * beside - src[v, s]
                new = state_row[v] - step_size * res
                partial[v, s] = new
                x_p[v * rows + s, 0:layers, :] = new
    edges = jnp.zeros((8, TILE), f32)
    for q in range(4):
        flat = xs[q][...].reshape(TILE, cells)
        edges = edges + lax.dot_general(
            edge_pick(q, cells), flat, (((1,), (1,)), ((), ())), preferred_element_type=f32
        )
    for v in range(var_count):
        rotor = state[v].astype(f32)
        for s in range(rows):
            for i in range(own_blocks):
                cut = slice(i * TILE, (i + 1) * TILE)
                wide_out[i, s, v : v + 1, :] = rotor[s : s + 1, cut]
                wide_out[i, rows + s, v : v + 1, :] = a_s[v, s, 0:1, cut]
                wide_out[i, 2 * rows + s, v : v + 1, :] = v_s[v, s, 0:1, cut]
    row8 = iota((8, TILE), 0)
    filled = row8 < var_count
    for i in range(own_blocks):
        if i in (0, own_blocks - 1):
            side = 4 if i else 0
            for s in range(rows):
                wide_out[i, 2 * rows + s, 6:8, :] = edges[side + 2 * s : side + 2 * s + 2]
        groups = []
        for s in range(rows):
            p_high, p_rest = split(wide_out[i, rows + s])
            u_high, u_rest = split(wide_out[i, 2 * rows + s])
            groups.append((
                jnp.where(filled, wide_out[i, s], pltpu.roll(u_rest, 6, 0)),
                jnp.where(filled, p_high, pltpu.roll(u_rest, 4, 0)),
                jnp.where(filled, p_rest, pltpu.roll(u_rest, 2, 0)),
                u_high,
            ))
        for n in range(4):
            out[i, n * 16 : n * 16 + 16, :] = jnp.concatenate([x[n] for x in groups], axis=0).astype(jnp.bfloat16)


def second_kernel(masks, *refs):
    pieces, refs = refs[: len(masks)], refs[len(masks) :]
    v_r, v_s, a_r, a_s, weights, margin, count = refs[:7]
    o_r, o_s, h_r, h_s, q_out, p_out, outer, inner, flux, held, spot, g = refs[7:]
    var_count, rows, layers, cells = a_r.shape
    total = weights.shape[1]
    own_blocks = cells // TILE
    entries = weights.shape[2]
    spread = REACH + own_blocks + 1
    first_block = lax.axis_index("circ") * own_blocks
    row8 = iota((8, TILE), 0)
    lane = iota((8, TILE), 1)
    lane_all = iota((layers, cells), 1)
    layer_all = iota((layers, cells), 0)
    edge = jnp.logical_or(lane_all == 0, lane_all == cells - 1)
    left = wrapped(first_block - 1 + total, total)
    right = wrapped(first_block + own_blocks, total)

    filled = row8 < var_count
    here = lax.axis_index("circ")
    shares = [
        (piece, n * own_blocks + i, mask, i)
        for piece, listed in zip(pieces, masks)
        for n, mask in enumerate(listed)
        for i in range(own_blocks)
    ]
    for piece, at, mask, i in shares:
        b = jnp.bitwise_xor(here, mask) * own_blocks + i
        tiles = [piece[at, n * 16 : n * 16 + 16, :].astype(f32) for n in range(4)]
        for s in range(rows):
            rotor, p_high, p_rest, u_high = [x[s * 8 : s * 8 + 8] for x in tiles]
            u_rest = jnp.where(
                row8 < 2, pltpu.roll(rotor, 2, 0), jnp.where(row8 < 4, pltpu.roll(p_high, 4, 0), pltpu.roll(p_rest, 6, 0))
            )
            g[b, s] = rotor
            g[b, rows + s] = p_high + p_rest
            g[b, 2 * rows + s] = u_high + jnp.where(filled, u_rest, 0.0)
    spot[0:2, :] = g[left, 2 * rows, 6:8, :]
    spot[2:4, :] = g[left, 2 * rows + 1, 6:8, :]
    spot[4:6, :] = g[right, 2 * rows, 6:8, :]
    spot[6:8, :] = g[right, 2 * rows + 1, 6:8, :]
    spots = spot[...]
    columns = [
        lax.dot_general(spots, edge_pick(q, cells), (((0,), (0,)), ((), ())), preferred_element_type=f32)
        for q in range(4)
    ]

    def block(s, b):
        primal = jnp.zeros((8, TILE), f32)
        for k in range(entries):
            live = jnp.where(k < count[s, b], 1.0, 0.0).astype(f32)
            primal = primal + (weights[s, b, k : k + 1, :] * live) * g[margin[s, k, b], s]
        primal = jnp.where(filled, primal, 0.0)
        adjoint = g[b, rows + s]
        return primal, flux_of(primal, adjoint)

    def advanced(s, b, moved):
        place = lax.rem(b, own_blocks)
        before = jnp.where(place == 0, carry, 0.0).astype(f32)
        after = jnp.where(place == own_blocks - 1, carry, 0.0).astype(f32)
        low = pltpu.roll(g[wrapped(b - 1 + total, total), rows + s], 1, 1)
        high = pltpu.roll(g[wrapped(b + 1, total), rows + s], TILE - 1, 1)
        base = g[b, 2 * rows + s]
        base = base + jnp.where(lane == 0, low * before, 0.0) + jnp.where(lane == TILE - 1, high * after, 0.0)
        return base - step_size * moved

    for s in range(rows):
        base = first_block - margin[s, 0, 0] - 5 + 4 * total
        for t in range(spread):
            b = wrapped(base - 1 + t, total)
            primal, moved = block(s, b)
            flux[s, t] = moved.astype(jnp.bfloat16).astype(f32)
            if 0 < t < spread - 1:
                q_out[s, t - 1] = primal
                p_out[s, t - 1] = advanced(s, b, moved)
        own = []
        for i in range(own_blocks):
            primal, moved = block(s, first_block + i)
            own.append(moved)
            q_out[s, spread - 2 + i] = primal
            p_out[s, spread - 2 + i] = advanced(s, first_block + i, moved)
        blank = [jnp.zeros((8, TILE), f32)] * (own_blocks - 2)
        side_flux = [block(s, left)[1], block(s, right)[1]]
        pulls = [
            pull_row(lambda t: flux[s, t + 1], weights, margin, count, s, slot, first_block, base, total)
            for slot in range(-1, own_blocks + 1)
        ]

        def at_sides(low, high):
            return jnp.concatenate([pltpu.roll(low, 1, 1), *blank, pltpu.roll(high, TILE - 1, 1)], axis=1)

        pulled = step_size * jnp.concatenate(pulls[1:-1], axis=1)
        pulled_side = step_size * at_sides(pulls[0], pulls[-1])
        pushed = step_size * jnp.concatenate(own, axis=1)
        pushed_side = step_size * at_sides(*side_flux)
        for v in range(var_count):
            at = (v * rows + s) * 8
            cut = slice(at, at + layers)
            o_r[v, s] = (
                v_r[v, s] + carry * columns[0][cut] + jnp.where(layer_all == layers - 1, pulled[v : v + 1], 0.0)
            )
            o_s[v, s] = v_s[v, s] + carry * columns[1][cut] - jnp.where(layer_all == 0, pushed[v : v + 1], 0.0)
            h_r[v, s] = columns[2][cut] + jnp.where(
                edge, carry * a_r[v, s] + jnp.where(layer_all == layers - 1, pulled_side[v : v + 1], 0.0), 0.0
            )
            h_s[v, s] = columns[3][cut] + jnp.where(
                edge, carry * a_s[v, s] - jnp.where(layer_all == 0, pushed_side[v : v + 1], 0.0), 0.0
            )

    last = jnp.concatenate([spots, jnp.ones((8, TILE), f32)], axis=0).astype(jnp.bfloat16)
    odd = jnp.bitwise_and(lax.axis_index("span"), 1)
    for to, s in ((inner, (1 - odd) * (rows - 1)), (outer, odd * (rows - 1))):
        for j in range(total // 2):
            to[j] = jnp.concatenate([g[2 * j, rows + s], g[2 * j + 1, rows + s]], axis=0).astype(jnp.bfloat16)
        for v in range(var_count):
            for n, ref in enumerate((a_r, a_s, o_r, o_s)):
                held[v, n * layers : (n + 1) * layers, :] = ref[v, s]
            for i in range(own_blocks):
                to[total // 2 + v * own_blocks + i] = held[v, :, i * TILE : (i + 1) * TILE].astype(jnp.bfloat16)
        to[total // 2 + var_count * own_blocks] = last


def third_kernel(
    outer, inner, o_r, o_s, h_r, h_s, q, p, a_r, a_s, jd_r, jd_s, jo_r, jo_s, src_r, src_s, weights, margin, count,
    out_r, out_s, flux, x_r, x_s, rows_low, rows_high,
):
    var_count, rows, layers, cells = a_r.shape
    total = weights.shape[1]
    own_blocks = cells // TILE
    spread = REACH + own_blocks + 1
    first_block = lax.axis_index("circ") * own_blocks
    lane = iota((8, TILE), 1)
    layer_all = iota((layers, cells), 0)
    end = total // 2 + var_count * own_blocks
    for x in (x_r, x_s):
        x[...] = jnp.zeros(x.shape, f32)
    odd = jnp.bitwise_and(lax.axis_index("span"), 1) == 1

    def low(n):
        return jnp.where(odd, inner[n].astype(f32), outer[n].astype(f32))

    def high(n):
        return jnp.where(odd, outer[n].astype(f32), inner[n].astype(f32))

    for side, to in ((low, rows_low), (high, rows_high)):
        for v in range(var_count):
            for i in range(own_blocks):
                to[v, :, i * TILE : (i + 1) * TILE] = side(total // 2 + v * own_blocks + i)
    ends = [low(end), high(end)]
    inside = [jnp.concatenate([x[8:9]] * own_blocks, axis=1) for x in ends]
    group = lax.rem(lax.shift_right_logical(lane, 3), rows)
    corner = jnp.where(group == 0, pltpu.roll(ends[0][0:8], (TILE - 8 * (rows - 1)) % TILE, 1), 0.0)
    corner = corner + jnp.where(group == rows - 1, pltpu.roll(ends[1][0:8], 8 * (rows - 1), 1), 0.0)
    columns = [
        lax.dot_general(corner, edge_pick(n, cells), (((0,), (0,)), ((), ())), preferred_element_type=f32)
        for n in range(2)
    ]

    def halo(side, b):
        both = side(lax.shift_right_logical(b, 1))
        return jnp.where(jnp.bitwise_and(b, 1) == 1, both[8:16], both[0:8])

    extra = []
    for s in range(rows):
        base = first_block - margin[s, 0, 0] - 5 + 4 * total
        own = []
        for t in range(spread - 2 + own_blocks):
            b = wrapped(base + t, total) if t < spread - 2 else first_block + t - (spread - 2)
            adjoint = p[s, t]
            if s == 0:
                adjoint = adjoint + carry * halo(low, b)
            if s == rows - 1:
                adjoint = adjoint + carry * halo(high, b)
            moved = flux_of(q[s, t], adjoint)
            if t < spread - 2:
                flux[s, t] = moved.astype(jnp.bfloat16).astype(f32)
            else:
                own.append(moved)
        pulls = [
            pull_row(lambda t: flux[s, t], weights, margin, count, s, slot, first_block, base, total)
            for slot in range(own_blocks)
        ]
        extra.append((step_size * jnp.concatenate(pulls, axis=1), -step_size * jnp.concatenate(own, axis=1)))

    fields = (
        (o_r, h_r, a_r, jd_r, jo_r, src_r, x_r, out_r, layers - 1),
        (o_s, h_s, a_s, jd_s, jo_s, src_s, x_s, out_s, 0),
    )
    for n, (o, h, a, jd, jo, src, x, out, layer) in enumerate(fields):
        old = slice(n * layers, (n + 1) * layers)
        new = slice((2 + n) * layers, (3 + n) * layers)
        for v in range(var_count):
            for s in range(rows):
                value = o[v, s]
                if s == 0:
                    value = value + carry * rows_low[v, old, :]
                if s == rows - 1:
                    value = value + carry * rows_high[v, old, :]
                x[v * rows + s, 0:layers, :] = value
        for s in range(rows):
            state_row = [x[v * rows + s, 0:layers, :] for v in range(var_count)]
            for v in range(var_count):
                wide = x[v * rows + s]
                beside = (lanes_apart(wide) + layers_apart(wide))[0:layers]
                at = (v * rows + s) * 8
                beside = beside + h[v, s] + carry * columns[n][at : at + layers]
                if s > 0:
                    beside = beside + x[v * rows + s - 1, 0:layers, :]
                else:
                    beside = beside + inside[0] * (rows_low[v, new, :] + carry * a[v, 0])
                if s < rows - 1:
                    beside = beside + x[v * rows + s + 1, 0:layers, :]
                else:
                    beside = beside + inside[1] * (rows_high[v, new, :] + carry * a[v, rows - 1])
                res = jacobian_row(jd, jo, state_row, v, s, var_count) - coupling * beside - src[v, s]
                out[v, s] = (
                    state_row[v] - step_size * res + jnp.where(layer_all == layer, extra[s][n][v : v + 1], 0.0)
                )


def per_device(
    adjoint_rotor,
    adjoint_stator,
    jac_diag_rotor,
    jac_diag_stator,
    jac_off_rotor,
    jac_off_stator,
    source_rotor,
    source_stator,
    rotor_state,
    margin_block,
    face_count,
    margin_weight,
):
    var_count, rows, layers, cells = adjoint_rotor.shape
    own_blocks = cells // TILE
    total = margin_block.shape[1]
    spread = REACH + own_blocks + 1
    field = jax.ShapeDtypeStruct(adjoint_rotor.shape, f32)
    vmem = pl.BlockSpec(memory_space=pltpu.VMEM)
    smem = pl.BlockSpec(memory_space=pltpu.SMEM)
    padded = pltpu.VMEM((TILE // 8, 8, cells), f32)

    margin = jnp.swapaxes(margin_block, 1, 2)
    arguments = (
        adjoint_rotor, adjoint_stator, jac_diag_rotor, jac_diag_stator, jac_off_rotor, jac_off_stator,
        source_rotor, source_stator, rotor_state, margin, face_count, margin_weight,
    )
    shapes = [jax.ShapeDtypeStruct(x.shape, x.dtype) for x in arguments]
    v_r, v_s, share, a_r, a_s, weights, margin, count = pl.pallas_call(
        first_kernel,
        out_shape=(
            field, field, jax.ShapeDtypeStruct((own_blocks, 64, TILE), jnp.bfloat16),
            shapes[0], shapes[1], shapes[11], shapes[9], shapes[10],
        ),
        in_specs=[pl.BlockSpec(memory_space=pltpu.HBM)] * 12,
        out_specs=(vmem,) * 8,
        scratch_shapes=[pltpu.VMEM(x.shape, x.dtype) for x in shapes[2:9]]
        + [padded] * 4
        + [pltpu.SemaphoreType.DMA((12,)), pltpu.VMEM((own_blocks, 3 * rows, 8, TILE), f32)],
        compiler_params=params,
        name="local_part",
    )(*[pltpu.with_memory_space_constraint(x, pltpu.HBM) for x in arguments])
    members = lax.axis_size("circ")
    pieces = [(share, [0])]
    mask = members // 2
    while mask > 0:
        if mask == 1 and len(pieces) > 1:
            pieces = pieces[::-1]
            pieces = [(jnp.concatenate([x for x, _ in pieces], axis=0), sum((m for _, m in pieces), []))]
        pairs = [(i, i ^ mask) for i in range(members)]
        moved = [(lax.ppermute(x, "circ", pairs), [m ^ mask for m in masks]) for x, masks in pieces]
        pieces = pieces + moved
        if mask > 2 and len(pieces) > 2:
            half = len(pieces) // 2
            pieces = [
                (jnp.concatenate([x for x, _ in part], axis=0), sum((m for _, m in part), []))
                for part in (pieces[:half], pieces[half:])
            ]
        mask //= 2
    masks = [m for _, m in pieces]
    tiles = jax.ShapeDtypeStruct((total // 2 + var_count * own_blocks + 1, 16, TILE), jnp.bfloat16)
    listed = jax.ShapeDtypeStruct((rows, spread - 2 + own_blocks, 8, TILE), f32)
    o_r, o_s, h_r, h_s, q, p, outer, inner = pl.pallas_call(
        functools.partial(second_kernel, masks),
        out_shape=(field, field, field, field, listed, listed, tiles, tiles),
        in_specs=[vmem] * (len(pieces) + 5) + [smem] * 2,
        out_specs=(vmem,) * 8,
        scratch_shapes=[
            pltpu.VMEM((rows, spread, 8, TILE), f32),
            pltpu.VMEM((var_count, 4 * layers, cells), f32),
            pltpu.VMEM((8, TILE), f32),
            pltpu.VMEM((total, 3 * rows, 8, TILE), f32),
        ],
        compiler_params=params,
        name="interface_part",
    )(*[x for x, _ in pieces], v_r, v_s, a_r, a_s, weights, margin, count)
    bands = lax.axis_size("span")
    near = [(i, i ^ 1) for i in range(bands)]
    far = [pair for i in range(1, bands - 1, 2) for pair in ((i, i + 1), (i + 1, i))]
    outer = lax.ppermute(outer, "span", far)
    inner = lax.ppermute(inner, "span", near)
    out_r, out_s = pl.pallas_call(
        third_kernel,
        out_shape=(field, field),
        in_specs=[vmem] * 17 + [smem] * 2,
        out_specs=(vmem,) * 2,
        scratch_shapes=[
            pltpu.VMEM((rows, spread - 2, 8, TILE), f32),
            padded,
            padded,
            pltpu.VMEM((var_count, 4 * layers, cells), f32),
            pltpu.VMEM((var_count, 4 * layers, cells), f32),
        ],
        compiler_params=params,
        name="final_part",
    )(
        outer, inner, o_r, o_s, h_r, h_s, q, p, a_r, a_s, jac_diag_rotor, jac_diag_stator,
        jac_off_rotor, jac_off_stator, source_rotor, source_stator, weights, margin, count,
    )
    return (out_r, out_s)


def solution(mesh):
    field = P(None, "span", None, "circ")
    placed = (
        (field,) * 4
        + (P(None, None, "span", None, "circ"),) * 2
        + (field,) * 2
        + (P(None, "span", "circ"), P("span", None, None), P("span", None), P("span", None, None, None))
    )
    return jax.shard_map(
        per_device, mesh=mesh, in_specs=placed, out_specs=(field, field), check_vma=False
    )
```

```python
import functools

import jax
import jax.numpy as jnp
from jax import lax
from jax.experimental import pallas as pl
from jax.experimental.pallas import tpu as pltpu
from jax.sharding import PartitionSpec as P

step_size = 0.1
coupling = 0.2
carry = step_size * coupling
REACH = 8
TILE = 128
f32 = jnp.float32
params = pltpu.CompilerParams(vmem_limit_bytes=24 * 1024 * 1024)


def iota(shape, dim):
    return lax.broadcasted_iota(jnp.int32, shape, dim)


def wrapped(x, count):
    if count & (count - 1) == 0:
        return jnp.bitwise_and(x, count - 1)
    return lax.rem(x + 4 * count, count)


def lanes_apart(x):
    cells = x.shape[1]
    lane = iota(x.shape, 1)
    before = jnp.where(lane == 0, 0.0, pltpu.roll(x, 1, 1))
    after = jnp.where(lane == cells - 1, 0.0, pltpu.roll(x, cells - 1, 1))
    return before + after


def layers_apart(x):
    return pltpu.roll(x, 1, 0) + pltpu.roll(x, 7, 0)


def edge_pick(row, cells):
    at = iota((8, cells), 0)
    lane = iota((8, cells), 1)
    first = jnp.logical_and(at == row, lane == 0)
    last = jnp.logical_and(at == 4 + row, lane == cells - 1)
    return jnp.where(jnp.logical_or(first, last), 1.0, 0.0).astype(f32)


def split(x):
    high = x.astype(jnp.bfloat16).astype(f32)
    return high, x - high


def flux_of(primal, adjoint):
    speeds = jnp.sqrt(1.0 + primal * primal)
    over = jnp.sum(primal * adjoint, axis=0, keepdims=True)
    under = 6.0 + jnp.sum(primal * primal, axis=0, keepdims=True)
    return speeds * adjoint + 0.5 * primal * (over / under)


def jacobian_row(diag, off, state, v, s, var_count):
    total = diag[v, s] * state[v]
    for w in range(var_count):
        total = total + off[w, v, s].astype(f32) * state[w]
    return total


def pull_row(flux, weights, margin, count, s, slot, first_block, base, total):
    target = wrapped(first_block + slot + total, total)
    acc = jnp.zeros((8, TILE), f32)
    for e in range(REACH):
        b = wrapped(base + slot + e, total)
        k = wrapped(target - margin[s, 0, b] + total, total)
        live = jnp.where(k < count[s, b], 1.0, 0.0).astype(f32)
        kept = jnp.minimum(k, weights.shape[2] - 1)
        acc = acc + (weights[s, b, pl.ds(kept, 1), :] * live) * flux(slot + e)
    return acc


def first_kernel(*refs):
    outer, refs = refs[:12], refs[12:]
    v_r, v_s, out, a_r, a_s, weights, margin, count = refs[:8]
    jd_r, jd_s, jo_r, jo_s, src_r, src_s, state = refs[8:15]
    xs, sems, wide_out = refs[15:19], refs[19], refs[20]
    var_count, rows, layers, cells = a_r.shape
    own_blocks = cells // TILE
    inner = (a_r, a_s, jd_r, jd_s, jo_r, jo_s, src_r, src_s, state, margin, count, weights)
    copies = [pltpu.make_async_copy(x, y, sems.at[n]) for n, (x, y) in enumerate(zip(outer, inner))]
    for copy in copies:
        copy.start()
    wide_out[...] = jnp.zeros(wide_out.shape, f32)
    for x in xs:
        x[...] = jnp.zeros(x.shape, f32)
    for copy in copies:
        copy.wait()
    fields = ((a_r, jd_r, jo_r, src_r, v_r, xs[0], xs[2]), (a_s, jd_s, jo_s, src_s, v_s, xs[1], xs[3]))
    for a, jd, jo, src, partial, x_a, x_p in fields:
        for v in range(var_count):
            for s in range(rows):
                x_a[v * rows + s, 0:layers, :] = a[v, s]
        for s in range(rows):
            state_row = [a[v, s] for v in range(var_count)]
            for v in range(var_count):
                wide = x_a[v * rows + s]
                beside = (lanes_apart(wide) + layers_apart(wide))[0:layers]
                if s > 0:
                    beside = beside + a[v, s - 1]
                if s < rows - 1:
                    beside = beside + a[v, s + 1]
                res = jacobian_row(jd, jo, state_row, v, s, var_count) - coupling * beside - src[v, s]
                new = state_row[v] - step_size * res
                partial[v, s] = new
                x_p[v * rows + s, 0:layers, :] = new
    edges = jnp.zeros((8, TILE), f32)
    for q in range(4):
        flat = xs[q][...].reshape(TILE, cells)
        edges = edges + lax.dot_general(
            edge_pick(q, cells), flat, (((1,), (1,)), ((), ())), preferred_element_type=f32
        )
    for v in range(var_count):
        rotor = state[v].astype(f32)
        for s in range(rows):
            for i in range(own_blocks):
                cut = slice(i * TILE, (i + 1) * TILE)
                wide_out[i, s, v : v + 1, :] = rotor[s : s + 1, cut]
                wide_out[i, rows + s, v : v + 1, :] = a_s[v, s, 0:1, cut]
                wide_out[i, 2 * rows + s, v : v + 1, :] = v_s[v, s, 0:1, cut]
    row8 = iota((8, TILE), 0)
    filled = row8 < var_count
    for i in range(own_blocks):
        if i in (0, own_blocks - 1):
            side = 4 if i else 0
            for s in range(rows):
                wide_out[i, 2 * rows + s, 6:8, :] = edges[side + 2 * s : side + 2 * s + 2]
        groups = []
        for s in range(rows):
            p_high, p_rest = split(wide_out[i, rows + s])
            u_high, u_rest = split(wide_out[i, 2 * rows + s])
            groups.append((
                jnp.where(filled, wide_out[i, s], pltpu.roll(u_rest, 6, 0)),
                jnp.where(filled, p_high, pltpu.roll(u_rest, 4, 0)),
                jnp.where(filled, p_rest, pltpu.roll(u_rest, 2, 0)),
                u_high,
            ))
        for n in range(4):
            out[i, n * 16 : n * 16 + 16, :] = jnp.concatenate([x[n] for x in groups], axis=0).astype(jnp.bfloat16)


def second_kernel(
    masks, mine, other, v_r, v_s, a_r, a_s, weights, margin, count,
    o_r, o_s, h_r, h_s, q_out, p_out, inner, outer, flux, held, spot, g,
):
    var_count, rows, layers, cells = a_r.shape
    total = 2 * mine.shape[0]
    own_blocks = cells // TILE
    entries = weights.shape[2]
    spread = REACH + own_blocks + 1
    first_block = lax.axis_index("circ") * own_blocks
    row8 = iota((8, TILE), 0)
    lane = iota((8, TILE), 1)
    lane_all = iota((layers, cells), 1)
    layer_all = iota((layers, cells), 0)
    edge = jnp.logical_or(lane_all == 0, lane_all == cells - 1)
    left = wrapped(first_block - 1 + total, total)
    right = wrapped(first_block + own_blocks, total)

    filled = row8 < var_count
    here = lax.axis_index("circ")
    for at in range(total):
        half, part = divmod(at, total // 2)
        place, i = divmod(part, own_blocks)
        mask = half + sum(m for n, m in enumerate(masks) if place >> n & 1)
        b = jnp.bitwise_xor(here, mask) * own_blocks + i
        whole = other if half else mine
        tiles = [whole[part, n * 16 : n * 16 + 16, :].astype(f32) for n in range(4)]
        for s in range(rows):
            rotor, p_high, p_rest, u_high = [x[s * 8 : s * 8 + 8] for x in tiles]
            u_rest = jnp.where(
                row8 < 2, pltpu.roll(rotor, 2, 0), jnp.where(row8 < 4, pltpu.roll(p_high, 4, 0), pltpu.roll(p_rest, 6, 0))
            )
            g[b, s] = rotor
            g[b, rows + s] = p_high + p_rest
            g[b, 2 * rows + s] = u_high + jnp.where(filled, u_rest, 0.0)
    spot[0:2, :] = g[left, 2 * rows, 6:8, :]
    spot[2:4, :] = g[left, 2 * rows + 1, 6:8, :]
    spot[4:6, :] = g[right, 2 * rows, 6:8, :]
    spot[6:8, :] = g[right, 2 * rows + 1, 6:8, :]
    spots = spot[...]
    columns = [
        lax.dot_general(spots, edge_pick(q, cells), (((0,), (0,)), ((), ())), preferred_element_type=f32)
        for q in range(4)
    ]

    def block(s, b):
        primal = jnp.zeros((8, TILE), f32)
        for k in range(entries):
            live = jnp.where(k < count[s, b], 1.0, 0.0).astype(f32)
            primal = primal + (weights[s, b, k : k + 1, :] * live) * g[margin[s, k, b], s]
        primal = jnp.where(filled, primal, 0.0)
        adjoint = g[b, rows + s]
        return primal, flux_of(primal, adjoint)

    def advanced(s, b, moved):
        place = lax.rem(b, own_blocks)
        before = jnp.where(place == 0, carry, 0.0).astype(f32)
        after = jnp.where(place == own_blocks - 1, carry, 0.0).astype(f32)
        low = pltpu.roll(g[wrapped(b - 1 + total, total), rows + s], 1, 1)
        high = pltpu.roll(g[wrapped(b + 1, total), rows + s], TILE - 1, 1)
        base = g[b, 2 * rows + s]
        base = base + jnp.where(lane == 0, low * before, 0.0) + jnp.where(lane == TILE - 1, high * after, 0.0)
        return base - step_size * moved

    for s in range(rows):
        base = first_block - margin[s, 0, 0] - 5 + 4 * total
        for t in range(spread):
            b = wrapped(base - 1 + t, total)
            primal, moved = block(s, b)
            flux[s, t] = moved.astype(jnp.bfloat16).astype(f32)
            if 0 < t < spread - 1:
                q_out[s, t - 1] = primal
                p_out[s, t - 1] = advanced(s, b, moved)
        own = []
        for i in range(own_blocks):
            primal, moved = block(s, first_block + i)
            own.append(moved)
            q_out[s, spread - 2 + i] = primal
            p_out[s, spread - 2 + i] = advanced(s, first_block + i, moved)
        blank = [jnp.zeros((8, TILE), f32)] * (own_blocks - 2)
        side_flux = [block(s, left)[1], block(s, right)[1]]
        pulls = [
            pull_row(lambda t: flux[s, t + 1], weights, margin, count, s, slot, first_block, base, total)
            for slot in range(-1, own_blocks + 1)
        ]

        def at_sides(low, high):
            return jnp.concatenate([pltpu.roll(low, 1, 1), *blank, pltpu.roll(high, TILE - 1, 1)], axis=1)

        pulled = step_size * jnp.concatenate(pulls[1:-1], axis=1)
        pulled_side = step_size * at_sides(pulls[0], pulls[-1])
        pushed = step_size * jnp.concatenate(own, axis=1)
        pushed_side = step_size * at_sides(*side_flux)
        for v in range(var_count):
            at = (v * rows + s) * 8
            cut = slice(at, at + layers)
            o_r[v, s] = (
                v_r[v, s] + carry * columns[0][cut] + jnp.where(layer_all == layers - 1, pulled[v : v + 1], 0.0)
            )
            o_s[v, s] = v_s[v, s] + carry * columns[1][cut] - jnp.where(layer_all == 0, pushed[v : v + 1], 0.0)
            h_r[v, s] = columns[2][cut] + jnp.where(
                edge, carry * a_r[v, s] + jnp.where(layer_all == layers - 1, pulled_side[v : v + 1], 0.0), 0.0
            )
            h_s[v, s] = columns[3][cut] + jnp.where(
                edge, carry * a_s[v, s] - jnp.where(layer_all == 0, pushed_side[v : v + 1], 0.0), 0.0
            )

    last = jnp.concatenate([spots, jnp.ones((8, TILE), f32)], axis=0).astype(jnp.bfloat16)
    odd = jnp.bitwise_and(lax.axis_index("span"), 1)
    for to, s in ((inner, (1 - odd) * (rows - 1)), (outer, odd * (rows - 1))):
        for j in range(total // 2):
            to[j] = jnp.concatenate([g[2 * j, rows + s], g[2 * j + 1, rows + s]], axis=0).astype(jnp.bfloat16)
        for v in range(var_count):
            for n, ref in enumerate((a_r, a_s, o_r, o_s)):
                held[v, n * layers : (n + 1) * layers, :] = ref[v, s]
            for i in range(own_blocks):
                to[total // 2 + v * own_blocks + i] = held[v, :, i * TILE : (i + 1) * TILE].astype(jnp.bfloat16)
        to[total // 2 + var_count * own_blocks] = last


def third_kernel(
    inner, outer, o_r, o_s, h_r, h_s, q, p, a_r, a_s, jd_r, jd_s, jo_r, jo_s, src_r, src_s, weights, margin, count,
    out_r, out_s, flux, x_r, x_s, rows_low, rows_high,
):
    var_count, rows, layers, cells = a_r.shape
    total = weights.shape[1]
    own_blocks = cells // TILE
    spread = REACH + own_blocks + 1
    first_block = lax.axis_index("circ") * own_blocks
    lane = iota((8, TILE), 1)
    layer_all = iota((layers, cells), 0)
    end = total // 2 + var_count * own_blocks
    for x in (x_r, x_s):
        x[...] = jnp.zeros(x.shape, f32)
    odd = jnp.bitwise_and(lax.axis_index("span"), 1) == 1

    def low(n):
        return jnp.where(odd, inner[n].astype(f32), outer[n].astype(f32))

    def high(n):
        return jnp.where(odd, outer[n].astype(f32), inner[n].astype(f32))

    for side, to in ((low, rows_low), (high, rows_high)):
        for v in range(var_count):
            for i in range(own_blocks):
                to[v, :, i * TILE : (i + 1) * TILE] = side(total // 2 + v * own_blocks + i)
    ends = [low(end), high(end)]
    inside = [jnp.concatenate([x[8:9]] * own_blocks, axis=1) for x in ends]
    group = lax.rem(lax.shift_right_logical(lane, 3), rows)
    corner = jnp.where(group == 0, pltpu.roll(ends[0][0:8], (TILE - 8 * (rows - 1)) % TILE, 1), 0.0)
    corner = corner + jnp.where(group == rows - 1, pltpu.roll(ends[1][0:8], 8 * (rows - 1), 1), 0.0)
    columns = [
        lax.dot_general(corner, edge_pick(n, cells), (((0,), (0,)), ((), ())), preferred_element_type=f32)
        for n in range(2)
    ]

    def halo(side, b):
        both = side(lax.shift_right_logical(b, 1))
        return jnp.where(jnp.bitwise_and(b, 1) == 1, both[8:16], both[0:8])

    extra = []
    for s in range(rows):
        base = first_block - margin[s, 0, 0] - 5 + 4 * total
        own = []
        for t in range(spread - 2 + own_blocks):
            b = wrapped(base + t, total) if t < spread - 2 else first_block + t - (spread - 2)
            adjoint = p[s, t]
            if s == 0:
                adjoint = adjoint + carry * halo(low, b)
            if s == rows - 1:
                adjoint = adjoint + carry * halo(high, b)
            moved = flux_of(q[s, t], adjoint)
            if t < spread - 2:
                flux[s, t] = moved.astype(jnp.bfloat16).astype(f32)
            else:
                own.append(moved)
        pulls = [
            pull_row(lambda t: flux[s, t], weights, margin, count, s, slot, first_block, base, total)
            for slot in range(own_blocks)
        ]
        extra.append((step_size * jnp.concatenate(pulls, axis=1), -step_size * jnp.concatenate(own, axis=1)))

    fields = (
        (o_r, h_r, a_r, jd_r, jo_r, src_r, x_r, out_r, layers - 1),
        (o_s, h_s, a_s, jd_s, jo_s, src_s, x_s, out_s, 0),
    )
    for n, (o, h, a, jd, jo, src, x, out, layer) in enumerate(fields):
        old = slice(n * layers, (n + 1) * layers)
        new = slice((2 + n) * layers, (3 + n) * layers)
        for v in range(var_count):
            for s in range(rows):
                value = o[v, s]
                if s == 0:
                    value = value + carry * rows_low[v, old, :]
                if s == rows - 1:
                    value = value + carry * rows_high[v, old, :]
                x[v * rows + s, 0:layers, :] = value
        for s in range(rows):
            state_row = [x[v * rows + s, 0:layers, :] for v in range(var_count)]
            for v in range(var_count):
                wide = x[v * rows + s]
                beside = (lanes_apart(wide) + layers_apart(wide))[0:layers]
                at = (v * rows + s) * 8
                beside = beside + h[v, s] + carry * columns[n][at : at + layers]
                if s > 0:
                    beside = beside + x[v * rows + s - 1, 0:layers, :]
                else:
                    beside = beside + inside[0] * (rows_low[v, new, :] + carry * a[v, 0])
                if s < rows - 1:
                    beside = beside + x[v * rows + s + 1, 0:layers, :]
                else:
                    beside = beside + inside[1] * (rows_high[v, new, :] + carry * a[v, rows - 1])
                res = jacobian_row(jd, jo, state_row, v, s, var_count) - coupling * beside - src[v, s]
                out[v, s] = (
                    state_row[v] - step_size * res + jnp.where(layer_all == layer, extra[s][n][v : v + 1], 0.0)
                )


def per_device(
    adjoint_rotor,
    adjoint_stator,
    jac_diag_rotor,
    jac_diag_stator,
    jac_off_rotor,
    jac_off_stator,
    source_rotor,
    source_stator,
    rotor_state,
    margin_block,
    face_count,
    margin_weight,
):
    var_count, rows, layers, cells = adjoint_rotor.shape
    own_blocks = cells // TILE
    total = margin_block.shape[1]
    spread = REACH + own_blocks + 1
    field = jax.ShapeDtypeStruct(adjoint_rotor.shape, f32)
    vmem = pl.BlockSpec(memory_space=pltpu.VMEM)
    smem = pl.BlockSpec(memory_space=pltpu.SMEM)
    padded = pltpu.VMEM((TILE // 8, 8, cells), f32)

    margin = jnp.swapaxes(margin_block, 1, 2)
    arguments = (
        adjoint_rotor, adjoint_stator, jac_diag_rotor, jac_diag_stator, jac_off_rotor, jac_off_stator,
        source_rotor, source_stator, rotor_state, margin, face_count, margin_weight,
    )
    shapes = [jax.ShapeDtypeStruct(x.shape, x.dtype) for x in arguments]
    v_r, v_s, share, a_r, a_s, weights, margin, count = pl.pallas_call(
        first_kernel,
        out_shape=(
            field, field, jax.ShapeDtypeStruct((own_blocks, 64, TILE), jnp.bfloat16),
            shapes[0], shapes[1], shapes[11], shapes[9], shapes[10],
        ),
        in_specs=[pl.BlockSpec(memory_space=pltpu.HBM)] * 12,
        out_specs=(vmem,) * 8,
        scratch_shapes=[pltpu.VMEM(x.shape, x.dtype) for x in shapes[2:9]]
        + [padded] * 4
        + [pltpu.SemaphoreType.DMA((12,)), pltpu.VMEM((own_blocks, 3 * rows, 8, TILE), f32)],
        compiler_params=params,
        name="local_part",
    )(*[pltpu.with_memory_space_constraint(x, pltpu.HBM) for x in arguments])
    members = lax.axis_size("circ")
    mine, masks = share, []
    mask = members // 2
    while mask > 0:
        other = lax.ppermute(mine, "circ", [(i, i ^ mask) for i in range(members)])
        if mask > 1:
            mine = jnp.concatenate([mine, other], axis=0)
            masks.append(mask)
        mask //= 2
    tiles = jax.ShapeDtypeStruct((total // 2 + var_count * own_blocks + 1, 16, TILE), jnp.bfloat16)
    listed = jax.ShapeDtypeStruct((rows, spread - 2 + own_blocks, 8, TILE), f32)
    o_r, o_s, h_r, h_s, q, p, inner, outer = pl.pallas_call(
        functools.partial(second_kernel, masks),
        out_shape=(field, field, field, field, listed, listed, tiles, tiles),
        in_specs=[vmem] * 7 + [smem] * 2,
        out_specs=(vmem,) * 8,
        scratch_shapes=[
            pltpu.VMEM((rows, spread, 8, TILE), f32),
            pltpu.VMEM((var_count, 4 * layers, cells), f32),
            pltpu.VMEM((8, TILE), f32),
            pltpu.VMEM((total, 3 * rows, 8, TILE), f32),
        ],
        compiler_params=params,
        name="interface_part",
    )(mine, other, v_r, v_s, a_r, a_s, weights, margin, count)
    bands = lax.axis_size("span")
    near = [(i, i ^ 1) for i in range(bands)]
    far = [pair for i in range(1, bands - 1, 2) for pair in ((i, i + 1), (i + 1, i))]
    inner = lax.ppermute(inner, "span", near)
    outer = lax.ppermute(outer, "span", far)
    out_r, out_s = pl.pallas_call(
        third_kernel,
        out_shape=(field, field),
        in_specs=[vmem] * 17 + [smem] * 2,
        out_specs=(vmem,) * 2,
        scratch_shapes=[
            pltpu.VMEM((rows, spread - 2, 8, TILE), f32),
            padded,
            padded,
            pltpu.VMEM((var_count, 4 * layers, cells), f32),
            pltpu.VMEM((var_count, 4 * layers, cells), f32),
        ],
        compiler_params=params,
        name="final_part",
    )(
        inner, outer, o_r, o_s, h_r, h_s, q, p, a_r, a_s, jac_diag_rotor, jac_diag_stator,
        jac_off_rotor, jac_off_stator, source_rotor, source_stator, weights, margin, count,
    )
    return (out_r, out_s)


def solution(mesh):
    field = P(None, "span", None, "circ")
    placed = (
        (field,) * 4
        + (P(None, None, "span", None, "circ"),) * 2
        + (field,) * 2
        + (P(None, "span", "circ"), P("span", None, None), P("span", None), P("span", None, None, None))
    )
    return jax.shard_map(
        per_device, mesh=mesh, in_specs=placed, out_specs=(field, field), check_vma=False
    )
```

```python
import functools

import jax
import jax.numpy as jnp
from jax import lax
from jax.experimental import pallas as pl
from jax.experimental.pallas import tpu as pltpu
from jax.sharding import PartitionSpec as P

step_size = 0.1
coupling = 0.2
carry = step_size * coupling
REACH = 8
TILE = 128
f32 = jnp.float32
params = pltpu.CompilerParams(vmem_limit_bytes=24 * 1024 * 1024)


def iota(shape, dim):
    return lax.broadcasted_iota(jnp.int32, shape, dim)


def wrapped(x, count):
    if count & (count - 1) == 0:
        return jnp.bitwise_and(x, count - 1)
    return lax.rem(x + 4 * count, count)


def lanes_apart(x):
    cells = x.shape[1]
    lane = iota(x.shape, 1)
    before = jnp.where(lane == 0, 0.0, pltpu.roll(x, 1, 1))
    after = jnp.where(lane == cells - 1, 0.0, pltpu.roll(x, cells - 1, 1))
    return before + after


def layers_apart(x):
    return pltpu.roll(x, 1, 0) + pltpu.roll(x, 7, 0)


def edge_pick(row, cells):
    at = iota((8, cells), 0)
    lane = iota((8, cells), 1)
    first = jnp.logical_and(at == row, lane == 0)
    last = jnp.logical_and(at == 4 + row, lane == cells - 1)
    return jnp.where(jnp.logical_or(first, last), 1.0, 0.0).astype(f32)


def split(x):
    high = x.astype(jnp.bfloat16).astype(f32)
    return high, x - high


def flux_parts(primal):
    square = primal * primal
    under = 6.0 + jnp.sum(square, axis=0, keepdims=True)
    return jnp.sqrt(1.0 + square), 0.5 * primal / under


def flux_of(primal, speeds, scaled, adjoint):
    return speeds * adjoint + scaled * jnp.sum(primal * adjoint, axis=0, keepdims=True)


def jacobian_row(diag, off, state, v, s, var_count):
    total = diag[v, s] * state[v]
    for w in range(var_count):
        total = total + off[w, v, s].astype(f32) * state[w]
    return total


def pull_row(flux, table, s, slot):
    acc = jnp.zeros((8, TILE), f32)
    for e in range(REACH):
        acc = acc + table[s, slot + 1, e : e + 1, :] * flux(slot + e)
    return acc


def window(margin, s, first_block, total):
    return first_block - margin[s, 0, 0] - 5 + 4 * total


def window_blocks(base, first_block, own_blocks, total):
    found = [wrapped(base - 1 + t, total) for t in range(REACH + own_blocks + 1)]
    sides = [wrapped(first_block - 1 + total, total), wrapped(first_block + own_blocks, total)]
    return found + [first_block + i for i in range(own_blocks)] + sides


def table_kernel(weights, margin, count, primal_table, pull_table):
    rows, total, entries, _ = weights.shape
    own_blocks = pull_table.shape[1] - 2
    first_block = lax.axis_index("circ") * own_blocks
    for s in range(rows):
        base = window(margin, s, first_block, total)
        blocks = window_blocks(base, first_block, own_blocks, total)
        entry = iota((entries, TILE), 0)
        for t, b in enumerate(blocks):
            primal_table[s, t] = jnp.where(entry < count[s, b], weights[s, b], 0.0)
        for slot in range(-1, own_blocks + 1):
            target = wrapped(first_block + slot + total, total)
            for e in range(REACH):
                b = blocks[slot + 1 + e]
                k = wrapped(target - margin[s, 0, b] + total, total)
                live = jnp.where(k < count[s, b], 1.0, 0.0).astype(f32)
                kept = jnp.minimum(k, entries - 1)
                pull_table[s, slot + 1, e : e + 1, :] = weights[s, b, pl.ds(kept, 1), :] * live


def first_kernel(*refs):
    outer, refs = refs[:12], refs[12:]
    v_r, v_s, out, a_r, a_s, weights, margin, count = refs[:8]
    jd_r, jd_s, jo_r, jo_s, src_r, src_s, state = refs[8:15]
    xs, sems, wide_out = refs[15:19], refs[19], refs[20]
    var_count, rows, layers, cells = a_r.shape
    own_blocks = cells // TILE
    inner = (a_r, a_s, jd_r, jd_s, jo_r, jo_s, src_r, src_s, state, margin, count, weights)
    copies = [pltpu.make_async_copy(x, y, sems.at[n]) for n, (x, y) in enumerate(zip(outer, inner))]
    for copy in copies:
        copy.start()
    wide_out[...] = jnp.zeros(wide_out.shape, f32)
    for x in xs:
        x[...] = jnp.zeros(x.shape, f32)
    for copy in copies:
        copy.wait()
    fields = ((a_r, jd_r, jo_r, src_r, v_r, xs[0], xs[2]), (a_s, jd_s, jo_s, src_s, v_s, xs[1], xs[3]))
    for a, jd, jo, src, partial, x_a, x_p in fields:
        for v in range(var_count):
            for s in range(rows):
                x_a[v * rows + s, 0:layers, :] = a[v, s]
        for s in range(rows):
            state_row = [a[v, s] for v in range(var_count)]
            for v in range(var_count):
                wide = x_a[v * rows + s]
                beside = (lanes_apart(wide) + layers_apart(wide))[0:layers]
                if s > 0:
                    beside = beside + a[v, s - 1]
                if s < rows - 1:
                    beside = beside + a[v, s + 1]
                res = jacobian_row(jd, jo, state_row, v, s, var_count) - coupling * beside - src[v, s]
                new = state_row[v] - step_size * res
                partial[v, s] = new
                x_p[v * rows + s, 0:layers, :] = new
    edges = jnp.zeros((8, TILE), f32)
    for q in range(4):
        flat = xs[q][...].reshape(TILE, cells)
        edges = edges + lax.dot_general(
            edge_pick(q, cells), flat, (((1,), (1,)), ((), ())), preferred_element_type=f32
        )
    for v in range(var_count):
        rotor = state[v].astype(f32)
        for s in range(rows):
            for i in range(own_blocks):
                cut = slice(i * TILE, (i + 1) * TILE)
                wide_out[i, s, v : v + 1, :] = rotor[s : s + 1, cut]
                wide_out[i, rows + s, v : v + 1, :] = a_s[v, s, 0:1, cut]
                wide_out[i, 2 * rows + s, v : v + 1, :] = v_s[v, s, 0:1, cut]
    row8 = iota((8, TILE), 0)
    filled = row8 < var_count
    for i in range(own_blocks):
        if i in (0, own_blocks - 1):
            side = 4 if i else 0
            for s in range(rows):
                wide_out[i, 2 * rows + s, 6:8, :] = edges[side + 2 * s : side + 2 * s + 2]
        groups = []
        for s in range(rows):
            p_high, p_rest = split(wide_out[i, rows + s])
            u_high, u_rest = split(wide_out[i, 2 * rows + s])
            groups.append((
                jnp.where(filled, wide_out[i, s], pltpu.roll(u_rest, 6, 0)),
                jnp.where(filled, p_high, pltpu.roll(u_rest, 4, 0)),
                jnp.where(filled, p_rest, pltpu.roll(u_rest, 2, 0)),
                u_high,
            ))
        for n in range(4):
            out[i, n * 16 : n * 16 + 16, :] = jnp.concatenate([x[n] for x in groups], axis=0).astype(jnp.bfloat16)


def second_kernel(
    masks, mine, other, v_r, v_s, a_r, a_s, primal_table, pull_table, margin_in,
    o_r, o_s, h_r, h_s, q_out, speeds_out, scaled_out, p_out, inner, outer, flux, held, spot, g, margin, sem,
):
    var_count, rows, layers, cells = a_r.shape
    fetch = pltpu.make_async_copy(margin_in, margin, sem)
    fetch.start()
    total = 2 * mine.shape[0]
    own_blocks = cells // TILE
    entries = primal_table.shape[2]
    spread = REACH + own_blocks + 1
    first_block = lax.axis_index("circ") * own_blocks
    row8 = iota((8, TILE), 0)
    lane = iota((8, TILE), 1)
    lane_all = iota((layers, cells), 1)
    layer_all = iota((layers, cells), 0)
    edge = jnp.logical_or(lane_all == 0, lane_all == cells - 1)
    left = wrapped(first_block - 1 + total, total)
    right = wrapped(first_block + own_blocks, total)

    filled = row8 < var_count
    here = lax.axis_index("circ")
    for at in range(total):
        half, part = divmod(at, total // 2)
        place, i = divmod(part, own_blocks)
        mask = half + sum(m for n, m in enumerate(masks) if place >> n & 1)
        b = jnp.bitwise_xor(here, mask) * own_blocks + i
        whole = other if half else mine
        tiles = [whole[part, n * 16 : n * 16 + 16, :].astype(f32) for n in range(4)]
        for s in range(rows):
            rotor, p_high, p_rest, u_high = [x[s * 8 : s * 8 + 8] for x in tiles]
            u_rest = jnp.where(
                row8 < 2, pltpu.roll(rotor, 2, 0), jnp.where(row8 < 4, pltpu.roll(p_high, 4, 0), pltpu.roll(p_rest, 6, 0))
            )
            g[b, s] = rotor
            g[b, rows + s] = p_high + p_rest
            g[b, 2 * rows + s] = u_high + jnp.where(filled, u_rest, 0.0)
    spot[0:2, :] = g[left, 2 * rows, 6:8, :]
    spot[2:4, :] = g[left, 2 * rows + 1, 6:8, :]
    spot[4:6, :] = g[right, 2 * rows, 6:8, :]
    spot[6:8, :] = g[right, 2 * rows + 1, 6:8, :]
    spots = spot[...]
    columns = [
        lax.dot_general(spots, edge_pick(q, cells), (((0,), (0,)), ((), ())), preferred_element_type=f32)
        for q in range(4)
    ]

    fetch.wait()

    def block(s, b, t):
        primal = jnp.zeros((8, TILE), f32)
        for k in range(entries):
            primal = primal + primal_table[s, t, k : k + 1, :] * g[margin[s, k, b], s]
        primal = jnp.where(filled, primal, 0.0)
        parts = flux_parts(primal)
        return (primal, *parts), flux_of(primal, *parts, g[b, rows + s])

    def keep(s, at, b, parts, moved):
        q_out[s, at], speeds_out[s, at], scaled_out[s, at] = parts
        p_out[s, at] = advanced(s, b, moved)

    def advanced(s, b, moved):
        place = lax.rem(b, own_blocks)
        before = jnp.where(place == 0, carry, 0.0).astype(f32)
        after = jnp.where(place == own_blocks - 1, carry, 0.0).astype(f32)
        low = pltpu.roll(g[wrapped(b - 1 + total, total), rows + s], 1, 1)
        high = pltpu.roll(g[wrapped(b + 1, total), rows + s], TILE - 1, 1)
        base = g[b, 2 * rows + s]
        base = base + jnp.where(lane == 0, low * before, 0.0) + jnp.where(lane == TILE - 1, high * after, 0.0)
        return base - step_size * moved

    for s in range(rows):
        base = window(margin, s, first_block, total)
        blocks = window_blocks(base, first_block, own_blocks, total)
        for t in range(spread):
            parts, moved = block(s, blocks[t], t)
            flux[s, t] = moved.astype(jnp.bfloat16).astype(f32)
            if 0 < t < spread - 1:
                keep(s, t - 1, blocks[t], parts, moved)
        own = []
        for i in range(own_blocks):
            parts, moved = block(s, first_block + i, spread + i)
            own.append(moved)
            keep(s, spread - 2 + i, first_block + i, parts, moved)
        blank = [jnp.zeros((8, TILE), f32)] * (own_blocks - 2)
        side_flux = [block(s, at, spread + own_blocks + n)[1] for n, at in enumerate((left, right))]
        pulls = [pull_row(lambda t: flux[s, t + 1], pull_table, s, slot) for slot in range(-1, own_blocks + 1)]

        def at_sides(low, high):
            return jnp.concatenate([pltpu.roll(low, 1, 1), *blank, pltpu.roll(high, TILE - 1, 1)], axis=1)

        pulled = step_size * jnp.concatenate(pulls[1:-1], axis=1)
        pulled_side = step_size * at_sides(pulls[0], pulls[-1])
        pushed = step_size * jnp.concatenate(own, axis=1)
        pushed_side = step_size * at_sides(*side_flux)
        for v in range(var_count):
            at = (v * rows + s) * 8
            cut = slice(at, at + layers)
            o_r[v, s] = (
                v_r[v, s] + carry * columns[0][cut] + jnp.where(layer_all == layers - 1, pulled[v : v + 1], 0.0)
            )
            o_s[v, s] = v_s[v, s] + carry * columns[1][cut] - jnp.where(layer_all == 0, pushed[v : v + 1], 0.0)
            h_r[v, s] = columns[2][cut] + jnp.where(
                edge, carry * a_r[v, s] + jnp.where(layer_all == layers - 1, pulled_side[v : v + 1], 0.0), 0.0
            )
            h_s[v, s] = columns[3][cut] + jnp.where(
                edge, carry * a_s[v, s] - jnp.where(layer_all == 0, pushed_side[v : v + 1], 0.0), 0.0
            )

    last = jnp.concatenate([spots, jnp.ones((8, TILE), f32)], axis=0).astype(jnp.bfloat16)
    odd = jnp.bitwise_and(lax.axis_index("span"), 1)
    for to, s in ((inner, (1 - odd) * (rows - 1)), (outer, odd * (rows - 1))):
        for j in range(total // 2):
            to[j] = jnp.concatenate([g[2 * j, rows + s], g[2 * j + 1, rows + s]], axis=0).astype(jnp.bfloat16)
        for v in range(var_count):
            for n, ref in enumerate((a_r, a_s, o_r, o_s)):
                held[v, n * layers : (n + 1) * layers, :] = ref[v, s]
            for i in range(own_blocks):
                to[total // 2 + v * own_blocks + i] = held[v, :, i * TILE : (i + 1) * TILE].astype(jnp.bfloat16)
        to[total // 2 + var_count * own_blocks] = last


def third_kernel(
    inner, outer, o_r, o_s, h_r, h_s, q, speeds, scaled, p, a_r, a_s, jd_r, jd_s, jo_r, jo_s, src_r, src_s,
    pull_table, margin_in, away_r, away_s, flux, x_r, x_s, rows_low, rows_high, out_r, out_s, margin, sems,
):
    fetch = pltpu.make_async_copy(margin_in, margin, sems.at[0])
    fetch.start()
    var_count, rows, layers, cells = a_r.shape
    total = margin.shape[2]
    own_blocks = cells // TILE
    spread = REACH + own_blocks + 1
    first_block = lax.axis_index("circ") * own_blocks
    lane = iota((8, TILE), 1)
    layer_all = iota((layers, cells), 0)
    end = total // 2 + var_count * own_blocks
    for x in (x_r, x_s):
        x[...] = jnp.zeros(x.shape, f32)
    odd = jnp.bitwise_and(lax.axis_index("span"), 1) == 1

    def low(n):
        return jnp.where(odd, inner[n].astype(f32), outer[n].astype(f32))

    def high(n):
        return jnp.where(odd, outer[n].astype(f32), inner[n].astype(f32))

    for side, to in ((low, rows_low), (high, rows_high)):
        for v in range(var_count):
            for i in range(own_blocks):
                to[v, :, i * TILE : (i + 1) * TILE] = side(total // 2 + v * own_blocks + i)
    ends = [low(end), high(end)]
    inside = [jnp.concatenate([x[8:9]] * own_blocks, axis=1) for x in ends]
    group = lax.rem(lax.shift_right_logical(lane, 3), rows)
    corner = jnp.where(group == 0, pltpu.roll(ends[0][0:8], (TILE - 8 * (rows - 1)) % TILE, 1), 0.0)
    corner = corner + jnp.where(group == rows - 1, pltpu.roll(ends[1][0:8], 8 * (rows - 1), 1), 0.0)
    columns = [
        lax.dot_general(corner, edge_pick(n, cells), (((0,), (0,)), ((), ())), preferred_element_type=f32)
        for n in range(2)
    ]

    def halo(side, b):
        both = side(lax.shift_right_logical(b, 1))
        return jnp.where(jnp.bitwise_and(b, 1) == 1, both[8:16], both[0:8])

    fields = (
        (o_r, h_r, a_r, jd_r, jo_r, src_r, x_r, out_r, layers - 1),
        (o_s, h_s, a_s, jd_s, jo_s, src_s, x_s, out_s, 0),
    )
    for n, (o, h, a, jd, jo, src, x, out, layer) in enumerate(fields):
        old = slice(n * layers, (n + 1) * layers)
        new = slice((2 + n) * layers, (3 + n) * layers)
        for v in range(var_count):
            for s in range(rows):
                value = o[v, s]
                if s == 0:
                    value = value + carry * rows_low[v, old, :]
                if s == rows - 1:
                    value = value + carry * rows_high[v, old, :]
                x[v * rows + s, 0:layers, :] = value
        for s in range(rows):
            state_row = [x[v * rows + s, 0:layers, :] for v in range(var_count)]
            for v in range(var_count):
                wide = x[v * rows + s]
                beside = (lanes_apart(wide) + layers_apart(wide))[0:layers]
                at = (v * rows + s) * 8
                beside = beside + h[v, s] + carry * columns[n][at : at + layers]
                if s > 0:
                    beside = beside + x[v * rows + s - 1, 0:layers, :]
                else:
                    beside = beside + inside[0] * (rows_low[v, new, :] + carry * a[v, 0])
                if s < rows - 1:
                    beside = beside + x[v * rows + s + 1, 0:layers, :]
                else:
                    beside = beside + inside[1] * (rows_high[v, new, :] + carry * a[v, rows - 1])
                res = jacobian_row(jd, jo, state_row, v, s, var_count) - coupling * beside - src[v, s]
                out[v, s] = state_row[v] - step_size * res
    fetch.wait()
    extra = []
    for s in range(rows):
        base = window(margin, s, first_block, total)
        own = []
        for t in range(spread - 2 + own_blocks):
            b = wrapped(base + t, total) if t < spread - 2 else first_block + t - (spread - 2)
            adjoint = p[s, t]
            if s == 0:
                adjoint = adjoint + carry * halo(low, b)
            if s == rows - 1:
                adjoint = adjoint + carry * halo(high, b)
            moved = flux_of(q[s, t], speeds[s, t], scaled[s, t], adjoint)
            if t < spread - 2:
                flux[s, t] = moved.astype(jnp.bfloat16).astype(f32)
            else:
                own.append(moved)
        pulls = [pull_row(lambda t: flux[s, t], pull_table, s, slot) for slot in range(own_blocks)]
        extra.append((step_size * jnp.concatenate(pulls, axis=1), -step_size * jnp.concatenate(own, axis=1)))

    copies = []
    for n, (out, away, layer) in enumerate(((out_r, away_r, layers - 1), (out_s, away_s, 0))):
        for s in range(rows):
            for v in range(var_count):
                out[v, s, layer : layer + 1, :] = out[v, s, layer : layer + 1, :] + extra[s][n][v : v + 1]
        copies.append(pltpu.make_async_copy(out, away, sems.at[1 + n]))
        copies[-1].start()
    for copy in copies:
        copy.wait()


def per_device(
    adjoint_rotor,
    adjoint_stator,
    jac_diag_rotor,
    jac_diag_stator,
    jac_off_rotor,
    jac_off_stator,
    source_rotor,
    source_stator,
    rotor_state,
    margin_block,
    face_count,
    margin_weight,
):
    var_count, rows, layers, cells = adjoint_rotor.shape
    own_blocks = cells // TILE
    total = margin_block.shape[1]
    spread = REACH + own_blocks + 1
    field = jax.ShapeDtypeStruct(adjoint_rotor.shape, f32)
    vmem = pl.BlockSpec(memory_space=pltpu.VMEM)
    smem = pl.BlockSpec(memory_space=pltpu.SMEM)
    anywhere = pl.BlockSpec(memory_space=pl.ANY)
    padded = pltpu.VMEM((TILE // 8, 8, cells), f32)

    margin = jnp.swapaxes(margin_block, 1, 2)
    arguments = (
        adjoint_rotor, adjoint_stator, jac_diag_rotor, jac_diag_stator, jac_off_rotor, jac_off_stator,
        source_rotor, source_stator, rotor_state, margin, face_count, margin_weight,
    )
    shapes = [jax.ShapeDtypeStruct(x.shape, x.dtype) for x in arguments]
    v_r, v_s, share, a_r, a_s, weights, margin, count = pl.pallas_call(
        first_kernel,
        out_shape=(
            field, field, jax.ShapeDtypeStruct((own_blocks, 64, TILE), jnp.bfloat16),
            shapes[0], shapes[1], shapes[11], shapes[9], shapes[10],
        ),
        in_specs=[pl.BlockSpec(memory_space=pltpu.HBM)] * 12,
        out_specs=(vmem,) * 8,
        scratch_shapes=[pltpu.VMEM(x.shape, x.dtype) for x in shapes[2:9]]
        + [padded] * 4
        + [pltpu.SemaphoreType.DMA((12,)), pltpu.VMEM((own_blocks, 3 * rows, 8, TILE), f32)],
        compiler_params=params,
        name="local_part",
    )(*[pltpu.with_memory_space_constraint(x, pltpu.HBM) for x in arguments])
    primal_table, pull_table = pl.pallas_call(
        table_kernel,
        out_shape=(
            jax.ShapeDtypeStruct((rows, spread + own_blocks + 2, margin_weight.shape[2], TILE), f32),
            jax.ShapeDtypeStruct((rows, own_blocks + 2, REACH, TILE), f32),
        ),
        in_specs=[vmem] + [smem] * 2,
        out_specs=(vmem,) * 2,
        compiler_params=params,
        name="weight_tables",
    )(weights, margin, count)
    members = lax.axis_size("circ")
    mine, masks = share, []
    mask = members // 2
    while mask > 0:
        other = lax.ppermute(mine, "circ", [(i, i ^ mask) for i in range(members)])
        if mask > 1:
            mine = jnp.concatenate([mine, other], axis=0)
            masks.append(mask)
        mask //= 2
    tiles = jax.ShapeDtypeStruct((total // 2 + var_count * own_blocks + 1, 16, TILE), jnp.bfloat16)
    listed = jax.ShapeDtypeStruct((rows, spread - 2 + own_blocks, 8, TILE), f32)
    o_r, o_s, h_r, h_s, q, speeds, scaled, p, inner, outer = pl.pallas_call(
        functools.partial(second_kernel, masks),
        out_shape=(field,) * 4 + (listed,) * 4 + (tiles,) * 2,
        in_specs=[vmem] * 8 + [anywhere],
        out_specs=(vmem,) * 10,
        scratch_shapes=[
            pltpu.VMEM((rows, spread, 8, TILE), f32),
            pltpu.VMEM((var_count, 4 * layers, cells), f32),
            pltpu.VMEM((8, TILE), f32),
            pltpu.VMEM((total, 3 * rows, 8, TILE), f32),
            pltpu.SMEM(margin.shape, jnp.int32),
            pltpu.SemaphoreType.DMA(()),
        ],
        compiler_params=params,
        name="interface_part",
    )(mine, other, v_r, v_s, a_r, a_s, primal_table, pull_table, margin)
    bands = lax.axis_size("span")
    near = [(i, i ^ 1) for i in range(bands)]
    far = [pair for i in range(1, bands - 1, 2) for pair in ((i, i + 1), (i + 1, i))]
    inner = lax.ppermute(inner, "span", near)
    outer = lax.ppermute(outer, "span", far)
    out_r, out_s = pl.pallas_call(
        third_kernel,
        out_shape=(field, field),
        in_specs=[vmem] * 19 + [anywhere],
        out_specs=(anywhere,) * 2,
        scratch_shapes=[
            pltpu.VMEM((rows, spread - 2, 8, TILE), f32),
            padded,
            padded,
            pltpu.VMEM((var_count, 4 * layers, cells), f32),
            pltpu.VMEM((var_count, 4 * layers, cells), f32),
            pltpu.VMEM(field.shape, f32),
            pltpu.VMEM(field.shape, f32),
            pltpu.SMEM(margin.shape, jnp.int32),
            pltpu.SemaphoreType.DMA((3,)),
        ],
        compiler_params=params,
        name="final_part",
    )(
        inner, outer, o_r, o_s, h_r, h_s, q, speeds, scaled, p, a_r, a_s, jac_diag_rotor, jac_diag_stator,
        jac_off_rotor, jac_off_stator, source_rotor, source_stator, pull_table, margin,
    )
    return (out_r, out_s)


def solution(mesh):
    field = P(None, "span", None, "circ")
    placed = (
        (field,) * 4
        + (P(None, None, "span", None, "circ"),) * 2
        + (field,) * 2
        + (P(None, "span", "circ"), P("span", None, None), P("span", None), P("span", None, None, None))
    )
    return jax.shard_map(
        per_device, mesh=mesh, in_specs=placed, out_specs=(field, field), check_vma=False
    )
```

```python
import functools

import jax
import jax.numpy as jnp
from jax import lax
from jax.experimental import pallas as pl
from jax.experimental.pallas import tpu as pltpu
from jax.sharding import PartitionSpec as P

step_size = 0.1
coupling = 0.2
carry = step_size * coupling
REACH = 8
TILE = 128
f32 = jnp.float32
params = pltpu.CompilerParams(vmem_limit_bytes=24 * 1024 * 1024)


def iota(shape, dim):
    return lax.broadcasted_iota(jnp.int32, shape, dim)


def wrapped(x, count):
    if count & (count - 1) == 0:
        return jnp.bitwise_and(x, count - 1)
    return lax.rem(x + 4 * count, count)


def lanes_apart(x):
    cells = x.shape[1]
    lane = iota(x.shape, 1)
    before = jnp.where(lane == 0, 0.0, pltpu.roll(x, 1, 1))
    after = jnp.where(lane == cells - 1, 0.0, pltpu.roll(x, cells - 1, 1))
    return before + after


def layers_apart(x):
    return pltpu.roll(x, 1, 0) + pltpu.roll(x, 7, 0)


def edge_pick(row, cells):
    at = iota((8, cells), 0)
    lane = iota((8, cells), 1)
    first = jnp.logical_and(at == row, lane == 0)
    last = jnp.logical_and(at == 4 + row, lane == cells - 1)
    return jnp.where(jnp.logical_or(first, last), 1.0, 0.0).astype(f32)


def split(x):
    high = x.astype(jnp.bfloat16).astype(f32)
    return high, x - high


def flux_parts(primal):
    square = primal * primal
    under = 6.0 + jnp.sum(square, axis=0, keepdims=True)
    return jnp.sqrt(1.0 + square), 0.5 * primal / under


def flux_of(primal, speeds, scaled, adjoint):
    return speeds * adjoint + scaled * jnp.sum(primal * adjoint, axis=0, keepdims=True)


def jacobian_row(diag, off, state, v, s, var_count):
    total = diag[v, s] * state[v]
    for w in range(var_count):
        total = total + off[w, v, s].astype(f32) * state[w]
    return total


def pull_row(flux, table, s, slot):
    acc = jnp.zeros((8, TILE), f32)
    for e in range(REACH):
        acc = acc + table[s, slot + 1, e : e + 1, :] * flux(slot + e)
    return acc


def window(margin, s, first_block, total):
    return first_block - margin[s, 0, 0] - 5 + 4 * total


def window_blocks(base, first_block, own_blocks, total):
    found = [wrapped(base - 1 + t, total) for t in range(REACH + own_blocks + 1)]
    sides = [wrapped(first_block - 1 + total, total), wrapped(first_block + own_blocks, total)]
    return found + [first_block + i for i in range(own_blocks)] + sides


def table_kernel(weights, margin, count, primal_table, pull_table):
    rows, total, entries, _ = weights.shape
    own_blocks = pull_table.shape[1] - 2
    first_block = lax.axis_index("circ") * own_blocks
    for s in range(rows):
        base = window(margin, s, first_block, total)
        blocks = window_blocks(base, first_block, own_blocks, total)
        entry = iota((entries, TILE), 0)
        for t, b in enumerate(blocks):
            primal_table[s, t] = jnp.where(entry < count[s, b], weights[s, b], 0.0)
        for slot in range(-1, own_blocks + 1):
            target = wrapped(first_block + slot + total, total)
            for e in range(REACH):
                b = blocks[slot + 1 + e]
                k = wrapped(target - margin[s, 0, b] + total, total)
                live = jnp.where(k < count[s, b], 1.0, 0.0).astype(f32)
                kept = jnp.minimum(k, entries - 1)
                pull_table[s, slot + 1, e : e + 1, :] = weights[s, b, pl.ds(kept, 1), :] * live


def first_kernel(*refs):
    outer, refs = refs[:12], refs[12:]
    v_r, v_s, out, a_r, a_s, weights, margin, count = refs[:8]
    jd_r, jd_s, jo_r, jo_s, src_r, src_s, state = refs[8:15]
    xs, sems, wide_out = refs[15:19], refs[19], refs[20]
    var_count, rows, layers, cells = a_r.shape
    own_blocks = cells // TILE
    inner = (a_r, a_s, jd_r, jd_s, jo_r, jo_s, src_r, src_s, state, margin, count, weights)
    copies = [pltpu.make_async_copy(x, y, sems.at[n]) for n, (x, y) in enumerate(zip(outer, inner))]
    for copy in copies:
        copy.start()
    wide_out[...] = jnp.zeros(wide_out.shape, f32)
    for x in xs:
        x[...] = jnp.zeros(x.shape, f32)
    for copy in copies:
        copy.wait()
    fields = ((a_r, jd_r, jo_r, src_r, v_r, xs[0], xs[2]), (a_s, jd_s, jo_s, src_s, v_s, xs[1], xs[3]))
    for a, jd, jo, src, partial, x_a, x_p in fields:
        for v in range(var_count):
            for s in range(rows):
                x_a[v * rows + s, 0:layers, :] = a[v, s]
        for s in range(rows):
            state_row = [a[v, s] for v in range(var_count)]
            for v in range(var_count):
                wide = x_a[v * rows + s]
                beside = (lanes_apart(wide) + layers_apart(wide))[0:layers]
                if s > 0:
                    beside = beside + a[v, s - 1]
                if s < rows - 1:
                    beside = beside + a[v, s + 1]
                res = jacobian_row(jd, jo, state_row, v, s, var_count) - coupling * beside - src[v, s]
                new = state_row[v] - step_size * res
                partial[v, s] = new
                x_p[v * rows + s, 0:layers, :] = new
    edges = jnp.zeros((8, TILE), f32)
    for q in range(4):
        flat = xs[q][...].reshape(TILE, cells)
        edges = edges + lax.dot_general(
            edge_pick(q, cells), flat, (((1,), (1,)), ((), ())), preferred_element_type=f32
        )
    for v in range(var_count):
        rotor = state[v].astype(f32)
        for s in range(rows):
            for i in range(own_blocks):
                cut = slice(i * TILE, (i + 1) * TILE)
                wide_out[i, s, v : v + 1, :] = rotor[s : s + 1, cut]
                wide_out[i, rows + s, v : v + 1, :] = a_s[v, s, 0:1, cut]
                wide_out[i, 2 * rows + s, v : v + 1, :] = v_s[v, s, 0:1, cut]
    row8 = iota((8, TILE), 0)
    filled = row8 < var_count
    for i in range(own_blocks):
        if i in (0, own_blocks - 1):
            side = 4 if i else 0
            for s in range(rows):
                wide_out[i, 2 * rows + s, 6:8, :] = edges[side + 2 * s : side + 2 * s + 2]
        groups = []
        for s in range(rows):
            p_high, p_rest = split(wide_out[i, rows + s])
            u_high, u_rest = split(wide_out[i, 2 * rows + s])
            groups.append((
                jnp.where(filled, wide_out[i, s], pltpu.roll(u_rest, 6, 0)),
                jnp.where(filled, p_high, pltpu.roll(u_rest, 4, 0)),
                jnp.where(filled, p_rest, pltpu.roll(u_rest, 2, 0)),
                u_high,
            ))
        for n in range(4):
            out[i, n * 16 : n * 16 + 16, :] = jnp.concatenate([x[n] for x in groups], axis=0).astype(jnp.bfloat16)


def second_kernel(
    masks, mine, other, v_r, v_s, a_r, a_s, primal_table, pull_table, margin_in,
    o_r, o_s, h_r, h_s, q_out, speeds_out, scaled_out, p_out, inner, outer, flux, held, spot, g, margin, sem,
):
    var_count, rows, layers, cells = a_r.shape
    fetch = pltpu.make_async_copy(margin_in, margin, sem)
    fetch.start()
    total = 2 * mine.shape[0]
    own_blocks = cells // TILE
    entries = primal_table.shape[2]
    spread = REACH + own_blocks + 1
    first_block = lax.axis_index("circ") * own_blocks
    row8 = iota((8, TILE), 0)
    lane = iota((8, TILE), 1)
    lane_all = iota((layers, cells), 1)
    layer_all = iota((layers, cells), 0)
    edge = jnp.logical_or(lane_all == 0, lane_all == cells - 1)
    left = wrapped(first_block - 1 + total, total)
    right = wrapped(first_block + own_blocks, total)

    filled = row8 < var_count
    here = lax.axis_index("circ")
    for at in range(total):
        half, part = divmod(at, total // 2)
        place, i = divmod(part, own_blocks)
        mask = half
        for n, m in enumerate(masks):
            mask ^= m if place >> n & 1 else 0
        b = jnp.bitwise_xor(here, mask) * own_blocks + i
        whole = other if half else mine
        tiles = [whole[part, n * 16 : n * 16 + 16, :].astype(f32) for n in range(4)]
        for s in range(rows):
            rotor, p_high, p_rest, u_high = [x[s * 8 : s * 8 + 8] for x in tiles]
            u_rest = jnp.where(
                row8 < 2, pltpu.roll(rotor, 2, 0), jnp.where(row8 < 4, pltpu.roll(p_high, 4, 0), pltpu.roll(p_rest, 6, 0))
            )
            g[b, s] = rotor
            g[b, rows + s] = p_high + p_rest
            g[b, 2 * rows + s] = u_high + jnp.where(filled, u_rest, 0.0)
    spot[0:2, :] = g[left, 2 * rows, 6:8, :]
    spot[2:4, :] = g[left, 2 * rows + 1, 6:8, :]
    spot[4:6, :] = g[right, 2 * rows, 6:8, :]
    spot[6:8, :] = g[right, 2 * rows + 1, 6:8, :]
    spots = spot[...]
    columns = [
        lax.dot_general(spots, edge_pick(q, cells), (((0,), (0,)), ((), ())), preferred_element_type=f32)
        for q in range(4)
    ]

    fetch.wait()

    def block(s, b, t):
        primal = jnp.zeros((8, TILE), f32)
        for k in range(entries):
            primal = primal + primal_table[s, t, k : k + 1, :] * g[margin[s, k, b], s]
        primal = jnp.where(filled, primal, 0.0)
        parts = flux_parts(primal)
        return (primal, *parts), flux_of(primal, *parts, g[b, rows + s])

    def keep(s, at, b, parts, moved):
        q_out[s, at], speeds_out[s, at], scaled_out[s, at] = parts
        p_out[s, at] = advanced(s, b, moved)

    def advanced(s, b, moved):
        place = lax.rem(b, own_blocks)
        before = jnp.where(place == 0, carry, 0.0).astype(f32)
        after = jnp.where(place == own_blocks - 1, carry, 0.0).astype(f32)
        low = pltpu.roll(g[wrapped(b - 1 + total, total), rows + s], 1, 1)
        high = pltpu.roll(g[wrapped(b + 1, total), rows + s], TILE - 1, 1)
        base = g[b, 2 * rows + s]
        base = base + jnp.where(lane == 0, low * before, 0.0) + jnp.where(lane == TILE - 1, high * after, 0.0)
        return base - step_size * moved

    for s in range(rows):
        base = window(margin, s, first_block, total)
        blocks = window_blocks(base, first_block, own_blocks, total)
        for t in range(spread):
            parts, moved = block(s, blocks[t], t)
            flux[s, t] = moved.astype(jnp.bfloat16).astype(f32)
            if 0 < t < spread - 1:
                keep(s, t - 1, blocks[t], parts, moved)
        own = []
        for i in range(own_blocks):
            parts, moved = block(s, first_block + i, spread + i)
            own.append(moved)
            keep(s, spread - 2 + i, first_block + i, parts, moved)
        blank = [jnp.zeros((8, TILE), f32)] * (own_blocks - 2)
        side_flux = [block(s, at, spread + own_blocks + n)[1] for n, at in enumerate((left, right))]
        pulls = [pull_row(lambda t: flux[s, t + 1], pull_table, s, slot) for slot in range(-1, own_blocks + 1)]

        def at_sides(low, high):
            return jnp.concatenate([pltpu.roll(low, 1, 1), *blank, pltpu.roll(high, TILE - 1, 1)], axis=1)

        pulled = step_size * jnp.concatenate(pulls[1:-1], axis=1)
        pulled_side = step_size * at_sides(pulls[0], pulls[-1])
        pushed = step_size * jnp.concatenate(own, axis=1)
        pushed_side = step_size * at_sides(*side_flux)
        for v in range(var_count):
            at = (v * rows + s) * 8
            cut = slice(at, at + layers)
            o_r[v, s] = (
                v_r[v, s] + carry * columns[0][cut] + jnp.where(layer_all == layers - 1, pulled[v : v + 1], 0.0)
            )
            o_s[v, s] = v_s[v, s] + carry * columns[1][cut] - jnp.where(layer_all == 0, pushed[v : v + 1], 0.0)
            h_r[v, s] = columns[2][cut] + jnp.where(
                edge, carry * a_r[v, s] + jnp.where(layer_all == layers - 1, pulled_side[v : v + 1], 0.0), 0.0
            )
            h_s[v, s] = columns[3][cut] + jnp.where(
                edge, carry * a_s[v, s] - jnp.where(layer_all == 0, pushed_side[v : v + 1], 0.0), 0.0
            )

    last = jnp.concatenate([spots, jnp.ones((8, TILE), f32)], axis=0).astype(jnp.bfloat16)
    odd = jnp.bitwise_and(lax.axis_index("span"), 1)
    for to, s in ((inner, (1 - odd) * (rows - 1)), (outer, odd * (rows - 1))):
        for j in range(total // 2):
            to[j] = jnp.concatenate([g[2 * j, rows + s], g[2 * j + 1, rows + s]], axis=0).astype(jnp.bfloat16)
        for v in range(var_count):
            for n, ref in enumerate((a_r, a_s, o_r, o_s)):
                held[v, n * layers : (n + 1) * layers, :] = ref[v, s]
            for i in range(own_blocks):
                to[total // 2 + v * own_blocks + i] = held[v, :, i * TILE : (i + 1) * TILE].astype(jnp.bfloat16)
        to[total // 2 + var_count * own_blocks] = last


def third_kernel(
    inner, outer, o_r, o_s, h_r, h_s, q, speeds, scaled, p, a_r, a_s, jd_r, jd_s, jo_r, jo_s, src_r, src_s,
    pull_table, margin_in, away_r, away_s, flux, x_r, x_s, rows_low, rows_high, out_r, out_s, margin, sems,
):
    fetch = pltpu.make_async_copy(margin_in, margin, sems.at[0])
    fetch.start()
    var_count, rows, layers, cells = a_r.shape
    total = margin.shape[2]
    own_blocks = cells // TILE
    spread = REACH + own_blocks + 1
    first_block = lax.axis_index("circ") * own_blocks
    lane = iota((8, TILE), 1)
    layer_all = iota((layers, cells), 0)
    end = total // 2 + var_count * own_blocks
    for x in (x_r, x_s):
        x[...] = jnp.zeros(x.shape, f32)
    odd = jnp.bitwise_and(lax.axis_index("span"), 1) == 1

    def low(n):
        return jnp.where(odd, inner[n].astype(f32), outer[n].astype(f32))

    def high(n):
        return jnp.where(odd, outer[n].astype(f32), inner[n].astype(f32))

    for side, to in ((low, rows_low), (high, rows_high)):
        for v in range(var_count):
            for i in range(own_blocks):
                to[v, :, i * TILE : (i + 1) * TILE] = side(total // 2 + v * own_blocks + i)
    ends = [low(end), high(end)]
    inside = [jnp.concatenate([x[8:9]] * own_blocks, axis=1) for x in ends]
    group = lax.rem(lax.shift_right_logical(lane, 3), rows)
    corner = jnp.where(group == 0, pltpu.roll(ends[0][0:8], (TILE - 8 * (rows - 1)) % TILE, 1), 0.0)
    corner = corner + jnp.where(group == rows - 1, pltpu.roll(ends[1][0:8], 8 * (rows - 1), 1), 0.0)
    columns = [
        lax.dot_general(corner, edge_pick(n, cells), (((0,), (0,)), ((), ())), preferred_element_type=f32)
        for n in range(2)
    ]

    def halo(side, b):
        both = side(lax.shift_right_logical(b, 1))
        return jnp.where(jnp.bitwise_and(b, 1) == 1, both[8:16], both[0:8])

    fields = (
        (o_r, h_r, a_r, jd_r, jo_r, src_r, x_r, out_r, layers - 1),
        (o_s, h_s, a_s, jd_s, jo_s, src_s, x_s, out_s, 0),
    )
    for n, (o, h, a, jd, jo, src, x, out, layer) in enumerate(fields):
        old = slice(n * layers, (n + 1) * layers)
        new = slice((2 + n) * layers, (3 + n) * layers)
        for v in range(var_count):
            for s in range(rows):
                value = o[v, s]
                if s == 0:
                    value = value + carry * rows_low[v, old, :]
                if s == rows - 1:
                    value = value + carry * rows_high[v, old, :]
                x[v * rows + s, 0:layers, :] = value
        for s in range(rows):
            state_row = [x[v * rows + s, 0:layers, :] for v in range(var_count)]
            for v in range(var_count):
                wide = x[v * rows + s]
                beside = (lanes_apart(wide) + layers_apart(wide))[0:layers]
                at = (v * rows + s) * 8
                beside = beside + h[v, s] + carry * columns[n][at : at + layers]
                if s > 0:
                    beside = beside + x[v * rows + s - 1, 0:layers, :]
                else:
                    beside = beside + inside[0] * (rows_low[v, new, :] + carry * a[v, 0])
                if s < rows - 1:
                    beside = beside + x[v * rows + s + 1, 0:layers, :]
                else:
                    beside = beside + inside[1] * (rows_high[v, new, :] + carry * a[v, rows - 1])
                res = jacobian_row(jd, jo, state_row, v, s, var_count) - coupling * beside - src[v, s]
                out[v, s] = state_row[v] - step_size * res
    fetch.wait()
    extra = []
    for s in range(rows):
        base = window(margin, s, first_block, total)
        own = []
        for t in range(spread - 2 + own_blocks):
            b = wrapped(base + t, total) if t < spread - 2 else first_block + t - (spread - 2)
            adjoint = p[s, t]
            if s == 0:
                adjoint = adjoint + carry * halo(low, b)
            if s == rows - 1:
                adjoint = adjoint + carry * halo(high, b)
            moved = flux_of(q[s, t], speeds[s, t], scaled[s, t], adjoint)
            if t < spread - 2:
                flux[s, t] = moved.astype(jnp.bfloat16).astype(f32)
            else:
                own.append(moved)
        pulls = [pull_row(lambda t: flux[s, t], pull_table, s, slot) for slot in range(own_blocks)]
        extra.append((step_size * jnp.concatenate(pulls, axis=1), -step_size * jnp.concatenate(own, axis=1)))

    copies = []
    for n, (out, away, layer) in enumerate(((out_r, away_r, layers - 1), (out_s, away_s, 0))):
        for s in range(rows):
            for v in range(var_count):
                out[v, s, layer : layer + 1, :] = out[v, s, layer : layer + 1, :] + extra[s][n][v : v + 1]
        copies.append(pltpu.make_async_copy(out, away, sems.at[1 + n]))
        copies[-1].start()
    for copy in copies:
        copy.wait()


def per_device(
    adjoint_rotor,
    adjoint_stator,
    jac_diag_rotor,
    jac_diag_stator,
    jac_off_rotor,
    jac_off_stator,
    source_rotor,
    source_stator,
    rotor_state,
    margin_block,
    face_count,
    margin_weight,
):
    var_count, rows, layers, cells = adjoint_rotor.shape
    own_blocks = cells // TILE
    total = margin_block.shape[1]
    spread = REACH + own_blocks + 1
    field = jax.ShapeDtypeStruct(adjoint_rotor.shape, f32)
    vmem = pl.BlockSpec(memory_space=pltpu.VMEM)
    smem = pl.BlockSpec(memory_space=pltpu.SMEM)
    anywhere = pl.BlockSpec(memory_space=pl.ANY)
    padded = pltpu.VMEM((TILE // 8, 8, cells), f32)

    margin = jnp.swapaxes(margin_block, 1, 2)
    arguments = (
        adjoint_rotor, adjoint_stator, jac_diag_rotor, jac_diag_stator, jac_off_rotor, jac_off_stator,
        source_rotor, source_stator, rotor_state, margin, face_count, margin_weight,
    )
    shapes = [jax.ShapeDtypeStruct(x.shape, x.dtype) for x in arguments]
    v_r, v_s, share, a_r, a_s, weights, margin, count = pl.pallas_call(
        first_kernel,
        out_shape=(
            field, field, jax.ShapeDtypeStruct((own_blocks, 64, TILE), jnp.bfloat16),
            shapes[0], shapes[1], shapes[11], shapes[9], shapes[10],
        ),
        in_specs=[pl.BlockSpec(memory_space=pltpu.HBM)] * 12,
        out_specs=(vmem,) * 8,
        scratch_shapes=[pltpu.VMEM(x.shape, x.dtype) for x in shapes[2:9]]
        + [padded] * 4
        + [pltpu.SemaphoreType.DMA((12,)), pltpu.VMEM((own_blocks, 3 * rows, 8, TILE), f32)],
        compiler_params=params,
        name="local_part",
    )(*[pltpu.with_memory_space_constraint(x, pltpu.HBM) for x in arguments])
    primal_table, pull_table = pl.pallas_call(
        table_kernel,
        out_shape=(
            jax.ShapeDtypeStruct((rows, spread + own_blocks + 2, margin_weight.shape[2], TILE), f32),
            jax.ShapeDtypeStruct((rows, own_blocks + 2, REACH, TILE), f32),
        ),
        in_specs=[vmem] + [smem] * 2,
        out_specs=(vmem,) * 2,
        compiler_params=params,
        name="weight_tables",
    )(weights, margin, count)
    members = lax.axis_size("circ")
    mine, masks = share, []
    mask = members // 2
    while mask > 0:
        hop = mask | 1
        other = lax.ppermute(mine, "circ", [(i, i ^ hop) for i in range(members)])
        if mask > 1:
            mine = jnp.concatenate([mine, other], axis=0)
            masks.append(hop)
        mask //= 2
    tiles = jax.ShapeDtypeStruct((total // 2 + var_count * own_blocks + 1, 16, TILE), jnp.bfloat16)
    listed = jax.ShapeDtypeStruct((rows, spread - 2 + own_blocks, 8, TILE), f32)
    o_r, o_s, h_r, h_s, q, speeds, scaled, p, inner, outer = pl.pallas_call(
        functools.partial(second_kernel, masks),
        out_shape=(field,) * 4 + (listed,) * 4 + (tiles,) * 2,
        in_specs=[vmem] * 8 + [anywhere],
        out_specs=(vmem,) * 10,
        scratch_shapes=[
            pltpu.VMEM((rows, spread, 8, TILE), f32),
            pltpu.VMEM((var_count, 4 * layers, cells), f32),
            pltpu.VMEM((8, TILE), f32),
            pltpu.VMEM((total, 3 * rows, 8, TILE), f32),
            pltpu.SMEM(margin.shape, jnp.int32),
            pltpu.SemaphoreType.DMA(()),
        ],
        compiler_params=params,
        name="interface_part",
    )(mine, other, v_r, v_s, a_r, a_s, primal_table, pull_table, margin)
    bands = lax.axis_size("span")
    near = [(i, i ^ 1) for i in range(bands)]
    far = [pair for i in range(1, bands - 1, 2) for pair in ((i, i + 1), (i + 1, i))]
    inner = lax.ppermute(inner, "span", near)
    outer = lax.ppermute(outer, "span", far)
    out_r, out_s = pl.pallas_call(
        third_kernel,
        out_shape=(field, field),
        in_specs=[vmem] * 19 + [anywhere],
        out_specs=(anywhere,) * 2,
        scratch_shapes=[
            pltpu.VMEM((rows, spread - 2, 8, TILE), f32),
            padded,
            padded,
            pltpu.VMEM((var_count, 4 * layers, cells), f32),
            pltpu.VMEM((var_count, 4 * layers, cells), f32),
            pltpu.VMEM(field.shape, f32),
            pltpu.VMEM(field.shape, f32),
            pltpu.SMEM(margin.shape, jnp.int32),
            pltpu.SemaphoreType.DMA((3,)),
        ],
        compiler_params=params,
        name="final_part",
    )(
        inner, outer, o_r, o_s, h_r, h_s, q, speeds, scaled, p, a_r, a_s, jac_diag_rotor, jac_diag_stator,
        jac_off_rotor, jac_off_stator, source_rotor, source_stator, pull_table, margin,
    )
    return (out_r, out_s)


def solution(mesh):
    field = P(None, "span", None, "circ")
    placed = (
        (field,) * 4
        + (P(None, None, "span", None, "circ"),) * 2
        + (field,) * 2
        + (P(None, "span", "circ"), P("span", None, None), P("span", None), P("span", None, None, None))
    )
    return jax.shard_map(
        per_device, mesh=mesh, in_specs=placed, out_specs=(field, field), check_vma=False
    )
```

```python
import functools

import jax
import jax.numpy as jnp
from jax import lax
from jax.experimental import pallas as pl
from jax.experimental.pallas import tpu as pltpu
from jax.sharding import PartitionSpec as P

step_size = 0.1
coupling = 0.2
carry = step_size * coupling
REACH = 8
TILE = 128
f32 = jnp.float32
params = pltpu.CompilerParams(vmem_limit_bytes=24 * 1024 * 1024)


def iota(shape, dim):
    return lax.broadcasted_iota(jnp.int32, shape, dim)


def wrapped(x, count):
    if count & (count - 1) == 0:
        return jnp.bitwise_and(x, count - 1)
    return lax.rem(x + 4 * count, count)


def lanes_apart(x):
    cells = x.shape[1]
    lane = iota(x.shape, 1)
    before = jnp.where(lane == 0, 0.0, pltpu.roll(x, 1, 1))
    after = jnp.where(lane == cells - 1, 0.0, pltpu.roll(x, cells - 1, 1))
    return before + after


def layers_apart(x):
    return pltpu.roll(x, 1, 0) + pltpu.roll(x, 7, 0)


def edge_pick(row, cells):
    at = iota((8, cells), 0)
    lane = iota((8, cells), 1)
    first = jnp.logical_and(at == row, lane == 0)
    last = jnp.logical_and(at == 4 + row, lane == cells - 1)
    return jnp.where(jnp.logical_or(first, last), 1.0, 0.0).astype(f32)


def split(x):
    high = x.astype(jnp.bfloat16).astype(f32)
    return high, x - high


def flux_parts(primal):
    square = primal * primal
    under = 6.0 + jnp.sum(square, axis=0, keepdims=True)
    return jnp.sqrt(1.0 + square), 0.5 * primal / under


def flux_of(primal, speeds, scaled, adjoint):
    return speeds * adjoint + scaled * jnp.sum(primal * adjoint, axis=0, keepdims=True)


def jacobian_row(diag, off, state, v, s, var_count):
    total = diag[v, s] * state[v]
    for w in range(var_count):
        total = total + off[w, v, s].astype(f32) * state[w]
    return total


def pull_row(flux, table, s, slot):
    acc = jnp.zeros((8, TILE), f32)
    for e in range(REACH):
        acc = acc + table[s, slot + 1, e : e + 1, :] * flux(slot + e)
    return acc


def window(margin, s, first_block, total):
    return first_block - margin[s, 0, 0] - 5 + 4 * total


def window_blocks(base, first_block, own_blocks, total):
    found = [wrapped(base - 1 + t, total) for t in range(REACH + own_blocks + 1)]
    sides = [wrapped(first_block - 1 + total, total), wrapped(first_block + own_blocks, total)]
    return found + [first_block + i for i in range(own_blocks)] + sides


def table_kernel(weights, margin, count, primal_table, pull_table):
    rows, total, entries, _ = weights.shape
    own_blocks = pull_table.shape[1] - 2
    first_block = lax.axis_index("circ") * own_blocks
    for s in range(rows):
        base = window(margin, s, first_block, total)
        blocks = window_blocks(base, first_block, own_blocks, total)
        entry = iota((entries, TILE), 0)
        for t, b in enumerate(blocks):
            primal_table[s, t] = jnp.where(entry < count[s, b], weights[s, b], 0.0)
        for slot in range(-1, own_blocks + 1):
            target = wrapped(first_block + slot + total, total)
            for e in range(REACH):
                b = blocks[slot + 1 + e]
                k = wrapped(target - margin[s, 0, b] + total, total)
                live = jnp.where(k < count[s, b], 1.0, 0.0).astype(f32)
                kept = jnp.minimum(k, entries - 1)
                pull_table[s, slot + 1, e : e + 1, :] = weights[s, b, pl.ds(kept, 1), :] * live


def first_kernel(*refs):
    outer, refs = refs[:12], refs[12:]
    v_r, v_s, out, a_r, a_s, weights, margin, count = refs[:8]
    jd_r, jd_s, jo_r, jo_s, src_r, src_s, state = refs[8:15]
    xs, sems, wide_out = refs[15:19], refs[19], refs[20]
    var_count, rows, layers, cells = a_r.shape
    own_blocks = cells // TILE
    inner = (a_r, a_s, jd_r, jd_s, jo_r, jo_s, src_r, src_s, state, margin, count, weights)
    copies = [pltpu.make_async_copy(x, y, sems.at[n]) for n, (x, y) in enumerate(zip(outer, inner))]
    for copy in copies:
        copy.start()
    wide_out[...] = jnp.zeros(wide_out.shape, f32)
    for x in xs:
        x[...] = jnp.zeros(x.shape, f32)
    for copy in copies:
        copy.wait()
    fields = ((a_r, jd_r, jo_r, src_r, v_r, xs[0], xs[2]), (a_s, jd_s, jo_s, src_s, v_s, xs[1], xs[3]))
    for a, jd, jo, src, partial, x_a, x_p in fields:
        for v in range(var_count):
            for s in range(rows):
                x_a[v * rows + s, 0:layers, :] = a[v, s]
        for s in range(rows):
            state_row = [a[v, s] for v in range(var_count)]
            for v in range(var_count):
                wide = x_a[v * rows + s]
                beside = (lanes_apart(wide) + layers_apart(wide))[0:layers]
                if s > 0:
                    beside = beside + a[v, s - 1]
                if s < rows - 1:
                    beside = beside + a[v, s + 1]
                res = jacobian_row(jd, jo, state_row, v, s, var_count) - coupling * beside - src[v, s]
                new = state_row[v] - step_size * res
                partial[v, s] = new
                x_p[v * rows + s, 0:layers, :] = new
    edges = jnp.zeros((8, TILE), f32)
    for q in range(4):
        flat = xs[q][...].reshape(TILE, cells)
        edges = edges + lax.dot_general(
            edge_pick(q, cells), flat, (((1,), (1,)), ((), ())), preferred_element_type=f32
        )
    for v in range(var_count):
        rotor = state[v].astype(f32)
        for s in range(rows):
            for i in range(own_blocks):
                cut = slice(i * TILE, (i + 1) * TILE)
                wide_out[i, s, v : v + 1, :] = rotor[s : s + 1, cut]
                wide_out[i, rows + s, v : v + 1, :] = a_s[v, s, 0:1, cut]
                wide_out[i, 2 * rows + s, v : v + 1, :] = v_s[v, s, 0:1, cut]
    row8 = iota((8, TILE), 0)
    filled = row8 < var_count
    for i in range(own_blocks):
        if i in (0, own_blocks - 1):
            side = 4 if i else 0
            for s in range(rows):
                wide_out[i, 2 * rows + s, 6:8, :] = edges[side + 2 * s : side + 2 * s + 2]
        groups = []
        for s in range(rows):
            p_high, p_rest = split(wide_out[i, rows + s])
            u_high, u_rest = split(wide_out[i, 2 * rows + s])
            groups.append((
                jnp.where(filled, wide_out[i, s], pltpu.roll(u_rest, 6, 0)),
                jnp.where(filled, p_high, pltpu.roll(u_rest, 4, 0)),
                jnp.where(filled, p_rest, pltpu.roll(u_rest, 2, 0)),
                u_high,
            ))
        for n in range(4):
            out[i, n * 16 : n * 16 + 16, :] = jnp.concatenate([x[n] for x in groups], axis=0).astype(jnp.bfloat16)


def second_kernel(
    masks, mine, other, v_r, v_s, a_r, a_s, primal_table, pull_table, margin_in,
    o_r, o_s, h_r, h_s, q_out, speeds_out, scaled_out, p_out, inner, outer, flux, held, spot, g, margin, sem,
):
    var_count, rows, layers, cells = a_r.shape
    fetch = pltpu.make_async_copy(margin_in, margin, sem)
    fetch.start()
    total = 2 * mine.shape[0]
    own_blocks = cells // TILE
    entries = primal_table.shape[2]
    spread = REACH + own_blocks + 1
    first_block = lax.axis_index("circ") * own_blocks
    row8 = iota((8, TILE), 0)
    lane = iota((8, TILE), 1)
    lane_all = iota((layers, cells), 1)
    layer_all = iota((layers, cells), 0)
    edge = jnp.logical_or(lane_all == 0, lane_all == cells - 1)
    left = wrapped(first_block - 1 + total, total)
    right = wrapped(first_block + own_blocks, total)

    filled = row8 < var_count
    here = lax.axis_index("circ")
    for at in range(total):
        half, part = divmod(at, total // 2)
        place, i = divmod(part, own_blocks)
        mask = half
        for n, m in enumerate(masks):
            mask ^= m if place >> n & 1 else 0
        b = jnp.bitwise_xor(here, mask) * own_blocks + i
        whole = other if half else mine
        tiles = [whole[part, n * 16 : n * 16 + 16, :].astype(f32) for n in range(4)]
        for s in range(rows):
            rotor, p_high, p_rest, u_high = [x[s * 8 : s * 8 + 8] for x in tiles]
            u_rest = jnp.where(
                row8 < 2, pltpu.roll(rotor, 2, 0), jnp.where(row8 < 4, pltpu.roll(p_high, 4, 0), pltpu.roll(p_rest, 6, 0))
            )
            g[b, s] = rotor
            g[b, rows + s] = p_high + p_rest
            g[b, 2 * rows + s] = u_high + jnp.where(filled, u_rest, 0.0)
    spot[0:2, :] = g[left, 2 * rows, 6:8, :]
    spot[2:4, :] = g[left, 2 * rows + 1, 6:8, :]
    spot[4:6, :] = g[right, 2 * rows, 6:8, :]
    spot[6:8, :] = g[right, 2 * rows + 1, 6:8, :]
    spots = spot[...]
    columns = [
        lax.dot_general(spots, edge_pick(q, cells), (((0,), (0,)), ((), ())), preferred_element_type=f32)
        for q in range(4)
    ]

    fetch.wait()

    def block(s, b, t):
        primal = jnp.zeros((8, TILE), f32)
        for k in range(entries):
            primal = primal + primal_table[s, t, k : k + 1, :] * g[margin[s, k, b], s]
        primal = jnp.where(filled, primal, 0.0)
        parts = flux_parts(primal)
        return (primal, *parts), flux_of(primal, *parts, g[b, rows + s])

    def keep(s, at, b, parts, moved):
        q_out[s, at], speeds_out[s, at], scaled_out[s, at] = parts
        p_out[s, at] = advanced(s, b, moved)

    def advanced(s, b, moved):
        place = lax.rem(b, own_blocks)
        before = jnp.where(place == 0, carry, 0.0).astype(f32)
        after = jnp.where(place == own_blocks - 1, carry, 0.0).astype(f32)
        low = pltpu.roll(g[wrapped(b - 1 + total, total), rows + s], 1, 1)
        high = pltpu.roll(g[wrapped(b + 1, total), rows + s], TILE - 1, 1)
        base = g[b, 2 * rows + s]
        base = base + jnp.where(lane == 0, low * before, 0.0) + jnp.where(lane == TILE - 1, high * after, 0.0)
        return base - step_size * moved

    for s in range(rows):
        base = window(margin, s, first_block, total)
        blocks = window_blocks(base, first_block, own_blocks, total)
        for t in range(spread):
            parts, moved = block(s, blocks[t], t)
            flux[s, t] = moved.astype(jnp.bfloat16).astype(f32)
            if 0 < t < spread - 1:
                keep(s, t - 1, blocks[t], parts, moved)
        own = []
        for i in range(own_blocks):
            parts, moved = block(s, first_block + i, spread + i)
            own.append(moved)
            keep(s, spread - 2 + i, first_block + i, parts, moved)
        blank = [jnp.zeros((8, TILE), f32)] * (own_blocks - 2)
        side_flux = [block(s, at, spread + own_blocks + n)[1] for n, at in enumerate((left, right))]
        pulls = [pull_row(lambda t: flux[s, t + 1], pull_table, s, slot) for slot in range(-1, own_blocks + 1)]

        def at_sides(low, high):
            return jnp.concatenate([pltpu.roll(low, 1, 1), *blank, pltpu.roll(high, TILE - 1, 1)], axis=1)

        pulled = step_size * jnp.concatenate(pulls[1:-1], axis=1)
        pulled_side = step_size * at_sides(pulls[0], pulls[-1])
        pushed = step_size * jnp.concatenate(own, axis=1)
        pushed_side = step_size * at_sides(*side_flux)
        for v in range(var_count):
            at = (v * rows + s) * 8
            cut = slice(at, at + layers)
            o_r[v, s] = (
                v_r[v, s] + carry * columns[0][cut] + jnp.where(layer_all == layers - 1, pulled[v : v + 1], 0.0)
            )
            o_s[v, s] = v_s[v, s] + carry * columns[1][cut] - jnp.where(layer_all == 0, pushed[v : v + 1], 0.0)
            h_r[v, s] = columns[2][cut] + jnp.where(
                edge, carry * a_r[v, s] + jnp.where(layer_all == layers - 1, pulled_side[v : v + 1], 0.0), 0.0
            )
            h_s[v, s] = columns[3][cut] + jnp.where(
                edge, carry * a_s[v, s] - jnp.where(layer_all == 0, pushed_side[v : v + 1], 0.0), 0.0
            )

    last = jnp.concatenate([spots, jnp.ones((8, TILE), f32)], axis=0).astype(jnp.bfloat16)
    odd = jnp.bitwise_and(lax.axis_index("span"), 1)
    for to, s in ((inner, (1 - odd) * (rows - 1)), (outer, odd * (rows - 1))):
        for j in range(total // 2):
            to[j] = jnp.concatenate([g[2 * j, rows + s], g[2 * j + 1, rows + s]], axis=0).astype(jnp.bfloat16)
        for v in range(var_count):
            for n, ref in enumerate((a_r, a_s, o_r, o_s)):
                held[v, n * layers : (n + 1) * layers, :] = ref[v, s]
            for i in range(own_blocks):
                to[total // 2 + v * own_blocks + i] = held[v, :, i * TILE : (i + 1) * TILE].astype(jnp.bfloat16)
        to[total // 2 + var_count * own_blocks] = last


def third_kernel(
    inner, outer, o_r, o_s, h_r, h_s, q, speeds, scaled, p, a_r, a_s, jd_r, jd_s, jo_r, jo_s, src_r, src_s,
    pull_table, margin_in, away_r, away_s, flux, x_r, x_s, rows_low, rows_high, out_r, out_s, margin, sems,
):
    fetch = pltpu.make_async_copy(margin_in, margin, sems.at[0])
    fetch.start()
    var_count, rows, layers, cells = a_r.shape
    total = margin.shape[2]
    own_blocks = cells // TILE
    spread = REACH + own_blocks + 1
    first_block = lax.axis_index("circ") * own_blocks
    lane = iota((8, TILE), 1)
    layer_all = iota((layers, cells), 0)
    end = total // 2 + var_count * own_blocks
    for x in (x_r, x_s):
        x[...] = jnp.zeros(x.shape, f32)
    odd = jnp.bitwise_and(lax.axis_index("span"), 1) == 1

    def low(n):
        return jnp.where(odd, inner[n].astype(f32), outer[n].astype(f32))

    def high(n):
        return jnp.where(odd, outer[n].astype(f32), inner[n].astype(f32))

    for side, to in ((low, rows_low), (high, rows_high)):
        for v in range(var_count):
            for i in range(own_blocks):
                to[v, :, i * TILE : (i + 1) * TILE] = side(total // 2 + v * own_blocks + i)
    ends = [low(end), high(end)]
    inside = [jnp.concatenate([x[8:9]] * own_blocks, axis=1) for x in ends]
    group = lax.rem(lax.shift_right_logical(lane, 3), rows)
    corner = jnp.where(group == 0, pltpu.roll(ends[0][0:8], (TILE - 8 * (rows - 1)) % TILE, 1), 0.0)
    corner = corner + jnp.where(group == rows - 1, pltpu.roll(ends[1][0:8], 8 * (rows - 1), 1), 0.0)
    columns = [
        lax.dot_general(corner, edge_pick(n, cells), (((0,), (0,)), ((), ())), preferred_element_type=f32)
        for n in range(2)
    ]

    def halo(side, b):
        both = side(lax.shift_right_logical(b, 1))
        return jnp.where(jnp.bitwise_and(b, 1) == 1, both[8:16], both[0:8])

    fields = (
        (o_r, h_r, a_r, jd_r, jo_r, src_r, x_r, out_r, layers - 1),
        (o_s, h_s, a_s, jd_s, jo_s, src_s, x_s, out_s, 0),
    )
    for n, (o, h, a, jd, jo, src, x, out, layer) in enumerate(fields):
        old = slice(n * layers, (n + 1) * layers)
        new = slice((2 + n) * layers, (3 + n) * layers)
        for v in range(var_count):
            for s in range(rows):
                value = o[v, s]
                if s == 0:
                    value = value + carry * rows_low[v, old, :]
                if s == rows - 1:
                    value = value + carry * rows_high[v, old, :]
                x[v * rows + s, 0:layers, :] = value
        for s in range(rows):
            state_row = [x[v * rows + s, 0:layers, :] for v in range(var_count)]
            for v in range(var_count):
                wide = x[v * rows + s]
                beside = (lanes_apart(wide) + layers_apart(wide))[0:layers]
                at = (v * rows + s) * 8
                beside = beside + h[v, s] + carry * columns[n][at : at + layers]
                if s > 0:
                    beside = beside + x[v * rows + s - 1, 0:layers, :]
                else:
                    beside = beside + inside[0] * (rows_low[v, new, :] + carry * a[v, 0])
                if s < rows - 1:
                    beside = beside + x[v * rows + s + 1, 0:layers, :]
                else:
                    beside = beside + inside[1] * (rows_high[v, new, :] + carry * a[v, rows - 1])
                res = jacobian_row(jd, jo, state_row, v, s, var_count) - coupling * beside - src[v, s]
                out[v, s] = state_row[v] - step_size * res
    fetch.wait()
    extra = []
    for s in range(rows):
        base = window(margin, s, first_block, total)
        own = []
        for t in range(spread - 2 + own_blocks):
            b = wrapped(base + t, total) if t < spread - 2 else first_block + t - (spread - 2)
            adjoint = p[s, t]
            if s == 0:
                adjoint = adjoint + carry * halo(low, b)
            if s == rows - 1:
                adjoint = adjoint + carry * halo(high, b)
            moved = flux_of(q[s, t], speeds[s, t], scaled[s, t], adjoint)
            if t < spread - 2:
                flux[s, t] = moved.astype(jnp.bfloat16).astype(f32)
            else:
                own.append(moved)
        pulls = [pull_row(lambda t: flux[s, t], pull_table, s, slot) for slot in range(own_blocks)]
        extra.append((step_size * jnp.concatenate(pulls, axis=1), -step_size * jnp.concatenate(own, axis=1)))

    copies = []
    for n, (out, away, layer) in enumerate(((out_r, away_r, layers - 1), (out_s, away_s, 0))):
        for s in range(rows):
            for v in range(var_count):
                out[v, s, layer : layer + 1, :] = out[v, s, layer : layer + 1, :] + extra[s][n][v : v + 1]
        copies.append(pltpu.make_async_copy(out, away, sems.at[1 + n]))
        copies[-1].start()
    for copy in copies:
        copy.wait()


def per_device(
    adjoint_rotor,
    adjoint_stator,
    jac_diag_rotor,
    jac_diag_stator,
    jac_off_rotor,
    jac_off_stator,
    source_rotor,
    source_stator,
    rotor_state,
    margin_block,
    face_count,
    margin_weight,
):
    var_count, rows, layers, cells = adjoint_rotor.shape
    own_blocks = cells // TILE
    total = margin_block.shape[1]
    spread = REACH + own_blocks + 1
    field = jax.ShapeDtypeStruct(adjoint_rotor.shape, f32)
    vmem = pl.BlockSpec(memory_space=pltpu.VMEM)
    smem = pl.BlockSpec(memory_space=pltpu.SMEM)
    anywhere = pl.BlockSpec(memory_space=pl.ANY)
    padded = pltpu.VMEM((TILE // 8, 8, cells), f32)

    margin = jnp.swapaxes(margin_block, 1, 2)
    arguments = (
        adjoint_rotor, adjoint_stator, jac_diag_rotor, jac_diag_stator, jac_off_rotor, jac_off_stator,
        source_rotor, source_stator, rotor_state, margin, face_count, margin_weight,
    )
    shapes = [jax.ShapeDtypeStruct(x.shape, x.dtype) for x in arguments]
    v_r, v_s, share, a_r, a_s, weights, margin, count = pl.pallas_call(
        first_kernel,
        out_shape=(
            field, field, jax.ShapeDtypeStruct((own_blocks, 64, TILE), jnp.bfloat16),
            shapes[0], shapes[1], shapes[11], shapes[9], shapes[10],
        ),
        in_specs=[pl.BlockSpec(memory_space=pltpu.HBM)] * 12,
        out_specs=(vmem,) * 8,
        scratch_shapes=[pltpu.VMEM(x.shape, x.dtype) for x in shapes[2:9]]
        + [padded] * 4
        + [pltpu.SemaphoreType.DMA((12,)), pltpu.VMEM((own_blocks, 3 * rows, 8, TILE), f32)],
        compiler_params=params,
        name="local_part",
    )(*[pltpu.with_memory_space_constraint(x, pltpu.HBM) for x in arguments])
    primal_table, pull_table = pl.pallas_call(
        table_kernel,
        out_shape=(
            jax.ShapeDtypeStruct((rows, spread + own_blocks + 2, margin_weight.shape[2], TILE), f32),
            jax.ShapeDtypeStruct((rows, own_blocks + 2, REACH, TILE), f32),
        ),
        in_specs=[vmem] + [smem] * 2,
        out_specs=(vmem,) * 2,
        compiler_params=params,
        name="weight_tables",
    )(weights, margin, count)
    members = lax.axis_size("circ")
    mine, masks = share, []
    mask = members // 2
    while mask > 0:
        hop = mask | 1
        other = lax.ppermute(mine, "circ", [(i, i ^ hop) for i in range(members)])
        if mask > 1:
            mine = jnp.concatenate([mine, other], axis=0)
            if not masks:
                mine, primal_table, pull_table = lax.optimization_barrier((mine, primal_table, pull_table))
            masks.append(hop)
        mask //= 2
    tiles = jax.ShapeDtypeStruct((total // 2 + var_count * own_blocks + 1, 16, TILE), jnp.bfloat16)
    listed = jax.ShapeDtypeStruct((rows, spread - 2 + own_blocks, 8, TILE), f32)
    o_r, o_s, h_r, h_s, q, speeds, scaled, p, inner, outer = pl.pallas_call(
        functools.partial(second_kernel, masks),
        out_shape=(field,) * 4 + (listed,) * 4 + (tiles,) * 2,
        in_specs=[vmem] * 8 + [anywhere],
        out_specs=(vmem,) * 10,
        scratch_shapes=[
            pltpu.VMEM((rows, spread, 8, TILE), f32),
            pltpu.VMEM((var_count, 4 * layers, cells), f32),
            pltpu.VMEM((8, TILE), f32),
            pltpu.VMEM((total, 3 * rows, 8, TILE), f32),
            pltpu.SMEM(margin.shape, jnp.int32),
            pltpu.SemaphoreType.DMA(()),
        ],
        compiler_params=params,
        name="interface_part",
    )(mine, other, v_r, v_s, a_r, a_s, primal_table, pull_table, margin)
    bands = lax.axis_size("span")
    near = [(i, i ^ 1) for i in range(bands)]
    far = [pair for i in range(1, bands - 1, 2) for pair in ((i, i + 1), (i + 1, i))]
    inner = lax.ppermute(inner, "span", near)
    outer = lax.ppermute(outer, "span", far)
    out_r, out_s = pl.pallas_call(
        third_kernel,
        out_shape=(field, field),
        in_specs=[vmem] * 19 + [anywhere],
        out_specs=(anywhere,) * 2,
        scratch_shapes=[
            pltpu.VMEM((rows, spread - 2, 8, TILE), f32),
            padded,
            padded,
            pltpu.VMEM((var_count, 4 * layers, cells), f32),
            pltpu.VMEM((var_count, 4 * layers, cells), f32),
            pltpu.VMEM(field.shape, f32),
            pltpu.VMEM(field.shape, f32),
            pltpu.SMEM(margin.shape, jnp.int32),
            pltpu.SemaphoreType.DMA((3,)),
        ],
        compiler_params=params,
        name="final_part",
    )(
        inner, outer, o_r, o_s, h_r, h_s, q, speeds, scaled, p, a_r, a_s, jac_diag_rotor, jac_diag_stator,
        jac_off_rotor, jac_off_stator, source_rotor, source_stator, pull_table, margin,
    )
    return (out_r, out_s)


def solution(mesh):
    field = P(None, "span", None, "circ")
    placed = (
        (field,) * 4
        + (P(None, None, "span", None, "circ"),) * 2
        + (field,) * 2
        + (P(None, "span", "circ"), P("span", None, None), P("span", None), P("span", None, None, None))
    )
    return jax.shard_map(
        per_device, mesh=mesh, in_specs=placed, out_specs=(field, field), check_vma=False
    )
```

```python
import functools

import jax
import jax.numpy as jnp
from jax import lax
from jax.experimental import pallas as pl
from jax.experimental.pallas import tpu as pltpu
from jax.sharding import PartitionSpec as P

step_size = 0.1
coupling = 0.2
carry = step_size * coupling
REACH = 8
TILE = 128
f32 = jnp.float32
params = pltpu.CompilerParams(vmem_limit_bytes=24 * 1024 * 1024)


def iota(shape, dim):
    return lax.broadcasted_iota(jnp.int32, shape, dim)


def wrapped(x, count):
    if count & (count - 1) == 0:
        return jnp.bitwise_and(x, count - 1)
    return lax.rem(x + 4 * count, count)


def lanes_apart(x):
    cells = x.shape[1]
    lane = iota(x.shape, 1)
    before = jnp.where(lane == 0, 0.0, pltpu.roll(x, 1, 1))
    after = jnp.where(lane == cells - 1, 0.0, pltpu.roll(x, cells - 1, 1))
    return before + after


def layers_apart(x):
    return pltpu.roll(x, 1, 0) + pltpu.roll(x, 7, 0)


def edge_pick(row, cells):
    at = iota((8, cells), 0)
    lane = iota((8, cells), 1)
    first = jnp.logical_and(at == row, lane == 0)
    last = jnp.logical_and(at == 4 + row, lane == cells - 1)
    return jnp.where(jnp.logical_or(first, last), 1.0, 0.0).astype(f32)


def split(x):
    high = x.astype(jnp.bfloat16).astype(f32)
    return high, x - high


def flux_parts(primal):
    square = primal * primal
    under = 6.0 + jnp.sum(square, axis=0, keepdims=True)
    return jnp.sqrt(1.0 + square), 0.5 * primal / under


def flux_of(primal, speeds, scaled, adjoint):
    return speeds * adjoint + scaled * jnp.sum(primal * adjoint, axis=0, keepdims=True)


def jacobian_row(diag, off, state, v, s, var_count):
    total = diag[v, s] * state[v]
    for w in range(var_count):
        total = total + off[w, v, s].astype(f32) * state[w]
    return total


def pull_row(flux, table, s, slot):
    acc = jnp.zeros((8, TILE), f32)
    for e in range(REACH):
        acc = acc + table[s, slot + 1, e : e + 1, :] * flux(slot + e)
    return acc


def window(margin, s, first_block, total):
    return first_block - margin[s, 0, 0] - 5 + 4 * total


def window_blocks(base, first_block, own_blocks, total):
    found = [wrapped(base - 1 + t, total) for t in range(REACH + own_blocks + 1)]
    sides = [wrapped(first_block - 1 + total, total), wrapped(first_block + own_blocks, total)]
    return found + [first_block + i for i in range(own_blocks)] + sides


def table_kernel(weights, margin, count, primal_table, pull_table):
    rows, total, entries, _ = weights.shape
    own_blocks = pull_table.shape[1] - 2
    first_block = lax.axis_index("circ") * own_blocks
    for s in range(rows):
        base = window(margin, s, first_block, total)
        blocks = window_blocks(base, first_block, own_blocks, total)
        entry = iota((entries, TILE), 0)
        for t, b in enumerate(blocks):
            primal_table[s, t] = jnp.where(entry < count[s, b], weights[s, b], 0.0)
        for slot in range(-1, own_blocks + 1):
            target = wrapped(first_block + slot + total, total)
            for e in range(REACH):
                b = blocks[slot + 1 + e]
                k = wrapped(target - margin[s, 0, b] + total, total)
                live = jnp.where(k < count[s, b], 1.0, 0.0).astype(f32)
                kept = jnp.minimum(k, entries - 1)
                pull_table[s, slot + 1, e : e + 1, :] = weights[s, b, pl.ds(kept, 1), :] * live


def first_kernel(*refs):
    outer, refs = refs[:12], refs[12:]
    v_r, v_s, out, a_r, a_s, weights, margin, count = refs[:8]
    jd_r, jd_s, jo_r, jo_s, src_r, src_s, state = refs[8:15]
    xs, sems, wide_out = refs[15:19], refs[19], refs[20]
    var_count, rows, layers, cells = a_r.shape
    own_blocks = cells // TILE
    inner = (a_r, a_s, jd_r, jd_s, jo_r, jo_s, src_r, src_s, state, margin, count, weights)
    copies = [pltpu.make_async_copy(x, y, sems.at[n]) for n, (x, y) in enumerate(zip(outer, inner))]
    for copy in copies:
        copy.start()
    wide_out[...] = jnp.zeros(wide_out.shape, f32)
    for x in xs:
        x[...] = jnp.zeros(x.shape, f32)
    for copy in copies[:9]:
        copy.wait()
    fields = ((a_r, jd_r, jo_r, src_r, v_r, xs[0], xs[2]), (a_s, jd_s, jo_s, src_s, v_s, xs[1], xs[3]))
    for a, jd, jo, src, partial, x_a, x_p in fields:
        for v in range(var_count):
            for s in range(rows):
                x_a[v * rows + s, 0:layers, :] = a[v, s]
        for s in range(rows):
            state_row = [a[v, s] for v in range(var_count)]
            for v in range(var_count):
                wide = x_a[v * rows + s]
                beside = (lanes_apart(wide) + layers_apart(wide))[0:layers]
                if s > 0:
                    beside = beside + a[v, s - 1]
                if s < rows - 1:
                    beside = beside + a[v, s + 1]
                res = jacobian_row(jd, jo, state_row, v, s, var_count) - coupling * beside - src[v, s]
                new = state_row[v] - step_size * res
                partial[v, s] = new
                x_p[v * rows + s, 0:layers, :] = new
    edges = jnp.zeros((8, TILE), f32)
    for q in range(4):
        flat = xs[q][...].reshape(TILE, cells)
        edges = edges + lax.dot_general(
            edge_pick(q, cells), flat, (((1,), (1,)), ((), ())), preferred_element_type=f32
        )
    for v in range(var_count):
        rotor = state[v].astype(f32)
        for s in range(rows):
            for i in range(own_blocks):
                cut = slice(i * TILE, (i + 1) * TILE)
                wide_out[i, s, v : v + 1, :] = rotor[s : s + 1, cut]
                wide_out[i, rows + s, v : v + 1, :] = a_s[v, s, 0:1, cut]
                wide_out[i, 2 * rows + s, v : v + 1, :] = v_s[v, s, 0:1, cut]
    row8 = iota((8, TILE), 0)
    filled = row8 < var_count
    for i in range(own_blocks):
        if i in (0, own_blocks - 1):
            side = 4 if i else 0
            for s in range(rows):
                wide_out[i, 2 * rows + s, 6:8, :] = edges[side + 2 * s : side + 2 * s + 2]
        groups = []
        for s in range(rows):
            p_high, p_rest = split(wide_out[i, rows + s])
            u_high, u_rest = split(wide_out[i, 2 * rows + s])
            groups.append((
                jnp.where(filled, wide_out[i, s], pltpu.roll(u_rest, 6, 0)),
                jnp.where(filled, p_high, pltpu.roll(u_rest, 4, 0)),
                jnp.where(filled, p_rest, pltpu.roll(u_rest, 2, 0)),
                u_high,
            ))
        for n in range(4):
            out[i, n * 16 : n * 16 + 16, :] = jnp.concatenate([x[n] for x in groups], axis=0).astype(jnp.bfloat16)
    for copy in copies[9:]:
        copy.wait()


def second_kernel(
    masks, mine, other, v_r, v_s, a_r, a_s, primal_table, pull_table, margin_in,
    o_r, o_s, h_r, h_s, q_out, speeds_out, scaled_out, p_out, inner, outer, flux, held, spot, g, margin, sem,
):
    var_count, rows, layers, cells = a_r.shape
    fetch = pltpu.make_async_copy(margin_in, margin, sem)
    fetch.start()
    total = 2 * mine.shape[0]
    own_blocks = cells // TILE
    entries = primal_table.shape[2]
    spread = REACH + own_blocks + 1
    first_block = lax.axis_index("circ") * own_blocks
    row8 = iota((8, TILE), 0)
    lane = iota((8, TILE), 1)
    lane_all = iota((layers, cells), 1)
    layer_all = iota((layers, cells), 0)
    edge = jnp.logical_or(lane_all == 0, lane_all == cells - 1)
    left = wrapped(first_block - 1 + total, total)
    right = wrapped(first_block + own_blocks, total)

    filled = row8 < var_count
    here = lax.axis_index("circ")
    for at in range(total):
        half, part = divmod(at, total // 2)
        place, i = divmod(part, own_blocks)
        mask = half
        for n, m in enumerate(masks):
            mask ^= m if place >> n & 1 else 0
        b = jnp.bitwise_xor(here, mask) * own_blocks + i
        whole = other if half else mine
        tiles = [whole[part, n * 16 : n * 16 + 16, :].astype(f32) for n in range(4)]
        for s in range(rows):
            rotor, p_high, p_rest, u_high = [x[s * 8 : s * 8 + 8] for x in tiles]
            u_rest = jnp.where(
                row8 < 2, pltpu.roll(rotor, 2, 0), jnp.where(row8 < 4, pltpu.roll(p_high, 4, 0), pltpu.roll(p_rest, 6, 0))
            )
            g[b, s] = rotor
            g[b, rows + s] = p_high + p_rest
            g[b, 2 * rows + s] = u_high + jnp.where(filled, u_rest, 0.0)
    spot[0:2, :] = g[left, 2 * rows, 6:8, :]
    spot[2:4, :] = g[left, 2 * rows + 1, 6:8, :]
    spot[4:6, :] = g[right, 2 * rows, 6:8, :]
    spot[6:8, :] = g[right, 2 * rows + 1, 6:8, :]
    spots = spot[...]
    columns = [
        lax.dot_general(spots, edge_pick(q, cells), (((0,), (0,)), ((), ())), preferred_element_type=f32)
        for q in range(4)
    ]

    fetch.wait()

    def block(s, b, t):
        primal = jnp.zeros((8, TILE), f32)
        for k in range(entries):
            primal = primal + primal_table[s, t, k : k + 1, :] * g[margin[s, k, b], s]
        primal = jnp.where(filled, primal, 0.0)
        parts = flux_parts(primal)
        return (primal, *parts), flux_of(primal, *parts, g[b, rows + s])

    def keep(s, at, b, parts, moved):
        q_out[s, at], speeds_out[s, at], scaled_out[s, at] = parts
        p_out[s, at] = advanced(s, b, moved)

    def advanced(s, b, moved):
        place = lax.rem(b, own_blocks)
        before = jnp.where(place == 0, carry, 0.0).astype(f32)
        after = jnp.where(place == own_blocks - 1, carry, 0.0).astype(f32)
        low = pltpu.roll(g[wrapped(b - 1 + total, total), rows + s], 1, 1)
        high = pltpu.roll(g[wrapped(b + 1, total), rows + s], TILE - 1, 1)
        base = g[b, 2 * rows + s]
        base = base + jnp.where(lane == 0, low * before, 0.0) + jnp.where(lane == TILE - 1, high * after, 0.0)
        return base - step_size * moved

    for s in range(rows):
        base = window(margin, s, first_block, total)
        blocks = window_blocks(base, first_block, own_blocks, total)
        for t in range(spread):
            parts, moved = block(s, blocks[t], t)
            flux[s, t] = moved.astype(jnp.bfloat16).astype(f32)
            if 0 < t < spread - 1:
                keep(s, t - 1, blocks[t], parts, moved)
        own = []
        for i in range(own_blocks):
            parts, moved = block(s, first_block + i, spread + i)
            own.append(moved)
            keep(s, spread - 2 + i, first_block + i, parts, moved)
        blank = [jnp.zeros((8, TILE), f32)] * (own_blocks - 2)
        side_flux = [block(s, at, spread + own_blocks + n)[1] for n, at in enumerate((left, right))]
        pulls = [pull_row(lambda t: flux[s, t + 1], pull_table, s, slot) for slot in range(-1, own_blocks + 1)]

        def at_sides(low, high):
            return jnp.concatenate([pltpu.roll(low, 1, 1), *blank, pltpu.roll(high, TILE - 1, 1)], axis=1)

        pulled = step_size * jnp.concatenate(pulls[1:-1], axis=1)
        pulled_side = step_size * at_sides(pulls[0], pulls[-1])
        pushed = step_size * jnp.concatenate(own, axis=1)
        pushed_side = step_size * at_sides(*side_flux)
        for v in range(var_count):
            at = (v * rows + s) * 8
            cut = slice(at, at + layers)
            o_r[v, s] = (
                v_r[v, s] + carry * columns[0][cut] + jnp.where(layer_all == layers - 1, pulled[v : v + 1], 0.0)
            )
            o_s[v, s] = v_s[v, s] + carry * columns[1][cut] - jnp.where(layer_all == 0, pushed[v : v + 1], 0.0)
            h_r[v, s] = columns[2][cut] + jnp.where(
                edge, carry * a_r[v, s] + jnp.where(layer_all == layers - 1, pulled_side[v : v + 1], 0.0), 0.0
            )
            h_s[v, s] = columns[3][cut] + jnp.where(
                edge, carry * a_s[v, s] - jnp.where(layer_all == 0, pushed_side[v : v + 1], 0.0), 0.0
            )

    last = jnp.concatenate([spots, jnp.ones((8, TILE), f32)], axis=0).astype(jnp.bfloat16)
    odd = jnp.bitwise_and(lax.axis_index("span"), 1)
    for to, s in ((inner, (1 - odd) * (rows - 1)), (outer, odd * (rows - 1))):
        for j in range(total // 2):
            to[j] = jnp.concatenate([g[2 * j, rows + s], g[2 * j + 1, rows + s]], axis=0).astype(jnp.bfloat16)
        for v in range(var_count):
            for n, ref in enumerate((a_r, a_s, o_r, o_s)):
                held[v, n * layers : (n + 1) * layers, :] = ref[v, s]
            for i in range(own_blocks):
                to[total // 2 + v * own_blocks + i] = held[v, :, i * TILE : (i + 1) * TILE].astype(jnp.bfloat16)
        to[total // 2 + var_count * own_blocks] = last


def third_kernel(
    ahead, outer, behind, o_r, o_s, h_r, h_s, q, speeds, scaled, p, a_r, a_s, jd_r, jd_s, jo_r, jo_s, src_r, src_s,
    pull_table, margin_in, away_r, away_s, flux, x_r, x_s, rows_low, rows_high, out_r, out_s, margin, sems,
):
    fetch = pltpu.make_async_copy(margin_in, margin, sems.at[0])
    fetch.start()
    var_count, rows, layers, cells = a_r.shape
    total = margin.shape[2]
    own_blocks = cells // TILE
    spread = REACH + own_blocks + 1
    first_block = lax.axis_index("circ") * own_blocks
    lane = iota((8, TILE), 1)
    layer_all = iota((layers, cells), 0)
    end = total // 2 + var_count * own_blocks
    for x in (x_r, x_s):
        x[...] = jnp.zeros(x.shape, f32)
    odd = jnp.bitwise_and(lax.axis_index("span"), 1) == 1

    def inner(n):
        return ahead[n].astype(f32) + behind[n].astype(f32)

    def low(n):
        return jnp.where(odd, inner(n), outer[n].astype(f32))

    def high(n):
        return jnp.where(odd, outer[n].astype(f32), inner(n))

    for side, to in ((low, rows_low), (high, rows_high)):
        for v in range(var_count):
            for i in range(own_blocks):
                to[v, :, i * TILE : (i + 1) * TILE] = side(total // 2 + v * own_blocks + i)
    ends = [low(end), high(end)]
    inside = [jnp.concatenate([x[8:9]] * own_blocks, axis=1) for x in ends]
    group = lax.rem(lax.shift_right_logical(lane, 3), rows)
    corner = jnp.where(group == 0, pltpu.roll(ends[0][0:8], (TILE - 8 * (rows - 1)) % TILE, 1), 0.0)
    corner = corner + jnp.where(group == rows - 1, pltpu.roll(ends[1][0:8], 8 * (rows - 1), 1), 0.0)
    columns = [
        lax.dot_general(corner, edge_pick(n, cells), (((0,), (0,)), ((), ())), preferred_element_type=f32)
        for n in range(2)
    ]

    def halo(side, b):
        both = side(lax.shift_right_logical(b, 1))
        return jnp.where(jnp.bitwise_and(b, 1) == 1, both[8:16], both[0:8])

    fields = (
        (o_r, h_r, a_r, jd_r, jo_r, src_r, x_r, out_r, layers - 1),
        (o_s, h_s, a_s, jd_s, jo_s, src_s, x_s, out_s, 0),
    )
    for n, (o, h, a, jd, jo, src, x, out, layer) in enumerate(fields):
        old = slice(n * layers, (n + 1) * layers)
        new = slice((2 + n) * layers, (3 + n) * layers)
        for v in range(var_count):
            for s in range(rows):
                value = o[v, s]
                if s == 0:
                    value = value + carry * rows_low[v, old, :]
                if s == rows - 1:
                    value = value + carry * rows_high[v, old, :]
                x[v * rows + s, 0:layers, :] = value
        for s in range(rows):
            state_row = [x[v * rows + s, 0:layers, :] for v in range(var_count)]
            for v in range(var_count):
                wide = x[v * rows + s]
                beside = (lanes_apart(wide) + layers_apart(wide))[0:layers]
                at = (v * rows + s) * 8
                beside = beside + h[v, s] + carry * columns[n][at : at + layers]
                if s > 0:
                    beside = beside + x[v * rows + s - 1, 0:layers, :]
                else:
                    beside = beside + inside[0] * (rows_low[v, new, :] + carry * a[v, 0])
                if s < rows - 1:
                    beside = beside + x[v * rows + s + 1, 0:layers, :]
                else:
                    beside = beside + inside[1] * (rows_high[v, new, :] + carry * a[v, rows - 1])
                res = jacobian_row(jd, jo, state_row, v, s, var_count) - coupling * beside - src[v, s]
                out[v, s] = state_row[v] - step_size * res
    fetch.wait()
    extra = []
    for s in range(rows):
        base = window(margin, s, first_block, total)
        own = []
        for t in range(spread - 2 + own_blocks):
            b = wrapped(base + t, total) if t < spread - 2 else first_block + t - (spread - 2)
            adjoint = p[s, t]
            if s == 0:
                adjoint = adjoint + carry * halo(low, b)
            if s == rows - 1:
                adjoint = adjoint + carry * halo(high, b)
            moved = flux_of(q[s, t], speeds[s, t], scaled[s, t], adjoint)
            if t < spread - 2:
                flux[s, t] = moved.astype(jnp.bfloat16).astype(f32)
            else:
                own.append(moved)
        pulls = [pull_row(lambda t: flux[s, t], pull_table, s, slot) for slot in range(own_blocks)]
        extra.append((step_size * jnp.concatenate(pulls, axis=1), -step_size * jnp.concatenate(own, axis=1)))

    copies = []
    for n, (out, away, layer) in enumerate(((out_r, away_r, layers - 1), (out_s, away_s, 0))):
        for s in range(rows):
            for v in range(var_count):
                out[v, s, layer : layer + 1, :] = out[v, s, layer : layer + 1, :] + extra[s][n][v : v + 1]
        copies.append(pltpu.make_async_copy(out, away, sems.at[1 + n]))
        copies[-1].start()
    for copy in copies:
        copy.wait()


def per_device(
    adjoint_rotor,
    adjoint_stator,
    jac_diag_rotor,
    jac_diag_stator,
    jac_off_rotor,
    jac_off_stator,
    source_rotor,
    source_stator,
    rotor_state,
    margin_block,
    face_count,
    margin_weight,
):
    var_count, rows, layers, cells = adjoint_rotor.shape
    own_blocks = cells // TILE
    total = margin_block.shape[1]
    spread = REACH + own_blocks + 1
    field = jax.ShapeDtypeStruct(adjoint_rotor.shape, f32)
    vmem = pl.BlockSpec(memory_space=pltpu.VMEM)
    smem = pl.BlockSpec(memory_space=pltpu.SMEM)
    anywhere = pl.BlockSpec(memory_space=pl.ANY)
    padded = pltpu.VMEM((TILE // 8, 8, cells), f32)

    margin = jnp.swapaxes(margin_block, 1, 2)
    arguments = (
        adjoint_rotor, adjoint_stator, jac_diag_rotor, jac_diag_stator, jac_off_rotor, jac_off_stator,
        source_rotor, source_stator, rotor_state, margin, face_count, margin_weight,
    )
    shapes = [jax.ShapeDtypeStruct(x.shape, x.dtype) for x in arguments]
    v_r, v_s, share, a_r, a_s, weights, margin, count = pl.pallas_call(
        first_kernel,
        out_shape=(
            field, field, jax.ShapeDtypeStruct((own_blocks, 64, TILE), jnp.bfloat16),
            shapes[0], shapes[1], shapes[11], shapes[9], shapes[10],
        ),
        in_specs=[pl.BlockSpec(memory_space=pltpu.HBM)] * 12,
        out_specs=(vmem,) * 8,
        scratch_shapes=[pltpu.VMEM(x.shape, x.dtype) for x in shapes[2:9]]
        + [padded] * 4
        + [pltpu.SemaphoreType.DMA((12,)), pltpu.VMEM((own_blocks, 3 * rows, 8, TILE), f32)],
        compiler_params=params,
        name="local_part",
    )(*[pltpu.with_memory_space_constraint(x, pltpu.HBM) for x in arguments])
    primal_table, pull_table = pl.pallas_call(
        table_kernel,
        out_shape=(
            jax.ShapeDtypeStruct((rows, spread + own_blocks + 2, margin_weight.shape[2], TILE), f32),
            jax.ShapeDtypeStruct((rows, own_blocks + 2, REACH, TILE), f32),
        ),
        in_specs=[vmem] + [smem] * 2,
        out_specs=(vmem,) * 2,
        compiler_params=params,
        name="weight_tables",
    )(weights, margin, count)
    members = lax.axis_size("circ")
    mine, masks = share, []
    mask = members // 2
    while mask > 0:
        hop = mask | 1
        other = lax.ppermute(mine, "circ", [(i, i ^ hop) for i in range(members)])
        if mask > 1:
            mine = jnp.concatenate([mine, other], axis=0)
            if not masks:
                mine, primal_table, pull_table = lax.optimization_barrier((mine, primal_table, pull_table))
            masks.append(hop)
        mask //= 2
    tiles = jax.ShapeDtypeStruct((total // 2 + var_count * own_blocks + 1, 16, TILE), jnp.bfloat16)
    listed = jax.ShapeDtypeStruct((rows, spread - 2 + own_blocks, 8, TILE), f32)
    o_r, o_s, h_r, h_s, q, speeds, scaled, p, inner, outer = pl.pallas_call(
        functools.partial(second_kernel, masks),
        out_shape=(field,) * 4 + (listed,) * 4 + (tiles,) * 2,
        in_specs=[vmem] * 8 + [anywhere],
        out_specs=(vmem,) * 10,
        scratch_shapes=[
            pltpu.VMEM((rows, spread, 8, TILE), f32),
            pltpu.VMEM((var_count, 4 * layers, cells), f32),
            pltpu.VMEM((8, TILE), f32),
            pltpu.VMEM((total, 3 * rows, 8, TILE), f32),
            pltpu.SMEM(margin.shape, jnp.int32),
            pltpu.SemaphoreType.DMA(()),
        ],
        compiler_params=params,
        name="interface_part",
    )(mine, other, v_r, v_s, a_r, a_s, primal_table, pull_table, margin)
    bands = lax.axis_size("span")
    near = [(i, i ^ 1) for i in range(bands)]
    far = [pair for i in range(1, bands - 1, 2) for pair in ((i, i + 1), (i + 1, i))]
    to_middle = [(i, j) for i, j in near if i % 4 in (0, 3)]
    from_middle = [(i, j) for i, j in near if i % 4 in (1, 2)]
    ahead = lax.ppermute(inner, "span", to_middle)
    outer = lax.ppermute(outer, "span", far)
    behind = lax.ppermute(inner, "span", from_middle)
    out_r, out_s = pl.pallas_call(
        third_kernel,
        out_shape=(field, field),
        in_specs=[vmem] * 20 + [anywhere],
        out_specs=(anywhere,) * 2,
        scratch_shapes=[
            pltpu.VMEM((rows, spread - 2, 8, TILE), f32),
            padded,
            padded,
            pltpu.VMEM((var_count, 4 * layers, cells), f32),
            pltpu.VMEM((var_count, 4 * layers, cells), f32),
            pltpu.VMEM(field.shape, f32),
            pltpu.VMEM(field.shape, f32),
            pltpu.SMEM(margin.shape, jnp.int32),
            pltpu.SemaphoreType.DMA((3,)),
        ],
        compiler_params=params,
        name="final_part",
    )(
        ahead, outer, behind, o_r, o_s, h_r, h_s, q, speeds, scaled, p, a_r, a_s, jac_diag_rotor, jac_diag_stator,
        jac_off_rotor, jac_off_stator, source_rotor, source_stator, pull_table, margin,
    )
    return (out_r, out_s)


def solution(mesh):
    field = P(None, "span", None, "circ")
    placed = (
        (field,) * 4
        + (P(None, None, "span", None, "circ"),) * 2
        + (field,) * 2
        + (P(None, "span", "circ"), P("span", None, None), P("span", None), P("span", None, None, None))
    )
    return jax.shard_map(
        per_device, mesh=mesh, in_specs=placed, out_specs=(field, field), check_vma=False
    )
```

```python
import functools

import jax
import jax.numpy as jnp
from jax import lax
from jax.experimental import pallas as pl
from jax.experimental.pallas import tpu as pltpu
from jax.sharding import PartitionSpec as P

step_size = 0.1
coupling = 0.2
carry = step_size * coupling
REACH = 8
TILE = 128
f32 = jnp.float32
params = pltpu.CompilerParams(vmem_limit_bytes=24 * 1024 * 1024)


def iota(shape, dim):
    return lax.broadcasted_iota(jnp.int32, shape, dim)


def wrapped(x, count):
    if count & (count - 1) == 0:
        return jnp.bitwise_and(x, count - 1)
    return lax.rem(x + 4 * count, count)


def lanes_apart(x):
    cells = x.shape[1]
    lane = iota(x.shape, 1)
    before = jnp.where(lane == 0, 0.0, pltpu.roll(x, 1, 1))
    after = jnp.where(lane == cells - 1, 0.0, pltpu.roll(x, cells - 1, 1))
    return before + after


def layers_apart(x):
    return pltpu.roll(x, 1, 0) + pltpu.roll(x, 7, 0)


def edge_pick(row, cells):
    at = iota((8, cells), 0)
    lane = iota((8, cells), 1)
    first = jnp.logical_and(at == row, lane == 0)
    last = jnp.logical_and(at == 4 + row, lane == cells - 1)
    return jnp.where(jnp.logical_or(first, last), 1.0, 0.0).astype(f32)


def split(x):
    high = x.astype(jnp.bfloat16).astype(f32)
    return high, x - high


def flux_parts(primal):
    square = primal * primal
    under = 6.0 + jnp.sum(square, axis=0, keepdims=True)
    return jnp.sqrt(1.0 + square), 0.5 * primal / under


def flux_of(primal, speeds, scaled, adjoint):
    return speeds * adjoint + scaled * jnp.sum(primal * adjoint, axis=0, keepdims=True)


def jacobian_row(diag, off, state, v, s, var_count):
    total = diag[v, s] * state[v]
    for w in range(var_count):
        total = total + off[w, v, s].astype(f32) * state[w]
    return total


def pull_row(flux, table, s, slot):
    acc = jnp.zeros((8, TILE), f32)
    for e in range(REACH):
        acc = acc + table[s, slot + 1, e : e + 1, :] * flux(slot + e)
    return acc


def window(margin, s, first_block, total):
    return first_block - margin[s, 0, 0] - 5 + 4 * total


def window_blocks(base, first_block, own_blocks, total):
    found = [wrapped(base - 1 + t, total) for t in range(REACH + own_blocks + 1)]
    sides = [wrapped(first_block - 1 + total, total), wrapped(first_block + own_blocks, total)]
    return found + [first_block + i for i in range(own_blocks)] + sides


def table_kernel(weights, margin, count, primal_table, pull_table):
    rows, total, entries, _ = weights.shape
    own_blocks = pull_table.shape[1] - 2
    first_block = lax.axis_index("circ") * own_blocks
    for s in range(rows):
        base = window(margin, s, first_block, total)
        blocks = window_blocks(base, first_block, own_blocks, total)
        entry = iota((entries, TILE), 0)
        for t, b in enumerate(blocks):
            primal_table[s, t] = jnp.where(entry < count[s, b], weights[s, b], 0.0)
        for slot in range(-1, own_blocks + 1):
            target = wrapped(first_block + slot + total, total)
            for e in range(REACH):
                b = blocks[slot + 1 + e]
                k = wrapped(target - margin[s, 0, b] + total, total)
                live = jnp.where(k < count[s, b], 1.0, 0.0).astype(f32)
                kept = jnp.minimum(k, entries - 1)
                pull_table[s, slot + 1, e : e + 1, :] = weights[s, b, pl.ds(kept, 1), :] * live


def first_kernel(*refs):
    outer, refs = refs[:12], refs[12:]
    v_r, v_s, out, a_r, a_s, weights, margin, count = refs[:8]
    jd_r, jd_s, jo_r, jo_s, src_r, src_s, state = refs[8:15]
    xs, sems, wide_out = refs[15:19], refs[19], refs[20]
    var_count, rows, layers, cells = a_r.shape
    own_blocks = cells // TILE
    inner = (a_r, a_s, jd_r, jd_s, jo_r, jo_s, src_r, src_s, state, margin, count, weights)
    copies = [pltpu.make_async_copy(x, y, sems.at[n]) for n, (x, y) in enumerate(zip(outer, inner))]
    for copy in copies:
        copy.start()
    wide_out[...] = jnp.zeros(wide_out.shape, f32)
    for x in xs:
        x[...] = jnp.zeros(x.shape, f32)
    for copy in copies:
        copy.wait()
    fields = ((a_r, jd_r, jo_r, src_r, v_r, xs[0], xs[2]), (a_s, jd_s, jo_s, src_s, v_s, xs[1], xs[3]))
    for a, jd, jo, src, partial, x_a, x_p in fields:
        for v in range(var_count):
            for s in range(rows):
                x_a[v * rows + s, 0:layers, :] = a[v, s]
        for s in range(rows):
            state_row = [a[v, s] for v in range(var_count)]
            for v in range(var_count):
                wide = x_a[v * rows + s]
                beside = (lanes_apart(wide) + layers_apart(wide))[0:layers]
                if s > 0:
                    beside = beside + a[v, s - 1]
                if s < rows - 1:
                    beside = beside + a[v, s + 1]
                res = jacobian_row(jd, jo, state_row, v, s, var_count) - coupling * beside - src[v, s]
                new = state_row[v] - step_size * res
                partial[v, s] = new
                x_p[v * rows + s, 0:layers, :] = new
    edges = jnp.zeros((8, TILE), f32)
    for q in range(4):
        flat = xs[q][...].reshape(TILE, cells)
        edges = edges + lax.dot_general(
            edge_pick(q, cells), flat, (((1,), (1,)), ((), ())), preferred_element_type=f32
        )
    for v in range(var_count):
        rotor = state[v].astype(f32)
        for s in range(rows):
            for i in range(own_blocks):
                cut = slice(i * TILE, (i + 1) * TILE)
                wide_out[i, s, v : v + 1, :] = rotor[s : s + 1, cut]
                wide_out[i, rows + s, v : v + 1, :] = a_s[v, s, 0:1, cut]
                wide_out[i, 2 * rows + s, v : v + 1, :] = v_s[v, s, 0:1, cut]
    row8 = iota((8, TILE), 0)
    filled = row8 < var_count
    for i in range(own_blocks):
        if i in (0, own_blocks - 1):
            side = 4 if i else 0
            for s in range(rows):
                wide_out[i, 2 * rows + s, 6:8, :] = edges[side + 2 * s : side + 2 * s + 2]
        groups = []
        for s in range(rows):
            p_high, p_rest = split(wide_out[i, rows + s])
            u_high, u_rest = split(wide_out[i, 2 * rows + s])
            groups.append((
                jnp.where(filled, wide_out[i, s], pltpu.roll(u_rest, 6, 0)),
                jnp.where(filled, p_high, pltpu.roll(u_rest, 4, 0)),
                jnp.where(filled, p_rest, pltpu.roll(u_rest, 2, 0)),
                u_high,
            ))
        for n in range(4):
            out[i, n * 16 : n * 16 + 16, :] = jnp.concatenate([x[n] for x in groups], axis=0).astype(jnp.bfloat16)


def second_kernel(
    masks, mine, other, v_r, v_s, a_r, a_s, primal_table, pull_table, margin_in,
    o_r, o_s, h_r, h_s, q_out, speeds_out, scaled_out, p_out, inner, outer, flux, held, spot, g, margin, sem,
):
    var_count, rows, layers, cells = a_r.shape
    fetch = pltpu.make_async_copy(margin_in, margin, sem)
    fetch.start()
    total = 2 * mine.shape[0]
    own_blocks = cells // TILE
    entries = primal_table.shape[2]
    spread = REACH + own_blocks + 1
    first_block = lax.axis_index("circ") * own_blocks
    row8 = iota((8, TILE), 0)
    lane = iota((8, TILE), 1)
    lane_all = iota((layers, cells), 1)
    layer_all = iota((layers, cells), 0)
    edge = jnp.logical_or(lane_all == 0, lane_all == cells - 1)
    left = wrapped(first_block - 1 + total, total)
    right = wrapped(first_block + own_blocks, total)

    filled = row8 < var_count
    here = lax.axis_index("circ")
    for at in range(total):
        half, part = divmod(at, total // 2)
        place, i = divmod(part, own_blocks)
        mask = half
        for n, m in enumerate(masks):
            mask ^= m if place >> n & 1 else 0
        b = jnp.bitwise_xor(here, mask) * own_blocks + i
        whole = other if half else mine
        tiles = [whole[part, n * 16 : n * 16 + 16, :].astype(f32) for n in range(4)]
        for s in range(rows):
            rotor, p_high, p_rest, u_high = [x[s * 8 : s * 8 + 8] for x in tiles]
            u_rest = jnp.where(
                row8 < 2, pltpu.roll(rotor, 2, 0), jnp.where(row8 < 4, pltpu.roll(p_high, 4, 0), pltpu.roll(p_rest, 6, 0))
            )
            g[b, s] = rotor
            g[b, rows + s] = p_high + p_rest
            g[b, 2 * rows + s] = u_high + jnp.where(filled, u_rest, 0.0)
    spot[0:2, :] = g[left, 2 * rows, 6:8, :]
    spot[2:4, :] = g[left, 2 * rows + 1, 6:8, :]
    spot[4:6, :] = g[right, 2 * rows, 6:8, :]
    spot[6:8, :] = g[right, 2 * rows + 1, 6:8, :]
    spots = spot[...]
    columns = [
        lax.dot_general(spots, edge_pick(q, cells), (((0,), (0,)), ((), ())), preferred_element_type=f32)
        for q in range(4)
    ]

    fetch.wait()

    def block(s, b, t):
        primal = jnp.zeros((8, TILE), f32)
        for k in range(entries):
            primal = primal + primal_table[s, t, k : k + 1, :] * g[margin[s, k, b], s]
        primal = jnp.where(filled, primal, 0.0)
        parts = flux_parts(primal)
        return (primal, *parts), flux_of(primal, *parts, g[b, rows + s])

    def keep(s, at, b, parts, moved):
        q_out[s, at], speeds_out[s, at], scaled_out[s, at] = parts
        p_out[s, at] = advanced(s, b, moved)

    def advanced(s, b, moved):
        place = lax.rem(b, own_blocks)
        before = jnp.where(place == 0, carry, 0.0).astype(f32)
        after = jnp.where(place == own_blocks - 1, carry, 0.0).astype(f32)
        low = pltpu.roll(g[wrapped(b - 1 + total, total), rows + s], 1, 1)
        high = pltpu.roll(g[wrapped(b + 1, total), rows + s], TILE - 1, 1)
        base = g[b, 2 * rows + s]
        base = base + jnp.where(lane == 0, low * before, 0.0) + jnp.where(lane == TILE - 1, high * after, 0.0)
        return base - step_size * moved

    for s in range(rows):
        base = window(margin, s, first_block, total)
        blocks = window_blocks(base, first_block, own_blocks, total)
        for t in range(spread):
            parts, moved = block(s, blocks[t], t)
            flux[s, t] = moved.astype(jnp.bfloat16).astype(f32)
            if 0 < t < spread - 1:
                keep(s, t - 1, blocks[t], parts, moved)
        own = []
        for i in range(own_blocks):
            parts, moved = block(s, first_block + i, spread + i)
            own.append(moved)
            keep(s, spread - 2 + i, first_block + i, parts, moved)
        blank = [jnp.zeros((8, TILE), f32)] * (own_blocks - 2)
        side_flux = [block(s, at, spread + own_blocks + n)[1] for n, at in enumerate((left, right))]
        pulls = [pull_row(lambda t: flux[s, t + 1], pull_table, s, slot) for slot in range(-1, own_blocks + 1)]

        def at_sides(low, high):
            return jnp.concatenate([pltpu.roll(low, 1, 1), *blank, pltpu.roll(high, TILE - 1, 1)], axis=1)

        pulled = step_size * jnp.concatenate(pulls[1:-1], axis=1)
        pulled_side = step_size * at_sides(pulls[0], pulls[-1])
        pushed = step_size * jnp.concatenate(own, axis=1)
        pushed_side = step_size * at_sides(*side_flux)
        for v in range(var_count):
            at = (v * rows + s) * 8
            cut = slice(at, at + layers)
            o_r[v, s] = (
                v_r[v, s] + carry * columns[0][cut] + jnp.where(layer_all == layers - 1, pulled[v : v + 1], 0.0)
            )
            o_s[v, s] = v_s[v, s] + carry * columns[1][cut] - jnp.where(layer_all == 0, pushed[v : v + 1], 0.0)
            h_r[v, s] = columns[2][cut] + jnp.where(
                edge, carry * a_r[v, s] + jnp.where(layer_all == layers - 1, pulled_side[v : v + 1], 0.0), 0.0
            )
            h_s[v, s] = columns[3][cut] + jnp.where(
                edge, carry * a_s[v, s] - jnp.where(layer_all == 0, pushed_side[v : v + 1], 0.0), 0.0
            )

    last = jnp.concatenate([spots, jnp.ones((8, TILE), f32)], axis=0).astype(jnp.bfloat16)
    odd = jnp.bitwise_and(lax.axis_index("span"), 1)
    for to, s in ((inner, (1 - odd) * (rows - 1)), (outer, odd * (rows - 1))):
        for j in range(total // 2):
            to[j] = jnp.concatenate([g[2 * j, rows + s], g[2 * j + 1, rows + s]], axis=0).astype(jnp.bfloat16)
        for v in range(var_count):
            for n, ref in enumerate((a_r, a_s, o_r, o_s)):
                held[v, n * layers : (n + 1) * layers, :] = ref[v, s]
            for i in range(own_blocks):
                to[total // 2 + v * own_blocks + i] = held[v, :, i * TILE : (i + 1) * TILE].astype(jnp.bfloat16)
        to[total // 2 + var_count * own_blocks] = last


def corner_of(tile, row, rows):
    lane = iota((8, TILE), 1)
    group = lax.rem(lax.shift_right_logical(lane, 3), rows)
    spot = tile.astype(f32)[0:8]
    first = jnp.where(group == 0, pltpu.roll(spot, (TILE - 8 * (rows - 1)) % TILE, 1), 0.0)
    final = jnp.where(group == rows - 1, pltpu.roll(spot, 8 * (rows - 1), 1), 0.0)
    return jnp.where(row == 0, first, final)


def corner_columns(corner, cells):
    return [
        lax.dot_general(corner, edge_pick(n, cells), (((0,), (0,)), ((), ())), preferred_element_type=f32)
        for n in range(2)
    ]


def row_flux(halo, row, margin, q, speeds, scaled, p, pull_table, flux, first_block, own_blocks, total):
    base = window(margin, row, first_block, total)
    spread = REACH + own_blocks + 1
    own = []
    for t in range(spread - 2 + own_blocks):
        b = wrapped(base + t, total) if t < spread - 2 else first_block + t - (spread - 2)
        both = halo[lax.shift_right_logical(b, 1)].astype(f32)
        beyond = jnp.where(jnp.bitwise_and(b, 1) == 1, both[8:16], both[0:8])
        moved = flux_of(q[row, t], speeds[row, t], scaled[row, t], p[row, t] + carry * beyond)
        if t < spread - 2:
            flux[t] = moved.astype(jnp.bfloat16).astype(f32)
        else:
            own.append(moved)
    pulls = [pull_row(lambda t: flux[t], pull_table, row, slot) for slot in range(own_blocks)]
    return step_size * jnp.concatenate(pulls, axis=1), -step_size * jnp.concatenate(own, axis=1)


def third_kernel(
    inner, o_r, o_s, h_r, h_s, q, speeds, scaled, p, a_r, a_s, jd_r, jd_s, jo_r, jo_s, src_r, src_s,
    pull_table, margin_in, part_r, part_s, flux, x_r, x_s, held, margin, sem,
):
    fetch = pltpu.make_async_copy(margin_in, margin, sem)
    fetch.start()
    var_count, rows, layers, cells = a_r.shape
    total = margin.shape[2]
    own_blocks = cells // TILE
    first_block = lax.axis_index("circ") * own_blocks
    end = total // 2 + var_count * own_blocks
    near_row = (1 - jnp.bitwise_and(lax.axis_index("span"), 1)) * (rows - 1)
    near = [jnp.where(near_row == s, 1.0, 0.0).astype(f32) for s in range(rows)]
    for x in (x_r, x_s):
        x[...] = jnp.zeros(x.shape, f32)
    for v in range(var_count):
        for i in range(own_blocks):
            held[v, :, i * TILE : (i + 1) * TILE] = inner[total // 2 + v * own_blocks + i].astype(f32)
    columns = corner_columns(corner_of(inner[end], near_row, rows), cells)
    fields = (
        (o_r, h_r, a_r, jd_r, jo_r, src_r, x_r, part_r),
        (o_s, h_s, a_s, jd_s, jo_s, src_s, x_s, part_s),
    )
    for n, (o, h, a, jd, jo, src, x, part) in enumerate(fields):
        old = slice(n * layers, (n + 1) * layers)
        new = slice((2 + n) * layers, (3 + n) * layers)
        for v in range(var_count):
            for s in range(rows):
                x[v * rows + s, 0:layers, :] = o[v, s] + (carry * near[s]) * held[v, old, :]
        for s in range(rows):
            state_row = [x[v * rows + s, 0:layers, :] for v in range(var_count)]
            for v in range(var_count):
                wide = x[v * rows + s]
                at = (v * rows + s) * 8
                beside = (lanes_apart(wide) + layers_apart(wide))[0:layers]
                beside = beside + h[v, s] + carry * columns[n][at : at + layers]
                beside = beside + near[s] * (held[v, new, :] + carry * a[v, s])
                if s > 0:
                    beside = beside + x[v * rows + s - 1, 0:layers, :]
                if s < rows - 1:
                    beside = beside + x[v * rows + s + 1, 0:layers, :]
                res = jacobian_row(jd, jo, state_row, v, s, var_count) - coupling * beside - src[v, s]
                part[v, s] = state_row[v] - step_size * res
    fetch.wait()
    extra = row_flux(
        inner, near_row, margin, q, speeds, scaled, p, pull_table, flux, first_block, own_blocks, total
    )
    for n, (part, layer) in enumerate(((part_r, layers - 1), (part_s, 0))):
        at = slice(layer, layer + 1)
        for v in range(var_count):
            part[v, near_row, at, :] = part[v, near_row, at, :] + extra[n][v : v + 1]


def fourth_kernel(
    bands, outer, part_r, part_s, q, speeds, scaled, p, a_r, a_s, jd_r, jd_s, jo_r, jo_s, pull_table, margin_in,
    away_r, away_s, flux, x_r, x_s, held, out_r, out_s, margin, sems,
):
    fetch = pltpu.make_async_copy(margin_in, margin, sems.at[0])
    fetch.start()
    var_count, rows, layers, cells = a_r.shape
    total = margin.shape[2]
    own_blocks = cells // TILE
    first_block = lax.axis_index("circ") * own_blocks
    end = total // 2 + var_count * own_blocks
    band = lax.axis_index("span")
    odd = jnp.bitwise_and(band, 1)
    far_row = odd * (rows - 1)
    inside = jnp.logical_and(band > 0, band < bands - 1)
    live = jnp.where(inside, carry, 0.0).astype(f32)
    next_row = far_row + 1 - 2 * odd
    for x in (x_r, x_s):
        x[...] = jnp.zeros(x.shape, f32)
    for v in range(var_count):
        for i in range(own_blocks):
            held[v, :, i * TILE : (i + 1) * TILE] = outer[total // 2 + v * own_blocks + i].astype(f32)
    columns = corner_columns(corner_of(outer[end], far_row, rows), cells)
    fields = ((part_r, a_r, jd_r, jo_r, x_r, out_r), (part_s, a_s, jd_s, jo_s, x_s, out_s))
    for n, (part, a, jd, jo, x, out) in enumerate(fields):
        old = slice(n * layers, (n + 1) * layers)
        new = slice((2 + n) * layers, (3 + n) * layers)
        for v in range(var_count):
            x[v, 0:layers, :] = carry * held[v, old, :]
        state_row = [x[v, 0:layers, :] for v in range(var_count)]
        for v in range(var_count):
            wide = x[v]
            beside = (lanes_apart(wide) + layers_apart(wide))[0:layers]
            for s in (0, rows - 1):
                at = (v * rows + s) * 8
                beside = beside + carry * columns[n][at : at + layers]
            extra = carry * (beside + held[v, new, :]) + (carry * live) * a[v, far_row]
            gone = jacobian_row(jd, jo, state_row, v, far_row, var_count)
            for s in range(rows):
                out[v, s] = part[v, s]
            out[v, far_row] = part[v, far_row] + state_row[v] - step_size * gone + extra
            out[v, next_row] = part[v, next_row] + carry * state_row[v]
    fetch.wait()
    extra = row_flux(
        outer, far_row, margin, q, speeds, scaled, p, pull_table, flux, first_block, own_blocks, total
    )
    copies = []
    for n, (out, away, layer) in enumerate(((out_r, away_r, layers - 1), (out_s, away_s, 0))):
        at = slice(layer, layer + 1)
        for v in range(var_count):
            out[v, far_row, at, :] = out[v, far_row, at, :] + extra[n][v : v + 1]
        copies.append(pltpu.make_async_copy(out, away, sems.at[1 + n]))
        copies[-1].start()
    for copy in copies:
        copy.wait()


def per_device(
    adjoint_rotor,
    adjoint_stator,
    jac_diag_rotor,
    jac_diag_stator,
    jac_off_rotor,
    jac_off_stator,
    source_rotor,
    source_stator,
    rotor_state,
    margin_block,
    face_count,
    margin_weight,
):
    var_count, rows, layers, cells = adjoint_rotor.shape
    own_blocks = cells // TILE
    total = margin_block.shape[1]
    spread = REACH + own_blocks + 1
    field = jax.ShapeDtypeStruct(adjoint_rotor.shape, f32)
    vmem = pl.BlockSpec(memory_space=pltpu.VMEM)
    smem = pl.BlockSpec(memory_space=pltpu.SMEM)
    anywhere = pl.BlockSpec(memory_space=pl.ANY)
    padded = pltpu.VMEM((TILE // 8, 8, cells), f32)

    margin = jnp.swapaxes(margin_block, 1, 2)
    arguments = (
        adjoint_rotor, adjoint_stator, jac_diag_rotor, jac_diag_stator, jac_off_rotor, jac_off_stator,
        source_rotor, source_stator, rotor_state, margin, face_count, margin_weight,
    )
    shapes = [jax.ShapeDtypeStruct(x.shape, x.dtype) for x in arguments]
    v_r, v_s, share, a_r, a_s, weights, margin, count = pl.pallas_call(
        first_kernel,
        out_shape=(
            field, field, jax.ShapeDtypeStruct((own_blocks, 64, TILE), jnp.bfloat16),
            shapes[0], shapes[1], shapes[11], shapes[9], shapes[10],
        ),
        in_specs=[pl.BlockSpec(memory_space=pltpu.HBM)] * 12,
        out_specs=(vmem,) * 8,
        scratch_shapes=[pltpu.VMEM(x.shape, x.dtype) for x in shapes[2:9]]
        + [padded] * 4
        + [pltpu.SemaphoreType.DMA((12,)), pltpu.VMEM((own_blocks, 3 * rows, 8, TILE), f32)],
        compiler_params=params,
        name="local_part",
    )(*[pltpu.with_memory_space_constraint(x, pltpu.HBM) for x in arguments])
    primal_table, pull_table = pl.pallas_call(
        table_kernel,
        out_shape=(
            jax.ShapeDtypeStruct((rows, spread + own_blocks + 2, margin_weight.shape[2], TILE), f32),
            jax.ShapeDtypeStruct((rows, own_blocks + 2, REACH, TILE), f32),
        ),
        in_specs=[vmem] + [smem] * 2,
        out_specs=(vmem,) * 2,
        compiler_params=params,
        name="weight_tables",
    )(weights, margin, count)
    members = lax.axis_size("circ")
    mine, masks = share, []
    mask = members // 2
    while mask > 0:
        hop = mask | 1
        other = lax.ppermute(mine, "circ", [(i, i ^ hop) for i in range(members)])
        if mask > 1:
            mine = jnp.concatenate([mine, other], axis=0)
            if not masks:
                mine, primal_table, pull_table = lax.optimization_barrier((mine, primal_table, pull_table))
            masks.append(hop)
        mask //= 2
    tiles = jax.ShapeDtypeStruct((total // 2 + var_count * own_blocks + 1, 16, TILE), jnp.bfloat16)
    listed = jax.ShapeDtypeStruct((rows, spread - 2 + own_blocks, 8, TILE), f32)
    o_r, o_s, h_r, h_s, q, speeds, scaled, p, inner, outer = pl.pallas_call(
        functools.partial(second_kernel, masks),
        out_shape=(field,) * 4 + (listed,) * 4 + (tiles,) * 2,
        in_specs=[vmem] * 8 + [anywhere],
        out_specs=(vmem,) * 10,
        scratch_shapes=[
            pltpu.VMEM((rows, spread, 8, TILE), f32),
            pltpu.VMEM((var_count, 4 * layers, cells), f32),
            pltpu.VMEM((8, TILE), f32),
            pltpu.VMEM((total, 3 * rows, 8, TILE), f32),
            pltpu.SMEM(margin.shape, jnp.int32),
            pltpu.SemaphoreType.DMA(()),
        ],
        compiler_params=params,
        name="interface_part",
    )(mine, other, v_r, v_s, a_r, a_s, primal_table, pull_table, margin)
    bands = lax.axis_size("span")
    near = [(i, i ^ 1) for i in range(bands)]
    far = [pair for i in range(1, bands - 1, 2) for pair in ((i, i + 1), (i + 1, i))]
    inner = lax.ppermute(inner, "span", near)
    outer = lax.ppermute(outer, "span", far)
    held = pltpu.VMEM((var_count, 4 * layers, cells), f32)
    flux = pltpu.VMEM((spread - 2, 8, TILE), f32)
    listing = pltpu.SMEM(margin.shape, jnp.int32)
    small = pltpu.VMEM((8, 8, cells), f32)
    part_r, part_s = pl.pallas_call(
        third_kernel,
        out_shape=(field, field),
        in_specs=[vmem] * 18 + [anywhere],
        out_specs=(vmem,) * 2,
        scratch_shapes=[flux, padded, padded, held, listing, pltpu.SemaphoreType.DMA(())],
        compiler_params=params,
        name="near_part",
    )(
        inner, o_r, o_s, h_r, h_s, q, speeds, scaled, p, a_r, a_s, jac_diag_rotor, jac_diag_stator,
        jac_off_rotor, jac_off_stator, source_rotor, source_stator, pull_table, margin,
    )
    out_r, out_s = pl.pallas_call(
        functools.partial(fourth_kernel, bands),
        out_shape=(field, field),
        in_specs=[vmem] * 14 + [anywhere],
        out_specs=(anywhere,) * 2,
        scratch_shapes=[
            flux, small, small, held, pltpu.VMEM(field.shape, f32), pltpu.VMEM(field.shape, f32), listing,
            pltpu.SemaphoreType.DMA((3,)),
        ],
        compiler_params=params,
        name="final_part",
    )(
        outer, part_r, part_s, q, speeds, scaled, p, a_r, a_s, jac_diag_rotor, jac_diag_stator,
        jac_off_rotor, jac_off_stator, pull_table, margin,
    )
    return (out_r, out_s)


def solution(mesh):
    field = P(None, "span", None, "circ")
    placed = (
        (field,) * 4
        + (P(None, None, "span", None, "circ"),) * 2
        + (field,) * 2
        + (P(None, "span", "circ"), P("span", None, None), P("span", None), P("span", None, None, None))
    )
    return jax.shard_map(
        per_device, mesh=mesh, in_specs=placed, out_specs=(field, field), check_vma=False
    )
```

```python
import functools

import jax
import jax.numpy as jnp
from jax import lax
from jax.experimental import pallas as pl
from jax.experimental.pallas import tpu as pltpu
from jax.sharding import PartitionSpec as P

step_size = 0.1
coupling = 0.2
carry = step_size * coupling
REACH = 8
TILE = 128
f32 = jnp.float32
params = pltpu.CompilerParams(vmem_limit_bytes=24 * 1024 * 1024)


def iota(shape, dim):
    return lax.broadcasted_iota(jnp.int32, shape, dim)


def wrapped(x, count):
    if count & (count - 1) == 0:
        return jnp.bitwise_and(x, count - 1)
    return lax.rem(x + 4 * count, count)


def lanes_apart(x):
    cells = x.shape[1]
    lane = iota(x.shape, 1)
    before = jnp.where(lane == 0, 0.0, pltpu.roll(x, 1, 1))
    after = jnp.where(lane == cells - 1, 0.0, pltpu.roll(x, cells - 1, 1))
    return before + after


def layers_apart(x):
    return pltpu.roll(x, 1, 0) + pltpu.roll(x, 7, 0)


def edge_pick(row, cells):
    at = iota((8, cells), 0)
    lane = iota((8, cells), 1)
    first = jnp.logical_and(at == row, lane == 0)
    last = jnp.logical_and(at == 4 + row, lane == cells - 1)
    return jnp.where(jnp.logical_or(first, last), 1.0, 0.0).astype(f32)


def split(x):
    high = x.astype(jnp.bfloat16).astype(f32)
    return high, x - high


def flux_parts(primal):
    square = primal * primal
    under = 6.0 + jnp.sum(square, axis=0, keepdims=True)
    return jnp.sqrt(1.0 + square), 0.5 * primal / under


def flux_of(primal, speeds, scaled, adjoint):
    return speeds * adjoint + scaled * jnp.sum(primal * adjoint, axis=0, keepdims=True)


def jacobian_row(diag, off, state, v, s, var_count):
    total = diag[v, s] * state[v]
    for w in range(var_count):
        total = total + off[w, v, s].astype(f32) * state[w]
    return total


def pull_row(flux, table, s, slot):
    acc = jnp.zeros((8, TILE), f32)
    for e in range(REACH):
        acc = acc + table[s, slot + 1, e : e + 1, :] * flux(slot + e)
    return acc


def window(margin, s, first_block, total):
    return first_block - margin[s, 0, 0] - 5 + 4 * total


def window_blocks(base, first_block, own_blocks, total):
    found = [wrapped(base - 1 + t, total) for t in range(REACH + own_blocks + 1)]
    sides = [wrapped(first_block - 1 + total, total), wrapped(first_block + own_blocks, total)]
    return found + [first_block + i for i in range(own_blocks)] + sides


def table_kernel(weights, margin, count, primal_table, pull_table):
    rows, total, entries, _ = weights.shape
    own_blocks = pull_table.shape[1] - 2
    first_block = lax.axis_index("circ") * own_blocks
    for s in range(rows):
        base = window(margin, s, first_block, total)
        blocks = window_blocks(base, first_block, own_blocks, total)
        entry = iota((entries, TILE), 0)
        for t, b in enumerate(blocks):
            primal_table[s, t] = jnp.where(entry < count[s, b], weights[s, b], 0.0)
        for slot in range(-1, own_blocks + 1):
            target = wrapped(first_block + slot + total, total)
            for e in range(REACH):
                b = blocks[slot + 1 + e]
                k = wrapped(target - margin[s, 0, b] + total, total)
                live = jnp.where(k < count[s, b], 1.0, 0.0).astype(f32)
                kept = jnp.minimum(k, entries - 1)
                pull_table[s, slot + 1, e : e + 1, :] = weights[s, b, pl.ds(kept, 1), :] * live


def first_kernel(*refs):
    outer, refs = refs[:12], refs[12:]
    v_r, v_s, out, a_r, a_s, weights, margin, count = refs[:8]
    jd_r, jd_s, jo_r, jo_s, src_r, src_s, state = refs[8:15]
    xs, sems, wide_out = refs[15:19], refs[19], refs[20]
    var_count, rows, layers, cells = a_r.shape
    own_blocks = cells // TILE
    inner = (a_r, a_s, jd_r, jd_s, jo_r, jo_s, src_r, src_s, state, margin, count, weights)
    copies = [pltpu.make_async_copy(x, y, sems.at[n]) for n, (x, y) in enumerate(zip(outer, inner))]
    for copy in copies:
        copy.start()
    wide_out[...] = jnp.zeros(wide_out.shape, f32)
    for x in xs:
        x[...] = jnp.zeros(x.shape, f32)
    for copy in copies:
        copy.wait()
    fields = ((a_r, jd_r, jo_r, src_r, v_r, xs[0], xs[2]), (a_s, jd_s, jo_s, src_s, v_s, xs[1], xs[3]))
    for a, jd, jo, src, partial, x_a, x_p in fields:
        for v in range(var_count):
            for s in range(rows):
                x_a[v * rows + s, 0:layers, :] = a[v, s]
        for s in range(rows):
            state_row = [a[v, s] for v in range(var_count)]
            for v in range(var_count):
                wide = x_a[v * rows + s]
                beside = (lanes_apart(wide) + layers_apart(wide))[0:layers]
                if s > 0:
                    beside = beside + a[v, s - 1]
                if s < rows - 1:
                    beside = beside + a[v, s + 1]
                res = jacobian_row(jd, jo, state_row, v, s, var_count) - coupling * beside - src[v, s]
                new = state_row[v] - step_size * res
                partial[v, s] = new
                x_p[v * rows + s, 0:layers, :] = new
    edges = jnp.zeros((8, TILE), f32)
    for q in range(4):
        flat = xs[q][...].reshape(TILE, cells)
        edges = edges + lax.dot_general(
            edge_pick(q, cells), flat, (((1,), (1,)), ((), ())), preferred_element_type=f32
        )
    for v in range(var_count):
        rotor = state[v].astype(f32)
        for s in range(rows):
            for i in range(own_blocks):
                cut = slice(i * TILE, (i + 1) * TILE)
                wide_out[i, s, v : v + 1, :] = rotor[s : s + 1, cut]
                wide_out[i, rows + s, v : v + 1, :] = a_s[v, s, 0:1, cut]
                wide_out[i, 2 * rows + s, v : v + 1, :] = v_s[v, s, 0:1, cut]
    row8 = iota((8, TILE), 0)
    filled = row8 < var_count
    for i in range(own_blocks):
        if i in (0, own_blocks - 1):
            side = 4 if i else 0
            for s in range(rows):
                wide_out[i, 2 * rows + s, 6:8, :] = edges[side + 2 * s : side + 2 * s + 2]
        groups = []
        for s in range(rows):
            p_high, p_rest = split(wide_out[i, rows + s])
            u_high, u_rest = split(wide_out[i, 2 * rows + s])
            groups.append((
                jnp.where(filled, wide_out[i, s], pltpu.roll(u_rest, 6, 0)),
                jnp.where(filled, p_high, pltpu.roll(u_rest, 4, 0)),
                jnp.where(filled, p_rest, pltpu.roll(u_rest, 2, 0)),
                u_high,
            ))
        for n in range(4):
            out[i, n * 16 : n * 16 + 16, :] = jnp.concatenate([x[n] for x in groups], axis=0).astype(jnp.bfloat16)


def second_kernel(
    masks, mine, other, v_r, v_s, a_r, a_s, primal_table, pull_table, margin_in,
    o_r, o_s, h_r, h_s, q_out, speeds_out, scaled_out, p_out, inner, outer, flux, held, spot, g, margin, sem,
):
    var_count, rows, layers, cells = a_r.shape
    fetch = pltpu.make_async_copy(margin_in, margin, sem)
    fetch.start()
    total = 2 * mine.shape[0]
    own_blocks = cells // TILE
    entries = primal_table.shape[2]
    spread = REACH + own_blocks + 1
    first_block = lax.axis_index("circ") * own_blocks
    row8 = iota((8, TILE), 0)
    lane = iota((8, TILE), 1)
    lane_all = iota((layers, cells), 1)
    layer_all = iota((layers, cells), 0)
    edge = jnp.logical_or(lane_all == 0, lane_all == cells - 1)
    left = wrapped(first_block - 1 + total, total)
    right = wrapped(first_block + own_blocks, total)

    filled = row8 < var_count
    here = lax.axis_index("circ")
    for at in range(total):
        half, part = divmod(at, total // 2)
        place, i = divmod(part, own_blocks)
        mask = half
        for n, m in enumerate(masks):
            mask ^= m if place >> n & 1 else 0
        b = jnp.bitwise_xor(here, mask) * own_blocks + i
        whole = other if half else mine
        tiles = [whole[part, n * 16 : n * 16 + 16, :].astype(f32) for n in range(4)]
        for s in range(rows):
            rotor, p_high, p_rest, u_high = [x[s * 8 : s * 8 + 8] for x in tiles]
            u_rest = jnp.where(
                row8 < 2, pltpu.roll(rotor, 2, 0), jnp.where(row8 < 4, pltpu.roll(p_high, 4, 0), pltpu.roll(p_rest, 6, 0))
            )
            g[b, s] = rotor
            g[b, rows + s] = p_high + p_rest
            g[b, 2 * rows + s] = u_high + jnp.where(filled, u_rest, 0.0)
    spot[0:2, :] = g[left, 2 * rows, 6:8, :]
    spot[2:4, :] = g[left, 2 * rows + 1, 6:8, :]
    spot[4:6, :] = g[right, 2 * rows, 6:8, :]
    spot[6:8, :] = g[right, 2 * rows + 1, 6:8, :]
    spots = spot[...]
    columns = [
        lax.dot_general(spots, edge_pick(q, cells), (((0,), (0,)), ((), ())), preferred_element_type=f32)
        for q in range(4)
    ]

    fetch.wait()

    def block(s, b, t):
        primal = jnp.zeros((8, TILE), f32)
        for k in range(entries):
            primal = primal + primal_table[s, t, k : k + 1, :] * g[margin[s, k, b], s]
        primal = jnp.where(filled, primal, 0.0)
        parts = flux_parts(primal)
        return (primal, *parts), flux_of(primal, *parts, g[b, rows + s])

    def keep(s, at, b, parts, moved):
        q_out[s, at], speeds_out[s, at], scaled_out[s, at] = parts
        p_out[s, at] = advanced(s, b, moved)

    def advanced(s, b, moved):
        place = lax.rem(b, own_blocks)
        before = jnp.where(place == 0, carry, 0.0).astype(f32)
        after = jnp.where(place == own_blocks - 1, carry, 0.0).astype(f32)
        low = pltpu.roll(g[wrapped(b - 1 + total, total), rows + s], 1, 1)
        high = pltpu.roll(g[wrapped(b + 1, total), rows + s], TILE - 1, 1)
        base = g[b, 2 * rows + s]
        base = base + jnp.where(lane == 0, low * before, 0.0) + jnp.where(lane == TILE - 1, high * after, 0.0)
        return base - step_size * moved

    for s in range(rows):
        base = window(margin, s, first_block, total)
        blocks = window_blocks(base, first_block, own_blocks, total)
        for t in range(spread):
            parts, moved = block(s, blocks[t], t)
            flux[s, t] = moved.astype(jnp.bfloat16).astype(f32)
            if 0 < t < spread - 1:
                keep(s, t - 1, blocks[t], parts, moved)
        own = []
        for i in range(own_blocks):
            parts, moved = block(s, first_block + i, spread + i)
            own.append(moved)
            keep(s, spread - 2 + i, first_block + i, parts, moved)
        blank = [jnp.zeros((8, TILE), f32)] * (own_blocks - 2)
        side_flux = [block(s, at, spread + own_blocks + n)[1] for n, at in enumerate((left, right))]
        pulls = [pull_row(lambda t: flux[s, t + 1], pull_table, s, slot) for slot in range(-1, own_blocks + 1)]

        def at_sides(low, high):
            return jnp.concatenate([pltpu.roll(low, 1, 1), *blank, pltpu.roll(high, TILE - 1, 1)], axis=1)

        pulled = step_size * jnp.concatenate(pulls[1:-1], axis=1)
        pulled_side = step_size * at_sides(pulls[0], pulls[-1])
        pushed = step_size * jnp.concatenate(own, axis=1)
        pushed_side = step_size * at_sides(*side_flux)
        for v in range(var_count):
            at = (v * rows + s) * 8
            cut = slice(at, at + layers)
            o_r[v, s] = (
                v_r[v, s] + carry * columns[0][cut] + jnp.where(layer_all == layers - 1, pulled[v : v + 1], 0.0)
            )
            o_s[v, s] = v_s[v, s] + carry * columns[1][cut] - jnp.where(layer_all == 0, pushed[v : v + 1], 0.0)
            h_r[v, s] = columns[2][cut] + jnp.where(
                edge, carry * a_r[v, s] + jnp.where(layer_all == layers - 1, pulled_side[v : v + 1], 0.0), 0.0
            )
            h_s[v, s] = columns[3][cut] + jnp.where(
                edge, carry * a_s[v, s] - jnp.where(layer_all == 0, pushed_side[v : v + 1], 0.0), 0.0
            )

    last = jnp.concatenate([spots, jnp.ones((8, TILE), f32)], axis=0).astype(jnp.bfloat16)
    odd = jnp.bitwise_and(lax.axis_index("span"), 1)
    for to, s in ((inner, (1 - odd) * (rows - 1)), (outer, odd * (rows - 1))):
        for j in range(total // 2):
            to[j] = jnp.concatenate([g[2 * j, rows + s], g[2 * j + 1, rows + s]], axis=0).astype(jnp.bfloat16)
        for v in range(var_count):
            for n, ref in enumerate((a_r, a_s, o_r, o_s)):
                held[v, n * layers : (n + 1) * layers, :] = ref[v, s]
            for i in range(own_blocks):
                to[total // 2 + v * own_blocks + i] = held[v, :, i * TILE : (i + 1) * TILE].astype(jnp.bfloat16)
        to[total // 2 + var_count * own_blocks] = last


def corner_of(tile, row, rows):
    lane = iota((8, TILE), 1)
    group = lax.rem(lax.shift_right_logical(lane, 3), rows)
    spot = tile.astype(f32)[0:8]
    first = jnp.where(group == 0, pltpu.roll(spot, (TILE - 8 * (rows - 1)) % TILE, 1), 0.0)
    final = jnp.where(group == rows - 1, pltpu.roll(spot, 8 * (rows - 1), 1), 0.0)
    return jnp.where(row == 0, first, final)


def corner_columns(corner, cells):
    return [
        lax.dot_general(corner, edge_pick(n, cells), (((0,), (0,)), ((), ())), preferred_element_type=f32)
        for n in range(2)
    ]


def row_flux(halo, row, base, q, speeds, scaled, p, pull_table, flux, first_block, own_blocks, total):
    spread = REACH + own_blocks + 1
    own = []
    for t in range(spread - 2 + own_blocks):
        b = wrapped(base + t, total) if t < spread - 2 else first_block + t - (spread - 2)
        both = halo[lax.shift_right_logical(b, 1)].astype(f32)
        beyond = jnp.where(jnp.bitwise_and(b, 1) == 1, both[8:16], both[0:8])
        moved = flux_of(q[row, t], speeds[row, t], scaled[row, t], p[row, t] + carry * beyond)
        if t < spread - 2:
            flux[t] = moved.astype(jnp.bfloat16).astype(f32)
        else:
            own.append(moved)
    pulls = [pull_row(lambda t: flux[t], pull_table, row, slot) for slot in range(own_blocks)]
    return step_size * jnp.concatenate(pulls, axis=1), -step_size * jnp.concatenate(own, axis=1)


def third_kernel(
    inner, o_r, o_s, h_r, h_s, q, speeds, scaled, p, a_r, a_s, jd_r, jd_s, jo_r, jo_s, src_r, src_s,
    pull_table, margin_in, part_r, part_s, start, flux, x_r, x_s, held, margin, sem,
):
    fetch = pltpu.make_async_copy(margin_in, margin, sem)
    fetch.start()
    var_count, rows, layers, cells = a_r.shape
    total = margin.shape[2]
    own_blocks = cells // TILE
    first_block = lax.axis_index("circ") * own_blocks
    end = total // 2 + var_count * own_blocks
    near_row = (1 - jnp.bitwise_and(lax.axis_index("span"), 1)) * (rows - 1)
    near = [jnp.where(near_row == s, 1.0, 0.0).astype(f32) for s in range(rows)]
    for x in (x_r, x_s):
        x[...] = jnp.zeros(x.shape, f32)
    for v in range(var_count):
        for i in range(own_blocks):
            held[v, :, i * TILE : (i + 1) * TILE] = inner[total // 2 + v * own_blocks + i].astype(f32)
    columns = corner_columns(corner_of(inner[end], near_row, rows), cells)
    fields = (
        (o_r, h_r, a_r, jd_r, jo_r, src_r, x_r, part_r),
        (o_s, h_s, a_s, jd_s, jo_s, src_s, x_s, part_s),
    )
    for n, (o, h, a, jd, jo, src, x, part) in enumerate(fields):
        old = slice(n * layers, (n + 1) * layers)
        new = slice((2 + n) * layers, (3 + n) * layers)
        for v in range(var_count):
            for s in range(rows):
                x[v * rows + s, 0:layers, :] = o[v, s] + (carry * near[s]) * held[v, old, :]
        for s in range(rows):
            state_row = [x[v * rows + s, 0:layers, :] for v in range(var_count)]
            for v in range(var_count):
                wide = x[v * rows + s]
                at = (v * rows + s) * 8
                beside = (lanes_apart(wide) + layers_apart(wide))[0:layers]
                beside = beside + h[v, s] + carry * columns[n][at : at + layers]
                beside = beside + near[s] * (held[v, new, :] + carry * a[v, s])
                if s > 0:
                    beside = beside + x[v * rows + s - 1, 0:layers, :]
                if s < rows - 1:
                    beside = beside + x[v * rows + s + 1, 0:layers, :]
                res = jacobian_row(jd, jo, state_row, v, s, var_count) - coupling * beside - src[v, s]
                part[v, s] = state_row[v] - step_size * res
    fetch.wait()
    extra = row_flux(
        inner, near_row, window(margin, near_row, first_block, total), q, speeds, scaled, p, pull_table, flux,
        first_block, own_blocks, total,
    )
    start[...] = jnp.full((8, TILE), window(margin, rows - 1 - near_row, first_block, total)).astype(f32)
    for n, (part, layer) in enumerate(((part_r, layers - 1), (part_s, 0))):
        at = slice(layer, layer + 1)
        for v in range(var_count):
            part[v, near_row, at, :] = part[v, near_row, at, :] + extra[n][v : v + 1]


def fourth_kernel(
    bands, outer, part_r, part_s, q, speeds, scaled, p, a_r, a_s, jd_r, jd_s, jo_r, jo_s, pull_table, start,
    away_r, away_s, flux, x_r, x_s, held, out_r, out_s, sems,
):
    var_count, rows, layers, cells = a_r.shape
    own_blocks = cells // TILE
    total = 2 * (outer.shape[0] - 1 - var_count * own_blocks)
    base = jnp.max(start[...]).astype(jnp.int32)
    own_blocks = cells // TILE
    first_block = lax.axis_index("circ") * own_blocks
    end = total // 2 + var_count * own_blocks
    band = lax.axis_index("span")
    odd = jnp.bitwise_and(band, 1)
    far_row = odd * (rows - 1)
    inside = jnp.logical_and(band > 0, band < bands - 1)
    live = jnp.where(inside, carry, 0.0).astype(f32)
    next_row = far_row + 1 - 2 * odd
    for x in (x_r, x_s):
        x[...] = jnp.zeros(x.shape, f32)
    for v in range(var_count):
        for i in range(own_blocks):
            held[v, :, i * TILE : (i + 1) * TILE] = outer[total // 2 + v * own_blocks + i].astype(f32)
    columns = corner_columns(corner_of(outer[end], far_row, rows), cells)
    fields = ((part_r, a_r, jd_r, jo_r, x_r, out_r), (part_s, a_s, jd_s, jo_s, x_s, out_s))
    for n, (part, a, jd, jo, x, out) in enumerate(fields):
        old = slice(n * layers, (n + 1) * layers)
        new = slice((2 + n) * layers, (3 + n) * layers)
        for v in range(var_count):
            x[v, 0:layers, :] = carry * held[v, old, :]
        state_row = [x[v, 0:layers, :] for v in range(var_count)]
        for v in range(var_count):
            wide = x[v]
            beside = (lanes_apart(wide) + layers_apart(wide))[0:layers]
            for s in (0, rows - 1):
                at = (v * rows + s) * 8
                beside = beside + carry * columns[n][at : at + layers]
            extra = carry * (beside + held[v, new, :]) + (carry * live) * a[v, far_row]
            gone = jacobian_row(jd, jo, state_row, v, far_row, var_count)
            for s in range(rows):
                out[v, s] = part[v, s]
            out[v, far_row] = part[v, far_row] + state_row[v] - step_size * gone + extra
            out[v, next_row] = part[v, next_row] + carry * state_row[v]
    extra = row_flux(
        outer, far_row, base, q, speeds, scaled, p, pull_table, flux, first_block, own_blocks, total
    )
    copies = []
    for n, (out, away, layer) in enumerate(((out_r, away_r, layers - 1), (out_s, away_s, 0))):
        at = slice(layer, layer + 1)
        for v in range(var_count):
            out[v, far_row, at, :] = out[v, far_row, at, :] + extra[n][v : v + 1]
        copies.append(pltpu.make_async_copy(out, away, sems.at[n]))
        copies[-1].start()
    for copy in copies:
        copy.wait()


def per_device(
    adjoint_rotor,
    adjoint_stator,
    jac_diag_rotor,
    jac_diag_stator,
    jac_off_rotor,
    jac_off_stator,
    source_rotor,
    source_stator,
    rotor_state,
    margin_block,
    face_count,
    margin_weight,
):
    var_count, rows, layers, cells = adjoint_rotor.shape
    own_blocks = cells // TILE
    total = margin_block.shape[1]
    spread = REACH + own_blocks + 1
    field = jax.ShapeDtypeStruct(adjoint_rotor.shape, f32)
    vmem = pl.BlockSpec(memory_space=pltpu.VMEM)
    smem = pl.BlockSpec(memory_space=pltpu.SMEM)
    anywhere = pl.BlockSpec(memory_space=pl.ANY)
    padded = pltpu.VMEM((TILE // 8, 8, cells), f32)

    margin = jnp.swapaxes(margin_block, 1, 2)
    arguments = (
        adjoint_rotor, adjoint_stator, jac_diag_rotor, jac_diag_stator, jac_off_rotor, jac_off_stator,
        source_rotor, source_stator, rotor_state, margin, face_count, margin_weight,
    )
    shapes = [jax.ShapeDtypeStruct(x.shape, x.dtype) for x in arguments]
    v_r, v_s, share, a_r, a_s, weights, margin, count = pl.pallas_call(
        first_kernel,
        out_shape=(
            field, field, jax.ShapeDtypeStruct((own_blocks, 64, TILE), jnp.bfloat16),
            shapes[0], shapes[1], shapes[11], shapes[9], shapes[10],
        ),
        in_specs=[pl.BlockSpec(memory_space=pltpu.HBM)] * 12,
        out_specs=(vmem,) * 8,
        scratch_shapes=[pltpu.VMEM(x.shape, x.dtype) for x in shapes[2:9]]
        + [padded] * 4
        + [pltpu.SemaphoreType.DMA((12,)), pltpu.VMEM((own_blocks, 3 * rows, 8, TILE), f32)],
        compiler_params=params,
        name="local_part",
    )(*[pltpu.with_memory_space_constraint(x, pltpu.HBM) for x in arguments])
    primal_table, pull_table = pl.pallas_call(
        table_kernel,
        out_shape=(
            jax.ShapeDtypeStruct((rows, spread + own_blocks + 2, margin_weight.shape[2], TILE), f32),
            jax.ShapeDtypeStruct((rows, own_blocks + 2, REACH, TILE), f32),
        ),
        in_specs=[vmem] + [smem] * 2,
        out_specs=(vmem,) * 2,
        compiler_params=params,
        name="weight_tables",
    )(weights, margin, count)
    members = lax.axis_size("circ")
    mine, masks = share, []
    mask = members // 2
    while mask > 0:
        hop = mask | 1
        other = lax.ppermute(mine, "circ", [(i, i ^ hop) for i in range(members)])
        if mask > 1:
            mine = jnp.concatenate([mine, other], axis=0)
            if not masks:
                mine, primal_table, pull_table = lax.optimization_barrier((mine, primal_table, pull_table))
            masks.append(hop)
        mask //= 2
    tiles = jax.ShapeDtypeStruct((total // 2 + var_count * own_blocks + 1, 16, TILE), jnp.bfloat16)
    listed = jax.ShapeDtypeStruct((rows, spread - 2 + own_blocks, 8, TILE), f32)
    o_r, o_s, h_r, h_s, q, speeds, scaled, p, inner, outer = pl.pallas_call(
        functools.partial(second_kernel, masks),
        out_shape=(field,) * 4 + (listed,) * 4 + (tiles,) * 2,
        in_specs=[vmem] * 8 + [anywhere],
        out_specs=(vmem,) * 10,
        scratch_shapes=[
            pltpu.VMEM((rows, spread, 8, TILE), f32),
            pltpu.VMEM((var_count, 4 * layers, cells), f32),
            pltpu.VMEM((8, TILE), f32),
            pltpu.VMEM((total, 3 * rows, 8, TILE), f32),
            pltpu.SMEM(margin.shape, jnp.int32),
            pltpu.SemaphoreType.DMA(()),
        ],
        compiler_params=params,
        name="interface_part",
    )(mine, other, v_r, v_s, a_r, a_s, primal_table, pull_table, margin)
    bands = lax.axis_size("span")
    near = [(i, i ^ 1) for i in range(bands)]
    far = [pair for i in range(1, bands - 1, 2) for pair in ((i, i + 1), (i + 1, i))]
    inner = lax.ppermute(inner, "span", near)
    outer = lax.ppermute(outer, "span", far)
    held = pltpu.VMEM((var_count, 4 * layers, cells), f32)
    flux = pltpu.VMEM((spread - 2, 8, TILE), f32)
    listing = pltpu.SMEM(margin.shape, jnp.int32)
    small = pltpu.VMEM((8, 8, cells), f32)
    part_r, part_s, start = pl.pallas_call(
        third_kernel,
        out_shape=(field, field, jax.ShapeDtypeStruct((8, TILE), f32)),
        in_specs=[vmem] * 18 + [anywhere],
        out_specs=(vmem,) * 3,
        scratch_shapes=[flux, padded, padded, held, listing, pltpu.SemaphoreType.DMA(())],
        compiler_params=params,
        name="near_part",
    )(
        inner, o_r, o_s, h_r, h_s, q, speeds, scaled, p, a_r, a_s, jac_diag_rotor, jac_diag_stator,
        jac_off_rotor, jac_off_stator, source_rotor, source_stator, pull_table, margin,
    )
    out_r, out_s = pl.pallas_call(
        functools.partial(fourth_kernel, bands),
        out_shape=(field, field),
        in_specs=[vmem] * 15,
        out_specs=(anywhere,) * 2,
        scratch_shapes=[
            flux, small, small, held, pltpu.VMEM(field.shape, f32), pltpu.VMEM(field.shape, f32),
            pltpu.SemaphoreType.DMA((2,)),
        ],
        compiler_params=params,
        name="final_part",
    )(
        outer, part_r, part_s, q, speeds, scaled, p, a_r, a_s, jac_diag_rotor, jac_diag_stator,
        jac_off_rotor, jac_off_stator, pull_table, start,
    )
    return (out_r, out_s)


def solution(mesh):
    field = P(None, "span", None, "circ")
    placed = (
        (field,) * 4
        + (P(None, None, "span", None, "circ"),) * 2
        + (field,) * 2
        + (P(None, "span", "circ"), P("span", None, None), P("span", None), P("span", None, None, None))
    )
    return jax.shard_map(
        per_device, mesh=mesh, in_specs=placed, out_specs=(field, field), check_vma=False
    )
```

```python
import functools

import jax
import jax.numpy as jnp
from jax import lax
from jax.experimental import pallas as pl
from jax.experimental.pallas import tpu as pltpu
from jax.sharding import PartitionSpec as P

step_size = 0.1
coupling = 0.2
carry = step_size * coupling
REACH = 8
TILE = 128
f32 = jnp.float32
params = pltpu.CompilerParams(vmem_limit_bytes=24 * 1024 * 1024)


def iota(shape, dim):
    return lax.broadcasted_iota(jnp.int32, shape, dim)


def wrapped(x, count):
    if count & (count - 1) == 0:
        return jnp.bitwise_and(x, count - 1)
    return lax.rem(x + 4 * count, count)


def lanes_apart(x):
    cells = x.shape[1]
    lane = iota(x.shape, 1)
    before = jnp.where(lane == 0, 0.0, pltpu.roll(x, 1, 1))
    after = jnp.where(lane == cells - 1, 0.0, pltpu.roll(x, cells - 1, 1))
    return before + after


def layers_apart(x):
    return pltpu.roll(x, 1, 0) + pltpu.roll(x, 7, 0)


def edge_pick(row, cells):
    at = iota((8, cells), 0)
    lane = iota((8, cells), 1)
    first = jnp.logical_and(at == row, lane == 0)
    last = jnp.logical_and(at == 4 + row, lane == cells - 1)
    return jnp.where(jnp.logical_or(first, last), 1.0, 0.0).astype(f32)


def split(x):
    high = x.astype(jnp.bfloat16).astype(f32)
    return high, x - high


def flux_parts(primal):
    square = primal * primal
    under = 6.0 + jnp.sum(square, axis=0, keepdims=True)
    return jnp.sqrt(1.0 + square), 0.5 * primal / under


def flux_of(primal, speeds, scaled, adjoint):
    return speeds * adjoint + scaled * jnp.sum(primal * adjoint, axis=0, keepdims=True)


def jacobian_row(diag, off, state, v, s, var_count):
    total = diag[v, s] * state[v]
    for w in range(var_count):
        total = total + off[w, v, s].astype(f32) * state[w]
    return total


def pull_row(flux, table, s, slot):
    acc = jnp.zeros((8, TILE), f32)
    for e in range(REACH):
        acc = acc + table[s, slot + 1, e : e + 1, :] * flux(slot + e)
    return acc


def window(margin, s, first_block, total):
    return first_block - margin[s, 0, 0] - 5 + 4 * total


def window_blocks(base, first_block, own_blocks, total):
    found = [wrapped(base - 1 + t, total) for t in range(REACH + own_blocks + 1)]
    sides = [wrapped(first_block - 1 + total, total), wrapped(first_block + own_blocks, total)]
    return found + [first_block + i for i in range(own_blocks)] + sides


def table_kernel(weights, margin, count, primal_table, pull_table):
    rows, total, entries, _ = weights.shape
    own_blocks = pull_table.shape[1] - 2
    first_block = lax.axis_index("circ") * own_blocks
    for s in range(rows):
        base = window(margin, s, first_block, total)
        blocks = window_blocks(base, first_block, own_blocks, total)
        entry = iota((entries, TILE), 0)
        for t, b in enumerate(blocks):
            primal_table[s, t] = jnp.where(entry < count[s, b], weights[s, b], 0.0)
        for slot in range(-1, own_blocks + 1):
            target = wrapped(first_block + slot + total, total)
            for e in range(REACH):
                b = blocks[slot + 1 + e]
                k = wrapped(target - margin[s, 0, b] + total, total)
                live = jnp.where(k < count[s, b], 1.0, 0.0).astype(f32)
                kept = jnp.minimum(k, entries - 1)
                pull_table[s, slot + 1, e : e + 1, :] = weights[s, b, pl.ds(kept, 1), :] * live


def first_kernel(*refs):
    outer, refs = refs[:12], refs[12:]
    v_r, v_s, out, a_r, a_s, weights, margin, count = refs[:8]
    jd_r, jd_s, jo_r, jo_s, src_r, src_s, state = refs[8:15]
    xs, sems, wide_out = refs[15:19], refs[19], refs[20]
    var_count, rows, layers, cells = a_r.shape
    own_blocks = cells // TILE
    inner = (a_r, a_s, jd_r, jd_s, jo_r, jo_s, src_r, src_s, state, margin, count, weights)
    copies = [pltpu.make_async_copy(x, y, sems.at[n]) for n, (x, y) in enumerate(zip(outer, inner))]
    for copy in copies:
        copy.start()
    wide_out[...] = jnp.zeros(wide_out.shape, f32)
    for x in xs:
        x[...] = jnp.zeros(x.shape, f32)
    for copy in copies:
        copy.wait()
    fields = ((a_r, jd_r, jo_r, src_r, v_r, xs[0], xs[2]), (a_s, jd_s, jo_s, src_s, v_s, xs[1], xs[3]))
    for a, jd, jo, src, partial, x_a, x_p in fields:
        for v in range(var_count):
            for s in range(rows):
                x_a[v * rows + s, 0:layers, :] = a[v, s]
        for s in range(rows):
            state_row = [a[v, s] for v in range(var_count)]
            for v in range(var_count):
                wide = x_a[v * rows + s]
                beside = (lanes_apart(wide) + layers_apart(wide))[0:layers]
                if s > 0:
                    beside = beside + a[v, s - 1]
                if s < rows - 1:
                    beside = beside + a[v, s + 1]
                res = jacobian_row(jd, jo, state_row, v, s, var_count) - coupling * beside - src[v, s]
                new = state_row[v] - step_size * res
                partial[v, s] = new
                x_p[v * rows + s, 0:layers, :] = new
    edges = jnp.zeros((8, TILE), f32)
    for q in range(4):
        flat = xs[q][...].reshape(TILE, cells)
        edges = edges + lax.dot_general(
            edge_pick(q, cells), flat, (((1,), (1,)), ((), ())), preferred_element_type=f32
        )
    for v in range(var_count):
        rotor = state[v].astype(f32)
        for s in range(rows):
            for i in range(own_blocks):
                cut = slice(i * TILE, (i + 1) * TILE)
                wide_out[i, s, v : v + 1, :] = rotor[s : s + 1, cut]
                wide_out[i, rows + s, v : v + 1, :] = a_s[v, s, 0:1, cut]
                wide_out[i, 2 * rows + s, v : v + 1, :] = v_s[v, s, 0:1, cut]
    row8 = iota((8, TILE), 0)
    filled = row8 < var_count
    for i in range(own_blocks):
        if i in (0, own_blocks - 1):
            side = 4 if i else 0
            for s in range(rows):
                wide_out[i, 2 * rows + s, 6:8, :] = edges[side + 2 * s : side + 2 * s + 2]
        groups = []
        for s in range(rows):
            p_high, p_rest = split(wide_out[i, rows + s])
            u_high, u_rest = split(wide_out[i, 2 * rows + s])
            groups.append((
                jnp.where(filled, wide_out[i, s], pltpu.roll(u_rest, 6, 0)),
                jnp.where(filled, p_high, pltpu.roll(u_rest, 4, 0)),
                jnp.where(filled, p_rest, pltpu.roll(u_rest, 2, 0)),
                u_high,
            ))
        for n in range(4):
            out[i, n * 16 : n * 16 + 16, :] = jnp.concatenate([x[n] for x in groups], axis=0).astype(jnp.bfloat16)


def second_kernel(
    masks, mine, other, v_r, v_s, a_r, a_s, primal_table, pull_table, margin_in,
    o_r, o_s, side_r, side_s, q_out, speeds_out, scaled_out, moved_out, inner, outer, spot, g, flux, held, margin, sem,
):
    var_count, rows, layers, cells = a_r.shape
    fetch = pltpu.make_async_copy(margin_in, margin, sem)
    fetch.start()
    total = 2 * mine.shape[0]
    own_blocks = cells // TILE
    entries = primal_table.shape[2]
    spread = REACH + own_blocks + 1
    first_block = lax.axis_index("circ") * own_blocks
    row8 = iota((8, TILE), 0)
    layer_all = iota((layers, cells), 0)
    left = wrapped(first_block - 1 + total, total)
    right = wrapped(first_block + own_blocks, total)

    filled = row8 < var_count
    here = lax.axis_index("circ")
    for at in range(total):
        half, part = divmod(at, total // 2)
        place, i = divmod(part, own_blocks)
        mask = half
        for n, m in enumerate(masks):
            mask ^= m if place >> n & 1 else 0
        b = jnp.bitwise_xor(here, mask) * own_blocks + i
        whole = other if half else mine
        tiles = [whole[part, n * 16 : n * 16 + 16, :].astype(f32) for n in range(4)]
        for s in range(rows):
            rotor, p_high, p_rest, u_high = [x[s * 8 : s * 8 + 8] for x in tiles]
            u_rest = jnp.where(
                row8 < 2, pltpu.roll(rotor, 2, 0), jnp.where(row8 < 4, pltpu.roll(p_high, 4, 0), pltpu.roll(p_rest, 6, 0))
            )
            g[b, s] = rotor
            g[b, rows + s] = p_high + p_rest
            g[b, 2 * rows + s] = u_high + jnp.where(filled, u_rest, 0.0)
    spot[0:2, :] = g[left, 2 * rows, 6:8, :]
    spot[2:4, :] = g[left, 2 * rows + 1, 6:8, :]
    spot[4:6, :] = g[right, 2 * rows, 6:8, :]
    spot[6:8, :] = g[right, 2 * rows + 1, 6:8, :]
    spots = spot[...]
    columns = [
        lax.dot_general(spots, edge_pick(q, cells), (((0,), (0,)), ((), ())), preferred_element_type=f32)
        for q in range(2)
    ]

    fetch.wait()

    def block(s, b, t):
        primal = jnp.zeros((8, TILE), f32)
        for k in range(entries):
            primal = primal + primal_table[s, t, k : k + 1, :] * g[margin[s, k, b], s]
        primal = jnp.where(filled, primal, 0.0)
        parts = flux_parts(primal)
        return (primal, *parts), flux_of(primal, *parts, g[b, rows + s])

    def keep(s, at, b, parts, moved):
        q_out[s, at], speeds_out[s, at], scaled_out[s, at] = parts
        moved_out[s, at] = moved

    for s in range(rows):
        base = window(margin, s, first_block, total)
        blocks = window_blocks(base, first_block, own_blocks, total)
        for t in range(spread):
            parts, moved = block(s, blocks[t], t)
            flux[s, t] = moved.astype(jnp.bfloat16).astype(f32)
            if 0 < t < spread - 1:
                keep(s, t - 1, blocks[t], parts, moved)
        own = []
        for i in range(own_blocks):
            parts, moved = block(s, first_block + i, spread + i)
            own.append(moved)
            keep(s, spread - 2 + i, first_block + i, parts, moved)
        blank = [jnp.zeros((8, TILE), f32)] * (own_blocks - 2)
        side_flux = [block(s, at, spread + own_blocks + n)[1] for n, at in enumerate((left, right))]
        pulls = [pull_row(lambda t: flux[s, t + 1], pull_table, s, slot) for slot in range(-1, own_blocks + 1)]

        def at_sides(low, high):
            return jnp.concatenate([pltpu.roll(low, 1, 1), *blank, pltpu.roll(high, TILE - 1, 1)], axis=1)

        pulled = step_size * jnp.concatenate(pulls[1:-1], axis=1)
        side_r[s] = step_size * at_sides(pulls[0], pulls[-1])
        pushed = step_size * jnp.concatenate(own, axis=1)
        side_s[s] = -step_size * at_sides(*side_flux)
        for v in range(var_count):
            at = (v * rows + s) * 8
            cut = slice(at, at + layers)
            o_r[v, s] = (
                v_r[v, s] + carry * columns[0][cut] + jnp.where(layer_all == layers - 1, pulled[v : v + 1], 0.0)
            )
            o_s[v, s] = v_s[v, s] + carry * columns[1][cut] - jnp.where(layer_all == 0, pushed[v : v + 1], 0.0)

    last = jnp.concatenate([spots, jnp.ones((8, TILE), f32)], axis=0).astype(jnp.bfloat16)
    odd = jnp.bitwise_and(lax.axis_index("span"), 1)
    for to, s in ((inner, (1 - odd) * (rows - 1)), (outer, odd * (rows - 1))):
        for j in range(total // 2):
            to[j] = jnp.concatenate([g[2 * j, rows + s], g[2 * j + 1, rows + s]], axis=0).astype(jnp.bfloat16)
        for v in range(var_count):
            for n, ref in enumerate((a_r, a_s, o_r, o_s)):
                held[v, n * layers : (n + 1) * layers, :] = ref[v, s]
            for i in range(own_blocks):
                to[total // 2 + v * own_blocks + i] = held[v, :, i * TILE : (i + 1) * TILE].astype(jnp.bfloat16)
        to[total // 2 + var_count * own_blocks] = last


def corner_of(tile, row, rows):
    lane = iota((8, TILE), 1)
    group = lax.rem(lax.shift_right_logical(lane, 3), rows)
    spot = tile.astype(f32)[0:8]
    first = jnp.where(group == 0, pltpu.roll(spot, (TILE - 8 * (rows - 1)) % TILE, 1), 0.0)
    final = jnp.where(group == rows - 1, pltpu.roll(spot, 8 * (rows - 1), 1), 0.0)
    return jnp.where(row == 0, first, final)


def corner_columns(corner, cells):
    return [
        lax.dot_general(corner, edge_pick(n, cells), (((0,), (0,)), ((), ())), preferred_element_type=f32)
        for n in range(2)
    ]


def row_flux(halo, row, base, q, speeds, scaled, p, pull_table, flux, first_block, own_blocks, total):
    spread = REACH + own_blocks + 1
    own = []
    for t in range(spread - 2 + own_blocks):
        b = wrapped(base + t, total) if t < spread - 2 else first_block + t - (spread - 2)
        both = halo[lax.shift_right_logical(b, 1)].astype(f32)
        beyond = jnp.where(jnp.bitwise_and(b, 1) == 1, both[8:16], both[0:8])
        moved = flux_of(q[row, t], speeds[row, t], scaled[row, t], p[row, t] + carry * beyond)
        if t < spread - 2:
            flux[t] = moved.astype(jnp.bfloat16).astype(f32)
        else:
            own.append(moved)
    pulls = [pull_row(lambda t: flux[t], pull_table, row, slot) for slot in range(own_blocks)]
    return step_size * jnp.concatenate(pulls, axis=1), -step_size * jnp.concatenate(own, axis=1)


def third_kernel(
    inner, o_r, o_s, side_r, side_s, q, speeds, scaled, pushed, spot, g, a_r, a_s, jd_r, jd_s, jo_r, jo_s, src_r, src_s,
    pull_table, margin_in, part_r, part_s, start, p, flux, x_r, x_s, held, margin, sem,
):
    fetch = pltpu.make_async_copy(margin_in, margin, sem)
    fetch.start()
    var_count, rows, layers, cells = a_r.shape
    total = margin.shape[2]
    own_blocks = cells // TILE
    first_block = lax.axis_index("circ") * own_blocks
    end = total // 2 + var_count * own_blocks
    near_row = (1 - jnp.bitwise_and(lax.axis_index("span"), 1)) * (rows - 1)
    near = [jnp.where(near_row == s, 1.0, 0.0).astype(f32) for s in range(rows)]
    for x in (x_r, x_s):
        x[...] = jnp.zeros(x.shape, f32)
    for v in range(var_count):
        for i in range(own_blocks):
            held[v, :, i * TILE : (i + 1) * TILE] = inner[total // 2 + v * own_blocks + i].astype(f32)
    lane_all = iota((layers, cells), 1)
    layer_all = iota((layers, cells), 0)
    lane = iota((8, TILE), 1)
    edge = jnp.logical_or(lane_all == 0, lane_all == cells - 1)
    beyond = [
        lax.dot_general(spot[...], edge_pick(n, cells), (((0,), (0,)), ((), ())), preferred_element_type=f32)
        for n in (2, 3)
    ]
    columns = corner_columns(corner_of(inner[end], near_row, rows), cells)
    fields = (
        (o_r, side_r, a_r, jd_r, jo_r, src_r, x_r, part_r, layers - 1),
        (o_s, side_s, a_s, jd_s, jo_s, src_s, x_s, part_s, 0),
    )
    for n, (o, side, a, jd, jo, src, x, part, layer) in enumerate(fields):
        old = slice(n * layers, (n + 1) * layers)
        new = slice((2 + n) * layers, (3 + n) * layers)
        for v in range(var_count):
            for s in range(rows):
                x[v * rows + s, 0:layers, :] = o[v, s] + (carry * near[s]) * held[v, old, :]
        for s in range(rows):
            state_row = [x[v * rows + s, 0:layers, :] for v in range(var_count)]
            for v in range(var_count):
                wide = x[v * rows + s]
                at = (v * rows + s) * 8
                beside = (lanes_apart(wide) + layers_apart(wide))[0:layers]
                beside = beside + beyond[n][at : at + layers] + carry * columns[n][at : at + layers]
                beside = beside + jnp.where(
                    edge, carry * a[v, s] + jnp.where(layer_all == layer, side[s, v : v + 1, :], 0.0), 0.0
                )
                beside = beside + near[s] * (held[v, new, :] + carry * a[v, s])
                if s > 0:
                    beside = beside + x[v * rows + s - 1, 0:layers, :]
                if s < rows - 1:
                    beside = beside + x[v * rows + s + 1, 0:layers, :]
                res = jacobian_row(jd, jo, state_row, v, s, var_count) - coupling * beside - src[v, s]
                part[v, s] = state_row[v] - step_size * res
    fetch.wait()

    def advanced(s, b, moved):
        place = lax.rem(b, own_blocks)
        before = jnp.where(place == 0, carry, 0.0).astype(f32)
        after = jnp.where(place == own_blocks - 1, carry, 0.0).astype(f32)
        low = pltpu.roll(g[wrapped(b - 1 + total, total), rows + s], 1, 1)
        high = pltpu.roll(g[wrapped(b + 1, total), rows + s], TILE - 1, 1)
        base = g[b, 2 * rows + s]
        base = base + jnp.where(lane == 0, low * before, 0.0) + jnp.where(lane == TILE - 1, high * after, 0.0)
        return base - step_size * moved

    spread = REACH + own_blocks + 1
    for s in range(rows):
        blocks = window_blocks(window(margin, s, first_block, total), first_block, own_blocks, total)
        for t, b in enumerate(blocks[1 : spread - 1] + blocks[spread : spread + own_blocks]):
            p[s, t] = advanced(s, b, pushed[s, t])
    extra = row_flux(
        inner, near_row, window(margin, near_row, first_block, total), q, speeds, scaled, p, pull_table, flux,
        first_block, own_blocks, total,
    )
    start[...] = jnp.full((8, TILE), window(margin, rows - 1 - near_row, first_block, total)).astype(f32)
    for n, (part, layer) in enumerate(((part_r, layers - 1), (part_s, 0))):
        at = slice(layer, layer + 1)
        for v in range(var_count):
            part[v, near_row, at, :] = part[v, near_row, at, :] + extra[n][v : v + 1]


def fourth_kernel(
    bands, outer, part_r, part_s, q, speeds, scaled, p, a_r, a_s, jd_r, jd_s, jo_r, jo_s, pull_table, start,
    away_r, away_s, flux, x_r, x_s, held, out_r, out_s, sems,
):
    var_count, rows, layers, cells = a_r.shape
    own_blocks = cells // TILE
    total = 2 * (outer.shape[0] - 1 - var_count * own_blocks)
    base = jnp.max(start[...]).astype(jnp.int32)
    own_blocks = cells // TILE
    first_block = lax.axis_index("circ") * own_blocks
    end = total // 2 + var_count * own_blocks
    band = lax.axis_index("span")
    odd = jnp.bitwise_and(band, 1)
    far_row = odd * (rows - 1)
    inside = jnp.logical_and(band > 0, band < bands - 1)
    live = jnp.where(inside, carry, 0.0).astype(f32)
    next_row = far_row + 1 - 2 * odd
    for x in (x_r, x_s):
        x[...] = jnp.zeros(x.shape, f32)
    for v in range(var_count):
        for i in range(own_blocks):
            held[v, :, i * TILE : (i + 1) * TILE] = outer[total // 2 + v * own_blocks + i].astype(f32)
    columns = corner_columns(corner_of(outer[end], far_row, rows), cells)
    fields = ((part_r, a_r, jd_r, jo_r, x_r, out_r), (part_s, a_s, jd_s, jo_s, x_s, out_s))
    for n, (part, a, jd, jo, x, out) in enumerate(fields):
        old = slice(n * layers, (n + 1) * layers)
        new = slice((2 + n) * layers, (3 + n) * layers)
        for v in range(var_count):
            x[v, 0:layers, :] = carry * held[v, old, :]
        state_row = [x[v, 0:layers, :] for v in range(var_count)]
        for v in range(var_count):
            wide = x[v]
            beside = (lanes_apart(wide) + layers_apart(wide))[0:layers]
            for s in (0, rows - 1):
                at = (v * rows + s) * 8
                beside = beside + carry * columns[n][at : at + layers]
            extra = carry * (beside + held[v, new, :]) + (carry * live) * a[v, far_row]
            gone = jacobian_row(jd, jo, state_row, v, far_row, var_count)
            for s in range(rows):
                out[v, s] = part[v, s]
            out[v, far_row] = part[v, far_row] + state_row[v] - step_size * gone + extra
            out[v, next_row] = part[v, next_row] + carry * state_row[v]
    extra = row_flux(
        outer, far_row, base, q, speeds, scaled, p, pull_table, flux, first_block, own_blocks, total
    )
    copies = []
    for n, (out, away, layer) in enumerate(((out_r, away_r, layers - 1), (out_s, away_s, 0))):
        at = slice(layer, layer + 1)
        for v in range(var_count):
            out[v, far_row, at, :] = out[v, far_row, at, :] + extra[n][v : v + 1]
        copies.append(pltpu.make_async_copy(out, away, sems.at[n]))
        copies[-1].start()
    for copy in copies:
        copy.wait()


def per_device(
    adjoint_rotor,
    adjoint_stator,
    jac_diag_rotor,
    jac_diag_stator,
    jac_off_rotor,
    jac_off_stator,
    source_rotor,
    source_stator,
    rotor_state,
    margin_block,
    face_count,
    margin_weight,
):
    var_count, rows, layers, cells = adjoint_rotor.shape
    own_blocks = cells // TILE
    total = margin_block.shape[1]
    spread = REACH + own_blocks + 1
    field = jax.ShapeDtypeStruct(adjoint_rotor.shape, f32)
    vmem = pl.BlockSpec(memory_space=pltpu.VMEM)
    smem = pl.BlockSpec(memory_space=pltpu.SMEM)
    anywhere = pl.BlockSpec(memory_space=pl.ANY)
    padded = pltpu.VMEM((TILE // 8, 8, cells), f32)

    margin = jnp.swapaxes(margin_block, 1, 2)
    arguments = (
        adjoint_rotor, adjoint_stator, jac_diag_rotor, jac_diag_stator, jac_off_rotor, jac_off_stator,
        source_rotor, source_stator, rotor_state, margin, face_count, margin_weight,
    )
    shapes = [jax.ShapeDtypeStruct(x.shape, x.dtype) for x in arguments]
    v_r, v_s, share, a_r, a_s, weights, margin, count = pl.pallas_call(
        first_kernel,
        out_shape=(
            field, field, jax.ShapeDtypeStruct((own_blocks, 64, TILE), jnp.bfloat16),
            shapes[0], shapes[1], shapes[11], shapes[9], shapes[10],
        ),
        in_specs=[pl.BlockSpec(memory_space=pltpu.HBM)] * 12,
        out_specs=(vmem,) * 8,
        scratch_shapes=[pltpu.VMEM(x.shape, x.dtype) for x in shapes[2:9]]
        + [padded] * 4
        + [pltpu.SemaphoreType.DMA((12,)), pltpu.VMEM((own_blocks, 3 * rows, 8, TILE), f32)],
        compiler_params=params,
        name="local_part",
    )(*[pltpu.with_memory_space_constraint(x, pltpu.HBM) for x in arguments])
    primal_table, pull_table = pl.pallas_call(
        table_kernel,
        out_shape=(
            jax.ShapeDtypeStruct((rows, spread + own_blocks + 2, margin_weight.shape[2], TILE), f32),
            jax.ShapeDtypeStruct((rows, own_blocks + 2, REACH, TILE), f32),
        ),
        in_specs=[vmem] + [smem] * 2,
        out_specs=(vmem,) * 2,
        compiler_params=params,
        name="weight_tables",
    )(weights, margin, count)
    members = lax.axis_size("circ")
    mine, masks = share, []
    mask = members // 2
    while mask > 0:
        hop = mask | 1
        other = lax.ppermute(mine, "circ", [(i, i ^ hop) for i in range(members)])
        if mask > 1:
            mine = jnp.concatenate([mine, other], axis=0)
            if not masks:
                mine, primal_table, pull_table = lax.optimization_barrier((mine, primal_table, pull_table))
            masks.append(hop)
        mask //= 2
    tiles = jax.ShapeDtypeStruct((total // 2 + var_count * own_blocks + 1, 16, TILE), jnp.bfloat16)
    sides = jax.ShapeDtypeStruct((rows, 8, cells), f32)
    corner = jax.ShapeDtypeStruct((8, TILE), f32)
    gathered = jax.ShapeDtypeStruct((total, 3 * rows, 8, TILE), f32)
    listed = jax.ShapeDtypeStruct((rows, spread - 2 + own_blocks, 8, TILE), f32)
    o_r, o_s, side_r, side_s, q, speeds, scaled, pushed, inner, outer, spot, g = pl.pallas_call(
        functools.partial(second_kernel, masks),
        out_shape=(field,) * 2 + (sides,) * 2 + (listed,) * 4 + (tiles,) * 2 + (corner, gathered),
        in_specs=[vmem] * 8 + [anywhere],
        out_specs=(vmem,) * 12,
        scratch_shapes=[
            pltpu.VMEM((rows, spread, 8, TILE), f32),
            pltpu.VMEM((var_count, 4 * layers, cells), f32),
            pltpu.SMEM(margin.shape, jnp.int32),
            pltpu.SemaphoreType.DMA(()),
        ],
        compiler_params=params,
        name="interface_part",
    )(mine, other, v_r, v_s, a_r, a_s, primal_table, pull_table, margin)
    bands = lax.axis_size("span")
    near = [(i, i ^ 1) for i in range(bands)]
    far = [pair for i in range(1, bands - 1, 2) for pair in ((i, i + 1), (i + 1, i))]
    inner = lax.ppermute(inner, "span", near)
    outer = lax.ppermute(outer, "span", far)
    held = pltpu.VMEM((var_count, 4 * layers, cells), f32)
    flux = pltpu.VMEM((spread - 2, 8, TILE), f32)
    listing = pltpu.SMEM(margin.shape, jnp.int32)
    small = pltpu.VMEM((8, 8, cells), f32)
    part_r, part_s, start, p = pl.pallas_call(
        third_kernel,
        out_shape=(field, field, corner, listed),
        in_specs=[vmem] * 20 + [anywhere],
        out_specs=(vmem,) * 4,
        scratch_shapes=[flux, padded, padded, held, listing, pltpu.SemaphoreType.DMA(())],
        compiler_params=params,
        name="near_part",
    )(
        inner, o_r, o_s, side_r, side_s, q, speeds, scaled, pushed, spot, g, a_r, a_s, jac_diag_rotor, jac_diag_stator,
        jac_off_rotor, jac_off_stator, source_rotor, source_stator, pull_table, margin,
    )
    out_r, out_s = pl.pallas_call(
        functools.partial(fourth_kernel, bands),
        out_shape=(field, field),
        in_specs=[vmem] * 15,
        out_specs=(anywhere,) * 2,
        scratch_shapes=[
            flux, small, small, held, pltpu.VMEM(field.shape, f32), pltpu.VMEM(field.shape, f32),
            pltpu.SemaphoreType.DMA((2,)),
        ],
        compiler_params=params,
        name="final_part",
    )(
        outer, part_r, part_s, q, speeds, scaled, p, a_r, a_s, jac_diag_rotor, jac_diag_stator,
        jac_off_rotor, jac_off_stator, pull_table, start,
    )
    return (out_r, out_s)


def solution(mesh):
    field = P(None, "span", None, "circ")
    placed = (
        (field,) * 4
        + (P(None, None, "span", None, "circ"),) * 2
        + (field,) * 2
        + (P(None, "span", "circ"), P("span", None, None), P("span", None), P("span", None, None, None))
    )
    return jax.shard_map(
        per_device, mesh=mesh, in_specs=placed, out_specs=(field, field), check_vma=False
    )
```

```python
import functools

import jax
import jax.numpy as jnp
from jax import lax
from jax.experimental import pallas as pl
from jax.experimental.pallas import tpu as pltpu
from jax.sharding import PartitionSpec as P

step_size = 0.1
coupling = 0.2
carry = step_size * coupling
REACH = 8
TILE = 128
f32 = jnp.float32
params = pltpu.CompilerParams(vmem_limit_bytes=24 * 1024 * 1024)


def iota(shape, dim):
    return lax.broadcasted_iota(jnp.int32, shape, dim)


def wrapped(x, count):
    if count & (count - 1) == 0:
        return jnp.bitwise_and(x, count - 1)
    return lax.rem(x + 4 * count, count)


def lanes_apart(x):
    cells = x.shape[1]
    lane = iota(x.shape, 1)
    before = jnp.where(lane == 0, 0.0, pltpu.roll(x, 1, 1))
    after = jnp.where(lane == cells - 1, 0.0, pltpu.roll(x, cells - 1, 1))
    return before + after


def layers_apart(x):
    return pltpu.roll(x, 1, 0) + pltpu.roll(x, 7, 0)


def edge_pick(row, cells):
    at = iota((8, cells), 0)
    lane = iota((8, cells), 1)
    first = jnp.logical_and(at == row, lane == 0)
    last = jnp.logical_and(at == 4 + row, lane == cells - 1)
    return jnp.where(jnp.logical_or(first, last), 1.0, 0.0).astype(f32)


def split(x):
    high = x.astype(jnp.bfloat16).astype(f32)
    return high, x - high


def flux_parts(primal):
    square = primal * primal
    under = 6.0 + jnp.sum(square, axis=0, keepdims=True)
    return jnp.sqrt(1.0 + square), 0.5 * primal / under


def flux_of(primal, speeds, scaled, adjoint):
    return speeds * adjoint + scaled * jnp.sum(primal * adjoint, axis=0, keepdims=True)


def jacobian_row(diag, off, state, v, s, var_count):
    total = diag[v, s] * state[v]
    for w in range(var_count):
        total = total + off[w, v, s].astype(f32) * state[w]
    return total


def pull_row(flux, table, s, slot):
    acc = jnp.zeros((8, TILE), f32)
    for e in range(REACH):
        acc = acc + table[s, slot + 1, e : e + 1, :] * flux(slot + e)
    return acc


def window(margin, s, first_block, total):
    return first_block - margin[s, 0, 0] - 5 + 4 * total


def window_blocks(base, first_block, own_blocks, total):
    found = [wrapped(base - 1 + t, total) for t in range(REACH + own_blocks + 1)]
    sides = [wrapped(first_block - 1 + total, total), wrapped(first_block + own_blocks, total)]
    return found + [first_block + i for i in range(own_blocks)] + sides


def table_kernel(weights, margin, count, primal_table, pull_table):
    rows, total, entries, _ = weights.shape
    own_blocks = pull_table.shape[1] - 2
    first_block = lax.axis_index("circ") * own_blocks
    for s in range(rows):
        base = window(margin, s, first_block, total)
        blocks = window_blocks(base, first_block, own_blocks, total)
        entry = iota((entries, TILE), 0)
        for t, b in enumerate(blocks):
            primal_table[s, t] = jnp.where(entry < count[s, b], weights[s, b], 0.0)
        for slot in range(-1, own_blocks + 1):
            target = wrapped(first_block + slot + total, total)
            for e in range(REACH):
                b = blocks[slot + 1 + e]
                k = wrapped(target - margin[s, 0, b] + total, total)
                live = jnp.where(k < count[s, b], 1.0, 0.0).astype(f32)
                kept = jnp.minimum(k, entries - 1)
                pull_table[s, slot + 1, e : e + 1, :] = weights[s, b, pl.ds(kept, 1), :] * live


def first_kernel(*refs):
    outer, refs = refs[:12], refs[12:]
    v_r, v_s, out, a_r, a_s, weights, margin, count = refs[:8]
    jd_r, jd_s, jo_r, jo_s, src_r, src_s, state = refs[8:15]
    xs, sems, wide_out = refs[15:19], refs[19], refs[20]
    var_count, rows, layers, cells = a_r.shape
    own_blocks = cells // TILE
    inner = (a_r, a_s, jd_r, jd_s, jo_r, jo_s, src_r, src_s, state, margin, count, weights)
    copies = [pltpu.make_async_copy(x, y, sems.at[n]) for n, (x, y) in enumerate(zip(outer, inner))]
    for copy in copies:
        copy.start()
    wide_out[...] = jnp.zeros(wide_out.shape, f32)
    for x in xs:
        x[...] = jnp.zeros(x.shape, f32)
    for copy in copies[:9]:
        copy.wait()
    fields = ((a_r, jd_r, jo_r, src_r, v_r, xs[0], xs[2]), (a_s, jd_s, jo_s, src_s, v_s, xs[1], xs[3]))
    for a, jd, jo, src, partial, x_a, x_p in fields:
        for v in range(var_count):
            for s in range(rows):
                x_a[v * rows + s, 0:layers, :] = a[v, s]
        for s in range(rows):
            state_row = [a[v, s] for v in range(var_count)]
            for v in range(var_count):
                wide = x_a[v * rows + s]
                beside = (lanes_apart(wide) + layers_apart(wide))[0:layers]
                if s > 0:
                    beside = beside + a[v, s - 1]
                if s < rows - 1:
                    beside = beside + a[v, s + 1]
                res = jacobian_row(jd, jo, state_row, v, s, var_count) - coupling * beside - src[v, s]
                new = state_row[v] - step_size * res
                partial[v, s] = new
                x_p[v * rows + s, 0:layers, :] = new
    edges = jnp.zeros((8, TILE), f32)
    for q in range(4):
        flat = xs[q][...].reshape(TILE, cells)
        edges = edges + lax.dot_general(
            edge_pick(q, cells), flat, (((1,), (1,)), ((), ())), preferred_element_type=f32
        )
    for v in range(var_count):
        rotor = state[v].astype(f32)
        for s in range(rows):
            for i in range(own_blocks):
                cut = slice(i * TILE, (i + 1) * TILE)
                wide_out[i, s, v : v + 1, :] = rotor[s : s + 1, cut]
                wide_out[i, rows + s, v : v + 1, :] = a_s[v, s, 0:1, cut]
                wide_out[i, 2 * rows + s, v : v + 1, :] = v_s[v, s, 0:1, cut]
    row8 = iota((8, TILE), 0)
    filled = row8 < var_count
    for i in range(own_blocks):
        if i in (0, own_blocks - 1):
            side = 4 if i else 0
            for s in range(rows):
                wide_out[i, 2 * rows + s, 6:8, :] = edges[side + 2 * s : side + 2 * s + 2]
        groups = []
        for s in range(rows):
            p_high, p_rest = split(wide_out[i, rows + s])
            u_high, u_rest = split(wide_out[i, 2 * rows + s])
            groups.append((
                jnp.where(filled, wide_out[i, s], pltpu.roll(u_rest, 6, 0)),
                jnp.where(filled, p_high, pltpu.roll(u_rest, 4, 0)),
                jnp.where(filled, p_rest, pltpu.roll(u_rest, 2, 0)),
                u_high,
            ))
        for n in range(4):
            out[i, n * 16 : n * 16 + 16, :] = jnp.concatenate([x[n] for x in groups], axis=0).astype(jnp.bfloat16)
    for copy in copies[9:]:
        copy.wait()


def second_kernel(
    masks, mine, other, v_r, v_s, a_r, a_s, primal_table, pull_table, margin_in,
    o_r, o_s, side_r, side_s, q_out, speeds_out, scaled_out, moved_out, inner, outer, spot, g, flux, held, margin, sem,
):
    var_count, rows, layers, cells = a_r.shape
    fetch = pltpu.make_async_copy(margin_in, margin, sem)
    fetch.start()
    total = 2 * mine.shape[0]
    own_blocks = cells // TILE
    entries = primal_table.shape[2]
    spread = REACH + own_blocks + 1
    first_block = lax.axis_index("circ") * own_blocks
    row8 = iota((8, TILE), 0)
    layer_all = iota((layers, cells), 0)
    left = wrapped(first_block - 1 + total, total)
    right = wrapped(first_block + own_blocks, total)

    filled = row8 < var_count
    here = lax.axis_index("circ")
    for at in range(total):
        half, part = divmod(at, total // 2)
        place, i = divmod(part, own_blocks)
        mask = half
        for n, m in enumerate(masks):
            mask ^= m if place >> n & 1 else 0
        b = jnp.bitwise_xor(here, mask) * own_blocks + i
        whole = other if half else mine
        tiles = [whole[part, n * 16 : n * 16 + 16, :].astype(f32) for n in range(4)]
        for s in range(rows):
            rotor, p_high, p_rest, u_high = [x[s * 8 : s * 8 + 8] for x in tiles]
            u_rest = jnp.where(
                row8 < 2, pltpu.roll(rotor, 2, 0), jnp.where(row8 < 4, pltpu.roll(p_high, 4, 0), pltpu.roll(p_rest, 6, 0))
            )
            g[b, s] = rotor
            g[b, rows + s] = p_high + p_rest
            g[b, 2 * rows + s] = u_high + jnp.where(filled, u_rest, 0.0)
    spot[0:2, :] = g[left, 2 * rows, 6:8, :]
    spot[2:4, :] = g[left, 2 * rows + 1, 6:8, :]
    spot[4:6, :] = g[right, 2 * rows, 6:8, :]
    spot[6:8, :] = g[right, 2 * rows + 1, 6:8, :]
    spots = spot[...]
    columns = [
        lax.dot_general(spots, edge_pick(q, cells), (((0,), (0,)), ((), ())), preferred_element_type=f32)
        for q in range(2)
    ]

    fetch.wait()

    def block(s, b, t):
        primal = jnp.zeros((8, TILE), f32)
        for k in range(entries):
            primal = primal + primal_table[s, t, k : k + 1, :] * g[margin[s, k, b], s]
        primal = jnp.where(filled, primal, 0.0)
        parts = flux_parts(primal)
        return (primal, *parts), flux_of(primal, *parts, g[b, rows + s])

    def keep(s, at, b, parts, moved):
        q_out[s, at], speeds_out[s, at], scaled_out[s, at] = parts
        moved_out[s, at] = moved

    for s in range(rows):
        base = window(margin, s, first_block, total)
        blocks = window_blocks(base, first_block, own_blocks, total)
        for t in range(spread):
            parts, moved = block(s, blocks[t], t)
            flux[s, t] = moved.astype(jnp.bfloat16).astype(f32)
            if 0 < t < spread - 1:
                keep(s, t - 1, blocks[t], parts, moved)
        own = []
        for i in range(own_blocks):
            parts, moved = block(s, first_block + i, spread + i)
            own.append(moved)
            keep(s, spread - 2 + i, first_block + i, parts, moved)
        blank = [jnp.zeros((8, TILE), f32)] * (own_blocks - 2)
        side_flux = [block(s, at, spread + own_blocks + n)[1] for n, at in enumerate((left, right))]
        pulls = [pull_row(lambda t: flux[s, t + 1], pull_table, s, slot) for slot in range(-1, own_blocks + 1)]

        def at_sides(low, high):
            return jnp.concatenate([pltpu.roll(low, 1, 1), *blank, pltpu.roll(high, TILE - 1, 1)], axis=1)

        pulled = step_size * jnp.concatenate(pulls[1:-1], axis=1)
        side_r[s] = step_size * at_sides(pulls[0], pulls[-1])
        pushed = step_size * jnp.concatenate(own, axis=1)
        side_s[s] = -step_size * at_sides(*side_flux)
        for v in range(var_count):
            at = (v * rows + s) * 8
            cut = slice(at, at + layers)
            o_r[v, s] = (
                v_r[v, s] + carry * columns[0][cut] + jnp.where(layer_all == layers - 1, pulled[v : v + 1], 0.0)
            )
            o_s[v, s] = v_s[v, s] + carry * columns[1][cut] - jnp.where(layer_all == 0, pushed[v : v + 1], 0.0)

    last = jnp.concatenate([spots, jnp.ones((8, TILE), f32)], axis=0).astype(jnp.bfloat16)
    odd = jnp.bitwise_and(lax.axis_index("span"), 1)
    for to, s in ((inner, (1 - odd) * (rows - 1)), (outer, odd * (rows - 1))):
        for j in range(total // 2):
            to[j] = jnp.concatenate([g[2 * j, rows + s], g[2 * j + 1, rows + s]], axis=0).astype(jnp.bfloat16)
        for v in range(var_count):
            for n, ref in enumerate((a_r, a_s, o_r, o_s)):
                held[v, n * layers : (n + 1) * layers, :] = ref[v, s]
            for i in range(own_blocks):
                to[total // 2 + v * own_blocks + i] = held[v, :, i * TILE : (i + 1) * TILE].astype(jnp.bfloat16)
        to[total // 2 + var_count * own_blocks] = last


def corner_of(tile, row, rows):
    lane = iota((8, TILE), 1)
    group = lax.rem(lax.shift_right_logical(lane, 3), rows)
    spot = tile.astype(f32)[0:8]
    first = jnp.where(group == 0, pltpu.roll(spot, (TILE - 8 * (rows - 1)) % TILE, 1), 0.0)
    final = jnp.where(group == rows - 1, pltpu.roll(spot, 8 * (rows - 1), 1), 0.0)
    return jnp.where(row == 0, first, final)


def corner_columns(corner, cells):
    return [
        lax.dot_general(corner, edge_pick(n, cells), (((0,), (0,)), ((), ())), preferred_element_type=f32)
        for n in range(2)
    ]


def row_flux(halo, row, base, q, speeds, scaled, p, pull_table, flux, first_block, own_blocks, total):
    spread = REACH + own_blocks + 1
    own = []
    for t in range(spread - 2 + own_blocks):
        b = wrapped(base + t, total) if t < spread - 2 else first_block + t - (spread - 2)
        both = halo[lax.shift_right_logical(b, 1)].astype(f32)
        beyond = jnp.where(jnp.bitwise_and(b, 1) == 1, both[8:16], both[0:8])
        moved = flux_of(q[row, t], speeds[row, t], scaled[row, t], p[row, t] + carry * beyond)
        if t < spread - 2:
            flux[t] = moved.astype(jnp.bfloat16).astype(f32)
        else:
            own.append(moved)
    pulls = [pull_row(lambda t: flux[t], pull_table, row, slot) for slot in range(own_blocks)]
    return step_size * jnp.concatenate(pulls, axis=1), -step_size * jnp.concatenate(own, axis=1)


def third_kernel(
    inner, o_r, o_s, side_r, side_s, q, speeds, scaled, pushed, spot, g, a_r, a_s, jd_r, jd_s, jo_r, jo_s, src_r, src_s,
    pull_table, margin_in, part_r, part_s, start, p, flux, x_r, x_s, held, margin, sem,
):
    fetch = pltpu.make_async_copy(margin_in, margin, sem)
    fetch.start()
    var_count, rows, layers, cells = a_r.shape
    total = margin.shape[2]
    own_blocks = cells // TILE
    first_block = lax.axis_index("circ") * own_blocks
    end = total // 2 + var_count * own_blocks
    near_row = (1 - jnp.bitwise_and(lax.axis_index("span"), 1)) * (rows - 1)
    near = [jnp.where(near_row == s, 1.0, 0.0).astype(f32) for s in range(rows)]
    for x in (x_r, x_s):
        x[...] = jnp.zeros(x.shape, f32)
    for v in range(var_count):
        for i in range(own_blocks):
            held[v, :, i * TILE : (i + 1) * TILE] = inner[total // 2 + v * own_blocks + i].astype(f32)
    lane_all = iota((layers, cells), 1)
    layer_all = iota((layers, cells), 0)
    lane = iota((8, TILE), 1)
    edge = jnp.logical_or(lane_all == 0, lane_all == cells - 1)
    beyond = [
        lax.dot_general(spot[...], edge_pick(n, cells), (((0,), (0,)), ((), ())), preferred_element_type=f32)
        for n in (2, 3)
    ]
    columns = corner_columns(corner_of(inner[end], near_row, rows), cells)
    fields = (
        (o_r, side_r, a_r, jd_r, jo_r, src_r, x_r, part_r, layers - 1),
        (o_s, side_s, a_s, jd_s, jo_s, src_s, x_s, part_s, 0),
    )
    for n, (o, side, a, jd, jo, src, x, part, layer) in enumerate(fields):
        old = slice(n * layers, (n + 1) * layers)
        new = slice((2 + n) * layers, (3 + n) * layers)
        for v in range(var_count):
            for s in range(rows):
                x[v * rows + s, 0:layers, :] = o[v, s] + (carry * near[s]) * held[v, old, :]
        for s in range(rows):
            state_row = [x[v * rows + s, 0:layers, :] for v in range(var_count)]
            for v in range(var_count):
                wide = x[v * rows + s]
                at = (v * rows + s) * 8
                beside = (lanes_apart(wide) + layers_apart(wide))[0:layers]
                beside = beside + beyond[n][at : at + layers] + carry * columns[n][at : at + layers]
                beside = beside + jnp.where(
                    edge, carry * a[v, s] + jnp.where(layer_all == layer, side[s, v : v + 1, :], 0.0), 0.0
                )
                beside = beside + near[s] * (held[v, new, :] + carry * a[v, s])
                if s > 0:
                    beside = beside + x[v * rows + s - 1, 0:layers, :]
                if s < rows - 1:
                    beside = beside + x[v * rows + s + 1, 0:layers, :]
                res = jacobian_row(jd, jo, state_row, v, s, var_count) - coupling * beside - src[v, s]
                part[v, s] = state_row[v] - step_size * res
    fetch.wait()

    def advanced(s, b, moved):
        place = lax.rem(b, own_blocks)
        before = jnp.where(place == 0, carry, 0.0).astype(f32)
        after = jnp.where(place == own_blocks - 1, carry, 0.0).astype(f32)
        low = pltpu.roll(g[wrapped(b - 1 + total, total), rows + s], 1, 1)
        high = pltpu.roll(g[wrapped(b + 1, total), rows + s], TILE - 1, 1)
        base = g[b, 2 * rows + s]
        base = base + jnp.where(lane == 0, low * before, 0.0) + jnp.where(lane == TILE - 1, high * after, 0.0)
        return base - step_size * moved

    spread = REACH + own_blocks + 1
    for s in range(rows):
        blocks = window_blocks(window(margin, s, first_block, total), first_block, own_blocks, total)
        for t, b in enumerate(blocks[1 : spread - 1] + blocks[spread : spread + own_blocks]):
            p[s, t] = advanced(s, b, pushed[s, t])
    extra = row_flux(
        inner, near_row, window(margin, near_row, first_block, total), q, speeds, scaled, p, pull_table, flux,
        first_block, own_blocks, total,
    )
    start[...] = jnp.full((8, TILE), window(margin, rows - 1 - near_row, first_block, total)).astype(f32)
    for n, (part, layer) in enumerate(((part_r, layers - 1), (part_s, 0))):
        at = slice(layer, layer + 1)
        for v in range(var_count):
            part[v, near_row, at, :] = part[v, near_row, at, :] + extra[n][v : v + 1]


def fourth_kernel(
    bands, outer, part_r, part_s, q, speeds, scaled, p, a_r, a_s, jd_r, jd_s, jo_r, jo_s, pull_table, start,
    away_r, away_s, flux, x_r, x_s, held, out_r, out_s, sems,
):
    var_count, rows, layers, cells = a_r.shape
    own_blocks = cells // TILE
    total = 2 * (outer.shape[0] - 1 - var_count * own_blocks)
    base = jnp.max(start[...]).astype(jnp.int32)
    own_blocks = cells // TILE
    first_block = lax.axis_index("circ") * own_blocks
    end = total // 2 + var_count * own_blocks
    band = lax.axis_index("span")
    odd = jnp.bitwise_and(band, 1)
    far_row = odd * (rows - 1)
    inside = jnp.logical_and(band > 0, band < bands - 1)
    live = jnp.where(inside, carry, 0.0).astype(f32)
    next_row = far_row + 1 - 2 * odd
    for x in (x_r, x_s):
        x[...] = jnp.zeros(x.shape, f32)
    for v in range(var_count):
        for i in range(own_blocks):
            held[v, :, i * TILE : (i + 1) * TILE] = outer[total // 2 + v * own_blocks + i].astype(f32)
    columns = corner_columns(corner_of(outer[end], far_row, rows), cells)
    fields = ((part_r, a_r, jd_r, jo_r, x_r, out_r), (part_s, a_s, jd_s, jo_s, x_s, out_s))
    for n, (part, a, jd, jo, x, out) in enumerate(fields):
        old = slice(n * layers, (n + 1) * layers)
        new = slice((2 + n) * layers, (3 + n) * layers)
        for v in range(var_count):
            x[v, 0:layers, :] = carry * held[v, old, :]
        state_row = [x[v, 0:layers, :] for v in range(var_count)]
        for v in range(var_count):
            wide = x[v]
            beside = (lanes_apart(wide) + layers_apart(wide))[0:layers]
            for s in (0, rows - 1):
                at = (v * rows + s) * 8
                beside = beside + carry * columns[n][at : at + layers]
            extra = carry * (beside + held[v, new, :]) + (carry * live) * a[v, far_row]
            gone = jacobian_row(jd, jo, state_row, v, far_row, var_count)
            for s in range(1, rows - 1):
                out[v, s] = part[v, s]
            out[v, far_row] = part[v, far_row] + state_row[v] - step_size * gone + extra
            out[v, next_row] = part[v, next_row] + carry * state_row[v]
    extra = row_flux(
        outer, far_row, base, q, speeds, scaled, p, pull_table, flux, first_block, own_blocks, total
    )
    copies = []
    for n, (out, away, layer) in enumerate(((out_r, away_r, layers - 1), (out_s, away_s, 0))):
        at = slice(layer, layer + 1)
        for v in range(var_count):
            out[v, far_row, at, :] = out[v, far_row, at, :] + extra[n][v : v + 1]
        copies.append(pltpu.make_async_copy(out, away, sems.at[n]))
        copies[-1].start()
    for copy in copies:
        copy.wait()


def per_device(
    adjoint_rotor,
    adjoint_stator,
    jac_diag_rotor,
    jac_diag_stator,
    jac_off_rotor,
    jac_off_stator,
    source_rotor,
    source_stator,
    rotor_state,
    margin_block,
    face_count,
    margin_weight,
):
    var_count, rows, layers, cells = adjoint_rotor.shape
    own_blocks = cells // TILE
    total = margin_block.shape[1]
    spread = REACH + own_blocks + 1
    field = jax.ShapeDtypeStruct(adjoint_rotor.shape, f32)
    vmem = pl.BlockSpec(memory_space=pltpu.VMEM)
    smem = pl.BlockSpec(memory_space=pltpu.SMEM)
    anywhere = pl.BlockSpec(memory_space=pl.ANY)
    padded = pltpu.VMEM((TILE // 8, 8, cells), f32)

    margin = jnp.swapaxes(margin_block, 1, 2)
    arguments = (
        adjoint_rotor, adjoint_stator, jac_diag_rotor, jac_diag_stator, jac_off_rotor, jac_off_stator,
        source_rotor, source_stator, rotor_state, margin, face_count, margin_weight,
    )
    shapes = [jax.ShapeDtypeStruct(x.shape, x.dtype) for x in arguments]
    v_r, v_s, share, a_r, a_s, weights, margin, count = pl.pallas_call(
        first_kernel,
        out_shape=(
            field, field, jax.ShapeDtypeStruct((own_blocks, 64, TILE), jnp.bfloat16),
            shapes[0], shapes[1], shapes[11], shapes[9], shapes[10],
        ),
        in_specs=[pl.BlockSpec(memory_space=pltpu.HBM)] * 12,
        out_specs=(vmem,) * 8,
        scratch_shapes=[pltpu.VMEM(x.shape, x.dtype) for x in shapes[2:9]]
        + [padded] * 4
        + [pltpu.SemaphoreType.DMA((12,)), pltpu.VMEM((own_blocks, 3 * rows, 8, TILE), f32)],
        compiler_params=params,
        name="local_part",
    )(*[pltpu.with_memory_space_constraint(x, pltpu.HBM) for x in arguments])
    primal_table, pull_table = pl.pallas_call(
        table_kernel,
        out_shape=(
            jax.ShapeDtypeStruct((rows, spread + own_blocks + 2, margin_weight.shape[2], TILE), f32),
            jax.ShapeDtypeStruct((rows, own_blocks + 2, REACH, TILE), f32),
        ),
        in_specs=[vmem] + [smem] * 2,
        out_specs=(vmem,) * 2,
        compiler_params=params,
        name="weight_tables",
    )(weights, margin, count)
    members = lax.axis_size("circ")
    mine, masks = share, []
    mask = members // 2
    while mask > 0:
        hop = mask | 1
        other = lax.ppermute(mine, "circ", [(i, i ^ hop) for i in range(members)])
        if mask > 1:
            mine = jnp.concatenate([mine, other], axis=0)
            if not masks:
                mine, primal_table, pull_table = lax.optimization_barrier((mine, primal_table, pull_table))
            masks.append(hop)
        mask //= 2
    tiles = jax.ShapeDtypeStruct((total // 2 + var_count * own_blocks + 1, 16, TILE), jnp.bfloat16)
    sides = jax.ShapeDtypeStruct((rows, 8, cells), f32)
    corner = jax.ShapeDtypeStruct((8, TILE), f32)
    gathered = jax.ShapeDtypeStruct((total, 3 * rows, 8, TILE), f32)
    listed = jax.ShapeDtypeStruct((rows, spread - 2 + own_blocks, 8, TILE), f32)
    o_r, o_s, side_r, side_s, q, speeds, scaled, pushed, inner, outer, spot, g = pl.pallas_call(
        functools.partial(second_kernel, masks),
        out_shape=(field,) * 2 + (sides,) * 2 + (listed,) * 4 + (tiles,) * 2 + (corner, gathered),
        in_specs=[vmem] * 8 + [anywhere],
        out_specs=(vmem,) * 12,
        scratch_shapes=[
            pltpu.VMEM((rows, spread, 8, TILE), f32),
            pltpu.VMEM((var_count, 4 * layers, cells), f32),
            pltpu.SMEM(margin.shape, jnp.int32),
            pltpu.SemaphoreType.DMA(()),
        ],
        compiler_params=params,
        name="interface_part",
    )(mine, other, v_r, v_s, a_r, a_s, primal_table, pull_table, margin)
    bands = lax.axis_size("span")
    near = [(i, i ^ 1) for i in range(bands)]
    far = [pair for i in range(1, bands - 1, 2) for pair in ((i, i + 1), (i + 1, i))]
    inner = lax.ppermute(inner, "span", near)
    outer = lax.ppermute(outer, "span", far)
    held = pltpu.VMEM((var_count, 4 * layers, cells), f32)
    flux = pltpu.VMEM((spread - 2, 8, TILE), f32)
    listing = pltpu.SMEM(margin.shape, jnp.int32)
    small = pltpu.VMEM((8, 8, cells), f32)
    part_r, part_s, start, p = pl.pallas_call(
        third_kernel,
        out_shape=(field, field, corner, listed),
        in_specs=[vmem] * 20 + [anywhere],
        out_specs=(vmem,) * 4,
        scratch_shapes=[flux, padded, padded, held, listing, pltpu.SemaphoreType.DMA(())],
        compiler_params=params,
        name="near_part",
    )(
        inner, o_r, o_s, side_r, side_s, q, speeds, scaled, pushed, spot, g, a_r, a_s, jac_diag_rotor, jac_diag_stator,
        jac_off_rotor, jac_off_stator, source_rotor, source_stator, pull_table, margin,
    )
    out_r, out_s = pl.pallas_call(
        functools.partial(fourth_kernel, bands),
        out_shape=(field, field),
        in_specs=[vmem] * 15,
        out_specs=(anywhere,) * 2,
        scratch_shapes=[
            flux, small, small, held, pltpu.VMEM(field.shape, f32), pltpu.VMEM(field.shape, f32),
            pltpu.SemaphoreType.DMA((2,)),
        ],
        compiler_params=params,
        name="final_part",
    )(
        outer, part_r, part_s, q, speeds, scaled, p, a_r, a_s, jac_diag_rotor, jac_diag_stator,
        jac_off_rotor, jac_off_stator, pull_table, start,
    )
    return (out_r, out_s)


def solution(mesh):
    field = P(None, "span", None, "circ")
    placed = (
        (field,) * 4
        + (P(None, None, "span", None, "circ"),) * 2
        + (field,) * 2
        + (P(None, "span", "circ"), P("span", None, None), P("span", None), P("span", None, None, None))
    )
    return jax.shard_map(
        per_device, mesh=mesh, in_specs=placed, out_specs=(field, field), check_vma=False
    )
```

```python
import functools

import jax
import jax.numpy as jnp
from jax import lax
from jax.experimental import pallas as pl
from jax.experimental.pallas import tpu as pltpu
from jax.sharding import PartitionSpec as P

step_size = 0.1
coupling = 0.2
carry = step_size * coupling
REACH = 8
TILE = 128
f32 = jnp.float32
params = pltpu.CompilerParams(vmem_limit_bytes=24 * 1024 * 1024)


def iota(shape, dim):
    return lax.broadcasted_iota(jnp.int32, shape, dim)


def wrapped(x, count):
    if count & (count - 1) == 0:
        return jnp.bitwise_and(x, count - 1)
    return lax.rem(x + 4 * count, count)


def lanes_apart(x):
    cells = x.shape[1]
    lane = iota(x.shape, 1)
    before = jnp.where(lane == 0, 0.0, pltpu.roll(x, 1, 1))
    after = jnp.where(lane == cells - 1, 0.0, pltpu.roll(x, cells - 1, 1))
    return before + after


def layers_apart(x):
    return pltpu.roll(x, 1, 0) + pltpu.roll(x, 7, 0)


def edge_pick(row, cells):
    at = iota((8, cells), 0)
    lane = iota((8, cells), 1)
    first = jnp.logical_and(at == row, lane == 0)
    last = jnp.logical_and(at == 4 + row, lane == cells - 1)
    return jnp.where(jnp.logical_or(first, last), 1.0, 0.0).astype(f32)


def split(x):
    high = x.astype(jnp.bfloat16).astype(f32)
    return high, x - high


def flux_parts(primal):
    square = primal * primal
    under = 6.0 + jnp.sum(square, axis=0, keepdims=True)
    return jnp.sqrt(1.0 + square), 0.5 * primal / under


def flux_of(primal, speeds, scaled, adjoint):
    return speeds * adjoint + scaled * jnp.sum(primal * adjoint, axis=0, keepdims=True)


def jacobian_row(diag, off, state, v, s, var_count):
    total = diag[v, s] * state[v]
    for w in range(var_count):
        total = total + off[w, v, s].astype(f32) * state[w]
    return total


def pull_row(flux, table, s, slot):
    acc = jnp.zeros((8, TILE), f32)
    for e in range(REACH):
        acc = acc + table[s, slot + 1, e : e + 1, :] * flux(slot + e)
    return acc


def window(margin, s, first_block, total):
    return first_block - margin[s, 0, 0] - 5 + 4 * total


def window_blocks(base, first_block, own_blocks, total):
    found = [wrapped(base - 1 + t, total) for t in range(REACH + own_blocks + 1)]
    sides = [wrapped(first_block - 1 + total, total), wrapped(first_block + own_blocks, total)]
    return found + [first_block + i for i in range(own_blocks)] + sides


def table_kernel(weights, margin, count, primal_table, pull_table):
    rows, total, entries, _ = weights.shape
    own_blocks = pull_table.shape[1] - 2
    first_block = lax.axis_index("circ") * own_blocks
    for s in range(rows):
        base = window(margin, s, first_block, total)
        blocks = window_blocks(base, first_block, own_blocks, total)
        entry = iota((entries, TILE), 0)
        for t, b in enumerate(blocks):
            primal_table[s, t] = jnp.where(entry < count[s, b], weights[s, b], 0.0)
        for slot in range(-1, own_blocks + 1):
            target = wrapped(first_block + slot + total, total)
            for e in range(REACH):
                b = blocks[slot + 1 + e]
                k = wrapped(target - margin[s, 0, b] + total, total)
                live = jnp.where(k < count[s, b], 1.0, 0.0).astype(f32)
                kept = jnp.minimum(k, entries - 1)
                pull_table[s, slot + 1, e : e + 1, :] = weights[s, b, pl.ds(kept, 1), :] * live


def first_kernel(*refs):
    outer, refs = refs[:12], refs[12:]
    v_r, v_s, out, a_r, a_s, weights, margin, count = refs[:8]
    jd_r, jd_s, jo_r, jo_s, src_r, src_s, state = refs[8:15]
    xs, sems, wide_out = refs[15:19], refs[19], refs[20]
    var_count, rows, layers, cells = a_r.shape
    own_blocks = cells // TILE
    inner = (a_r, a_s, jd_r, jd_s, jo_r, jo_s, src_r, src_s, state, margin, count, weights)
    copies = [pltpu.make_async_copy(x, y, sems.at[n]) for n, (x, y) in enumerate(zip(outer, inner))]
    for copy in copies:
        copy.start()
    wide_out[...] = jnp.zeros(wide_out.shape, f32)
    for x in xs:
        x[...] = jnp.zeros(x.shape, f32)
    for copy in copies:
        copy.wait()
    fields = ((a_r, jd_r, jo_r, src_r, v_r, xs[0], xs[2]), (a_s, jd_s, jo_s, src_s, v_s, xs[1], xs[3]))
    for a, jd, jo, src, partial, x_a, x_p in fields:
        for v in range(var_count):
            for s in range(rows):
                x_a[v * rows + s, 0:layers, :] = a[v, s]
        for s in range(rows):
            state_row = [a[v, s] for v in range(var_count)]
            for v in range(var_count):
                wide = x_a[v * rows + s]
                beside = (lanes_apart(wide) + layers_apart(wide))[0:layers]
                if s > 0:
                    beside = beside + a[v, s - 1]
                if s < rows - 1:
                    beside = beside + a[v, s + 1]
                res = jacobian_row(jd, jo, state_row, v, s, var_count) - coupling * beside - src[v, s]
                new = state_row[v] - step_size * res
                partial[v, s] = new
                x_p[v * rows + s, 0:layers, :] = new
    edges = jnp.zeros((8, TILE), f32)
    for q in range(4):
        flat = xs[q][...].reshape(TILE, cells)
        edges = edges + lax.dot_general(
            edge_pick(q, cells), flat, (((1,), (1,)), ((), ())), preferred_element_type=f32
        )
    for v in range(var_count):
        rotor = state[v].astype(f32)
        for s in range(rows):
            for i in range(own_blocks):
                cut = slice(i * TILE, (i + 1) * TILE)
                wide_out[i, s, v : v + 1, :] = rotor[s : s + 1, cut]
                wide_out[i, rows + s, v : v + 1, :] = a_s[v, s, 0:1, cut]
                wide_out[i, 2 * rows + s, v : v + 1, :] = v_s[v, s, 0:1, cut]
    row8 = iota((8, TILE), 0)
    filled = row8 < var_count
    for i in range(own_blocks):
        if i in (0, own_blocks - 1):
            side = 4 if i else 0
            for s in range(rows):
                wide_out[i, 2 * rows + s, 6:8, :] = edges[side + 2 * s : side + 2 * s + 2]
        groups = []
        for s in range(rows):
            p_high, p_rest = split(wide_out[i, rows + s])
            u_high, u_rest = split(wide_out[i, 2 * rows + s])
            groups.append((
                jnp.where(filled, wide_out[i, s], pltpu.roll(u_rest, 6, 0)),
                jnp.where(filled, p_high, pltpu.roll(u_rest, 4, 0)),
                jnp.where(filled, p_rest, pltpu.roll(u_rest, 2, 0)),
                u_high,
            ))
        for n in range(4):
            out[i, n * 16 : n * 16 + 16, :] = jnp.concatenate([x[n] for x in groups], axis=0).astype(jnp.bfloat16)


def second_kernel(
    masks, mine, other, v_r, v_s, a_r, a_s, primal_table, pull_table, margin_in,
    o_r, o_s, side_r, side_s, q_out, speeds_out, scaled_out, moved_out, inner, outer, spot, g, flux, held, margin, sem,
):
    var_count, rows, layers, cells = a_r.shape
    fetch = pltpu.make_async_copy(margin_in, margin, sem)
    fetch.start()
    total = 2 * mine.shape[0]
    own_blocks = cells // TILE
    entries = primal_table.shape[2]
    spread = REACH + own_blocks + 1
    first_block = lax.axis_index("circ") * own_blocks
    row8 = iota((8, TILE), 0)
    layer_all = iota((layers, cells), 0)
    left = wrapped(first_block - 1 + total, total)
    right = wrapped(first_block + own_blocks, total)

    filled = row8 < var_count
    here = lax.axis_index("circ")
    for at in range(total):
        half, part = divmod(at, total // 2)
        place, i = divmod(part, own_blocks)
        mask = half
        for n, m in enumerate(masks):
            mask ^= m if place >> n & 1 else 0
        b = jnp.bitwise_xor(here, mask) * own_blocks + i
        whole = other if half else mine
        tiles = [whole[part, n * 16 : n * 16 + 16, :].astype(f32) for n in range(4)]
        for s in range(rows):
            rotor, p_high, p_rest, u_high = [x[s * 8 : s * 8 + 8] for x in tiles]
            u_rest = jnp.where(
                row8 < 2, pltpu.roll(rotor, 2, 0), jnp.where(row8 < 4, pltpu.roll(p_high, 4, 0), pltpu.roll(p_rest, 6, 0))
            )
            g[b, s] = rotor
            g[b, rows + s] = p_high + p_rest
            g[b, 2 * rows + s] = u_high + jnp.where(filled, u_rest, 0.0)
    spot[0:2, :] = g[left, 2 * rows, 6:8, :]
    spot[2:4, :] = g[left, 2 * rows + 1, 6:8, :]
    spot[4:6, :] = g[right, 2 * rows, 6:8, :]
    spot[6:8, :] = g[right, 2 * rows + 1, 6:8, :]
    spots = spot[...]
    columns = [
        lax.dot_general(spots, edge_pick(q, cells), (((0,), (0,)), ((), ())), preferred_element_type=f32)
        for q in range(2)
    ]

    last = jnp.concatenate([spots, jnp.ones((8, TILE), f32)], axis=0).astype(jnp.bfloat16)
    odd = jnp.bitwise_and(lax.axis_index("span"), 1)
    ends = ((inner, (1 - odd) * (rows - 1)), (outer, odd * (rows - 1)))
    for to, s in ends:
        for j in range(total // 2):
            to[j] = jnp.concatenate([g[2 * j, rows + s], g[2 * j + 1, rows + s]], axis=0).astype(jnp.bfloat16)
        to[total // 2 + var_count * own_blocks] = last
    fetch.wait()

    def block(s, b, t):
        primal = jnp.zeros((8, TILE), f32)
        for k in range(entries):
            primal = primal + primal_table[s, t, k : k + 1, :] * g[margin[s, k, b], s]
        primal = jnp.where(filled, primal, 0.0)
        parts = flux_parts(primal)
        return (primal, *parts), flux_of(primal, *parts, g[b, rows + s])

    def keep(s, at, b, parts, moved):
        q_out[s, at], speeds_out[s, at], scaled_out[s, at] = parts
        moved_out[s, at] = moved

    for s in range(rows):
        base = window(margin, s, first_block, total)
        blocks = window_blocks(base, first_block, own_blocks, total)
        for t in range(spread):
            parts, moved = block(s, blocks[t], t)
            flux[s, t] = moved.astype(jnp.bfloat16).astype(f32)
            if 0 < t < spread - 1:
                keep(s, t - 1, blocks[t], parts, moved)
        own = []
        for i in range(own_blocks):
            parts, moved = block(s, first_block + i, spread + i)
            own.append(moved)
            keep(s, spread - 2 + i, first_block + i, parts, moved)
        blank = [jnp.zeros((8, TILE), f32)] * (own_blocks - 2)
        side_flux = [block(s, at, spread + own_blocks + n)[1] for n, at in enumerate((left, right))]
        pulls = [pull_row(lambda t: flux[s, t + 1], pull_table, s, slot) for slot in range(-1, own_blocks + 1)]

        def at_sides(low, high):
            return jnp.concatenate([pltpu.roll(low, 1, 1), *blank, pltpu.roll(high, TILE - 1, 1)], axis=1)

        pulled = step_size * jnp.concatenate(pulls[1:-1], axis=1)
        side_r[s] = step_size * at_sides(pulls[0], pulls[-1])
        pushed = step_size * jnp.concatenate(own, axis=1)
        side_s[s] = -step_size * at_sides(*side_flux)
        for v in range(var_count):
            at = (v * rows + s) * 8
            cut = slice(at, at + layers)
            o_r[v, s] = (
                v_r[v, s] + carry * columns[0][cut] + jnp.where(layer_all == layers - 1, pulled[v : v + 1], 0.0)
            )
            o_s[v, s] = v_s[v, s] + carry * columns[1][cut] - jnp.where(layer_all == 0, pushed[v : v + 1], 0.0)

    for to, s in ends:
        for v in range(var_count):
            for n, ref in enumerate((a_r, a_s, o_r, o_s)):
                held[v, n * layers : (n + 1) * layers, :] = ref[v, s]
            for i in range(own_blocks):
                to[total // 2 + v * own_blocks + i] = held[v, :, i * TILE : (i + 1) * TILE].astype(jnp.bfloat16)


def corner_of(tile, row, rows):
    lane = iota((8, TILE), 1)
    group = lax.rem(lax.shift_right_logical(lane, 3), rows)
    spot = tile.astype(f32)[0:8]
    first = jnp.where(group == 0, pltpu.roll(spot, (TILE - 8 * (rows - 1)) % TILE, 1), 0.0)
    final = jnp.where(group == rows - 1, pltpu.roll(spot, 8 * (rows - 1), 1), 0.0)
    return jnp.where(row == 0, first, final)


def corner_columns(corner, cells):
    return [
        lax.dot_general(corner, edge_pick(n, cells), (((0,), (0,)), ((), ())), preferred_element_type=f32)
        for n in range(2)
    ]


def row_flux(halo, row, base, q, speeds, scaled, p, pull_table, flux, first_block, own_blocks, total):
    spread = REACH + own_blocks + 1
    own = []
    for t in range(spread - 2 + own_blocks):
        b = wrapped(base + t, total) if t < spread - 2 else first_block + t - (spread - 2)
        both = halo[lax.shift_right_logical(b, 1)].astype(f32)
        beyond = jnp.where(jnp.bitwise_and(b, 1) == 1, both[8:16], both[0:8])
        moved = flux_of(q[row, t], speeds[row, t], scaled[row, t], p[row, t] + carry * beyond)
        if t < spread - 2:
            flux[t] = moved.astype(jnp.bfloat16).astype(f32)
        else:
            own.append(moved)
    pulls = [pull_row(lambda t: flux[t], pull_table, row, slot) for slot in range(own_blocks)]
    return step_size * jnp.concatenate(pulls, axis=1), -step_size * jnp.concatenate(own, axis=1)


def third_kernel(
    inner, o_r, o_s, side_r, side_s, q, speeds, scaled, pushed, spot, g, a_r, a_s, jd_r, jd_s, jo_r, jo_s, src_r, src_s,
    pull_table, margin_in, part_r, part_s, start, p, flux, x_r, x_s, held, margin, sem,
):
    fetch = pltpu.make_async_copy(margin_in, margin, sem)
    fetch.start()
    var_count, rows, layers, cells = a_r.shape
    total = margin.shape[2]
    own_blocks = cells // TILE
    first_block = lax.axis_index("circ") * own_blocks
    end = total // 2 + var_count * own_blocks
    near_row = (1 - jnp.bitwise_and(lax.axis_index("span"), 1)) * (rows - 1)
    near = [jnp.where(near_row == s, 1.0, 0.0).astype(f32) for s in range(rows)]
    for x in (x_r, x_s):
        x[...] = jnp.zeros(x.shape, f32)
    for v in range(var_count):
        for i in range(own_blocks):
            held[v, :, i * TILE : (i + 1) * TILE] = inner[total // 2 + v * own_blocks + i].astype(f32)
    lane_all = iota((layers, cells), 1)
    layer_all = iota((layers, cells), 0)
    lane = iota((8, TILE), 1)
    edge = jnp.logical_or(lane_all == 0, lane_all == cells - 1)
    beyond = [
        lax.dot_general(spot[...], edge_pick(n, cells), (((0,), (0,)), ((), ())), preferred_element_type=f32)
        for n in (2, 3)
    ]
    columns = corner_columns(corner_of(inner[end], near_row, rows), cells)
    fields = (
        (o_r, side_r, a_r, jd_r, jo_r, src_r, x_r, part_r, layers - 1),
        (o_s, side_s, a_s, jd_s, jo_s, src_s, x_s, part_s, 0),
    )
    for n, (o, side, a, jd, jo, src, x, part, layer) in enumerate(fields):
        old = slice(n * layers, (n + 1) * layers)
        new = slice((2 + n) * layers, (3 + n) * layers)
        for v in range(var_count):
            for s in range(rows):
                x[v * rows + s, 0:layers, :] = o[v, s] + (carry * near[s]) * held[v, old, :]
        for s in range(rows):
            state_row = [x[v * rows + s, 0:layers, :] for v in range(var_count)]
            for v in range(var_count):
                wide = x[v * rows + s]
                at = (v * rows + s) * 8
                beside = (lanes_apart(wide) + layers_apart(wide))[0:layers]
                beside = beside + beyond[n][at : at + layers] + carry * columns[n][at : at + layers]
                beside = beside + jnp.where(
                    edge, carry * a[v, s] + jnp.where(layer_all == layer, side[s, v : v + 1, :], 0.0), 0.0
                )
                beside = beside + near[s] * (held[v, new, :] + carry * a[v, s])
                if s > 0:
                    beside = beside + x[v * rows + s - 1, 0:layers, :]
                if s < rows - 1:
                    beside = beside + x[v * rows + s + 1, 0:layers, :]
                res = jacobian_row(jd, jo, state_row, v, s, var_count) - coupling * beside - src[v, s]
                part[v, s] = state_row[v] - step_size * res
    fetch.wait()

    def advanced(s, b, moved):
        place = lax.rem(b, own_blocks)
        before = jnp.where(place == 0, carry, 0.0).astype(f32)
        after = jnp.where(place == own_blocks - 1, carry, 0.0).astype(f32)
        low = pltpu.roll(g[wrapped(b - 1 + total, total), rows + s], 1, 1)
        high = pltpu.roll(g[wrapped(b + 1, total), rows + s], TILE - 1, 1)
        base = g[b, 2 * rows + s]
        base = base + jnp.where(lane == 0, low * before, 0.0) + jnp.where(lane == TILE - 1, high * after, 0.0)
        return base - step_size * moved

    spread = REACH + own_blocks + 1
    for s in range(rows):
        blocks = window_blocks(window(margin, s, first_block, total), first_block, own_blocks, total)
        for t, b in enumerate(blocks[1 : spread - 1] + blocks[spread : spread + own_blocks]):
            p[s, t] = advanced(s, b, pushed[s, t])
    extra = row_flux(
        inner, near_row, window(margin, near_row, first_block, total), q, speeds, scaled, p, pull_table, flux,
        first_block, own_blocks, total,
    )
    start[...] = jnp.full((8, TILE), window(margin, rows - 1 - near_row, first_block, total)).astype(f32)
    for n, (part, layer) in enumerate(((part_r, layers - 1), (part_s, 0))):
        at = slice(layer, layer + 1)
        for v in range(var_count):
            part[v, near_row, at, :] = part[v, near_row, at, :] + extra[n][v : v + 1]


def fourth_kernel(
    bands, outer, part_r, part_s, q, speeds, scaled, p, a_r, a_s, jd_r, jd_s, jo_r, jo_s, pull_table, start,
    away_r, away_s, flux, x_r, x_s, held, out_r, out_s, sems,
):
    var_count, rows, layers, cells = a_r.shape
    own_blocks = cells // TILE
    total = 2 * (outer.shape[0] - 1 - var_count * own_blocks)
    base = jnp.max(start[...]).astype(jnp.int32)
    own_blocks = cells // TILE
    first_block = lax.axis_index("circ") * own_blocks
    end = total // 2 + var_count * own_blocks
    band = lax.axis_index("span")
    odd = jnp.bitwise_and(band, 1)
    far_row = odd * (rows - 1)
    inside = jnp.logical_and(band > 0, band < bands - 1)
    live = jnp.where(inside, carry, 0.0).astype(f32)
    next_row = far_row + 1 - 2 * odd
    for x in (x_r, x_s):
        x[...] = jnp.zeros(x.shape, f32)
    for v in range(var_count):
        for i in range(own_blocks):
            held[v, :, i * TILE : (i + 1) * TILE] = outer[total // 2 + v * own_blocks + i].astype(f32)
    columns = corner_columns(corner_of(outer[end], far_row, rows), cells)
    fields = ((part_r, a_r, jd_r, jo_r, x_r, out_r), (part_s, a_s, jd_s, jo_s, x_s, out_s))
    for n, (part, a, jd, jo, x, out) in enumerate(fields):
        old = slice(n * layers, (n + 1) * layers)
        new = slice((2 + n) * layers, (3 + n) * layers)
        for v in range(var_count):
            x[v, 0:layers, :] = carry * held[v, old, :]
        state_row = [x[v, 0:layers, :] for v in range(var_count)]
        for v in range(var_count):
            wide = x[v]
            beside = (lanes_apart(wide) + layers_apart(wide))[0:layers]
            for s in (0, rows - 1):
                at = (v * rows + s) * 8
                beside = beside + carry * columns[n][at : at + layers]
            extra = carry * (beside + held[v, new, :]) + (carry * live) * a[v, far_row]
            gone = jacobian_row(jd, jo, state_row, v, far_row, var_count)
            for s in range(rows):
                out[v, s] = part[v, s]
            out[v, far_row] = part[v, far_row] + state_row[v] - step_size * gone + extra
            out[v, next_row] = part[v, next_row] + carry * state_row[v]
    extra = row_flux(
        outer, far_row, base, q, speeds, scaled, p, pull_table, flux, first_block, own_blocks, total
    )
    copies = []
    for n, (out, away, layer) in enumerate(((out_r, away_r, layers - 1), (out_s, away_s, 0))):
        at = slice(layer, layer + 1)
        for v in range(var_count):
            out[v, far_row, at, :] = out[v, far_row, at, :] + extra[n][v : v + 1]
        copies.append(pltpu.make_async_copy(out, away, sems.at[n]))
        copies[-1].start()
    for copy in copies:
        copy.wait()


def per_device(
    adjoint_rotor,
    adjoint_stator,
    jac_diag_rotor,
    jac_diag_stator,
    jac_off_rotor,
    jac_off_stator,
    source_rotor,
    source_stator,
    rotor_state,
    margin_block,
    face_count,
    margin_weight,
):
    var_count, rows, layers, cells = adjoint_rotor.shape
    own_blocks = cells // TILE
    total = margin_block.shape[1]
    spread = REACH + own_blocks + 1
    field = jax.ShapeDtypeStruct(adjoint_rotor.shape, f32)
    vmem = pl.BlockSpec(memory_space=pltpu.VMEM)
    smem = pl.BlockSpec(memory_space=pltpu.SMEM)
    anywhere = pl.BlockSpec(memory_space=pl.ANY)
    padded = pltpu.VMEM((TILE // 8, 8, cells), f32)

    margin = jnp.swapaxes(margin_block, 1, 2)
    arguments = (
        adjoint_rotor, adjoint_stator, jac_diag_rotor, jac_diag_stator, jac_off_rotor, jac_off_stator,
        source_rotor, source_stator, rotor_state, margin, face_count, margin_weight,
    )
    shapes = [jax.ShapeDtypeStruct(x.shape, x.dtype) for x in arguments]
    v_r, v_s, share, a_r, a_s, weights, margin, count = pl.pallas_call(
        first_kernel,
        out_shape=(
            field, field, jax.ShapeDtypeStruct((own_blocks, 64, TILE), jnp.bfloat16),
            shapes[0], shapes[1], shapes[11], shapes[9], shapes[10],
        ),
        in_specs=[pl.BlockSpec(memory_space=pltpu.HBM)] * 12,
        out_specs=(vmem,) * 8,
        scratch_shapes=[pltpu.VMEM(x.shape, x.dtype) for x in shapes[2:9]]
        + [padded] * 4
        + [pltpu.SemaphoreType.DMA((12,)), pltpu.VMEM((own_blocks, 3 * rows, 8, TILE), f32)],
        compiler_params=params,
        name="local_part",
    )(*[pltpu.with_memory_space_constraint(x, pltpu.HBM) for x in arguments])
    primal_table, pull_table = pl.pallas_call(
        table_kernel,
        out_shape=(
            jax.ShapeDtypeStruct((rows, spread + own_blocks + 2, margin_weight.shape[2], TILE), f32),
            jax.ShapeDtypeStruct((rows, own_blocks + 2, REACH, TILE), f32),
        ),
        in_specs=[vmem] + [smem] * 2,
        out_specs=(vmem,) * 2,
        compiler_params=params,
        name="weight_tables",
    )(weights, margin, count)
    members = lax.axis_size("circ")
    mine, masks = share, []
    mask = members // 2
    while mask > 0:
        hop = mask | 1
        other = lax.ppermute(mine, "circ", [(i, i ^ hop) for i in range(members)])
        if mask > 1:
            mine = jnp.concatenate([mine, other], axis=0)
            if not masks:
                mine, primal_table, pull_table = lax.optimization_barrier((mine, primal_table, pull_table))
            masks.append(hop)
        mask //= 2
    tiles = jax.ShapeDtypeStruct((total // 2 + var_count * own_blocks + 1, 16, TILE), jnp.bfloat16)
    sides = jax.ShapeDtypeStruct((rows, 8, cells), f32)
    corner = jax.ShapeDtypeStruct((8, TILE), f32)
    gathered = jax.ShapeDtypeStruct((total, 3 * rows, 8, TILE), f32)
    listed = jax.ShapeDtypeStruct((rows, spread - 2 + own_blocks, 8, TILE), f32)
    o_r, o_s, side_r, side_s, q, speeds, scaled, pushed, inner, outer, spot, g = pl.pallas_call(
        functools.partial(second_kernel, masks),
        out_shape=(field,) * 2 + (sides,) * 2 + (listed,) * 4 + (tiles,) * 2 + (corner, gathered),
        in_specs=[vmem] * 8 + [anywhere],
        out_specs=(vmem,) * 12,
        scratch_shapes=[
            pltpu.VMEM((rows, spread, 8, TILE), f32),
            pltpu.VMEM((var_count, 4 * layers, cells), f32),
            pltpu.SMEM(margin.shape, jnp.int32),
            pltpu.SemaphoreType.DMA(()),
        ],
        compiler_params=params,
        name="interface_part",
    )(mine, other, v_r, v_s, a_r, a_s, primal_table, pull_table, margin)
    bands = lax.axis_size("span")
    near = [(i, i ^ 1) for i in range(bands)]
    far = [pair for i in range(1, bands - 1, 2) for pair in ((i, i + 1), (i + 1, i))]
    inner = lax.ppermute(inner, "span", near)
    outer = lax.ppermute(outer, "span", far)
    held = pltpu.VMEM((var_count, 4 * layers, cells), f32)
    flux = pltpu.VMEM((spread - 2, 8, TILE), f32)
    listing = pltpu.SMEM(margin.shape, jnp.int32)
    small = pltpu.VMEM((8, 8, cells), f32)
    part_r, part_s, start, p = pl.pallas_call(
        third_kernel,
        out_shape=(field, field, corner, listed),
        in_specs=[vmem] * 20 + [anywhere],
        out_specs=(vmem,) * 4,
        scratch_shapes=[flux, padded, padded, held, listing, pltpu.SemaphoreType.DMA(())],
        compiler_params=params,
        name="near_part",
    )(
        inner, o_r, o_s, side_r, side_s, q, speeds, scaled, pushed, spot, g, a_r, a_s, jac_diag_rotor, jac_diag_stator,
        jac_off_rotor, jac_off_stator, source_rotor, source_stator, pull_table, margin,
    )
    out_r, out_s = pl.pallas_call(
        functools.partial(fourth_kernel, bands),
        out_shape=(field, field),
        in_specs=[vmem] * 15,
        out_specs=(anywhere,) * 2,
        scratch_shapes=[
            flux, small, small, held, pltpu.VMEM(field.shape, f32), pltpu.VMEM(field.shape, f32),
            pltpu.SemaphoreType.DMA((2,)),
        ],
        compiler_params=params,
        name="final_part",
    )(
        outer, part_r, part_s, q, speeds, scaled, p, a_r, a_s, jac_diag_rotor, jac_diag_stator,
        jac_off_rotor, jac_off_stator, pull_table, start,
    )
    return (out_r, out_s)


def solution(mesh):
    field = P(None, "span", None, "circ")
    placed = (
        (field,) * 4
        + (P(None, None, "span", None, "circ"),) * 2
        + (field,) * 2
        + (P(None, "span", "circ"), P("span", None, None), P("span", None), P("span", None, None, None))
    )
    return jax.shard_map(
        per_device, mesh=mesh, in_specs=placed, out_specs=(field, field), check_vma=False
    )
```
